32 devices in a mesh: ctx: 16 (over z, y, core), fsdp: 2 (over x).
Axes of the slice: x: 2, y: 2, z: 4, core: 2. Of those that a mesh axis runs over, the one named last changes fastest.
Arguments:
- hidden: bfloat16 [1024, 4, 2048], P('ctx', 'fsdp'), may hold values from -6 to 6
- cotangent: bfloat16 [1024, 4, 2048], P('ctx', 'fsdp'), may hold values from -6 to 6
- pairing: int32 [16], replicated, may hold values from 0 to 15, each once
- ln1_gain: bfloat16 [2048], P(('ctx', 'fsdp')), may hold values from 0.5 to 1.5
- ln1_bias: bfloat16 [2048], P(('ctx', 'fsdp')), may hold values from -3 to 3
- qkv_weight: bfloat16 [2048, 6144], P(('ctx', 'fsdp')), may hold values from -0.125 to 0.125
- qkv_bias: bfloat16 [6144], P(('ctx', 'fsdp')), may hold values from -3 to 3
- out_weight: bfloat16 [2048, 2048], P(('ctx', 'fsdp')), may hold values from -2 to 2
- out_bias: bfloat16 [2048], P(('ctx', 'fsdp')), may hold values from -3 to 3
- ln2_gain: bfloat16 [2048], P(('ctx', 'fsdp')), may hold values from 0.5 to 1.5
- ln2_bias: bfloat16 [2048], P(('ctx', 'fsdp')), may hold values from -3 to 3
- up_weight: bfloat16 [2048, 8192], P(('ctx', 'fsdp')), may hold values from -0.125 to 0.125
- up_bias: bfloat16 [8192], P(('ctx', 'fsdp')), may hold values from -3 to 3
- down_weight: bfloat16 [2048, 8192], P(('ctx', 'fsdp')), may hold values from -0.0625 to 0.0625
- down_bias: bfloat16 [2048], P(('ctx', 'fsdp')), may hold values from -3 to 3
Outputs:
- output: bfloat16 [1024, 4, 2048], P('ctx', 'fsdp')
- grad_hidden: float32 [1024, 4, 2048], P('ctx', 'fsdp')
- grad_ln1_gain: float32 [2048], P(('ctx', 'fsdp'))
- grad_ln1_bias: float32 [2048], P(('ctx', 'fsdp'))
- grad_qkv_weight: float32 [2048, 6144], P(('ctx', 'fsdp'))
- grad_qkv_bias: float32 [6144], P(('ctx', 'fsdp'))
- grad_out_weight: float32 [2048, 2048], P(('ctx', 'fsdp'))
- grad_out_bias: float32 [2048], P(('ctx', 'fsdp'))
- grad_ln2_gain: float32 [2048], P(('ctx', 'fsdp'))
- grad_ln2_bias: float32 [2048], P(('ctx', 'fsdp'))
- grad_up_weight: float32 [2048, 8192], P(('ctx', 'fsdp'))
- grad_up_bias: float32 [8192], P(('ctx', 'fsdp'))
- grad_down_weight: float32 [2048, 8192], P(('ctx', 'fsdp'))
- grad_down_bias: float32 [2048], P(('ctx', 'fsdp'))
The draws below stay inside these ranges and needn't reach their ends.
Inputs may be any that keep to these rules, and one draw needn't show every extreme that they name: `pairing`: each device number appears once.
All inputs are finite; a program needn't handle non-finite values.
Results may differ from the reference program's by a relative error of at most 0.0095.
Values may be sent and summed in bfloat16 or wider, within the bound.
A program may use at most 640 MiB of HBM per device.

```python
import jax
import jax.numpy as jnp
from jax import lax

D = 2048
HEADS = 8
HEAD = 256
ROT = 64
FF = 8192
BLK = 32
LENGTH = 1024
BATCH = 4
N_CTX = 16


def spiked(values, key, source, target, shards_of, factor):
    owner, partner = [(jnp.arange(values.shape[position]) // (values.shape[position] // shards_of)).reshape([-1 if axis == position else 1 for axis in range(values.ndim)]) for position in (source, target)]
    chosen = jax.random.permutation(key, shards_of)[partner]
    strong = (owner == chosen) | (owner == (partner + shards_of // 2) % shards_of)
    return jnp.where(strong, factor * values, values)


def block_levels(own_key, extent, pieces, least, largest):
    def one(position, shards_of):
        steps = jax.random.uniform(jax.random.fold_in(jax.random.fold_in(own_key, 6), position), (shards_of,), jnp.float32, least / len(pieces), largest / len(pieces))
        return jnp.repeat(jnp.exp(steps), extent[position] // shards_of).reshape((-1,) + (1,) * (len(extent) - position - 1))

    loudness = one(*pieces[0])
    for cut in pieces[1:]:
        loudness = loudness * one(*cut)
    return loudness


def centred(own_key, dims, scale, limit, split=(), kind=jnp.bfloat16):
    entries = scale * jax.random.normal(own_key, dims, jnp.float32)
    if split:
        entries = entries * block_levels(own_key, dims, split, -0.22, 0.18)
    return jnp.clip(entries, -limit, limit).astype(kind)


def heavy_noise(own_key, extent, scale, limit, shards, heavy, held_as=jnp.bfloat16):
    drawn = scale * jax.random.normal(own_key, extent, jnp.float32)
    if shards:
        drawn = drawn * block_levels(own_key, extent, shards, -0.22, 0.18)
    return jnp.clip(spiked(drawn, jax.random.fold_in(own_key, 3), *heavy), -limit, limit).astype(held_as)


def setup_inputs(seed: int = 0) -> dict:
    streams_of = jax.random.split(jax.random.key(seed), 16)
    hidden = centred(streams_of[0], (LENGTH, BATCH, D), 1.0, 6.0, ((0, 16), (1, 2)))
    cotangent = heavy_noise(streams_of[1], (LENGTH, BATCH, D), 1.0, 6.0, ((0, 16), (1, 2)), (0, 2, 16, 2.0))
    pairing = jax.random.permutation(streams_of[2], N_CTX).astype(jnp.int32)
    ln1_gain = jnp.clip(1.0 + 0.1 * jax.random.normal(streams_of[3], (D,), jnp.float32), 0.5, 1.5).astype(jnp.bfloat16)
    ln1_bias = centred(streams_of[4], (D,), 0.3, 3.0, ((0, 32),))
    qkv_weight = centred(streams_of[5], (D, 3 * D), D ** -0.5, 0.125, ((0, 32),))
    qkv_bias = centred(streams_of[6], (3 * D,), 0.5, 3.0, ((0, 32),))
    out_weight = centred(streams_of[7], (D, D), (max(D // 256, 1)) ** -0.5, 2.0, ((0, 32),))
    out_bias = centred(streams_of[8], (D,), 0.5, 3.0, ((0, 32),))
    ln2_gain = jnp.clip(1.0 + 0.1 * jax.random.normal(streams_of[9], (D,), jnp.float32), 0.5, 1.5).astype(jnp.bfloat16)
    ln2_bias = centred(streams_of[10], (D,), 0.3, 3.0, ((0, 32),))
    up_weight = centred(streams_of[11], (D, FF), D ** -0.5, 0.125, ((0, 32),))
    up_bias = centred(streams_of[12], (FF,), 0.5, 3.0, ((0, 32),))
    down_weight = centred(streams_of[13], (D, FF), FF ** -0.5, 0.0625, ((0, 32),))
    down_bias = centred(streams_of[14], (D,), 0.5, 3.0, ((0, 32),))
    return {"hidden": hidden, "cotangent": cotangent, "pairing": pairing, "ln1_gain": ln1_gain, "ln1_bias": ln1_bias, "qkv_weight": qkv_weight, "qkv_bias": qkv_bias, "out_weight": out_weight, "out_bias": out_bias, "ln2_gain": ln2_gain, "ln2_bias": ln2_bias, "up_weight": up_weight, "up_bias": up_bias, "down_weight": down_weight, "down_bias": down_bias}


@jax.custom_vjp
def low(v):
    return lax.optimization_barrier(v.astype(jnp.bfloat16)).astype(jnp.float32)

@jax.custom_vjp
def low_back(v):
    return v

def low_keep(v):
    return (low(v), None)

def low_pass(kept, grad):
    return (grad,)

def back_keep(v):
    return (v, None)

def back_low(kept, grad):
    return (low(grad),)
low.defvjp(low_keep, low_pass)
low_back.defvjp(back_keep, back_low)
LN_EPSILON = 1e-05
VERY_LOW = -1e+30
TOP_PRECISION = lax.Precision.HIGHEST

def layer_norm(values, ln_gain, ln_shift):
    average = lax.optimization_barrier(jnp.mean(values, axis=-1, keepdims=True))
    centered = values - average
    spread = lax.optimization_barrier(jnp.mean(centered * centered, axis=-1, keepdims=True))
    return centered * lax.rsqrt(spread + LN_EPSILON) * ln_gain + ln_shift

def rotate(values, positions):
    half_rot = ROT // 2
    frequency = 1.0 / 10000.0 ** (jnp.arange(half_rot).astype(values.dtype) * 2.0 / ROT)
    angles = positions.astype(values.dtype)[:, None] * frequency[None, :]
    shape_out = (angles.shape[0],) + (1,) * (values.ndim - 2) + (ROT,)
    cosine = jnp.concatenate([jnp.cos(angles), jnp.cos(angles)], axis=-1).reshape(shape_out)
    sine_part = jnp.concatenate([jnp.sin(angles), jnp.sin(angles)], axis=-1).reshape(shape_out)
    rot_part = values[..., :ROT]
    turned = jnp.concatenate([-rot_part[..., half_rot:], rot_part[..., :half_rot]], axis=-1)
    return jnp.concatenate([rot_part * cosine + turned * sine_part, values[..., ROT:]], axis=-1)

def token_positions(pairing):
    row_ids = jnp.arange(LENGTH, dtype=jnp.int32)
    device_ids = row_ids // (2 * BLK)
    within = row_ids % (2 * BLK)
    owned_block = pairing[device_ids].astype(jnp.int32)
    blocks = jnp.where(within < BLK, owned_block, 2 * N_CTX - 1 - owned_block)
    return (blocks * BLK + within % BLK).astype(jnp.int32)

def attend_block(query_rows, query_pos, keys_rot, value_rows, key_pos):
    scaling = HEAD ** (-0.5)
    scores = low_back(jnp.einsum('qhd,khd->hqk', query_rows, keys_rot, precision=TOP_PRECISION) * scaling)
    allowed = key_pos[None, None, :] <= query_pos[None, :, None]
    masked = jnp.where(allowed, scores, VERY_LOW)
    highest = lax.optimization_barrier(jnp.max(masked, axis=-1, keepdims=True))
    weights = jnp.where(allowed, jnp.exp(masked - highest), 0.0)
    weights = weights / lax.optimization_barrier(jnp.sum(weights, axis=-1, keepdims=True))
    return jnp.einsum('hqk,khd->qhd', low(weights), value_rows, precision=TOP_PRECISION)

def one_sequence(params, hidden_rows, positions):
    gain_one, shift_one, w_qkv, b_qkv, w_out, b_out, gain_two, shift_two, w_up, b_up, w_down, b_down = params
    normed_one = layer_norm(hidden_rows, gain_one, shift_one)
    projected = low_back(jnp.dot(low(normed_one), w_qkv, precision=TOP_PRECISION) + b_qkv)
    queries = low(rotate(projected[:, :D].reshape(LENGTH, HEADS, HEAD), positions))
    keys_rot = low(rotate(projected[:, D:2 * D].reshape(LENGTH, HEADS, HEAD), positions))
    value_rows = low(projected[:, 2 * D:].reshape(LENGTH, HEADS, HEAD))
    query_block = 512 if LENGTH % 512 == 0 else LENGTH
    block_count = LENGTH // query_block

    def per_block(blocks):
        return attend_block(blocks[0], blocks[1], keys_rot, value_rows, positions)
    attended = lax.map(jax.checkpoint(per_block), (queries.reshape(block_count, query_block, HEADS, HEAD), positions.reshape(block_count, query_block)))
    attended = low_back(low(attended.reshape(LENGTH, D)))
    branch_attn = jnp.dot(attended, w_out, precision=TOP_PRECISION) + b_out
    normed_two = layer_norm(hidden_rows, gain_two, shift_two)
    inner_act = low_back(jnp.dot(low(normed_two), w_up, precision=TOP_PRECISION) + b_up)
    activated = low(jax.nn.gelu(inner_act, approximate=False))
    branch_mlp = jnp.dot(activated, w_down.T, precision=TOP_PRECISION) + b_down
    return hidden_rows + branch_attn + branch_mlp

def reference(hidden, cotangent, pairing, ln1_gain, ln1_bias, qkv_weight, qkv_bias, out_weight, out_bias, ln2_gain, ln2_bias, up_weight, up_bias, down_weight, down_bias):
    positions = token_positions(pairing)
    params = jax.tree.map(lambda member: member.astype(jnp.float32), (ln1_gain, ln1_bias, qkv_weight, qkv_bias, out_weight, out_bias, ln2_gain, ln2_bias, up_weight, up_bias, down_weight, down_bias))

    def forward(weights_all, hidden_f):

        def per_sequence(rows):
            return one_sequence(weights_all, rows, positions)
        return jnp.swapaxes(lax.map(jax.checkpoint(per_sequence), jnp.swapaxes(hidden_f, 0, 1)), 0, 1)
    result, pullback = jax.vjp(forward, params, hidden.astype(jnp.float32))
    grads, grad_hidden = pullback(cotangent.astype(jnp.float32))
    return (result.astype(jnp.bfloat16), grad_hidden, grads[0], grads[1], grads[2], grads[3], grads[4], grads[5], grads[6], grads[7], grads[8], grads[9], grads[10], grads[11])
```

```python
import jax
import jax.numpy as jnp
from jax import lax
from jax.experimental import pallas as pl
from jax.experimental.pallas import tpu as pltpu
from jax.sharding import PartitionSpec as P

HEAD = 256
ROT = 64


LN_EPSILON = 1e-05
VERY_LOW = -1e30


def layer_norm(values, ln_gain, ln_shift):
    average = jnp.mean(values, axis=-1, keepdims=True)
    centered = values - average
    spread = jnp.mean(centered * centered, axis=-1, keepdims=True)
    return centered * lax.rsqrt(spread + LN_EPSILON) * ln_gain + ln_shift


def gelu_exact(values):
    return jax.nn.gelu(values, approximate=False)


def rotate(values, positions):
    half_rot = ROT // 2
    frequency = 1.0 / 10000.0 ** (jnp.arange(half_rot).astype(values.dtype) * 2.0 / ROT)
    angles = positions.astype(values.dtype)[:, None] * frequency[None, :]
    shape_out = (angles.shape[0],) + (1,) * (values.ndim - 2) + (ROT,)
    cosine = jnp.concatenate([jnp.cos(angles), jnp.cos(angles)], axis=-1).reshape(shape_out)
    sine_part = jnp.concatenate([jnp.sin(angles), jnp.sin(angles)], axis=-1).reshape(shape_out)
    rot_part = values[..., :ROT]
    turned = jnp.concatenate([-rot_part[..., half_rot:], rot_part[..., :half_rot]], axis=-1)
    return jnp.concatenate([rot_part * cosine + turned * sine_part, values[..., ROT:]], axis=-1)


def row_positions(pairing, first_row, row_count, block_rows, ctx_count):
    row_ids = first_row + jnp.arange(row_count, dtype=jnp.int32)
    device_ids = row_ids // (2 * block_rows)
    within = row_ids % (2 * block_rows)
    matches = device_ids[:, None] == jnp.arange(ctx_count, dtype=jnp.int32)[None, :]
    owned_block = jnp.sum(jnp.where(matches, pairing[None, :], 0), axis=1)
    blocks = jnp.where(within < block_rows, owned_block, 2 * ctx_count - 1 - owned_block)
    return blocks * block_rows + within % block_rows


def heads_view(values, row_total, seq_count):
    return values.reshape(row_total, seq_count, -1, HEAD)


def contract_rows(left, right):
    return lax.dot_general(
        left, right, (((0,), (0,)), ((), ())), preferred_element_type=jnp.float32
    )


def contract_cols(left, right):
    return lax.dot_general(
        left, right, (((1,), (1,)), ((), ())), preferred_element_type=jnp.float32
    )


def pair_grads(
    query_rows, grad_rows, log_rows, delta_rows, query_pos, key_heads, value_heads, key_pos, scaling
):
    scores = (
        jnp.einsum("qshd,kshd->shqk", query_rows, key_heads, preferred_element_type=jnp.float32)
        * scaling
    )
    allowed = key_pos[None, None, None, :] <= query_pos[None, None, :, None]
    probabilities = jnp.where(allowed, jnp.exp(scores - log_rows[..., None]), 0.0)
    prob_grad = jnp.einsum(
        "qshd,kshd->shqk", grad_rows, value_heads, preferred_element_type=jnp.float32
    )
    score_grad = (probabilities * (prob_grad - delta_rows[..., None])).astype(jnp.bfloat16)
    return (score_grad, probabilities.astype(jnp.bfloat16))


def general_body(
    hidden,
    cotangent,
    pairing,
    ln1_gain,
    ln1_bias,
    qkv_weight,
    qkv_bias,
    out_weight,
    out_bias,
    ln2_gain,
    ln2_bias,
    up_weight,
    up_bias,
    down_weight,
    down_bias,
):
    local_rows, seq_count, model_width = hidden.shape
    block_rows = local_rows // 2
    ctx_count = lax.axis_size("ctx")
    head_count = model_width // HEAD
    scaling = HEAD ** (-0.5)
    tokens = local_rows * seq_count
    total_rows = local_rows * ctx_count
    params = (
        lax.all_gather(ln1_gain, ("ctx", "fsdp"), axis=0, tiled=True),
        lax.all_gather(ln1_bias, ("ctx", "fsdp"), axis=0, tiled=True),
        lax.all_gather(qkv_weight, ("ctx", "fsdp"), axis=0, tiled=True),
        lax.all_gather(qkv_bias, ("ctx", "fsdp"), axis=0, tiled=True),
        lax.all_gather(out_weight, ("ctx", "fsdp"), axis=0, tiled=True),
        lax.all_gather(out_bias, ("ctx", "fsdp"), axis=0, tiled=True),
        lax.all_gather(ln2_gain, ("ctx", "fsdp"), axis=0, tiled=True),
        lax.all_gather(ln2_bias, ("ctx", "fsdp"), axis=0, tiled=True),
        lax.all_gather(up_weight, ("ctx", "fsdp"), axis=0, tiled=True),
        lax.all_gather(up_bias, ("ctx", "fsdp"), axis=0, tiled=True),
        lax.all_gather(down_weight, ("ctx", "fsdp"), axis=0, tiled=True),
        lax.all_gather(down_bias, ("ctx", "fsdp"), axis=0, tiled=True),
    )
    (
        gain_one,
        shift_one,
        w_qkv,
        b_qkv,
        w_out,
        b_out,
        gain_two,
        shift_two,
        w_up,
        b_up,
        w_down,
        b_down,
    ) = params
    ff_width = w_up.shape[1]
    hidden_f = hidden.astype(jnp.float32).reshape(tokens, model_width)
    own_pos = row_positions(
        pairing, lax.axis_index("ctx") * local_rows, local_rows, block_rows, ctx_count
    )
    normed_one, ln_one_pull = jax.vjp(
        layer_norm, hidden_f, gain_one.astype(jnp.float32), shift_one.astype(jnp.float32)
    )
    normed_one_low = normed_one.astype(jnp.bfloat16)
    projected = jnp.dot(normed_one_low, w_qkv, preferred_element_type=jnp.float32) + b_qkv.astype(
        jnp.float32
    )
    query_f, rotation_pull = jax.vjp(
        lambda values: rotate(values, own_pos),
        heads_view(projected[:, :model_width], local_rows, seq_count),
    )
    query_b = query_f.astype(jnp.bfloat16)
    key_b = (
        rotate(
            heads_view(projected[:, model_width : 2 * model_width], local_rows, seq_count), own_pos
        )
        .astype(jnp.bfloat16)
        .reshape(local_rows, seq_count, model_width)
    )
    value_b = (
        projected[:, 2 * model_width :]
        .astype(jnp.bfloat16)
        .reshape(local_rows, seq_count, model_width)
    )
    running_max = jnp.full((seq_count, head_count, local_rows), VERY_LOW, jnp.float32)
    key_piece = lax.all_gather(key_b, "ctx", axis=0, tiled=True)
    value_piece = lax.all_gather(value_b, "ctx", axis=0, tiled=True)
    row_total = key_piece.shape[0]
    key_pos = row_positions(pairing, jnp.int32(0), row_total, block_rows, ctx_count)
    scores = (
        jnp.einsum(
            "qshd,kshd->shqk",
            query_b,
            heads_view(key_piece, row_total, seq_count),
            preferred_element_type=jnp.float32,
        )
        * scaling
    )
    allowed = key_pos[None, None, None, :] <= own_pos[None, None, :, None]
    piece_max = jnp.max(jnp.where(allowed, scores, VERY_LOW), axis=-1)
    new_max = jnp.maximum(running_max, piece_max)
    weights = jnp.where(allowed, jnp.exp(scores - new_max[..., None]), 0.0)
    new_total = jnp.sum(weights, axis=-1)
    mixture = jnp.einsum(
        "shqk,kshd->qshd",
        weights.astype(jnp.bfloat16),
        heads_view(value_piece, row_total, seq_count),
        preferred_element_type=jnp.float32,
    )
    log_total = new_max + jnp.log(new_total)
    attended = mixture / jnp.transpose(new_total, (2, 0, 1))[..., None]
    attended_low = attended.astype(jnp.bfloat16).reshape(tokens, model_width)
    branch_attn = jnp.dot(attended_low, w_out, preferred_element_type=jnp.float32) + b_out.astype(
        jnp.float32
    )
    normed_two, ln_two_pull = jax.vjp(
        layer_norm, hidden_f, gain_two.astype(jnp.float32), shift_two.astype(jnp.float32)
    )
    normed_two_low = normed_two.astype(jnp.bfloat16)
    inner_act = jnp.dot(normed_two_low, w_up, preferred_element_type=jnp.float32) + b_up.astype(
        jnp.float32
    )
    activated_f, gelu_pull = jax.vjp(gelu_exact, inner_act)
    activated = activated_f.astype(jnp.bfloat16)
    branch_mlp = contract_cols(activated, w_down) + b_down.astype(jnp.float32)
    output = (
        (hidden_f + branch_attn + branch_mlp)
        .astype(jnp.bfloat16)
        .reshape(local_rows, seq_count, model_width)
    )
    back_qkv, back_out, back_up, back_down = (
        lax.all_gather(qkv_weight, ("ctx", "fsdp"), axis=0, tiled=True),
        lax.all_gather(out_weight, ("ctx", "fsdp"), axis=0, tiled=True),
        lax.all_gather(up_weight, ("ctx", "fsdp"), axis=0, tiled=True),
        lax.all_gather(down_weight, ("ctx", "fsdp"), axis=0, tiled=True),
    )
    grad_out = cotangent.reshape(tokens, model_width)
    grad_f = grad_out.astype(jnp.float32)
    bias_sum = jnp.sum(grad_f, axis=0)
    up_grad = jnp.dot(grad_out, back_down, preferred_element_type=jnp.float32)
    inner_grad = gelu_pull(up_grad)[0].astype(jnp.bfloat16)
    norm_two_grad = contract_cols(inner_grad, back_up)
    dx_two, dgain_two, dshift_two = ln_two_pull(norm_two_grad)
    up_bias_sum = jnp.sum(inner_grad, axis=0, dtype=jnp.float32)
    mlp_small = jnp.concatenate(
        [
            up_bias_sum.reshape(model_width, -1),
            jnp.stack([bias_sum, dgain_two, dshift_two], axis=1),
        ],
        axis=1,
    )
    up_w_sum, down_w_sum, mlp_small_sum = (
        lax.psum_scatter(
            contract_rows(normed_two_low, inner_grad),
            ("ctx", "fsdp"),
            scatter_dimension=0,
            tiled=True,
        ),
        lax.psum_scatter(
            contract_rows(grad_out, activated), ("ctx", "fsdp"), scatter_dimension=0, tiled=True
        ),
        lax.psum_scatter(mlp_small, ("ctx", "fsdp"), scatter_dimension=0, tiled=True),
    )
    ratio = ff_width // model_width
    attn_grad = contract_cols(grad_out, back_out).astype(jnp.bfloat16)
    out_w_grad = contract_rows(attended_low, grad_out)
    grad_heads = heads_view(attn_grad, local_rows, seq_count)
    row_delta = jnp.einsum("qshd,qshd->shq", grad_heads.astype(jnp.float32), attended)
    keys_all, values_all = (
        lax.all_gather(key_b, "ctx", axis=0, tiled=True),
        lax.all_gather(value_b, "ctx", axis=0, tiled=True),
    )
    key_block = 512
    block_count = total_rows // key_block
    starts = jnp.arange(block_count, dtype=jnp.int32) * key_block

    def query_step(query_grad, inputs):
        key_piece, value_piece, offset = inputs
        key_pos = row_positions(pairing, offset, key_block, block_rows, ctx_count)
        key_heads = heads_view(key_piece, key_block, seq_count)
        value_heads = heads_view(value_piece, key_block, seq_count)
        score_grad, unused = pair_grads(
            query_b,
            grad_heads,
            log_total,
            row_delta,
            own_pos,
            key_heads,
            value_heads,
            key_pos,
            scaling,
        )
        query_grad = (
            query_grad
            + jnp.einsum(
                "shqk,kshd->qshd", score_grad, key_heads, preferred_element_type=jnp.float32
            )
            * scaling
        )
        return (query_grad, None)

    query_grad, unused_out = lax.scan(
        query_step,
        jnp.zeros((local_rows, seq_count, head_count, HEAD), jnp.float32),
        (
            keys_all.reshape(block_count, key_block, seq_count, model_width),
            values_all.reshape(block_count, key_block, seq_count, model_width),
            starts,
        ),
    )
    queries_all, grads_all = (
        lax.all_gather(query_b, "ctx", axis=0, tiled=True),
        lax.all_gather(grad_heads, "ctx", axis=0, tiled=True),
    )
    logs_all, deltas_all = (
        lax.all_gather(log_total, "ctx", axis=2, tiled=True),
        lax.all_gather(row_delta, "ctx", axis=2, tiled=True),
    )
    own_keys = heads_view(key_b, local_rows, seq_count)
    own_values = heads_view(value_b, local_rows, seq_count)

    def key_step(carry, inputs):
        key_acc, value_acc = carry
        query_piece, grad_piece, log_piece, delta_piece, offset = inputs
        query_pos = row_positions(pairing, offset, key_block, block_rows, ctx_count)
        score_grad, probs_low = pair_grads(
            query_piece,
            grad_piece,
            log_piece,
            delta_piece,
            query_pos,
            own_keys,
            own_values,
            own_pos,
            scaling,
        )
        key_acc = (
            key_acc
            + jnp.einsum(
                "shqk,qshd->kshd", score_grad, query_piece, preferred_element_type=jnp.float32
            )
            * scaling
        )
        value_acc = value_acc + jnp.einsum(
            "shqk,qshd->kshd", probs_low, grad_piece, preferred_element_type=jnp.float32
        )
        return ((key_acc, value_acc), None)

    empty_acc = jnp.zeros((local_rows, seq_count, head_count, HEAD), jnp.float32)
    log_blocks = jnp.moveaxis(logs_all.reshape(seq_count, head_count, block_count, key_block), 2, 0)
    delta_blocks = jnp.moveaxis(
        deltas_all.reshape(seq_count, head_count, block_count, key_block), 2, 0
    )
    (key_sum, value_sum), unused_keys = lax.scan(
        key_step,
        (empty_acc, empty_acc),
        (
            queries_all.reshape(block_count, key_block, seq_count, head_count, HEAD),
            grads_all.reshape(block_count, key_block, seq_count, head_count, HEAD),
            log_blocks,
            delta_blocks,
            starts,
        ),
    )
    key_owned = key_sum.reshape(local_rows, seq_count, model_width)
    value_owned = value_sum.reshape(local_rows, seq_count, model_width)
    query_pre = rotation_pull(query_grad)[0].reshape(tokens, model_width)
    key_pre = rotation_pull(heads_view(key_owned, local_rows, seq_count))[0].reshape(
        tokens, model_width
    )
    value_pre = value_owned.reshape(tokens, model_width)
    projected_grad = jnp.concatenate([query_pre, key_pre, value_pre], axis=1).astype(jnp.bfloat16)
    norm_one_grad = contract_cols(projected_grad, back_qkv)
    dx_one, dgain_one, dshift_one = ln_one_pull(norm_one_grad)
    qkv_bias_sum = jnp.sum(projected_grad, axis=0, dtype=jnp.float32)
    attn_small = jnp.concatenate(
        [
            qkv_bias_sum.reshape(model_width, -1),
            jnp.stack([bias_sum, dgain_one, dshift_one], axis=1),
        ],
        axis=1,
    )
    qkv_w_sum, out_w_sum, attn_small_sum = (
        lax.psum_scatter(
            contract_rows(normed_one_low, projected_grad),
            ("ctx", "fsdp"),
            scatter_dimension=0,
            tiled=True,
        ),
        lax.psum_scatter(out_w_grad, ("ctx", "fsdp"), scatter_dimension=0, tiled=True),
        lax.psum_scatter(attn_small, ("ctx", "fsdp"), scatter_dimension=0, tiled=True),
    )
    grad_hidden = (grad_f + dx_one + dx_two).reshape(local_rows, seq_count, model_width)
    return (
        output,
        grad_hidden,
        attn_small_sum[:, 4],
        attn_small_sum[:, 5],
        qkv_w_sum,
        attn_small_sum[:, :3].reshape(-1),
        out_w_sum,
        attn_small_sum[:, 3],
        mlp_small_sum[:, ratio + 1],
        mlp_small_sum[:, ratio + 2],
        up_w_sum,
        mlp_small_sum[:, :ratio].reshape(-1),
        down_w_sum,
        mlp_small_sum[:, ratio],
    )


MESH = pl.DeviceIdType.MESH
CORES = 2
LINE_Y = 2
VMEM_BYTES = 60 * 2**20


def split_fits(mesh):
    return mesh.shape["ctx"] == 16 and mesh.shape["fsdp"] == 2


class Place:
    def __init__(self, ctx_count):
        self.chips = ctx_count // CORES
        self.line = self.chips // LINE_Y
        index = lax.axis_index("ctx")
        self.c = index % CORES
        self.chip = index // CORES
        self.y = self.chip % LINE_Y
        self.z = self.chip // LINE_Y
        self.x = lax.axis_index("fsdp")

    def at(self, z, y, c, x):
        return ((z * LINE_Y + y) * CORES + c, x)

    def other_core(self):
        return self.at(self.z, self.y, 1 - self.c, self.x)

    def other_plane(self):
        return self.at(self.z, self.y, self.c, 1 - self.x)

    def other_y(self):
        return self.at(self.z, 1 - self.y, self.c, self.x)

    def plane_offsets(self):
        return [(dz, dy) for dz in range(self.line) for dy in range(LINE_Y) if dz or dy]

    def shifted(self, dz, dy):
        return (self.z + dz) % self.line, (self.y + dy) % LINE_Y


class Copies:
    def __init__(self, send, recv, local):
        self.send, self.recv, self.local = send, recv, local
        self.remotes, self.locals = 0, 0

    def remote(self, src, dst, device):
        i = self.remotes
        self.remotes += 1
        return pltpu.make_async_remote_copy(
            src_ref=src,
            dst_ref=dst,
            send_sem=self.send.at[i],
            recv_sem=self.recv.at[i],
            device_id=device,
            device_id_type=MESH,
        )

    def inside(self, src, dst):
        i = self.locals
        self.locals += 1
        return pltpu.make_async_copy(src, dst, self.local.at[i])


def greet(place):
    barrier = pltpu.get_barrier_semaphore()
    partners = [place.other_core(), place.other_plane()]
    for dz, dy in place.plane_offsets():
        z, y = place.shifted(dz, dy)
        partners.append(place.at(z, y, place.c, place.x))
    for partner in partners:
        pl.semaphore_signal(barrier, inc=1, device_id=partner, device_id_type=MESH)
    pl.semaphore_wait(barrier, len(partners))


class TokenGather:
    def __init__(self, place, copies, own, whole):
        self.place = place
        self.whole = whole
        c, chip, z, y = place.c, place.chip, place.z, place.y
        self.first = copies.remote(own.at[1 - c], whole.at[chip, c], place.other_core())
        self.mine = copies.inside(own.at[c], whole.at[chip, c])
        last = place.line - 1
        up = place.at(jnp.minimum(z + 1, last), y, c, place.x)
        down = place.at(jnp.maximum(z - 1, 0), y, c, place.x)

        def pair(zz):
            return whole.at[jnp.clip(zz, 0, last) * LINE_Y + y]

        self.ups = [copies.remote(pair(z - j), pair(z - j), up) for j in range(last)]
        self.downs = [copies.remote(pair(z + j), pair(z + j), down) for j in range(last)]
        self.over_own = copies.remote(pair(z), pair(z), place.other_y())
        self.over_ups = [copies.remote(pair(z - 1 - j), pair(z - 1 - j), place.other_y()) for j in range(last)]
        self.over_downs = [copies.remote(pair(z + 1 + j), pair(z + 1 + j), place.other_y()) for j in range(last)]
        self.last = last

    def start(self):
        self.mine.start()
        self.first.start()

    def spread(self):
        self.mine.wait()
        self.first.wait_recv()
        z = self.place.z
        pl.when(z < self.last)(lambda: self.ups[0].start())
        pl.when(z > 0)(lambda: self.downs[0].start())
        self.over_own.start()

    def step(self, j):
        z, last = self.place.z, self.last

        @pl.when(z - 1 - j >= 0)
        def _():
            self.ups[j].wait_recv()
            if j + 1 < last:
                pl.when(z < last)(lambda: self.ups[j + 1].start())
            self.over_ups[j].start()

        @pl.when(z + 1 + j <= last)
        def _():
            self.downs[j].wait_recv()
            if j + 1 < last:
                pl.when(z > 0)(lambda: self.downs[j + 1].start())
            self.over_downs[j].start()

    def finish(self):
        z, last = self.place.z, self.last
        self.over_own.wait_recv()
        for j in range(last):
            pl.when(z - 1 - j >= 0)(lambda: self.over_ups[j].wait_recv())
            pl.when(z + 1 + j <= last)(lambda: self.over_downs[j].wait_recv())

    def drain(self):
        z, last = self.place.z, self.last
        self.first.wait_send()
        self.over_own.wait_send()
        for j in range(last):
            pl.when((z - j >= 0) & (z < last))(lambda: self.ups[j].wait_send())
            pl.when((z + j <= last) & (z > 0))(lambda: self.downs[j].wait_send())
            pl.when(z - 1 - j >= 0)(lambda: self.over_ups[j].wait_send())
            pl.when(z + 1 + j <= last)(lambda: self.over_downs[j].wait_send())


class WeightGather:
    def __init__(self, place, copies, pieces, whole):
        self.place = place
        group = 2 * place.c + place.x
        self.scattered = []
        for dz, dy in place.plane_offsets():
            z, y = place.shifted(dz, dy)
            device = place.at(z, y, place.c, place.x)
            for src, dst in pieces(z * LINE_Y + y, place.chip, group):
                self.scattered.append(copies.remote(src, dst, device))
        self.kept = [copies.inside(src, dst) for src, dst in pieces(place.chip, place.chip, group)]
        mine = whole.at[:, group]
        self.across = copies.remote(mine, mine, place.other_plane())
        pair = whole.at[:, pl.ds(2 * place.c, 2)]
        self.swap = copies.remote(pair, pair, place.other_core())

    def scatter(self):
        for copy in self.scattered + self.kept:
            copy.start()

    def cross(self):
        for copy in self.kept:
            copy.wait()
        for copy in self.scattered:
            copy.wait_recv()
        self.across.start()

    def share(self):
        self.across.wait_recv()
        self.swap.start()

    def finish(self):
        self.swap.wait_recv()

    def drain(self):
        for copy in self.scattered + [self.across, self.swap]:
            copy.wait_send()


def gather_kernel(
    ctx_count,
    hid,
    cot,
    qkv,
    up,
    down,
    out,
    small,
    hid_all,
    cot_all,
    qkv_all,
    up_all,
    down_all,
    out_all,
    small_all,
    send,
    recv,
    local,
):
    place = Place(ctx_count)
    copies = Copies(send, recv, local)
    width = out.shape[1]
    head = qkv_all.shape[3] // 3
    part = up_all.shape[3]

    def qkv_pieces(to, row, group):
        return [
            (
                qkv.at[:, pl.ds(pl.multiple_of(k * width + to * head, head), head)],
                qkv_all.at[row, group, :, pl.ds(k * head, head)],
            )
            for k in range(3)
        ]

    def slice_pieces(source, whole):
        return lambda to, row, group: [
            (source.at[:, pl.ds(pl.multiple_of(to * part, part), part)], whole.at[row, group])
        ]

    hid_g = TokenGather(place, copies, hid, hid_all)
    cot_g = TokenGather(place, copies, cot, cot_all)
    small_g = WeightGather(place, copies, lambda to, row, group: [(small, small_all.at[row, group])], small_all)
    qkv_g = WeightGather(place, copies, qkv_pieces, qkv_all)
    up_g = WeightGather(place, copies, slice_pieces(up, up_all), up_all)
    down_g = WeightGather(place, copies, slice_pieces(down, down_all), down_all)
    group = 2 * place.c + place.x
    out_mine = copies.inside(out, out_all.at[group])
    out_across = copies.remote(out, out_all.at[group], place.other_plane())
    out_pair = out_all.at[pl.ds(2 * place.c, 2)]
    out_swap = copies.remote(out_pair, out_pair, place.other_core())

    greet(place)
    hid_g.start()
    cot_g.start()
    small_g.scatter()
    qkv_g.scatter()
    hid_g.spread()
    out_mine.start()
    out_across.start()
    up_g.scatter()
    small_g.cross()
    hid_g.step(0)
    qkv_g.cross()
    small_g.share()
    hid_g.step(1)
    cot_g.spread()
    hid_g.step(2)
    down_g.scatter()
    qkv_g.share()
    cot_g.step(0)
    up_g.cross()
    cot_g.step(1)
    cot_g.step(2)
    out_mine.wait()
    out_across.wait_recv()
    out_swap.start()
    down_g.cross()
    up_g.share()
    down_g.share()
    hid_g.finish()
    cot_g.finish()
    for gather in (small_g, qkv_g, up_g, down_g):
        gather.finish()
    out_swap.wait_recv()
    for gather in (hid_g, cot_g, small_g, qkv_g, up_g, down_g):
        gather.drain()
    out_across.wait_send()
    out_swap.wait_send()


def gather_all(ctx_count, hid, cot, qkv, up, down, out, small):
    chips = ctx_count // CORES
    rows = qkv.shape[0]
    groups = CORES * 2
    shapes = [
        ((chips, CORES) + hid.shape[1:], hid.dtype),
        ((chips, CORES) + cot.shape[1:], cot.dtype),
        ((chips, groups, rows, qkv.shape[1] // chips), qkv.dtype),
        ((chips, groups, rows, up.shape[1] // chips), up.dtype),
        ((chips, groups, rows, down.shape[1] // chips), down.dtype),
        ((groups, rows, out.shape[1]), out.dtype),
        ((chips, groups) + small.shape, small.dtype),
    ]
    operands = (hid, cot, qkv, up, down, out, small)
    anywhere = pl.BlockSpec(memory_space=pl.ANY)
    return pl.pallas_call(
        lambda *refs: gather_kernel(ctx_count, *refs),
        out_shape=[jax.ShapeDtypeStruct(*shape) for shape in shapes],
        in_specs=[anywhere] * len(operands),
        out_specs=[anywhere] * len(shapes),
        scratch_shapes=[
            pltpu.SemaphoreType.DMA((88,)),
            pltpu.SemaphoreType.DMA((88,)),
            pltpu.SemaphoreType.DMA((16,)),
        ],
        compiler_params=pltpu.CompilerParams(
            collective_id=0, has_side_effects=True, vmem_limit_bytes=VMEM_BYTES
        ),
        name="gather_all",
    )(*operands)


def add_into(total, other, steps):
    @pl.loop(0, steps)
    def _(k):
        both = total[k].astype(jnp.float32) + other[k].astype(jnp.float32)
        total[k] = both.astype(total.dtype)


class GradScatter:
    def __init__(self, place, copies, partial, kept, from_core, from_plane, result):
        self.place = place
        c, x, chip = place.c, place.x, place.chip
        self.kept, self.from_core, self.from_plane = kept, from_core, from_plane
        self.load = copies.inside(partial.at[:, pl.ds(2 * c, 2)], kept)
        self.swap = copies.remote(partial.at[:, pl.ds(2 * (1 - c), 2)], from_core, place.other_core())
        self.across = copies.remote(kept.at[:, 1 - x], from_plane, place.other_plane())
        self.scattered = []
        for dz, dy in place.plane_offsets():
            z, y = place.shifted(dz, dy)
            self.scattered.append(
                copies.remote(kept.at[z * LINE_Y + y, x], result.at[chip], place.at(z, y, c, x))
            )
        self.own = copies.inside(kept.at[chip, x], result.at[chip])

    def start(self):
        self.load.start()
        self.swap.start()

    def cross(self):
        self.load.wait()
        self.swap.wait_recv()
        add_into(self.kept, self.from_core, self.kept.shape[0])
        self.across.start()

    def scatter(self):
        self.across.wait_recv()
        x = self.place.x

        @pl.loop(0, self.kept.shape[0])
        def _(k):
            both = self.kept[k, x].astype(jnp.float32) + self.from_plane[k].astype(jnp.float32)
            self.kept[k, x] = both.astype(self.kept.dtype)

        for copy in self.scattered + [self.own]:
            copy.start()

    def finish(self):
        self.own.wait()
        for copy in self.scattered:
            copy.wait_recv()

    def drain(self):
        for copy in self.scattered + [self.swap, self.across]:
            copy.wait_send()


class TokenScatter:
    def __init__(self, place, copies, partial, kept, from_y, from_z, total, result):
        self.place = place
        z, y, c, x = place.z, place.y, place.c, place.x
        self.kept, self.from_y, self.from_z, self.total = kept, from_y, from_z, total
        self.load = copies.inside(partial.at[:, y], kept)
        self.over = copies.remote(partial.at[:, 1 - y], from_y, place.other_y())
        self.along = []
        for dz in range(1, place.line):
            to = (z + dz) % place.line
            self.along.append(copies.remote(kept.at[to], from_z.at[dz - 1], place.at(to, y, c, x)))
        self.swap = copies.remote(total.at[1 - c], result.at[c], place.other_core())
        self.own = copies.inside(total.at[c], result.at[c])

    def start(self):
        self.load.start()
        self.over.start()

    def along_z(self):
        self.load.wait()
        self.over.wait_recv()
        add_into(self.kept, self.from_y, self.kept.shape[0])
        for copy in self.along:
            copy.start()

    def reduce(self):
        for copy in self.along:
            copy.wait_recv()
        z = self.place.z

        @pl.loop(0, CORES)
        def _(k):
            total = self.kept[z, k].astype(jnp.float32)
            for dz in range(self.place.line - 1):
                total = total + self.from_z[dz, k].astype(jnp.float32)
            self.total[k] = total

        self.swap.start()
        self.own.start()

    def finish(self):
        self.own.wait()
        self.swap.wait_recv()

    def drain(self):
        self.over.wait_send()
        for copy in self.along:
            copy.wait_send()
        self.swap.wait_send()


def scatter_kernel(ctx_count, count_grads, *refs):
    place = Place(ctx_count)
    take = iter(refs)
    grads = [next(take) for _ in range(count_grads)]
    grad_out, out_part, hid_part = next(take), next(take), next(take)
    grad_results = [next(take) for _ in range(count_grads)]
    grad_out_result, out_result, hid_result = next(take), next(take), next(take)
    grad_scratch = [[next(take) for _ in range(3)] for _ in range(count_grads)]
    grad_out_scratch = [next(take) for _ in range(3)]
    token_scratch = [[next(take) for _ in range(4)] for _ in range(2)]
    copies = Copies(next(take), next(take), next(take))
    scatters = [
        GradScatter(place, copies, grads[i], *grad_scratch[i], grad_results[i]) for i in range(count_grads)
    ]
    outs_s = TokenScatter(place, copies, out_part, *token_scratch[0], out_result)
    hid_s = TokenScatter(place, copies, hid_part, *token_scratch[1], hid_result)
    c, x = place.c, place.x
    kept, from_core, from_plane = grad_out_scratch
    load = copies.inside(grad_out.at[pl.ds(2 * c, 2)], kept)
    swap = copies.remote(grad_out.at[pl.ds(2 * (1 - c), 2)], from_core, place.other_core())
    across = copies.remote(kept.at[1 - x], from_plane, place.other_plane())
    own = copies.inside(kept.at[x], grad_out_result)

    greet(place)
    for scatter in scatters:
        scatter.start()
    load.start()
    swap.start()
    outs_s.start()
    for scatter in scatters:
        scatter.cross()
    load.wait()
    swap.wait_recv()
    add_into(kept, from_core, 2)
    across.start()
    hid_s.start()
    scatters[0].scatter()
    outs_s.along_z()
    for scatter in scatters[1:]:
        scatter.scatter()
    across.wait_recv()
    kept[x] = (kept[x].astype(jnp.float32) + from_plane[...].astype(jnp.float32)).astype(kept.dtype)
    own.start()
    hid_s.along_z()
    outs_s.reduce()
    hid_s.reduce()
    for scatter in scatters + [outs_s, hid_s]:
        scatter.finish()
    own.wait()
    for scatter in scatters + [outs_s, hid_s]:
        scatter.drain()
    swap.wait_send()
    across.wait_send()


def scatter_all(ctx_count, grads, grad_out, out_part, hid_part):
    chips = ctx_count // CORES
    line = chips // LINE_Y
    count = len(grads)
    grad_out_shape = grad_out.shape[1:]
    token = (CORES,) + out_part.shape[3:]
    out_shape = [jax.ShapeDtypeStruct((chips,) + g.shape[2:], g.dtype) for g in grads]
    out_shape += [jax.ShapeDtypeStruct(grad_out_shape, grad_out.dtype)]
    out_shape += [jax.ShapeDtypeStruct(token, jnp.float32)] * 2
    scratch = []
    for g in grads:
        scratch.append(pltpu.VMEM((chips, 2) + g.shape[2:], g.dtype))
        scratch.append(pltpu.VMEM((chips, 2) + g.shape[2:], g.dtype))
        scratch.append(pltpu.VMEM((chips,) + g.shape[2:], g.dtype))
    scratch.append(pltpu.VMEM((2,) + grad_out_shape, grad_out.dtype))
    scratch.append(pltpu.VMEM((2,) + grad_out_shape, grad_out.dtype))
    scratch.append(pltpu.VMEM(grad_out_shape, grad_out.dtype))
    for part in (out_part, hid_part):
        scratch.append(pltpu.VMEM((line,) + token, part.dtype))
        scratch.append(pltpu.VMEM((line,) + token, part.dtype))
        scratch.append(pltpu.VMEM((line - 1,) + token, part.dtype))
        scratch.append(pltpu.VMEM(token, jnp.float32))
    operands = list(grads) + [grad_out, out_part, hid_part]
    anywhere = pl.BlockSpec(memory_space=pl.ANY)
    return pl.pallas_call(
        lambda *refs: scatter_kernel(ctx_count, count, *refs),
        out_shape=out_shape,
        in_specs=[anywhere] * len(operands),
        out_specs=[anywhere] * len(out_shape),
        scratch_shapes=scratch
        + [
            pltpu.SemaphoreType.DMA((64,)),
            pltpu.SemaphoreType.DMA((64,)),
            pltpu.SemaphoreType.DMA((16,)),
        ],
        compiler_params=pltpu.CompilerParams(
            collective_id=1, has_side_effects=True, vmem_limit_bytes=VMEM_BYTES
        ),
        name="scatter_all",
    )(*operands)


def split_body(
    hidden,
    cotangent,
    pairing,
    ln1_gain,
    ln1_bias,
    qkv_weight,
    qkv_bias,
    out_weight,
    out_bias,
    ln2_gain,
    ln2_bias,
    up_weight,
    up_bias,
    down_weight,
    down_bias,
):
    local_rows, seq_count, width = hidden.shape
    ctx_count = lax.axis_size("ctx")
    chips = ctx_count // CORES
    total_rows = local_rows * ctx_count
    scaling = HEAD ** (-0.5)
    f32, b16 = jnp.float32, jnp.bfloat16
    head_id = lax.axis_index("ctx") // CORES

    owned = width // (ctx_count * 2)
    vectors = (ln1_gain, ln1_bias, ln2_gain, ln2_bias, out_bias, down_bias, qkv_bias, up_bias)
    flat = jnp.concatenate([v.astype(f32) for v in vectors])
    used = flat.shape[0]
    small_rows = 8 * (-(-used // 1024))
    small = jnp.pad(flat, (0, small_rows * 128 - used)).reshape(small_rows, 128)

    hid_all, cot_all, w_qkv, w_up, w_down, w_out, small_all = gather_all(
        ctx_count,
        jnp.swapaxes(hidden, 0, 1),
        jnp.swapaxes(cotangent, 0, 1),
        qkv_weight,
        up_weight,
        down_weight,
        out_weight,
        small,
    )
    w_qkv = w_qkv.reshape(width, -1)
    w_up = w_up.reshape(width, -1)
    w_down = w_down.reshape(width, -1)
    w_out = w_out.reshape(-1, width)
    part = w_up.shape[1]
    smalls = small_all.reshape(ctx_count * 2, -1)
    full = []
    at = 0
    for v in vectors:
        full.append(smalls[:, at : at + v.shape[0]].reshape(-1))
        at += v.shape[0]
    gain_one, shift_one, gain_two, shift_two, b_out, b_down, b_qkv, b_up = full
    b_qkv = lax.dynamic_slice_in_dim(b_qkv.reshape(3, -1), head_id * HEAD, HEAD, axis=1).reshape(-1)
    b_up = lax.dynamic_slice_in_dim(b_up, head_id * part, part)

    x = hid_all.reshape(total_rows, width).astype(f32)
    cot = cot_all.reshape(total_rows, width)
    average = jnp.mean(x, axis=-1, keepdims=True)
    spread = jnp.mean((x - average) ** 2, axis=-1, keepdims=True)
    xhat = (x - average) * lax.rsqrt(spread + LN_EPSILON)
    norm_one = (xhat * gain_one + shift_one).astype(b16)
    norm_two = (xhat * gain_two + shift_two).astype(b16)
    positions = row_positions(pairing, jnp.int32(0), total_rows, local_rows // 2, ctx_count)

    projected = jnp.dot(norm_one, w_qkv, preferred_element_type=f32) + b_qkv
    (query_f, key_f), rotation_pull = jax.vjp(
        lambda q, k: (rotate(q, positions), rotate(k, positions)),
        projected[:, :HEAD],
        projected[:, HEAD : 2 * HEAD],
    )
    query, key = query_f.astype(b16), key_f.astype(b16)
    value = projected[:, 2 * HEAD :].astype(b16)
    scores = contract_cols(query, key) * scaling
    allowed = positions[None, :] <= positions[:, None]
    highest = jnp.max(jnp.where(allowed, scores, VERY_LOW), axis=-1, keepdims=True)
    weights = jnp.where(allowed, jnp.exp(scores - highest), 0.0)
    probs = weights / jnp.sum(weights, axis=-1, keepdims=True)
    probs_low = probs.astype(b16)
    attended = jnp.dot(probs_low, value, preferred_element_type=f32)
    attended_low = attended.astype(b16)

    inner = jnp.dot(norm_two, w_up, preferred_element_type=f32) + b_up
    activated_f, gelu_pull = jax.vjp(gelu_exact, inner)
    activated = activated_f.astype(b16)
    out_part = jnp.dot(attended_low, w_out, preferred_element_type=f32) + contract_cols(activated, w_down)

    up_grad = jnp.dot(cot, w_down, preferred_element_type=f32)
    inner_grad = gelu_pull(up_grad)[0].astype(b16)
    norm_two_grad = contract_cols(inner_grad, w_up)
    grad_up = contract_rows(norm_two, inner_grad)
    grad_down = contract_rows(cot, activated)

    attended_grad = contract_cols(cot, w_out).astype(b16)
    grad_out = contract_rows(attended_low, cot)
    row_delta = jnp.sum(attended_grad.astype(f32) * attended, axis=-1, keepdims=True)
    prob_grad = contract_cols(attended_grad, value)
    score_grad = (probs * (prob_grad - row_delta)).astype(b16)
    query_grad = jnp.dot(score_grad, key, preferred_element_type=f32) * scaling
    key_grad = contract_rows(score_grad, query) * scaling
    value_grad = contract_rows(probs_low, attended_grad)
    query_pre, key_pre = rotation_pull((query_grad, key_grad))
    projected_grad = jnp.concatenate([query_pre, key_pre, value_grad], axis=1).astype(b16)
    norm_one_grad = contract_cols(projected_grad, w_qkv)
    grad_qkv = contract_rows(norm_one, projected_grad)
    hid_part = norm_one_grad * gain_one + norm_two_grad * gain_two

    cot_sum = jnp.where(head_id == 0, jnp.sum(cot.astype(f32), axis=0), 0.0)
    qkv_sum = jnp.sum(projected_grad.astype(f32), axis=0).reshape(3, HEAD)
    qkv_sum = lax.dynamic_update_slice_in_dim(
        jnp.zeros((3, width), f32), qkv_sum, head_id * HEAD, axis=1
    )
    up_sum = lax.dynamic_update_slice_in_dim(
        jnp.zeros((part * chips,), f32),
        jnp.sum(inner_grad.astype(f32), axis=0),
        head_id * part,
        axis=0,
    )
    sums = (
        jnp.sum(norm_one_grad * xhat, axis=0),
        jnp.sum(norm_one_grad, axis=0),
        jnp.sum(norm_two_grad * xhat, axis=0),
        jnp.sum(norm_two_grad, axis=0),
        cot_sum,
        qkv_sum,
        up_sum,
    )
    tiles = jnp.concatenate([v.reshape(ctx_count * 2, -1) for v in sums], axis=1)
    tile_used = tiles.shape[1]
    tile_rows = 8 * (-(-tile_used // 1024))
    tiles = jnp.pad(tiles, ((0, 0), (0, tile_rows * 128 - tile_used)))

    groups = 2 * CORES
    line = chips // LINE_Y
    by_owner = (chips, groups, owned, -1)
    by_rows = (line, LINE_Y, CORES, local_rows, width)
    small_sum, qkv_sum, up_sum, down_sum, out_sum, out_rows, hid_rows = scatter_all(
        ctx_count,
        [
            tiles.reshape(chips, groups, tile_rows, 128),
            grad_qkv.astype(b16).reshape(by_owner),
            grad_up.astype(b16).reshape(by_owner),
            grad_down.astype(b16).reshape(by_owner),
        ],
        grad_out.astype(b16).reshape(groups, owned, width),
        out_part.astype(b16).reshape(by_rows),
        hid_part.astype(b16).reshape(by_rows),
    )

    own = hidden.astype(f32)
    output = (own + jnp.swapaxes(out_rows, 0, 1) + (b_out + b_down)).astype(b16)
    average = jnp.mean(own, axis=-1, keepdims=True)
    spread = jnp.mean((own - average) ** 2, axis=-1, keepdims=True)
    scale = lax.rsqrt(spread + LN_EPSILON)
    xhat = (own - average) * scale
    e = jnp.swapaxes(hid_rows, 0, 1)
    grad_hidden = cotangent.astype(f32) + scale * (
        e - jnp.mean(e, axis=-1, keepdims=True) - xhat * jnp.mean(e * xhat, axis=-1, keepdims=True)
    )
    mine = jnp.sum(small_sum, axis=0).reshape(-1)
    cuts = []
    at = 0
    for v in sums:
        step = v.size // (ctx_count * 2)
        cuts.append(mine[at : at + step])
        at += step

    def columns(pieces, thirds):
        rows = pieces.shape[1]
        split = pieces.astype(f32).reshape(chips, rows, thirds, -1)
        return jnp.transpose(split, (1, 2, 0, 3)).reshape(rows, -1)

    return (
        output,
        grad_hidden,
        cuts[0],
        cuts[1],
        columns(qkv_sum, 3),
        cuts[5],
        out_sum.astype(f32),
        cuts[4],
        cuts[2],
        cuts[3],
        columns(up_sum, 1),
        cuts[6],
        columns(down_sum, 1),
        cuts[4],
    )


def solution(mesh):
    body = split_body if split_fits(mesh) else general_body
    return jax.shard_map(
        body,
        mesh=mesh,
        in_specs=(
            P("ctx", "fsdp", None),
            P("ctx", "fsdp", None),
            P(),
            P(("ctx", "fsdp")),
            P(("ctx", "fsdp")),
            P(("ctx", "fsdp"), None),
            P(("ctx", "fsdp")),
            P(("ctx", "fsdp"), None),
            P(("ctx", "fsdp")),
            P(("ctx", "fsdp")),
            P(("ctx", "fsdp")),
            P(("ctx", "fsdp"), None),
            P(("ctx", "fsdp")),
            P(("ctx", "fsdp"), None),
            P(("ctx", "fsdp")),
        ),
        out_specs=(
            P("ctx", "fsdp", None),
            P("ctx", "fsdp", None),
            P(("ctx", "fsdp")),
            P(("ctx", "fsdp")),
            P(("ctx", "fsdp"), None),
            P(("ctx", "fsdp")),
            P(("ctx", "fsdp"), None),
            P(("ctx", "fsdp")),
            P(("ctx", "fsdp")),
            P(("ctx", "fsdp")),
            P(("ctx", "fsdp"), None),
            P(("ctx", "fsdp")),
            P(("ctx", "fsdp"), None),
            P(("ctx", "fsdp")),
        ),
        check_vma=False,
    )
```

```python
import jax
import jax.numpy as jnp
from jax import lax
from jax.experimental import pallas as pl
from jax.experimental.pallas import tpu as pltpu
from jax.sharding import PartitionSpec as P

HEAD = 256
ROT = 64


LN_EPSILON = 1e-05
VERY_LOW = -1e30


def layer_norm(values, ln_gain, ln_shift):
    average = jnp.mean(values, axis=-1, keepdims=True)
    centered = values - average
    spread = jnp.mean(centered * centered, axis=-1, keepdims=True)
    return centered * lax.rsqrt(spread + LN_EPSILON) * ln_gain + ln_shift


def gelu_exact(values):
    return jax.nn.gelu(values, approximate=False)


def rotate(values, positions):
    half_rot = ROT // 2
    frequency = 1.0 / 10000.0 ** (jnp.arange(half_rot).astype(values.dtype) * 2.0 / ROT)
    angles = positions.astype(values.dtype)[:, None] * frequency[None, :]
    shape_out = (angles.shape[0],) + (1,) * (values.ndim - 2) + (ROT,)
    cosine = jnp.concatenate([jnp.cos(angles), jnp.cos(angles)], axis=-1).reshape(shape_out)
    sine_part = jnp.concatenate([jnp.sin(angles), jnp.sin(angles)], axis=-1).reshape(shape_out)
    rot_part = values[..., :ROT]
    turned = jnp.concatenate([-rot_part[..., half_rot:], rot_part[..., :half_rot]], axis=-1)
    return jnp.concatenate([rot_part * cosine + turned * sine_part, values[..., ROT:]], axis=-1)


def row_positions(pairing, first_row, row_count, block_rows, ctx_count):
    row_ids = first_row + jnp.arange(row_count, dtype=jnp.int32)
    device_ids = row_ids // (2 * block_rows)
    within = row_ids % (2 * block_rows)
    matches = device_ids[:, None] == jnp.arange(ctx_count, dtype=jnp.int32)[None, :]
    owned_block = jnp.sum(jnp.where(matches, pairing[None, :], 0), axis=1)
    blocks = jnp.where(within < block_rows, owned_block, 2 * ctx_count - 1 - owned_block)
    return blocks * block_rows + within % block_rows


def heads_view(values, row_total, seq_count):
    return values.reshape(row_total, seq_count, -1, HEAD)


def contract_rows(left, right):
    return lax.dot_general(
        left, right, (((0,), (0,)), ((), ())), preferred_element_type=jnp.float32
    )


def contract_cols(left, right):
    return lax.dot_general(
        left, right, (((1,), (1,)), ((), ())), preferred_element_type=jnp.float32
    )


def pair_grads(
    query_rows, grad_rows, log_rows, delta_rows, query_pos, key_heads, value_heads, key_pos, scaling
):
    scores = (
        jnp.einsum("qshd,kshd->shqk", query_rows, key_heads, preferred_element_type=jnp.float32)
        * scaling
    )
    allowed = key_pos[None, None, None, :] <= query_pos[None, None, :, None]
    probabilities = jnp.where(allowed, jnp.exp(scores - log_rows[..., None]), 0.0)
    prob_grad = jnp.einsum(
        "qshd,kshd->shqk", grad_rows, value_heads, preferred_element_type=jnp.float32
    )
    score_grad = (probabilities * (prob_grad - delta_rows[..., None])).astype(jnp.bfloat16)
    return (score_grad, probabilities.astype(jnp.bfloat16))


def general_body(
    hidden,
    cotangent,
    pairing,
    ln1_gain,
    ln1_bias,
    qkv_weight,
    qkv_bias,
    out_weight,
    out_bias,
    ln2_gain,
    ln2_bias,
    up_weight,
    up_bias,
    down_weight,
    down_bias,
):
    local_rows, seq_count, model_width = hidden.shape
    block_rows = local_rows // 2
    ctx_count = lax.axis_size("ctx")
    head_count = model_width // HEAD
    scaling = HEAD ** (-0.5)
    tokens = local_rows * seq_count
    total_rows = local_rows * ctx_count
    params = (
        lax.all_gather(ln1_gain, ("ctx", "fsdp"), axis=0, tiled=True),
        lax.all_gather(ln1_bias, ("ctx", "fsdp"), axis=0, tiled=True),
        lax.all_gather(qkv_weight, ("ctx", "fsdp"), axis=0, tiled=True),
        lax.all_gather(qkv_bias, ("ctx", "fsdp"), axis=0, tiled=True),
        lax.all_gather(out_weight, ("ctx", "fsdp"), axis=0, tiled=True),
        lax.all_gather(out_bias, ("ctx", "fsdp"), axis=0, tiled=True),
        lax.all_gather(ln2_gain, ("ctx", "fsdp"), axis=0, tiled=True),
        lax.all_gather(ln2_bias, ("ctx", "fsdp"), axis=0, tiled=True),
        lax.all_gather(up_weight, ("ctx", "fsdp"), axis=0, tiled=True),
        lax.all_gather(up_bias, ("ctx", "fsdp"), axis=0, tiled=True),
        lax.all_gather(down_weight, ("ctx", "fsdp"), axis=0, tiled=True),
        lax.all_gather(down_bias, ("ctx", "fsdp"), axis=0, tiled=True),
    )
    (
        gain_one,
        shift_one,
        w_qkv,
        b_qkv,
        w_out,
        b_out,
        gain_two,
        shift_two,
        w_up,
        b_up,
        w_down,
        b_down,
    ) = params
    ff_width = w_up.shape[1]
    hidden_f = hidden.astype(jnp.float32).reshape(tokens, model_width)
    own_pos = row_positions(
        pairing, lax.axis_index("ctx") * local_rows, local_rows, block_rows, ctx_count
    )
    normed_one, ln_one_pull = jax.vjp(
        layer_norm, hidden_f, gain_one.astype(jnp.float32), shift_one.astype(jnp.float32)
    )
    normed_one_low = normed_one.astype(jnp.bfloat16)
    projected = jnp.dot(normed_one_low, w_qkv, preferred_element_type=jnp.float32) + b_qkv.astype(
        jnp.float32
    )
    query_f, rotation_pull = jax.vjp(
        lambda values: rotate(values, own_pos),
        heads_view(projected[:, :model_width], local_rows, seq_count),
    )
    query_b = query_f.astype(jnp.bfloat16)
    key_b = (
        rotate(
            heads_view(projected[:, model_width : 2 * model_width], local_rows, seq_count), own_pos
        )
        .astype(jnp.bfloat16)
        .reshape(local_rows, seq_count, model_width)
    )
    value_b = (
        projected[:, 2 * model_width :]
        .astype(jnp.bfloat16)
        .reshape(local_rows, seq_count, model_width)
    )
    running_max = jnp.full((seq_count, head_count, local_rows), VERY_LOW, jnp.float32)
    key_piece = lax.all_gather(key_b, "ctx", axis=0, tiled=True)
    value_piece = lax.all_gather(value_b, "ctx", axis=0, tiled=True)
    row_total = key_piece.shape[0]
    key_pos = row_positions(pairing, jnp.int32(0), row_total, block_rows, ctx_count)
    scores = (
        jnp.einsum(
            "qshd,kshd->shqk",
            query_b,
            heads_view(key_piece, row_total, seq_count),
            preferred_element_type=jnp.float32,
        )
        * scaling
    )
    allowed = key_pos[None, None, None, :] <= own_pos[None, None, :, None]
    piece_max = jnp.max(jnp.where(allowed, scores, VERY_LOW), axis=-1)
    new_max = jnp.maximum(running_max, piece_max)
    weights = jnp.where(allowed, jnp.exp(scores - new_max[..., None]), 0.0)
    new_total = jnp.sum(weights, axis=-1)
    mixture = jnp.einsum(
        "shqk,kshd->qshd",
        weights.astype(jnp.bfloat16),
        heads_view(value_piece, row_total, seq_count),
        preferred_element_type=jnp.float32,
    )
    log_total = new_max + jnp.log(new_total)
    attended = mixture / jnp.transpose(new_total, (2, 0, 1))[..., None]
    attended_low = attended.astype(jnp.bfloat16).reshape(tokens, model_width)
    branch_attn = jnp.dot(attended_low, w_out, preferred_element_type=jnp.float32) + b_out.astype(
        jnp.float32
    )
    normed_two, ln_two_pull = jax.vjp(
        layer_norm, hidden_f, gain_two.astype(jnp.float32), shift_two.astype(jnp.float32)
    )
    normed_two_low = normed_two.astype(jnp.bfloat16)
    inner_act = jnp.dot(normed_two_low, w_up, preferred_element_type=jnp.float32) + b_up.astype(
        jnp.float32
    )
    activated_f, gelu_pull = jax.vjp(gelu_exact, inner_act)
    activated = activated_f.astype(jnp.bfloat16)
    branch_mlp = contract_cols(activated, w_down) + b_down.astype(jnp.float32)
    output = (
        (hidden_f + branch_attn + branch_mlp)
        .astype(jnp.bfloat16)
        .reshape(local_rows, seq_count, model_width)
    )
    back_qkv, back_out, back_up, back_down = (
        lax.all_gather(qkv_weight, ("ctx", "fsdp"), axis=0, tiled=True),
        lax.all_gather(out_weight, ("ctx", "fsdp"), axis=0, tiled=True),
        lax.all_gather(up_weight, ("ctx", "fsdp"), axis=0, tiled=True),
        lax.all_gather(down_weight, ("ctx", "fsdp"), axis=0, tiled=True),
    )
    grad_out = cotangent.reshape(tokens, model_width)
    grad_f = grad_out.astype(jnp.float32)
    bias_sum = jnp.sum(grad_f, axis=0)
    up_grad = jnp.dot(grad_out, back_down, preferred_element_type=jnp.float32)
    inner_grad = gelu_pull(up_grad)[0].astype(jnp.bfloat16)
    norm_two_grad = contract_cols(inner_grad, back_up)
    dx_two, dgain_two, dshift_two = ln_two_pull(norm_two_grad)
    up_bias_sum = jnp.sum(inner_grad, axis=0, dtype=jnp.float32)
    mlp_small = jnp.concatenate(
        [
            up_bias_sum.reshape(model_width, -1),
            jnp.stack([bias_sum, dgain_two, dshift_two], axis=1),
        ],
        axis=1,
    )
    up_w_sum, down_w_sum, mlp_small_sum = (
        lax.psum_scatter(
            contract_rows(normed_two_low, inner_grad),
            ("ctx", "fsdp"),
            scatter_dimension=0,
            tiled=True,
        ),
        lax.psum_scatter(
            contract_rows(grad_out, activated), ("ctx", "fsdp"), scatter_dimension=0, tiled=True
        ),
        lax.psum_scatter(mlp_small, ("ctx", "fsdp"), scatter_dimension=0, tiled=True),
    )
    ratio = ff_width // model_width
    attn_grad = contract_cols(grad_out, back_out).astype(jnp.bfloat16)
    out_w_grad = contract_rows(attended_low, grad_out)
    grad_heads = heads_view(attn_grad, local_rows, seq_count)
    row_delta = jnp.einsum("qshd,qshd->shq", grad_heads.astype(jnp.float32), attended)
    keys_all, values_all = (
        lax.all_gather(key_b, "ctx", axis=0, tiled=True),
        lax.all_gather(value_b, "ctx", axis=0, tiled=True),
    )
    key_block = 512
    block_count = total_rows // key_block
    starts = jnp.arange(block_count, dtype=jnp.int32) * key_block

    def query_step(query_grad, inputs):
        key_piece, value_piece, offset = inputs
        key_pos = row_positions(pairing, offset, key_block, block_rows, ctx_count)
        key_heads = heads_view(key_piece, key_block, seq_count)
        value_heads = heads_view(value_piece, key_block, seq_count)
        score_grad, unused = pair_grads(
            query_b,
            grad_heads,
            log_total,
            row_delta,
            own_pos,
            key_heads,
            value_heads,
            key_pos,
            scaling,
        )
        query_grad = (
            query_grad
            + jnp.einsum(
                "shqk,kshd->qshd", score_grad, key_heads, preferred_element_type=jnp.float32
            )
            * scaling
        )
        return (query_grad, None)

    query_grad, unused_out = lax.scan(
        query_step,
        jnp.zeros((local_rows, seq_count, head_count, HEAD), jnp.float32),
        (
            keys_all.reshape(block_count, key_block, seq_count, model_width),
            values_all.reshape(block_count, key_block, seq_count, model_width),
            starts,
        ),
    )
    queries_all, grads_all = (
        lax.all_gather(query_b, "ctx", axis=0, tiled=True),
        lax.all_gather(grad_heads, "ctx", axis=0, tiled=True),
    )
    logs_all, deltas_all = (
        lax.all_gather(log_total, "ctx", axis=2, tiled=True),
        lax.all_gather(row_delta, "ctx", axis=2, tiled=True),
    )
    own_keys = heads_view(key_b, local_rows, seq_count)
    own_values = heads_view(value_b, local_rows, seq_count)

    def key_step(carry, inputs):
        key_acc, value_acc = carry
        query_piece, grad_piece, log_piece, delta_piece, offset = inputs
        query_pos = row_positions(pairing, offset, key_block, block_rows, ctx_count)
        score_grad, probs_low = pair_grads(
            query_piece,
            grad_piece,
            log_piece,
            delta_piece,
            query_pos,
            own_keys,
            own_values,
            own_pos,
            scaling,
        )
        key_acc = (
            key_acc
            + jnp.einsum(
                "shqk,qshd->kshd", score_grad, query_piece, preferred_element_type=jnp.float32
            )
            * scaling
        )
        value_acc = value_acc + jnp.einsum(
            "shqk,qshd->kshd", probs_low, grad_piece, preferred_element_type=jnp.float32
        )
        return ((key_acc, value_acc), None)

    empty_acc = jnp.zeros((local_rows, seq_count, head_count, HEAD), jnp.float32)
    log_blocks = jnp.moveaxis(logs_all.reshape(seq_count, head_count, block_count, key_block), 2, 0)
    delta_blocks = jnp.moveaxis(
        deltas_all.reshape(seq_count, head_count, block_count, key_block), 2, 0
    )
    (key_sum, value_sum), unused_keys = lax.scan(
        key_step,
        (empty_acc, empty_acc),
        (
            queries_all.reshape(block_count, key_block, seq_count, head_count, HEAD),
            grads_all.reshape(block_count, key_block, seq_count, head_count, HEAD),
            log_blocks,
            delta_blocks,
            starts,
        ),
    )
    key_owned = key_sum.reshape(local_rows, seq_count, model_width)
    value_owned = value_sum.reshape(local_rows, seq_count, model_width)
    query_pre = rotation_pull(query_grad)[0].reshape(tokens, model_width)
    key_pre = rotation_pull(heads_view(key_owned, local_rows, seq_count))[0].reshape(
        tokens, model_width
    )
    value_pre = value_owned.reshape(tokens, model_width)
    projected_grad = jnp.concatenate([query_pre, key_pre, value_pre], axis=1).astype(jnp.bfloat16)
    norm_one_grad = contract_cols(projected_grad, back_qkv)
    dx_one, dgain_one, dshift_one = ln_one_pull(norm_one_grad)
    qkv_bias_sum = jnp.sum(projected_grad, axis=0, dtype=jnp.float32)
    attn_small = jnp.concatenate(
        [
            qkv_bias_sum.reshape(model_width, -1),
            jnp.stack([bias_sum, dgain_one, dshift_one], axis=1),
        ],
        axis=1,
    )
    qkv_w_sum, out_w_sum, attn_small_sum = (
        lax.psum_scatter(
            contract_rows(normed_one_low, projected_grad),
            ("ctx", "fsdp"),
            scatter_dimension=0,
            tiled=True,
        ),
        lax.psum_scatter(out_w_grad, ("ctx", "fsdp"), scatter_dimension=0, tiled=True),
        lax.psum_scatter(attn_small, ("ctx", "fsdp"), scatter_dimension=0, tiled=True),
    )
    grad_hidden = (grad_f + dx_one + dx_two).reshape(local_rows, seq_count, model_width)
    return (
        output,
        grad_hidden,
        attn_small_sum[:, 4],
        attn_small_sum[:, 5],
        qkv_w_sum,
        attn_small_sum[:, :3].reshape(-1),
        out_w_sum,
        attn_small_sum[:, 3],
        mlp_small_sum[:, ratio + 1],
        mlp_small_sum[:, ratio + 2],
        up_w_sum,
        mlp_small_sum[:, :ratio].reshape(-1),
        down_w_sum,
        mlp_small_sum[:, ratio],
    )


MESH = pl.DeviceIdType.MESH
CORES = 2
LINE_Y = 2
VMEM_BYTES = 60 * 2**20


def split_fits(mesh):
    return mesh.shape["ctx"] == 16 and mesh.shape["fsdp"] == 2


class Place:
    def __init__(self, ctx_count):
        self.chips = ctx_count // CORES
        self.line = self.chips // LINE_Y
        index = lax.axis_index("ctx")
        self.c = index % CORES
        self.chip = index // CORES
        self.y = self.chip % LINE_Y
        self.z = self.chip // LINE_Y
        self.x = lax.axis_index("fsdp")

    def at(self, z, y, c, x):
        return ((z * LINE_Y + y) * CORES + c, x)

    def other_core(self):
        return self.at(self.z, self.y, 1 - self.c, self.x)

    def other_plane(self):
        return self.at(self.z, self.y, self.c, 1 - self.x)

    def other_y(self):
        return self.at(self.z, 1 - self.y, self.c, self.x)

    def plane_offsets(self):
        return [(dz, dy) for dz in range(self.line) for dy in range(LINE_Y) if dz or dy]

    def shifted(self, dz, dy):
        return (self.z + dz) % self.line, (self.y + dy) % LINE_Y


class Copies:
    def __init__(self, send, recv, local):
        self.send, self.recv, self.local = send, recv, local
        self.remotes, self.locals = 0, 0

    def reserve(self, count):
        self.remotes += count
        return self.remotes - count

    def remote(self, src, dst, device):
        return self.remote_at(self.reserve(1), src, dst, device)

    def remote_at(self, i, src, dst, device):
        return pltpu.make_async_remote_copy(
            src_ref=src,
            dst_ref=dst,
            send_sem=self.send.at[i],
            recv_sem=self.recv.at[i],
            device_id=device,
            device_id_type=MESH,
        )

    def inside(self, src, dst):
        i = self.locals
        self.locals += 1
        return pltpu.make_async_copy(src, dst, self.local.at[i])


def greet(place):
    barrier = pltpu.get_barrier_semaphore()
    partners = [place.other_core(), place.other_plane()]
    for dz, dy in place.plane_offsets():
        z, y = place.shifted(dz, dy)
        partners.append(place.at(z, y, place.c, place.x))
    for partner in partners:
        pl.semaphore_signal(barrier, inc=1, device_id=partner, device_id_type=MESH)
    pl.semaphore_wait(barrier, len(partners))


class TokenGather:
    def __init__(self, place, copies, own, whole):
        self.place = place
        self.whole = whole
        c, chip, z, y = place.c, place.chip, place.z, place.y
        rows = own.shape[1]
        block = whole.at[pl.ds(pl.multiple_of((chip * CORES + c) * rows, rows), rows)]
        self.first = copies.remote(own.at[1 - c], block, place.other_core())
        self.mine = copies.inside(own.at[c], block)
        last = place.line - 1
        up = place.at(jnp.minimum(z + 1, last), y, c, place.x)
        down = place.at(jnp.maximum(z - 1, 0), y, c, place.x)

        def pair(zz):
            first = (jnp.clip(zz, 0, last) * LINE_Y + y) * CORES * rows
            return whole.at[pl.ds(pl.multiple_of(first, CORES * rows), CORES * rows)]

        self.ups = [copies.remote(pair(z - j), pair(z - j), up) for j in range(last)]
        self.downs = [copies.remote(pair(z + j), pair(z + j), down) for j in range(last)]
        self.over_own = copies.remote(pair(z), pair(z), place.other_y())
        self.over_ups = [copies.remote(pair(z - 1 - j), pair(z - 1 - j), place.other_y()) for j in range(last)]
        self.over_downs = [copies.remote(pair(z + 1 + j), pair(z + 1 + j), place.other_y()) for j in range(last)]
        self.last = last

    def start(self):
        self.mine.start()
        self.first.start()

    def spread(self):
        self.mine.wait()
        self.first.wait_recv()
        z = self.place.z
        pl.when(z < self.last)(lambda: self.ups[0].start())
        pl.when(z > 0)(lambda: self.downs[0].start())
        self.over_own.start()

    def step(self, j):
        z, last = self.place.z, self.last

        @pl.when(z - 1 - j >= 0)
        def _():
            self.ups[j].wait_recv()
            if j + 1 < last:
                pl.when(z < last)(lambda: self.ups[j + 1].start())
            self.over_ups[j].start()

        @pl.when(z + 1 + j <= last)
        def _():
            self.downs[j].wait_recv()
            if j + 1 < last:
                pl.when(z > 0)(lambda: self.downs[j + 1].start())
            self.over_downs[j].start()

    def finish(self):
        z, last = self.place.z, self.last
        self.over_own.wait_recv()
        for j in range(last):
            pl.when(z - 1 - j >= 0)(lambda: self.over_ups[j].wait_recv())
            pl.when(z + 1 + j <= last)(lambda: self.over_downs[j].wait_recv())

    def drain(self):
        z, last = self.place.z, self.last
        self.first.wait_send()
        self.over_own.wait_send()
        for j in range(last):
            pl.when((z - j >= 0) & (z < last))(lambda: self.ups[j].wait_send())
            pl.when((z + j <= last) & (z > 0))(lambda: self.downs[j].wait_send())
            pl.when(z - 1 - j >= 0)(lambda: self.over_ups[j].wait_send())
            pl.when(z + 1 + j <= last)(lambda: self.over_downs[j].wait_send())


class WeightGather:
    def __init__(self, place, copies, pieces, whole):
        self.place = place
        group = 2 * place.c + place.x
        self.scattered = []
        for dz, dy in place.plane_offsets():
            z, y = place.shifted(dz, dy)
            device = place.at(z, y, place.c, place.x)
            for src, dst in pieces(z * LINE_Y + y, place.chip, group):
                self.scattered.append(copies.remote(src, dst, device))
        self.kept = [copies.inside(src, dst) for src, dst in pieces(place.chip, place.chip, group)]
        mine = whole.at[:, group]
        self.across = copies.remote(mine, mine, place.other_plane())
        pair = whole.at[:, pl.ds(2 * place.c, 2)]
        self.swap = copies.remote(pair, pair, place.other_core())

    def scatter(self):
        for copy in self.scattered + self.kept:
            copy.start()

    def cross(self):
        for copy in self.kept:
            copy.wait()
        for copy in self.scattered:
            copy.wait_recv()
        self.across.start()

    def share(self):
        self.across.wait_recv()
        self.swap.start()

    def finish(self):
        self.swap.wait_recv()

    def drain(self):
        for copy in self.scattered + [self.across, self.swap]:
            copy.wait_send()


def nn(left, right):
    return lax.dot_general(left, right, (((1,), (0,)), ((), ())), preferred_element_type=jnp.float32)


def tile(i, size):
    return pl.ds(pl.multiple_of(i * size, size), size)


def flat_rows(values):
    return values.reshape(-1, values.shape[-1])


GAIN_ONE, SHIFT_ONE, GAIN_TWO, SHIFT_TWO, OUT_BIAS, DOWN_BIAS, QKV_BIAS, UP_BIAS, SMALL_ROWS = (
    0,
    1,
    2,
    3,
    4,
    5,
    6,
    9,
    16,
)
LANES = 128


def lanes_of(shape):
    return lax.broadcasted_iota(jnp.int32, shape, len(shape) - 1)


def assemble_small(place, small, vec, qkv_rows, qkv_bias, up_bias):
    chips, groups = small.shape[:2]
    low = lanes_of((1, LANES)) < LANES // 2
    for pair in range(chips * groups // 2):
        chip, group = pair // (groups // 2), pair % (groups // 2) * 2
        for row in range(4):
            a = small[chip, group, row : row + 1, :]
            b = small[chip, group + 1, row : row + 1, :]
            vec[row : row + 1, pair * LANES : (pair + 1) * LANES] = jnp.where(low, a, b)
        qkv_rows[3 * pair : 3 * pair + 1, :] = small[chip, group, QKV_BIAS : QKV_BIAS + 1, :]
        a = small[chip, group, QKV_BIAS + 1 : QKV_BIAS + 2, :]
        b = small[chip, group + 1, QKV_BIAS + 1 : QKV_BIAS + 2, :]
        qkv_rows[3 * pair + 1 : 3 * pair + 2, :] = jnp.where(low, a, b)
        qkv_rows[3 * pair + 2 : 3 * pair + 3, :] = small[chip, group + 1, QKV_BIAS + 2 : QKV_BIAS + 3, :]
    third = qkv_rows.shape[0] // 3
    per_head = HEAD // LANES
    for k in range(3):
        for u in range(per_head):
            at = (k * per_head + u) * LANES
            qkv_bias[0:1, at : at + LANES] = qkv_rows[pl.ds(k * third + place.chip * per_head + u, 1), :]
    for group in range(groups):
        for u in range(2):
            at = (group * 2 + u) * LANES
            row = UP_BIAS + u
            up_bias[0:1, at : at + LANES] = small[pl.ds(place.chip, 1), group, row : row + 1, :].reshape(1, LANES)


def norm_rows(start, count, hid, vec, norm_one, norm_two, stats):
    step = 16

    @pl.loop(0, count // step)
    def _(i):
        at = pl.ds(pl.multiple_of(start + i * step, step), step)
        x = hid[at, :].astype(jnp.float32)
        average = jnp.mean(x, axis=1, keepdims=True)
        centered = x - average
        scale = lax.rsqrt(jnp.mean(centered * centered, axis=1, keepdims=True) + LN_EPSILON)
        stats[at, 0:1] = average
        stats[at, 1:2] = scale
        xhat = centered * scale
        norm_one[at, :] = (xhat * vec[0:1, :] + vec[1:2, :]).astype(jnp.bfloat16)
        norm_two[at, :] = (xhat * vec[2:3, :] + vec[3:4, :]).astype(jnp.bfloat16)


def turned_half(values):
    half_rot = ROT // 2
    lane = lanes_of(values.shape)
    width = values.shape[-1]
    return jnp.where(
        lane < half_rot,
        pltpu.roll(values, width - half_rot, 1),
        jnp.where(lane < ROT, pltpu.roll(values, half_rot, 1), 0.0),
    )


def project(norm_one, weight, bias, cosine, sine, query, key, value):
    step = 256

    @pl.loop(0, norm_one.shape[0] // step)
    def _(i):
        at = tile(i, step)
        both = nn(norm_one[at, :], flat_rows(weight[...])) + bias[0:1, :]
        cos, sin = cosine[at, :], sine[at, :]
        for k, target in enumerate((query, key)):
            first = both[:, k * HEAD : k * HEAD + LANES]
            target[at, 0:LANES] = (first * cos + turned_half(first) * sin).astype(jnp.bfloat16)
            target[at, LANES:HEAD] = both[:, k * HEAD + LANES : (k + 1) * HEAD].astype(jnp.bfloat16)
        value[at, :] = both[:, 2 * HEAD :].astype(jnp.bfloat16)


def attend(query, key, value, sine, key_pos, attended, attended_low, probs, probs_low):
    step = 256

    @pl.loop(0, query.shape[0] // step)
    def _(i):
        at = tile(i, step)
        scores = contract_cols(query[at, :], key[...]) * HEAD**-0.5
        allowed = key_pos[0:1, :] <= sine[at, ROT : ROT + 1]
        scores = jnp.where(allowed, scores, VERY_LOW)
        highest = jnp.max(scores, axis=1, keepdims=True)
        weights = jnp.where(allowed, jnp.exp(scores - highest), 0.0)
        weights = weights / jnp.sum(weights, axis=1, keepdims=True)
        low = weights.astype(jnp.bfloat16)
        probs[at, :] = weights
        probs_low[at, :] = low
        total = nn(low, value[...])
        attended[at, :] = total
        attended_low[at, :] = total.astype(jnp.bfloat16)


def feed_inner(norm_two, weight, bias, activated, slope):
    step = 128

    @pl.loop(0, norm_two.shape[0] // step)
    def _(i):
        at = tile(i, step)
        inner = nn(norm_two[at, :], flat_rows(weight[...])) + bias[0:1, :]
        normal = 0.5 + 0.5 * lax.erf(inner * 0.5**0.5)
        activated[at, :] = (inner * normal).astype(jnp.bfloat16)
        density = (2.0 * jnp.pi) ** -0.5 * jnp.exp(-0.5 * inner * inner)
        slope[at, :] = normal + inner * density


def attended_grads(cot, weight, attended_low, attended_grad, weight_grad):
    @pl.loop(0, cot.shape[0] // 256)
    def _(i):
        at = tile(i, 256)
        attended_grad[at, :] = contract_cols(cot[at, :], flat_rows(weight[...])).astype(jnp.bfloat16)

    @pl.loop(0, cot.shape[1] // 512)
    def _(i):
        at = tile(i, 512)
        grad = contract_rows(attended_low[...], cot[:, at]).astype(jnp.bfloat16)
        weight_grad[:, :, at] = grad.reshape(weight_grad.shape[0], weight_grad.shape[1], 512)


def attention_grads(
    query, key, value, cosine, sine, attended, attended_grad, probs, probs_low, score_grad, projected_grad
):
    step = 256
    scaling = HEAD**-0.5

    def put(at, k, grad):
        first = grad[:, 0:LANES]
        back = first * cosine[at, :] - turned_half(first) * sine[at, :]
        projected_grad[at, k * HEAD : k * HEAD + LANES] = back.astype(jnp.bfloat16)
        projected_grad[at, k * HEAD + LANES : (k + 1) * HEAD] = grad[:, LANES:].astype(jnp.bfloat16)

    @pl.loop(0, query.shape[0] // step)
    def _(i):
        at = tile(i, step)
        own = attended_grad[at, :]
        row_delta = jnp.sum(own.astype(jnp.float32) * attended[at, :], axis=1, keepdims=True)
        grad = (probs[at, :] * (contract_cols(own, value[...]) - row_delta)).astype(jnp.bfloat16)
        score_grad[at, :] = grad
        put(at, 0, nn(grad, key[...]) * scaling)

    @pl.loop(0, query.shape[0] // step)
    def _(i):
        at = tile(i, step)
        put(at, 1, contract_rows(score_grad[:, at], query[...]) * scaling)
        projected_grad[at, 2 * HEAD :] = contract_rows(probs_low[:, at], attended_grad[...]).astype(jnp.bfloat16)


def weight_grads(tokens, grads, result):
    chips, groups, rows = result.shape[:3]
    step = groups * rows

    @pl.loop(0, chips)
    def _(k):
        grad = contract_rows(tokens[:, tile(k, step)], grads[...]).astype(jnp.bfloat16)
        result[k] = grad.reshape(result.shape[1:])


def column_sums(values, result):
    step = 16

    def add(i, total):
        return total + values[tile(i, step), :].astype(jnp.float32)

    total = lax.fori_loop(0, values.shape[0] // step, add, jnp.zeros((step, values.shape[1]), jnp.float32))
    result[0:1, :] = jnp.sum(total, axis=0, keepdims=True)


def gather_kernel(
    ctx_count,
    hid,
    cot,
    qkv,
    up,
    down,
    out,
    small,
    cosine_in,
    sine_in,
    key_pos_in,
    hid_all,
    cot_all,
    qkv_all,
    up_all,
    down_all,
    out_all,
    small_all,
    attended_low_out,
    projected_grad_out,
    norm_two_out,
    activated_out,
    slope_out,
    qkv_grad_out,
    down_grad_out,
    out_grad_out,
    vec_out,
    stats_out,
    qkv_sum_out,
    cot_sum_out,
    hid_v,
    cot_v,
    qkv_v,
    up_v,
    out_v,
    small_v,
    cosine,
    sine,
    key_pos,
    vec,
    qkv_rows,
    qkv_bias,
    up_bias,
    norm_one,
    norm_two,
    stats,
    query,
    key,
    value,
    attended,
    attended_low,
    probs,
    probs_low,
    activated,
    slope,
    attended_grad,
    score_grad,
    projected_grad,
    out_grad,
    qkv_sum,
    cot_sum,
    send,
    recv,
    local,
):
    place = Place(ctx_count)
    copies = Copies(send, recv, local)
    width = out.shape[1]
    head = qkv_all.shape[3] // 3
    part = up_all.shape[3]

    def qkv_pieces(to, row, group):
        return [
            (
                qkv.at[:, pl.ds(pl.multiple_of(k * width + to * head, head), head)],
                qkv_all.at[row, group, :, pl.ds(k * head, head)],
            )
            for k in range(3)
        ]

    def slice_pieces(source, whole):
        return lambda to, row, group: [
            (source.at[:, pl.ds(pl.multiple_of(to * part, part), part)], whole.at[row, group])
        ]

    hid_g = TokenGather(place, copies, hid, hid_all)
    cot_g = TokenGather(place, copies, cot, cot_all)
    small_g = WeightGather(place, copies, lambda to, row, group: [(small, small_all.at[row, group])], small_all)
    qkv_g = WeightGather(place, copies, qkv_pieces, qkv_all)
    up_g = WeightGather(place, copies, slice_pieces(up, up_all), up_all)
    down_g = WeightGather(place, copies, slice_pieces(down, down_all), down_all)
    group = 2 * place.c + place.x
    out_mine = copies.inside(out, out_all.at[group])
    out_across = copies.remote(out, out_all.at[group], place.other_plane())
    out_pair = out_all.at[pl.ds(2 * place.c, 2)]
    out_swap = copies.remote(out_pair, out_pair, place.other_core())
    loads = {
        name: copies.inside(src, dst)
        for name, src, dst in (
            ("cosine", cosine_in, cosine),
            ("sine", sine_in, sine),
            ("key_pos", key_pos_in, key_pos),
            ("small", small_all, small_v),
            ("hid", hid_all, hid_v),
            ("cot", cot_all, cot_v),
            ("qkv", qkv_all, qkv_v),
            ("up", up_all, up_v),
            ("out", out_all, out_v),
        )
    }
    stores = {
        name: copies.inside(src, dst)
        for name, src, dst in (
            ("vec", vec, vec_out),
            ("stats", stats, stats_out),
            ("attended_low", attended_low, attended_low_out),
            ("norm_two", norm_two, norm_two_out),
            ("activated", activated, activated_out),
            ("slope", slope, slope_out),
            ("out_grad", out_grad, out_grad_out),
            ("projected_grad", projected_grad, projected_grad_out),
            ("qkv_grad", qkv_v, qkv_grad_out),
            ("down_grad", up_v, down_grad_out),
            ("qkv_sum", qkv_sum, qkv_sum_out),
            ("cot_sum", cot_sum, cot_sum_out),
        )
    }

    def fetch(name):
        loads[name].start()
        loads[name].wait()

    for name in ("cosine", "sine", "key_pos"):
        loads[name].start()
    greet(place)
    hid_g.start()
    cot_g.start()
    small_g.scatter()
    qkv_g.scatter()
    hid_g.spread()
    out_mine.start()
    out_across.start()
    up_g.scatter()
    small_g.cross()
    hid_g.step(0)
    qkv_g.cross()
    small_g.share()
    hid_g.step(1)
    cot_g.spread()
    hid_g.step(2)
    down_g.scatter()
    small_g.finish()
    fetch("small")
    assemble_small(place, small_v, vec, qkv_rows, qkv_bias, up_bias)
    stores["vec"].start()
    qkv_g.share()
    cot_g.step(0)
    hid_g.finish()
    fetch("hid")
    rows = hid_v.shape[0]
    norm_rows(0, rows // 2, hid_v, vec, norm_one, norm_two, stats)
    cot_g.step(1)
    up_g.cross()
    norm_rows(rows // 2, rows // 2, hid_v, vec, norm_one, norm_two, stats)
    stores["norm_two"].start()
    stores["stats"].start()
    cot_g.step(2)
    qkv_g.finish()
    fetch("qkv")
    for name in ("cosine", "sine", "key_pos"):
        loads[name].wait()
    project(norm_one, qkv_v, qkv_bias, cosine, sine, query, key, value)
    out_mine.wait()
    out_across.wait_recv()
    out_swap.start()
    down_g.cross()
    up_g.share()
    attend(query, key, value, sine, key_pos, attended, attended_low, probs, probs_low)
    stores["attended_low"].start()
    up_g.finish()
    fetch("up")
    down_g.share()
    feed_inner(norm_two, up_v, up_bias, activated, slope)
    stores["activated"].start()
    stores["slope"].start()
    cot_g.finish()
    loads["cot"].start()
    out_swap.wait_recv()
    fetch("out")
    loads["cot"].wait()
    attended_grads(cot_v, out_v, attended_low, attended_grad, out_grad)
    stores["out_grad"].start()
    weight_grads(cot_v, activated, up_v)
    stores["down_grad"].start()
    column_sums(cot_v, cot_sum)
    stores["cot_sum"].start()
    attention_grads(
        query, key, value, cosine, sine, attended, attended_grad, probs, probs_low, score_grad, projected_grad
    )
    stores["projected_grad"].start()
    weight_grads(norm_one, projected_grad, qkv_v)
    stores["qkv_grad"].start()
    column_sums(projected_grad, qkv_sum)
    stores["qkv_sum"].start()
    down_g.finish()
    for store in stores.values():
        store.wait()
    for gather in (hid_g, cot_g, small_g, qkv_g, up_g, down_g):
        gather.drain()
    out_across.wait_send()
    out_swap.wait_send()


def gather_all(ctx_count, hid, cot, qkv, up, down, out, small, cosine, sine, key_pos):
    f32, b16 = jnp.float32, jnp.bfloat16
    chips = ctx_count // CORES
    rows = qkv.shape[0]
    groups = CORES * 2
    tokens = ctx_count * hid.shape[1]
    width = out.shape[1]
    head3, part = qkv.shape[1] // chips, up.shape[1] // chips
    head = head3 // 3
    qkv_s = ((chips, groups, rows, head3), b16)
    part_s = ((chips, groups, rows, part), b16)
    out_s = ((groups, rows, width), b16)
    small_s = ((chips, groups) + small.shape, f32)
    wide_s, narrow_s = ((tokens, width), b16), ((tokens, head), b16)
    results = [
        wide_s,
        wide_s,
        qkv_s,
        part_s,
        part_s,
        out_s,
        small_s,
        narrow_s,
        ((tokens, head3), b16),
        wide_s,
        ((tokens, part), b16),
        ((tokens, part), f32),
        qkv_s,
        part_s,
        out_s,
        ((8, width), f32),
        ((tokens, LANES), f32),
        ((8, head3), f32),
        ((8, width), f32),
    ]
    scratch = [
        wide_s,
        wide_s,
        qkv_s,
        part_s,
        out_s,
        small_s,
        ((tokens, LANES), f32),
        ((tokens, LANES), f32),
        ((8, tokens), f32),
        ((8, width), f32),
        ((3 * width // LANES, LANES), f32),
        ((8, head3), f32),
        ((8, part), f32),
        wide_s,
        wide_s,
        ((tokens, LANES), f32),
        narrow_s,
        narrow_s,
        narrow_s,
        ((tokens, head), f32),
        narrow_s,
        ((tokens, tokens), f32),
        ((tokens, tokens), b16),
        ((tokens, part), b16),
        ((tokens, part), f32),
        narrow_s,
        ((tokens, tokens), b16),
        ((tokens, head3), b16),
        out_s,
        ((8, head3), f32),
        ((8, width), f32),
    ]
    operands = (hid, cot, qkv, up, down, out, small, cosine, sine, key_pos)
    anywhere = pl.BlockSpec(memory_space=pl.ANY)
    return pl.pallas_call(
        lambda *refs: gather_kernel(ctx_count, *refs),
        out_shape=[jax.ShapeDtypeStruct(*shape) for shape in results],
        in_specs=[anywhere] * len(operands),
        out_specs=[anywhere] * len(results),
        scratch_shapes=[pltpu.VMEM(*shape) for shape in scratch]
        + [
            pltpu.SemaphoreType.DMA((88,)),
            pltpu.SemaphoreType.DMA((88,)),
            pltpu.SemaphoreType.DMA((40,)),
        ],
        compiler_params=pltpu.CompilerParams(
            collective_id=0, has_side_effects=True, vmem_limit_bytes=VMEM_BYTES
        ),
        name="gather_all",
    )(*operands)


def add_rows(total, other, count):
    step = 16
    per = total.shape[-2] // step

    @pl.loop(0, count * per)
    def _(i):
        k, at = i // per, tile(i % per, step)
        both = total[k, at, :].astype(jnp.float32) + other[k, at, :].astype(jnp.float32)
        total[k, at, :] = both.astype(total.dtype)


def add_tiles(total, other, pieces):
    rows = total.shape[-2]

    @pl.loop(0, pieces)
    def _(k):
        both = total[k].astype(jnp.float32) + other[k].astype(jnp.float32)
        total[k] = both.astype(total.dtype)


class GradScatter:
    def __init__(self, place, copies, partial, kept, from_core, from_plane, result):
        self.place = place
        c, x, chip = place.c, place.x, place.chip
        self.kept, self.from_core, self.from_plane = kept, from_core, from_plane
        given = partial
        if partial.shape != kept.shape:
            self.load = copies.inside(partial.at[:, pl.ds(2 * c, 2)], kept)
            given = partial.at[:, pl.ds(2 * (1 - c), 2)]
        self.swap = copies.remote(given, from_core, place.other_core())
        self.across = copies.remote(kept.at[:, 1 - x], from_plane, place.other_plane())
        self.scattered = []
        for dz, dy in place.plane_offsets():
            z, y = place.shifted(dz, dy)
            self.scattered.append(
                copies.remote(kept.at[z * LINE_Y + y, x], result.at[chip], place.at(z, y, c, x))
            )
        self.own = copies.inside(kept.at[chip, x], result.at[chip])

    def start(self):
        self.load.start()
        self.swap.start()

    def cross(self, loaded=True):
        if loaded:
            self.load.wait()
        self.swap.wait_recv()
        x = self.place.x
        self.add(1 - x, self.from_core.at[:, 1 - x])
        self.across.start()
        self.add(x, self.from_core.at[:, x])

    def add(self, x, other):
        step = 16
        per = self.kept.shape[2] // step

        @pl.loop(0, self.kept.shape[0] * per)
        def _(i):
            k, at = i // per, tile(i % per, step)
            both = self.kept[k, x, at, :].astype(jnp.float32) + other[k, at, :].astype(jnp.float32)
            self.kept[k, x, at, :] = both.astype(self.kept.dtype)

    def scatter(self):
        self.across.wait_recv()
        self.add(self.place.x, self.from_plane)
        for copy in self.scattered + [self.own]:
            copy.start()

    def finish(self):
        self.own.wait()
        for copy in self.scattered:
            copy.wait_recv()

    def drain(self):
        for copy in self.scattered + [self.swap, self.across]:
            copy.wait_send()


def weight_grads_by_core(place, tokens, grads, kept, given):
    chips, half, rows = kept.shape[:3]
    step = 2 * half * rows

    @pl.loop(0, chips)
    def _(k):
        grad = contract_rows(tokens[:, tile(k, step)], grads[...]).astype(jnp.bfloat16)
        grad = grad.reshape((2,) + kept.shape[1:])
        kept[k] = jnp.where(place.c == 0, grad[0], grad[1])
        given[k] = jnp.where(place.c == 0, grad[1], grad[0])


class TokenScatter:
    def __init__(self, place, copies, part, from_y, slots, total, result):
        self.place = place
        z, y, c, x = place.z, place.y, place.c, place.x
        self.part, self.from_y, self.slots, self.total = part, from_y, slots, total
        self.line = place.line
        last = self.line - 1
        self.last = last
        self.copies = copies
        self.over_base = copies.reserve(self.line)
        up = place.at(jnp.minimum(z + 1, last), y, c, x)
        down = place.at(jnp.maximum(z - 1, 0), y, c, x)
        self.ups = {d: copies.remote(part.at[d, y], slots.at[d], up) for d in range(1, self.line)}
        self.downs = {}
        for d in range(last):
            slot = jnp.where(z - 1 == d, last + 1, d)
            self.downs[d] = copies.remote(part.at[d, y], slots.at[slot], down)
        self.swap = copies.remote(total.at[1 - c], result.at[c], place.other_core())
        self.own = copies.inside(total.at[c], result.at[c])

    def over(self, k):
        y = self.place.y
        return self.copies.remote_at(
            self.over_base + k, self.part.at[k, 1 - y], self.from_y.at[k], self.place.other_y()
        )

    def combine(self, k):
        self.over(k).wait_recv()
        add_rows(self.part.at[k, self.place.y], self.from_y.at[k], CORES)

    def step(self, j):
        z, y, last = self.place.z, self.place.y, self.last
        above, below = last - j, j

        @pl.when(z < above)
        def _():
            self.combine(above)

            @pl.when(z > 0)
            def _():
                self.ups[above].wait_recv()
                add_rows(self.part.at[above, y], self.slots.at[above], CORES)

            self.ups[above].start()

        @pl.when(z > below)
        def _():
            self.combine(below)

            @pl.when(z < last)
            def _():
                self.downs[below].wait_recv()
                add_rows(self.part.at[below, y], self.slots.at[below], CORES)

            self.downs[below].start()

    def reduce(self):
        z, y, last = self.place.z, self.place.y, self.last
        self.combine(z)
        for d in range(1, self.line):
            pl.when(z == d)(lambda: self.ups[d].wait_recv())
        for d in range(last):
            pl.when(z == d)(lambda: self.downs[d].wait_recv())
        step = 16
        per = self.total.shape[1] // step

        @pl.loop(0, CORES * per)
        def _(i):
            k, at = i // per, tile(i % per, step)
            self.total[k, at, :] = self.part[z, y, k, at, :].astype(jnp.float32)

        def add(slot):
            @pl.loop(0, CORES * per)
            def _(i):
                k, at = i // per, tile(i % per, step)
                self.total[k, at, :] += self.slots[slot, k, at, :].astype(jnp.float32)

        pl.when(z > 0)(lambda: add(z))
        pl.when(z < last)(lambda: add(last + 1))
        self.swap.start()
        self.own.start()

    def finish(self):
        self.swap.wait_recv()

    def drain(self):
        z, last = self.place.z, self.last
        for k in range(self.line):
            self.over(k).wait_send()
        for d, copy in self.ups.items():
            pl.when(z < d)(lambda: copy.wait_send())
        for d, copy in self.downs.items():
            pl.when(z > d)(lambda: copy.wait_send())


def scatter_order(i, last):
    odd = i % 2
    return (1 - odd) * (last - i // 2) + odd * (i // 2)


def output_parts(scatter, attended_low, activated, out_weight, down_weight):
    @pl.loop(0, scatter.line)
    def _(i):
        k = scatter_order(i, scatter.last)
        part = scatter.part
        at = tile(k, part.shape[1] * part.shape[2] * part.shape[3])
        rows = nn(attended_low[at, :], flat_rows(out_weight[...]))
        rows = rows + contract_cols(activated[at, :], flat_rows(down_weight[...]))
        part[k] = rows.astype(part.dtype).reshape(part.shape[1:])
        scatter.over(k).start()


def inner_grads(cot, down_weight, slope, slope_loads, inner_grad):
    step = slope.shape[1]
    for i, load in enumerate(slope_loads):
        load.wait()
        at = slice(i * step, (i + 1) * step)
        grad = nn(cot[at, :], flat_rows(down_weight[...])) * slope[i % 2]
        inner_grad[at, :] = grad.astype(jnp.bfloat16)
        if i + 2 < len(slope_loads):
            slope_loads[i + 2].start()


def hidden_parts(scatter, inner_grad, up_weight, projected_grad, qkv_weight, hid, stats, vec, sums):
    sums[...] = jnp.zeros_like(sums)

    def by_eight(values):
        return jnp.sum(values.reshape(-1, 8, values.shape[1]), axis=0)

    @pl.loop(0, scatter.line)
    def _(i):
        k = scatter_order(i, scatter.last)
        part = scatter.part
        size = part.shape[2] * part.shape[3]

        @pl.loop(0, LINE_Y)
        def _(y):
            at = tile(k * LINE_Y + y, size)
            one = contract_cols(projected_grad[at, :], flat_rows(qkv_weight[...]))
            two = contract_cols(inner_grad[at, :], flat_rows(up_weight[...]))
            xhat = (hid[at, :].astype(jnp.float32) - stats[at, 0:1]) * stats[at, 1:2]
            sums[0] += by_eight(one * xhat)
            sums[1] += by_eight(one)
            sums[2] += by_eight(two * xhat)
            sums[3] += by_eight(two)
            rows = one * vec[0:1, :] + two * vec[2:3, :]
            part[k, y] = rows.astype(part.dtype).reshape(part.shape[2:])

        scatter.over(k).start()


COT_SUM, UP_SUM, QKV_SUM = 4, 5, 7


def pack_small(place, sums, cot_sum, up_sum, qkv_sum, qkv_rows, tiles):
    chips, groups = tiles.shape[:2]
    tiles[...] = jnp.zeros_like(tiles)
    qkv_rows[...] = jnp.zeros_like(qkv_rows)
    third = qkv_rows.shape[0] // 3
    per_head = HEAD // LANES
    for k in range(3):
        for u in range(per_head):
            at = (k * per_head + u) * LANES
            qkv_rows[pl.ds(k * third + place.chip * per_head + u, 1), :] = qkv_sum[0:1, at : at + LANES]
    first = jnp.where(place.chip == 0, 1.0, 0.0)
    norm_sums = [jnp.sum(sums[row], axis=0, keepdims=True) for row in range(4)]
    norm_sums.append(cot_sum[0:1, :] * first)
    for pair in range(chips * groups // 2):
        chip, group = pair // (groups // 2), pair % (groups // 2) * 2
        at = slice(pair * LANES, (pair + 1) * LANES)
        for g in (group, group + 1):
            for row in range(5):
                tiles[chip, g, row : row + 1, :] = norm_sums[row][:, at]
            tiles[chip, g, QKV_SUM : QKV_SUM + 3, :] = qkv_rows[3 * pair : 3 * pair + 3, :]
    for group in range(groups):
        for u in range(2):
            at = (group * 2 + u) * LANES
            row = UP_SUM + u
            values = up_sum[0:1, at : at + LANES].reshape(1, 1, LANES)
            tiles[pl.ds(place.chip, 1), group, row : row + 1, :] = values


def scatter_kernel(
    ctx_count,
    hid_in,
    cot_in,
    qkv_in,
    up_in,
    down_in,
    out_in,
    attended_low_in,
    projected_grad_in,
    norm_two_in,
    activated_in,
    slope_in,
    stats_in,
    vec_in,
    qkv_sum_in,
    cot_sum_in,
    qkv_grad,
    down_grad,
    out_grad,
    small_result,
    qkv_result,
    up_result,
    down_result,
    out_grad_result,
    out_result,
    hid_result,
    wide,
    weight,
    slope,
    act,
    attended_low,
    out_weight,
    qkv_weight,
    projected_grad,
    stats,
    vec,
    qkv_sum,
    cot_sum,
    up_sum,
    sums,
    qkv_rows,
    tiles,
    small_kept,
    small_core,
    small_plane,
    qkv_kept,
    qkv_core,
    qkv_plane,
    up_kept,
    up_core,
    up_plane,
    down_kept,
    down_core,
    down_plane,
    out_kept,
    out_core,
    out_plane,
    out_part,
    out_from_y,
    out_slots,
    hid_part,
    hid_from_y,
    hid_slots,
    total,
    send,
    recv,
    local,
):
    place = Place(ctx_count)
    copies = Copies(send, recv, local)
    c, x = place.c, place.x
    qkv_s = GradScatter(place, copies, qkv_grad, qkv_kept, qkv_core, qkv_plane, qkv_result)
    down_s = GradScatter(place, copies, down_grad, down_kept, down_core, down_plane, down_result)
    up_s = GradScatter(place, copies, down_core, up_kept, up_core, up_plane, up_result)
    small_s = GradScatter(place, copies, tiles, small_kept, small_core, small_plane, small_result)
    outs_s = TokenScatter(place, copies, out_part, out_from_y, out_slots, total, out_result)
    hid_s = TokenScatter(place, copies, hid_part, hid_from_y, hid_slots, total, hid_result)
    out_load = copies.inside(out_grad.at[pl.ds(2 * c, 2)], out_kept)
    out_swap = copies.remote(out_grad.at[pl.ds(2 * (1 - c), 2)], out_core, place.other_core())
    out_across = copies.remote(out_kept.at[1 - x], out_plane, place.other_plane())
    out_own = copies.inside(out_kept.at[x], out_grad_result)
    loads = {
        name: copies.inside(src, dst)
        for name, src, dst in (
            ("activated", activated_in, act),
            ("attended_low", attended_low_in, attended_low),
            ("out", out_in, out_weight),
            ("down", down_in, weight),
            ("cot", cot_in, wide),
            ("norm_two", norm_two_in, wide),
            ("qkv", qkv_in, qkv_weight),
            ("projected_grad", projected_grad_in, projected_grad),
            ("stats", stats_in, stats),
            ("vec", vec_in, vec),
            ("qkv_sum", qkv_sum_in, qkv_sum),
            ("cot_sum", cot_sum_in, cot_sum),
            ("up", up_in, weight),
            ("hid", hid_in, wide),
        )
    }
    early = ("activated", "attended_low", "out", "down", "cot", "qkv", "projected_grad")
    early += ("stats", "vec", "qkv_sum", "cot_sum")

    def out_cross():
        out_load.wait()
        out_swap.wait_recv()
        add_rows(out_kept, out_core, 2)
        out_across.start()

    def out_finish():
        out_across.wait_recv()
        step = 16

        @pl.loop(0, out_plane.shape[0] // step)
        def _(i):
            at = tile(i, step)
            both = out_kept[x, at, :].astype(jnp.float32) + out_plane[at, :].astype(jnp.float32)
            out_kept[x, at, :] = both.astype(out_kept.dtype)

        out_own.start()

    step = slope.shape[1]
    slope_loads = [
        copies.inside(slope_in.at[pl.ds(i * step, step)], slope.at[i % 2]) for i in range(slope_in.shape[0] // step)
    ]
    for name in early:
        loads[name].start()
    slope_loads[0].start()
    slope_loads[1].start()
    greet(place)
    down_s.start()
    qkv_s.start()
    out_load.start()
    out_swap.start()
    for name in ("activated", "attended_low", "out", "down"):
        loads[name].wait()
    output_parts(outs_s, attended_low, act, out_weight, weight)
    down_s.cross()
    qkv_s.cross()
    out_cross()
    loads["cot"].wait()
    inner_grads(wide, weight, slope, slope_loads, act)
    loads["up"].start()
    loads["norm_two"].start()
    outs_s.step(0)
    loads["norm_two"].wait()
    weight_grads_by_core(place, wide, act, up_kept, down_core)
    up_s.swap.start()
    loads["hid"].start()
    outs_s.step(1)
    column_sums(act, up_sum)
    down_s.scatter()
    for name in ("qkv", "projected_grad", "stats", "vec", "up", "hid"):
        loads[name].wait()
    hidden_parts(hid_s, act, weight, projected_grad, qkv_weight, wide, stats, vec, sums)
    up_s.cross(loaded=False)
    outs_s.step(2)
    qkv_s.scatter()
    for name in ("qkv_sum", "cot_sum"):
        loads[name].wait()
    pack_small(place, sums, cot_sum, up_sum, qkv_sum, qkv_rows, tiles)
    small_s.start()
    outs_s.reduce()
    small_s.cross()
    out_finish()
    up_s.scatter()
    small_s.scatter()
    hid_s.step(0)
    hid_s.step(1)
    hid_s.step(2)
    outs_s.own.wait()
    outs_s.swap.wait_send()
    hid_s.reduce()
    grads = (qkv_s, down_s, up_s, small_s)
    for scatter in grads + (outs_s, hid_s):
        scatter.finish()
    out_own.wait()
    hid_s.own.wait()
    hid_s.swap.wait_send()
    for scatter in grads + (outs_s, hid_s):
        scatter.drain()
    out_swap.wait_send()
    out_across.wait_send()


def scatter_all(ctx_count, local_rows, operands):
    f32, b16 = jnp.float32, jnp.bfloat16
    hid, _, w_qkv, w_up, _, w_out = operands[:6]
    chips, groups, rows, head3 = w_qkv.shape
    part = w_up.shape[3]
    tokens, width = hid.shape
    line = chips // LINE_Y
    small = (SMALL_ROWS, LANES)
    token = (CORES, local_rows, width)
    results = [
        ((chips,) + small, f32),
        ((chips, rows, head3), b16),
        ((chips, rows, part), b16),
        ((chips, rows, part), b16),
        ((rows, width), b16),
        (token, f32),
        (token, f32),
    ]
    scratch = [
        ((tokens, width), b16),
        (w_up.shape, b16),
        ((2, 256, part), f32),
        ((tokens, part), b16),
        ((tokens, head3 // 3), b16),
        (w_out.shape, b16),
        (w_qkv.shape, b16),
        ((tokens, head3), b16),
        ((tokens, LANES), f32),
        ((8, width), f32),
        ((8, head3), f32),
        ((8, width), f32),
        ((8, part), f32),
        ((4, 8, width), f32),
        ((3 * width // LANES, LANES), f32),
        ((chips, groups) + small, f32),
    ]
    for shape, dtype in ((small, f32), ((rows, head3), b16), ((rows, part), b16), ((rows, part), b16)):
        scratch += [((chips, 2) + shape, dtype)] * 2 + [((chips,) + shape, dtype)]
    scratch += [((2, rows, width), b16)] * 2 + [((rows, width), b16)]
    for _ in range(2):
        scratch += [
            ((line, LINE_Y) + token, b16),
            ((line,) + token, b16),
            ((line + 1,) + token, b16),
        ]
    scratch += [(token, f32)]
    anywhere = pl.BlockSpec(memory_space=pl.ANY)
    return pl.pallas_call(
        lambda *refs: scatter_kernel(ctx_count, *refs),
        out_shape=[jax.ShapeDtypeStruct(*shape) for shape in results],
        in_specs=[anywhere] * len(operands),
        out_specs=[anywhere] * len(results),
        scratch_shapes=[pltpu.VMEM(*shape) for shape in scratch]
        + [
            pltpu.SemaphoreType.DMA((80,)),
            pltpu.SemaphoreType.DMA((80,)),
            pltpu.SemaphoreType.DMA((40,)),
        ],
        compiler_params=pltpu.CompilerParams(
            collective_id=1, has_side_effects=True, vmem_limit_bytes=VMEM_BYTES
        ),
        name="scatter_all",
    )(*operands)


def small_tile(ln1_gain, ln1_bias, ln2_gain, ln2_bias, out_bias, down_bias, qkv_bias, up_bias):
    half = LANES // 2

    def put(values, row, lane):
        values = values.astype(jnp.float32).reshape(1, -1)
        return lax.pad(
            values,
            jnp.float32(0),
            ((row, SMALL_ROWS - 1 - row, 0), (lane, LANES - lane - values.shape[1], 0)),
        )

    total = jnp.zeros((SMALL_ROWS, LANES), jnp.float32)
    for row, values in (
        (GAIN_ONE, ln1_gain),
        (SHIFT_ONE, ln1_bias),
        (GAIN_TWO, ln2_gain),
        (SHIFT_TWO, ln2_bias),
        (OUT_BIAS, out_bias),
        (DOWN_BIAS, down_bias),
    ):
        total = total + put(values, row, 0) + put(values, row, half)
    total = total + put(qkv_bias[:LANES], QKV_BIAS, 0)
    total = total + put(qkv_bias[LANES:], QKV_BIAS + 1, 0) + put(qkv_bias[:half], QKV_BIAS + 1, half)
    total = total + put(qkv_bias[half:], QKV_BIAS + 2, 0)
    return total + put(up_bias[:LANES], UP_BIAS, 0) + put(up_bias[LANES:], UP_BIAS + 1, 0)


def rotation_tables(positions):
    half_rot = ROT // 2
    where = positions.astype(jnp.float32)[:, None]
    frequency = 1.0 / 10000.0 ** (jnp.arange(half_rot).astype(jnp.float32) * 2.0 / ROT)
    angles = where * frequency[None, :]
    cos, sin = jnp.cos(angles), jnp.sin(angles)
    rest = jnp.ones((positions.shape[0], LANES - ROT), jnp.float32)
    return (
        jnp.concatenate([cos, cos, rest], axis=1),
        jnp.concatenate([-sin, sin, rest * where], axis=1),
    )


def split_body(
    hidden,
    cotangent,
    pairing,
    ln1_gain,
    ln1_bias,
    qkv_weight,
    qkv_bias,
    out_weight,
    out_bias,
    ln2_gain,
    ln2_bias,
    up_weight,
    up_bias,
    down_weight,
    down_bias,
):
    local_rows, seq_count, width = hidden.shape
    ctx_count = lax.axis_size("ctx")
    chips = ctx_count // CORES
    total_rows = local_rows * ctx_count
    f32, b16 = jnp.float32, jnp.bfloat16
    head_id = lax.axis_index("ctx") // CORES
    owned = width // (ctx_count * 2)
    positions = row_positions(pairing, jnp.int32(0), total_rows, local_rows // 2, ctx_count)
    cosine, sine = rotation_tables(positions)
    key_pos = jnp.broadcast_to(positions.astype(f32)[None, :], (8, total_rows))

    (
        hid_all,
        cot_all,
        w_qkv,
        w_up,
        w_down,
        w_out,
        small_all,
        attended_low,
        projected_grad,
        norm_two,
        activated,
        slope,
        grad_qkv,
        grad_down,
        grad_out,
        vec,
        stats,
        qkv_sum,
        cot_sum,
    ) = gather_all(
        ctx_count,
        jnp.swapaxes(hidden, 0, 1),
        jnp.swapaxes(cotangent, 0, 1),
        qkv_weight,
        up_weight,
        down_weight,
        out_weight,
        small_tile(ln1_gain, ln1_bias, ln2_gain, ln2_bias, out_bias, down_bias, qkv_bias, up_bias),
        cosine,
        sine,
        key_pos,
    )
    smalls = small_all.reshape(ctx_count * 2, SMALL_ROWS, LANES)
    b_both = (smalls[:, OUT_BIAS, :owned] + smalls[:, DOWN_BIAS, :owned]).reshape(-1)
    small_sum, qkv_rows, up_rows, down_rows, out_sum, out_rows, hid_rows = scatter_all(
        ctx_count,
        local_rows,
        (
            hid_all,
            cot_all,
            w_qkv,
            w_up,
            w_down,
            w_out,
            attended_low,
            projected_grad,
            norm_two,
            activated,
            slope,
            stats,
            vec,
            qkv_sum,
            cot_sum,
            grad_qkv,
            grad_down,
            grad_out,
        ),
    )

    own = hidden.astype(f32)
    output = (own + jnp.swapaxes(out_rows, 0, 1) + b_both).astype(b16)
    average = jnp.mean(own, axis=-1, keepdims=True)
    spread = jnp.mean((own - average) ** 2, axis=-1, keepdims=True)
    scale = lax.rsqrt(spread + LN_EPSILON)
    xhat = (own - average) * scale
    e = jnp.swapaxes(hid_rows, 0, 1)
    grad_hidden = cotangent.astype(f32) + scale * (
        e - jnp.mean(e, axis=-1, keepdims=True) - xhat * jnp.mean(e * xhat, axis=-1, keepdims=True)
    )
    small = jnp.sum(small_sum, axis=0)
    odd = lax.axis_index("fsdp") == 1
    halves = jnp.where(odd, small[: COT_SUM + 1, owned:], small[: COT_SUM + 1, :owned])
    three = small[QKV_SUM : QKV_SUM + 3].reshape(-1)
    qkv_bias_sum = jnp.where(odd, three[3 * owned :], three[: 3 * owned])
    up_bias_sum = small[UP_SUM : UP_SUM + 2].reshape(-1)

    def columns(pieces, thirds):
        rows = pieces.shape[1]
        split = pieces.astype(f32).reshape(chips, rows, thirds, -1)
        return jnp.transpose(split, (1, 2, 0, 3)).reshape(rows, -1)

    return (
        output,
        grad_hidden,
        halves[0],
        halves[1],
        columns(qkv_rows, 3),
        qkv_bias_sum,
        out_sum.astype(f32),
        halves[COT_SUM],
        halves[2],
        halves[3],
        columns(up_rows, 1),
        up_bias_sum,
        columns(down_rows, 1),
        halves[COT_SUM],
    )


def solution(mesh):
    body = split_body if split_fits(mesh) else general_body
    return jax.shard_map(
        body,
        mesh=mesh,
        in_specs=(
            P("ctx", "fsdp", None),
            P("ctx", "fsdp", None),
            P(),
            P(("ctx", "fsdp")),
            P(("ctx", "fsdp")),
            P(("ctx", "fsdp"), None),
            P(("ctx", "fsdp")),
            P(("ctx", "fsdp"), None),
            P(("ctx", "fsdp")),
            P(("ctx", "fsdp")),
            P(("ctx", "fsdp")),
            P(("ctx", "fsdp"), None),
            P(("ctx", "fsdp")),
            P(("ctx", "fsdp"), None),
            P(("ctx", "fsdp")),
        ),
        out_specs=(
            P("ctx", "fsdp", None),
            P("ctx", "fsdp", None),
            P(("ctx", "fsdp")),
            P(("ctx", "fsdp")),
            P(("ctx", "fsdp"), None),
            P(("ctx", "fsdp")),
            P(("ctx", "fsdp"), None),
            P(("ctx", "fsdp")),
            P(("ctx", "fsdp")),
            P(("ctx", "fsdp")),
            P(("ctx", "fsdp"), None),
            P(("ctx", "fsdp")),
            P(("ctx", "fsdp"), None),
            P(("ctx", "fsdp")),
        ),
        check_vma=False,
    )
```

```python
import functools

import jax
import jax.numpy as jnp
from jax import lax
from jax.experimental import pallas as pl
from jax.experimental.pallas import tpu as pltpu
from jax.sharding import PartitionSpec as P

HEAD = 256
ROT = 64


LN_EPSILON = 1e-05
VERY_LOW = -1e30


def layer_norm(values, ln_gain, ln_shift):
    average = jnp.mean(values, axis=-1, keepdims=True)
    centered = values - average
    spread = jnp.mean(centered * centered, axis=-1, keepdims=True)
    return centered * lax.rsqrt(spread + LN_EPSILON) * ln_gain + ln_shift


def gelu_exact(values):
    return jax.nn.gelu(values, approximate=False)


def rotate(values, positions):
    half_rot = ROT // 2
    frequency = 1.0 / 10000.0 ** (jnp.arange(half_rot).astype(values.dtype) * 2.0 / ROT)
    angles = positions.astype(values.dtype)[:, None] * frequency[None, :]
    shape_out = (angles.shape[0],) + (1,) * (values.ndim - 2) + (ROT,)
    cosine = jnp.concatenate([jnp.cos(angles), jnp.cos(angles)], axis=-1).reshape(shape_out)
    sine_part = jnp.concatenate([jnp.sin(angles), jnp.sin(angles)], axis=-1).reshape(shape_out)
    rot_part = values[..., :ROT]
    turned = jnp.concatenate([-rot_part[..., half_rot:], rot_part[..., :half_rot]], axis=-1)
    return jnp.concatenate([rot_part * cosine + turned * sine_part, values[..., ROT:]], axis=-1)


def row_positions(pairing, first_row, row_count, block_rows, ctx_count):
    row_ids = first_row + jnp.arange(row_count, dtype=jnp.int32)
    device_ids = row_ids // (2 * block_rows)
    within = row_ids % (2 * block_rows)
    matches = device_ids[:, None] == jnp.arange(ctx_count, dtype=jnp.int32)[None, :]
    owned_block = jnp.sum(jnp.where(matches, pairing[None, :], 0), axis=1)
    blocks = jnp.where(within < block_rows, owned_block, 2 * ctx_count - 1 - owned_block)
    return blocks * block_rows + within % block_rows


def heads_view(values, row_total, seq_count):
    return values.reshape(row_total, seq_count, -1, HEAD)


def contract_rows(left, right):
    return lax.dot_general(
        left, right, (((0,), (0,)), ((), ())), preferred_element_type=jnp.float32
    )


def contract_cols(left, right):
    return lax.dot_general(
        left, right, (((1,), (1,)), ((), ())), preferred_element_type=jnp.float32
    )


def pair_grads(
    query_rows, grad_rows, log_rows, delta_rows, query_pos, key_heads, value_heads, key_pos, scaling
):
    scores = (
        jnp.einsum("qshd,kshd->shqk", query_rows, key_heads, preferred_element_type=jnp.float32)
        * scaling
    )
    allowed = key_pos[None, None, None, :] <= query_pos[None, None, :, None]
    probabilities = jnp.where(allowed, jnp.exp(scores - log_rows[..., None]), 0.0)
    prob_grad = jnp.einsum(
        "qshd,kshd->shqk", grad_rows, value_heads, preferred_element_type=jnp.float32
    )
    score_grad = (probabilities * (prob_grad - delta_rows[..., None])).astype(jnp.bfloat16)
    return (score_grad, probabilities.astype(jnp.bfloat16))


def general_body(
    hidden,
    cotangent,
    pairing,
    ln1_gain,
    ln1_bias,
    qkv_weight,
    qkv_bias,
    out_weight,
    out_bias,
    ln2_gain,
    ln2_bias,
    up_weight,
    up_bias,
    down_weight,
    down_bias,
):
    local_rows, seq_count, model_width = hidden.shape
    block_rows = local_rows // 2
    ctx_count = lax.axis_size("ctx")
    head_count = model_width // HEAD
    scaling = HEAD ** (-0.5)
    tokens = local_rows * seq_count
    total_rows = local_rows * ctx_count
    params = (
        lax.all_gather(ln1_gain, ("ctx", "fsdp"), axis=0, tiled=True),
        lax.all_gather(ln1_bias, ("ctx", "fsdp"), axis=0, tiled=True),
        lax.all_gather(qkv_weight, ("ctx", "fsdp"), axis=0, tiled=True),
        lax.all_gather(qkv_bias, ("ctx", "fsdp"), axis=0, tiled=True),
        lax.all_gather(out_weight, ("ctx", "fsdp"), axis=0, tiled=True),
        lax.all_gather(out_bias, ("ctx", "fsdp"), axis=0, tiled=True),
        lax.all_gather(ln2_gain, ("ctx", "fsdp"), axis=0, tiled=True),
        lax.all_gather(ln2_bias, ("ctx", "fsdp"), axis=0, tiled=True),
        lax.all_gather(up_weight, ("ctx", "fsdp"), axis=0, tiled=True),
        lax.all_gather(up_bias, ("ctx", "fsdp"), axis=0, tiled=True),
        lax.all_gather(down_weight, ("ctx", "fsdp"), axis=0, tiled=True),
        lax.all_gather(down_bias, ("ctx", "fsdp"), axis=0, tiled=True),
    )
    (
        gain_one,
        shift_one,
        w_qkv,
        b_qkv,
        w_out,
        b_out,
        gain_two,
        shift_two,
        w_up,
        b_up,
        w_down,
        b_down,
    ) = params
    ff_width = w_up.shape[1]
    hidden_f = hidden.astype(jnp.float32).reshape(tokens, model_width)
    own_pos = row_positions(
        pairing, lax.axis_index("ctx") * local_rows, local_rows, block_rows, ctx_count
    )
    normed_one, ln_one_pull = jax.vjp(
        layer_norm, hidden_f, gain_one.astype(jnp.float32), shift_one.astype(jnp.float32)
    )
    normed_one_low = normed_one.astype(jnp.bfloat16)
    projected = jnp.dot(normed_one_low, w_qkv, preferred_element_type=jnp.float32) + b_qkv.astype(
        jnp.float32
    )
    query_f, rotation_pull = jax.vjp(
        lambda values: rotate(values, own_pos),
        heads_view(projected[:, :model_width], local_rows, seq_count),
    )
    query_b = query_f.astype(jnp.bfloat16)
    key_b = (
        rotate(
            heads_view(projected[:, model_width : 2 * model_width], local_rows, seq_count), own_pos
        )
        .astype(jnp.bfloat16)
        .reshape(local_rows, seq_count, model_width)
    )
    value_b = (
        projected[:, 2 * model_width :]
        .astype(jnp.bfloat16)
        .reshape(local_rows, seq_count, model_width)
    )
    running_max = jnp.full((seq_count, head_count, local_rows), VERY_LOW, jnp.float32)
    key_piece = lax.all_gather(key_b, "ctx", axis=0, tiled=True)
    value_piece = lax.all_gather(value_b, "ctx", axis=0, tiled=True)
    row_total = key_piece.shape[0]
    key_pos = row_positions(pairing, jnp.int32(0), row_total, block_rows, ctx_count)
    scores = (
        jnp.einsum(
            "qshd,kshd->shqk",
            query_b,
            heads_view(key_piece, row_total, seq_count),
            preferred_element_type=jnp.float32,
        )
        * scaling
    )
    allowed = key_pos[None, None, None, :] <= own_pos[None, None, :, None]
    piece_max = jnp.max(jnp.where(allowed, scores, VERY_LOW), axis=-1)
    new_max = jnp.maximum(running_max, piece_max)
    weights = jnp.where(allowed, jnp.exp(scores - new_max[..., None]), 0.0)
    new_total = jnp.sum(weights, axis=-1)
    mixture = jnp.einsum(
        "shqk,kshd->qshd",
        weights.astype(jnp.bfloat16),
        heads_view(value_piece, row_total, seq_count),
        preferred_element_type=jnp.float32,
    )
    log_total = new_max + jnp.log(new_total)
    attended = mixture / jnp.transpose(new_total, (2, 0, 1))[..., None]
    attended_low = attended.astype(jnp.bfloat16).reshape(tokens, model_width)
    branch_attn = jnp.dot(attended_low, w_out, preferred_element_type=jnp.float32) + b_out.astype(
        jnp.float32
    )
    normed_two, ln_two_pull = jax.vjp(
        layer_norm, hidden_f, gain_two.astype(jnp.float32), shift_two.astype(jnp.float32)
    )
    normed_two_low = normed_two.astype(jnp.bfloat16)
    inner_act = jnp.dot(normed_two_low, w_up, preferred_element_type=jnp.float32) + b_up.astype(
        jnp.float32
    )
    activated_f, gelu_pull = jax.vjp(gelu_exact, inner_act)
    activated = activated_f.astype(jnp.bfloat16)
    branch_mlp = contract_cols(activated, w_down) + b_down.astype(jnp.float32)
    output = (
        (hidden_f + branch_attn + branch_mlp)
        .astype(jnp.bfloat16)
        .reshape(local_rows, seq_count, model_width)
    )
    back_qkv, back_out, back_up, back_down = (
        lax.all_gather(qkv_weight, ("ctx", "fsdp"), axis=0, tiled=True),
        lax.all_gather(out_weight, ("ctx", "fsdp"), axis=0, tiled=True),
        lax.all_gather(up_weight, ("ctx", "fsdp"), axis=0, tiled=True),
        lax.all_gather(down_weight, ("ctx", "fsdp"), axis=0, tiled=True),
    )
    grad_out = cotangent.reshape(tokens, model_width)
    grad_f = grad_out.astype(jnp.float32)
    bias_sum = jnp.sum(grad_f, axis=0)
    up_grad = jnp.dot(grad_out, back_down, preferred_element_type=jnp.float32)
    inner_grad = gelu_pull(up_grad)[0].astype(jnp.bfloat16)
    norm_two_grad = contract_cols(inner_grad, back_up)
    dx_two, dgain_two, dshift_two = ln_two_pull(norm_two_grad)
    up_bias_sum = jnp.sum(inner_grad, axis=0, dtype=jnp.float32)
    mlp_small = jnp.concatenate(
        [
            up_bias_sum.reshape(model_width, -1),
            jnp.stack([bias_sum, dgain_two, dshift_two], axis=1),
        ],
        axis=1,
    )
    up_w_sum, down_w_sum, mlp_small_sum = (
        lax.psum_scatter(
            contract_rows(normed_two_low, inner_grad),
            ("ctx", "fsdp"),
            scatter_dimension=0,
            tiled=True,
        ),
        lax.psum_scatter(
            contract_rows(grad_out, activated), ("ctx", "fsdp"), scatter_dimension=0, tiled=True
        ),
        lax.psum_scatter(mlp_small, ("ctx", "fsdp"), scatter_dimension=0, tiled=True),
    )
    ratio = ff_width // model_width
    attn_grad = contract_cols(grad_out, back_out).astype(jnp.bfloat16)
    out_w_grad = contract_rows(attended_low, grad_out)
    grad_heads = heads_view(attn_grad, local_rows, seq_count)
    row_delta = jnp.einsum("qshd,qshd->shq", grad_heads.astype(jnp.float32), attended)
    keys_all, values_all = (
        lax.all_gather(key_b, "ctx", axis=0, tiled=True),
        lax.all_gather(value_b, "ctx", axis=0, tiled=True),
    )
    key_block = 512
    block_count = total_rows // key_block
    starts = jnp.arange(block_count, dtype=jnp.int32) * key_block

    def query_step(query_grad, inputs):
        key_piece, value_piece, offset = inputs
        key_pos = row_positions(pairing, offset, key_block, block_rows, ctx_count)
        key_heads = heads_view(key_piece, key_block, seq_count)
        value_heads = heads_view(value_piece, key_block, seq_count)
        score_grad, unused = pair_grads(
            query_b,
            grad_heads,
            log_total,
            row_delta,
            own_pos,
            key_heads,
            value_heads,
            key_pos,
            scaling,
        )
        query_grad = (
            query_grad
            + jnp.einsum(
                "shqk,kshd->qshd", score_grad, key_heads, preferred_element_type=jnp.float32
            )
            * scaling
        )
        return (query_grad, None)

    query_grad, unused_out = lax.scan(
        query_step,
        jnp.zeros((local_rows, seq_count, head_count, HEAD), jnp.float32),
        (
            keys_all.reshape(block_count, key_block, seq_count, model_width),
            values_all.reshape(block_count, key_block, seq_count, model_width),
            starts,
        ),
    )
    queries_all, grads_all = (
        lax.all_gather(query_b, "ctx", axis=0, tiled=True),
        lax.all_gather(grad_heads, "ctx", axis=0, tiled=True),
    )
    logs_all, deltas_all = (
        lax.all_gather(log_total, "ctx", axis=2, tiled=True),
        lax.all_gather(row_delta, "ctx", axis=2, tiled=True),
    )
    own_keys = heads_view(key_b, local_rows, seq_count)
    own_values = heads_view(value_b, local_rows, seq_count)

    def key_step(carry, inputs):
        key_acc, value_acc = carry
        query_piece, grad_piece, log_piece, delta_piece, offset = inputs
        query_pos = row_positions(pairing, offset, key_block, block_rows, ctx_count)
        score_grad, probs_low = pair_grads(
            query_piece,
            grad_piece,
            log_piece,
            delta_piece,
            query_pos,
            own_keys,
            own_values,
            own_pos,
            scaling,
        )
        key_acc = (
            key_acc
            + jnp.einsum(
                "shqk,qshd->kshd", score_grad, query_piece, preferred_element_type=jnp.float32
            )
            * scaling
        )
        value_acc = value_acc + jnp.einsum(
            "shqk,qshd->kshd", probs_low, grad_piece, preferred_element_type=jnp.float32
        )
        return ((key_acc, value_acc), None)

    empty_acc = jnp.zeros((local_rows, seq_count, head_count, HEAD), jnp.float32)
    log_blocks = jnp.moveaxis(logs_all.reshape(seq_count, head_count, block_count, key_block), 2, 0)
    delta_blocks = jnp.moveaxis(
        deltas_all.reshape(seq_count, head_count, block_count, key_block), 2, 0
    )
    (key_sum, value_sum), unused_keys = lax.scan(
        key_step,
        (empty_acc, empty_acc),
        (
            queries_all.reshape(block_count, key_block, seq_count, head_count, HEAD),
            grads_all.reshape(block_count, key_block, seq_count, head_count, HEAD),
            log_blocks,
            delta_blocks,
            starts,
        ),
    )
    key_owned = key_sum.reshape(local_rows, seq_count, model_width)
    value_owned = value_sum.reshape(local_rows, seq_count, model_width)
    query_pre = rotation_pull(query_grad)[0].reshape(tokens, model_width)
    key_pre = rotation_pull(heads_view(key_owned, local_rows, seq_count))[0].reshape(
        tokens, model_width
    )
    value_pre = value_owned.reshape(tokens, model_width)
    projected_grad = jnp.concatenate([query_pre, key_pre, value_pre], axis=1).astype(jnp.bfloat16)
    norm_one_grad = contract_cols(projected_grad, back_qkv)
    dx_one, dgain_one, dshift_one = ln_one_pull(norm_one_grad)
    qkv_bias_sum = jnp.sum(projected_grad, axis=0, dtype=jnp.float32)
    attn_small = jnp.concatenate(
        [
            qkv_bias_sum.reshape(model_width, -1),
            jnp.stack([bias_sum, dgain_one, dshift_one], axis=1),
        ],
        axis=1,
    )
    qkv_w_sum, out_w_sum, attn_small_sum = (
        lax.psum_scatter(
            contract_rows(normed_one_low, projected_grad),
            ("ctx", "fsdp"),
            scatter_dimension=0,
            tiled=True,
        ),
        lax.psum_scatter(out_w_grad, ("ctx", "fsdp"), scatter_dimension=0, tiled=True),
        lax.psum_scatter(attn_small, ("ctx", "fsdp"), scatter_dimension=0, tiled=True),
    )
    grad_hidden = (grad_f + dx_one + dx_two).reshape(local_rows, seq_count, model_width)
    return (
        output,
        grad_hidden,
        attn_small_sum[:, 4],
        attn_small_sum[:, 5],
        qkv_w_sum,
        attn_small_sum[:, :3].reshape(-1),
        out_w_sum,
        attn_small_sum[:, 3],
        mlp_small_sum[:, ratio + 1],
        mlp_small_sum[:, ratio + 2],
        up_w_sum,
        mlp_small_sum[:, :ratio].reshape(-1),
        down_w_sum,
        mlp_small_sum[:, ratio],
    )


MESH = pl.DeviceIdType.MESH
CORES = 2
LINE_Y = 2
VMEM_BYTES = 60 * 2**20


def split_fits(mesh):
    return mesh.shape["ctx"] == 16 and mesh.shape["fsdp"] == 2


class Place:
    def __init__(self, ctx_count):
        self.chips = ctx_count // CORES
        self.line = self.chips // LINE_Y
        index = lax.axis_index("ctx")
        self.c = index % CORES
        self.chip = index // CORES
        self.y = self.chip % LINE_Y
        self.z = self.chip // LINE_Y
        self.x = lax.axis_index("fsdp")

    def at(self, z, y, c, x):
        return ((z * LINE_Y + y) * CORES + c, x)

    def other_core(self):
        return self.at(self.z, self.y, 1 - self.c, self.x)

    def other_plane(self):
        return self.at(self.z, self.y, self.c, 1 - self.x)

    def other_y(self):
        return self.at(self.z, 1 - self.y, self.c, self.x)

    def plane_offsets(self):
        return [(dz, dy) for dz in range(self.line) for dy in range(LINE_Y) if dz or dy]

    def shifted(self, dz, dy):
        return (self.z + dz) % self.line, (self.y + dy) % LINE_Y


class Copies:
    def __init__(self, send, recv, local):
        self.send, self.recv, self.local = send, recv, local
        self.remotes, self.locals = 0, 0

    def reserve(self, count):
        self.remotes += count
        return self.remotes - count

    def remote(self, src, dst, device):
        return self.remote_at(self.reserve(1), src, dst, device)

    def remote_at(self, i, src, dst, device):
        return pltpu.make_async_remote_copy(
            src_ref=src,
            dst_ref=dst,
            send_sem=self.send.at[i],
            recv_sem=self.recv.at[i],
            device_id=device,
            device_id_type=MESH,
        )

    def inside(self, src, dst):
        i = self.locals
        self.locals += 1
        return pltpu.make_async_copy(src, dst, self.local.at[i])


def greet(place):
    barrier = pltpu.get_barrier_semaphore()
    partners = [place.other_core(), place.other_plane()]
    for dz, dy in place.plane_offsets():
        z, y = place.shifted(dz, dy)
        partners.append(place.at(z, y, place.c, place.x))
    for partner in partners:
        pl.semaphore_signal(barrier, inc=1, device_id=partner, device_id_type=MESH)
    pl.semaphore_wait(barrier, len(partners))


class TokenGather:
    def __init__(self, place, copies, own, whole):
        self.place = place
        self.whole = whole
        c, chip, z, y = place.c, place.chip, place.z, place.y
        rows = own.shape[1]
        block = whole.at[pl.ds(pl.multiple_of((chip * CORES + c) * rows, rows), rows)]
        self.first = copies.remote(own.at[1 - c], block, place.other_core())
        self.mine = copies.inside(own.at[c], block)
        last = place.line - 1
        up = place.at(jnp.minimum(z + 1, last), y, c, place.x)
        down = place.at(jnp.maximum(z - 1, 0), y, c, place.x)

        def pair(zz):
            first = (jnp.clip(zz, 0, last) * LINE_Y + y) * CORES * rows
            return whole.at[pl.ds(pl.multiple_of(first, CORES * rows), CORES * rows)]

        self.ups = [copies.remote(pair(z - j), pair(z - j), up) for j in range(last)]
        self.downs = [copies.remote(pair(z + j), pair(z + j), down) for j in range(last)]
        self.over_own = copies.remote(pair(z), pair(z), place.other_y())
        self.over_ups = [copies.remote(pair(z - 1 - j), pair(z - 1 - j), place.other_y()) for j in range(last)]
        self.over_downs = [copies.remote(pair(z + 1 + j), pair(z + 1 + j), place.other_y()) for j in range(last)]
        self.last = last

    def start(self):
        self.mine.start()
        self.first.start()

    def spread(self):
        self.mine.wait()
        self.first.wait_recv()
        z = self.place.z
        pl.when(z < self.last)(lambda: self.ups[0].start())
        pl.when(z > 0)(lambda: self.downs[0].start())
        self.over_own.start()

    def step(self, j):
        z, last = self.place.z, self.last

        @pl.when(z - 1 - j >= 0)
        def _():
            self.ups[j].wait_recv()
            if j + 1 < last:
                pl.when(z < last)(lambda: self.ups[j + 1].start())
            self.over_ups[j].start()

        @pl.when(z + 1 + j <= last)
        def _():
            self.downs[j].wait_recv()
            if j + 1 < last:
                pl.when(z > 0)(lambda: self.downs[j + 1].start())
            self.over_downs[j].start()

    def finish(self):
        z, last = self.place.z, self.last
        self.over_own.wait_recv()
        for j in range(last):
            pl.when(z - 1 - j >= 0)(lambda: self.over_ups[j].wait_recv())
            pl.when(z + 1 + j <= last)(lambda: self.over_downs[j].wait_recv())

    def drain(self):
        z, last = self.place.z, self.last
        self.first.wait_send()
        self.over_own.wait_send()
        for j in range(last):
            pl.when((z - j >= 0) & (z < last))(lambda: self.ups[j].wait_send())
            pl.when((z + j <= last) & (z > 0))(lambda: self.downs[j].wait_send())
            pl.when(z - 1 - j >= 0)(lambda: self.over_ups[j].wait_send())
            pl.when(z + 1 + j <= last)(lambda: self.over_downs[j].wait_send())


class WeightGather:
    def __init__(self, place, copies, pieces, whole, columns=slice(None)):
        self.place = place
        group = 2 * place.c + place.x
        self.by_chip = []
        for dz, dy in place.plane_offsets():
            z, y = place.shifted(dz, dy)
            device = place.at(z, y, place.c, place.x)
            self.by_chip.append(
                [copies.remote(src, dst, device) for src, dst in pieces(z * LINE_Y + y, place.chip, group)]
            )
        self.kept = [copies.inside(src, dst) for src, dst in pieces(place.chip, place.chip, group)]
        mine = whole.at[:, group, :, columns]
        self.across = copies.remote(mine, mine, place.other_plane())
        pair = whole.at[:, pl.ds(2 * place.c, 2), :, columns]
        self.swap = copies.remote(pair, pair, place.other_core())

    def send(self, i):
        for copy in self.by_chip[i] + (self.kept if i == 0 else []):
            copy.start()

    def scatter(self):
        for i in range(len(self.by_chip)):
            self.send(i)

    def cross(self):
        for copy in self.kept:
            copy.wait()
        for copies in self.by_chip:
            for copy in copies:
                copy.wait_recv()
        self.across.start()

    def share(self):
        self.across.wait_recv()
        self.swap.start()

    def finish(self):
        self.swap.wait_recv()

    def drain(self):
        for copy in sum(self.by_chip, []) + [self.across, self.swap]:
            copy.wait_send()


NORM_PARTS = 4
GATHER_ORDER = (
    "qkv 6",
    "hid spread",
    "up b 0",
    "up a 0",
    "out start",
    "qkv 1",
    "qkv 0",
    "hid 0",
    "small cross",
    "up a 1",
    "qkv 2",
    "small share",
    "down b 0",
    "up b 5",
    "up b 2",
    "hid 1",
    "up a 3",
    "small done",
    "up a 5",
    "out share",
    "qkv 5",
    "cot spread",
    "qkv 3",
    "qkv 4",
    "up a 4",
    "qkv cross",
    "hid 2",
    "down a 0",
    "up a 6",
    "up a 2",
    "up b 1",
    "up b 3",
    "cot 0",
    "up a cross",
    "hid done",
    "norm",
    "up b 4",
    "up b 6",
    "qkv share",
    "norm",
    "down a 2",
    "cot 1",
    "down a 1",
    "down a 4",
    "up b cross",
    "down a 5",
    "norm",
    "norm",
    "norm done",
    "up a share",
    "project",
    "down a 6",
    "down a 3",
    "cot 2",
    "up b share",
    "attend",
    "down a cross",
    "down b 3",
    "down b 2",
    "down b 5",
    "inner",
    "down b 4",
    "down b 6",
    "down b 1",
    "cot done",
    "out grads",
    "down b cross",
    "down grads",
    "attention back",
    "down a share",
    "down b share",
    "qkv grads",
)


def nn(left, right):
    return lax.dot_general(left, right, (((1,), (0,)), ((), ())), preferred_element_type=jnp.float32)


def tile(i, size):
    return pl.ds(pl.multiple_of(i * size, size), size)


def flat_rows(values):
    return values.reshape(-1, values.shape[-1])


GAIN_ONE, SHIFT_ONE, GAIN_TWO, SHIFT_TWO, OUT_BIAS, DOWN_BIAS, QKV_BIAS, UP_BIAS, SMALL_ROWS = (
    0,
    1,
    2,
    3,
    4,
    5,
    6,
    9,
    16,
)
LANES = 128


def lanes_of(shape):
    return lax.broadcasted_iota(jnp.int32, shape, len(shape) - 1)


def assemble_small(place, small, vec, qkv_rows, qkv_bias, up_bias):
    chips, groups = small.shape[:2]
    low = lanes_of((1, LANES)) < LANES // 2
    for pair in range(chips * groups // 2):
        chip, group = pair // (groups // 2), pair % (groups // 2) * 2
        for row in range(4):
            a = small[chip, group, row : row + 1, :]
            b = small[chip, group + 1, row : row + 1, :]
            vec[row : row + 1, pair * LANES : (pair + 1) * LANES] = jnp.where(low, a, b)
        qkv_rows[3 * pair : 3 * pair + 1, :] = small[chip, group, QKV_BIAS : QKV_BIAS + 1, :]
        a = small[chip, group, QKV_BIAS + 1 : QKV_BIAS + 2, :]
        b = small[chip, group + 1, QKV_BIAS + 1 : QKV_BIAS + 2, :]
        qkv_rows[3 * pair + 1 : 3 * pair + 2, :] = jnp.where(low, a, b)
        qkv_rows[3 * pair + 2 : 3 * pair + 3, :] = small[chip, group + 1, QKV_BIAS + 2 : QKV_BIAS + 3, :]
    third = qkv_rows.shape[0] // 3
    per_head = HEAD // LANES
    for k in range(3):
        for u in range(per_head):
            at = (k * per_head + u) * LANES
            qkv_bias[0:1, at : at + LANES] = qkv_rows[pl.ds(k * third + place.chip * per_head + u, 1), :]
    for group in range(groups):
        for u in range(2):
            at = (group * 2 + u) * LANES
            row = UP_BIAS + u
            up_bias[0:1, at : at + LANES] = small[pl.ds(place.chip, 1), group, row : row + 1, :].reshape(1, LANES)


def norm_rows(start, count, hid, vec, norm_one, norm_two, stats):
    step = 16

    @pl.loop(0, count // step)
    def _(i):
        at = pl.ds(pl.multiple_of(start + i * step, step), step)
        x = hid[at, :].astype(jnp.float32)
        average = jnp.mean(x, axis=1, keepdims=True)
        centered = x - average
        scale = lax.rsqrt(jnp.mean(centered * centered, axis=1, keepdims=True) + LN_EPSILON)
        stats[at, 0:1] = average
        stats[at, 1:2] = scale
        xhat = centered * scale
        norm_one[at, :] = (xhat * vec[0:1, :] + vec[1:2, :]).astype(jnp.bfloat16)
        norm_two[at, :] = (xhat * vec[2:3, :] + vec[3:4, :]).astype(jnp.bfloat16)


def turned_half(values):
    half_rot = ROT // 2
    lane = lanes_of(values.shape)
    width = values.shape[-1]
    return jnp.where(
        lane < half_rot,
        pltpu.roll(values, width - half_rot, 1),
        jnp.where(lane < ROT, pltpu.roll(values, half_rot, 1), 0.0),
    )


def project(norm_one, weight, bias, cosine, sine, query, key, value):
    step = 256

    @pl.loop(0, norm_one.shape[0] // step)
    def _(i):
        at = tile(i, step)
        both = nn(norm_one[at, :], flat_rows(weight[...])) + bias[0:1, :]
        cos, sin = cosine[at, :], sine[at, :]
        for k, target in enumerate((query, key)):
            first = both[:, k * HEAD : k * HEAD + LANES]
            target[at, 0:LANES] = (first * cos + turned_half(first) * sin).astype(jnp.bfloat16)
            target[at, LANES:HEAD] = both[:, k * HEAD + LANES : (k + 1) * HEAD].astype(jnp.bfloat16)
        value[at, :] = both[:, 2 * HEAD :].astype(jnp.bfloat16)


def attend(query, key, value, sine, key_pos, attended, attended_low, probs, probs_low):
    step = 256

    @pl.loop(0, query.shape[0] // step)
    def _(i):
        at = tile(i, step)
        scores = contract_cols(query[at, :], key[...]) * HEAD**-0.5
        allowed = key_pos[0:1, :] <= sine[at, ROT : ROT + 1]
        scores = jnp.where(allowed, scores, VERY_LOW)
        highest = jnp.max(scores, axis=1, keepdims=True)
        weights = jnp.where(allowed, jnp.exp(scores - highest), 0.0)
        weights = weights / jnp.sum(weights, axis=1, keepdims=True)
        low = weights.astype(jnp.bfloat16)
        probs[at, :] = weights
        probs_low[at, :] = low
        total = nn(low, value[...])
        attended[at, :] = total
        attended_low[at, :] = total.astype(jnp.bfloat16)


def feed_inner(norm_two, weight, bias, activated, slope):
    step = 128

    @pl.loop(0, norm_two.shape[0] // step)
    def _(i):
        at = tile(i, step)
        inner = nn(norm_two[at, :], flat_rows(weight[...])) + bias[0:1, :]
        normal = 0.5 + 0.5 * lax.erf(inner * 0.5**0.5)
        activated[at, :] = (inner * normal).astype(jnp.bfloat16)
        density = (2.0 * jnp.pi) ** -0.5 * jnp.exp(-0.5 * inner * inner)
        slope[at, :] = normal + inner * density


def attended_grads(cot, weight, attended_low, attended_grad, weight_grad):
    @pl.loop(0, cot.shape[0] // 256)
    def _(i):
        at = tile(i, 256)
        attended_grad[at, :] = contract_cols(cot[at, :], flat_rows(weight[...])).astype(jnp.bfloat16)

    @pl.loop(0, cot.shape[1] // 512)
    def _(i):
        at = tile(i, 512)
        grad = contract_rows(attended_low[...], cot[:, at]).astype(jnp.bfloat16)
        weight_grad[:, :, at] = grad.reshape(weight_grad.shape[0], weight_grad.shape[1], 512)


def attention_grads(
    query, key, value, cosine, sine, attended, attended_grad, probs, probs_low, score_grad, projected_grad
):
    step = 256
    scaling = HEAD**-0.5

    def put(at, k, grad):
        first = grad[:, 0:LANES]
        back = first * cosine[at, :] - turned_half(first) * sine[at, :]
        projected_grad[at, k * HEAD : k * HEAD + LANES] = back.astype(jnp.bfloat16)
        projected_grad[at, k * HEAD + LANES : (k + 1) * HEAD] = grad[:, LANES:].astype(jnp.bfloat16)

    @pl.loop(0, query.shape[0] // step)
    def _(i):
        at = tile(i, step)
        own = attended_grad[at, :]
        row_delta = jnp.sum(own.astype(jnp.float32) * attended[at, :], axis=1, keepdims=True)
        grad = (probs[at, :] * (contract_cols(own, value[...]) - row_delta)).astype(jnp.bfloat16)
        score_grad[at, :] = grad
        put(at, 0, nn(grad, key[...]) * scaling)

    @pl.loop(0, query.shape[0] // step)
    def _(i):
        at = tile(i, step)
        put(at, 1, contract_rows(score_grad[:, at], query[...]) * scaling)
        projected_grad[at, 2 * HEAD :] = contract_rows(probs_low[:, at], attended_grad[...]).astype(jnp.bfloat16)


def weight_grads(tokens, grads, result):
    chips, groups, rows = result.shape[:3]
    step = groups * rows

    @pl.loop(0, chips)
    def _(k):
        grad = contract_rows(tokens[:, tile(k, step)], grads[...]).astype(jnp.bfloat16)
        result[k] = grad.reshape(result.shape[1:])


def column_sums(values, result):
    step = 16

    def add(i, total):
        return total + values[tile(i, step), :].astype(jnp.float32)

    total = lax.fori_loop(0, values.shape[0] // step, add, jnp.zeros((step, values.shape[1]), jnp.float32))
    result[0:1, :] = jnp.sum(total, axis=0, keepdims=True)


def gather_kernel(
    ctx_count,
    hid,
    cot,
    qkv,
    up,
    down,
    out,
    small,
    cosine_in,
    sine_in,
    key_pos_in,
    hid_all,
    cot_all,
    qkv_all,
    up_all,
    down_all,
    out_all,
    small_all,
    attended_low_out,
    projected_grad_out,
    norm_two_out,
    activated_out,
    slope_out,
    qkv_grad_out,
    down_grad_out,
    out_grad_out,
    vec_out,
    stats_out,
    qkv_sum_out,
    cot_sum_out,
    hid_v,
    cot_v,
    qkv_v,
    up_v,
    out_v,
    small_v,
    cosine,
    sine,
    key_pos,
    vec,
    qkv_rows,
    qkv_bias,
    up_bias,
    norm_one,
    norm_two,
    stats,
    query,
    key,
    value,
    attended,
    attended_low,
    probs,
    probs_low,
    activated,
    slope,
    attended_grad,
    score_grad,
    projected_grad,
    out_grad,
    qkv_sum,
    cot_sum,
    send,
    recv,
    local,
):
    place = Place(ctx_count)
    copies = Copies(send, recv, local)
    width = out.shape[1]
    head = qkv_all.shape[3] // 3
    part = up_all.shape[3]

    def qkv_pieces(to, row, group):
        return [
            (
                qkv.at[:, pl.ds(pl.multiple_of(k * width + to * head, head), head)],
                qkv_all.at[row, group, :, pl.ds(k * head, head)],
            )
            for k in range(3)
        ]

    half = part // 2

    def half_gather(source, whole, first):
        columns = pl.ds(first, half)

        def pieces(to, row, group):
            given = pl.ds(pl.multiple_of(to * part + first, half), half)
            return [(source.at[:, given], whole.at[row, group, :, columns])]

        return WeightGather(place, copies, pieces, whole, columns)

    hid_g = TokenGather(place, copies, hid, hid_all)
    cot_g = TokenGather(place, copies, cot, cot_all)
    small_g = WeightGather(place, copies, lambda to, row, group: [(small, small_all.at[row, group])], small_all)
    qkv_g = WeightGather(place, copies, qkv_pieces, qkv_all)
    weights = {"qkv": qkv_g}
    for name, source, whole in (("up", up, up_all), ("down", down, down_all)):
        weights[name + " a"] = half_gather(source, whole, 0)
        weights[name + " b"] = half_gather(source, whole, half)
    group = 2 * place.c + place.x
    out_mine = copies.inside(out, out_all.at[group])
    out_across = copies.remote(out, out_all.at[group], place.other_plane())
    out_pair = out_all.at[pl.ds(2 * place.c, 2)]
    out_swap = copies.remote(out_pair, out_pair, place.other_core())
    loads = {
        name: copies.inside(src, dst)
        for name, src, dst in (
            ("cosine", cosine_in, cosine),
            ("sine", sine_in, sine),
            ("key_pos", key_pos_in, key_pos),
            ("small", small_all, small_v),
            ("hid", hid_all, hid_v),
            ("cot", cot_all, cot_v),
            ("qkv", qkv_all, qkv_v),
            ("up", up_all, up_v),
            ("out", out_all, out_v),
        )
    }
    stores = {
        name: copies.inside(src, dst)
        for name, src, dst in (
            ("vec", vec, vec_out),
            ("stats", stats, stats_out),
            ("attended_low", attended_low, attended_low_out),
            ("norm_two", norm_two, norm_two_out),
            ("activated", activated, activated_out),
            ("slope", slope, slope_out),
            ("out_grad", out_grad, out_grad_out),
            ("projected_grad", projected_grad, projected_grad_out),
            ("qkv_grad", qkv_v, qkv_grad_out),
            ("down_grad", up_v, down_grad_out),
            ("qkv_sum", qkv_sum, qkv_sum_out),
            ("cot_sum", cot_sum, cot_sum_out),
        )
    }

    def fetch(name):
        loads[name].start()
        loads[name].wait()

    rows = hid_v.shape[0]
    normed = iter(range(NORM_PARTS))

    def norm_next():
        part_rows = rows // NORM_PARTS
        norm_rows(next(normed) * part_rows, part_rows, hid_v, vec, norm_one, norm_two, stats)

    def norm_done():
        stores["norm_two"].start()
        stores["stats"].start()

    def small_done():
        small_g.finish()
        fetch("small")
        assemble_small(place, small_v, vec, qkv_rows, qkv_bias, up_bias)
        stores["vec"].start()

    def hid_done():
        hid_g.finish()
        fetch("hid")

    def project_all():
        qkv_g.finish()
        fetch("qkv")
        for name in ("cosine", "sine", "key_pos"):
            loads[name].wait()
        project(norm_one, qkv_v, qkv_bias, cosine, sine, query, key, value)

    def attend_all():
        attend(query, key, value, sine, key_pos, attended, attended_low, probs, probs_low)
        stores["attended_low"].start()

    def inner_all():
        weights["up a"].finish()
        weights["up b"].finish()
        fetch("up")
        feed_inner(norm_two, up_v, up_bias, activated, slope)
        stores["activated"].start()
        stores["slope"].start()

    def out_start():
        out_mine.start()
        out_across.start()

    def out_share():
        out_mine.wait()
        out_across.wait_recv()
        out_swap.start()

    def cot_done():
        cot_g.finish()
        loads["cot"].start()
        out_swap.wait_recv()
        fetch("out")
        loads["cot"].wait()

    def out_grads():
        attended_grads(cot_v, out_v, attended_low, attended_grad, out_grad)
        stores["out_grad"].start()

    def down_grads():
        weight_grads(cot_v, activated, up_v)
        stores["down_grad"].start()
        column_sums(cot_v, cot_sum)
        stores["cot_sum"].start()

    def attention_back():
        attention_grads(
            query, key, value, cosine, sine, attended, attended_grad, probs, probs_low, score_grad, projected_grad
        )
        stores["projected_grad"].start()

    def qkv_grads():
        weight_grads(norm_one, projected_grad, qkv_v)
        stores["qkv_grad"].start()
        column_sums(projected_grad, qkv_sum)
        stores["qkv_sum"].start()

    steps = {
        "hid spread": hid_g.spread,
        "cot spread": cot_g.spread,
        "small cross": small_g.cross,
        "small share": small_g.share,
        "small done": small_done,
        "out start": out_start,
        "out share": out_share,
        "hid done": hid_done,
        "norm": norm_next,
        "norm done": norm_done,
        "project": project_all,
        "attend": attend_all,
        "inner": inner_all,
        "cot done": cot_done,
        "out grads": out_grads,
        "down grads": down_grads,
        "attention back": attention_back,
        "qkv grads": qkv_grads,
    }
    for j in range(place.line - 1):
        steps["hid %d" % j] = functools.partial(hid_g.step, j)
        steps["cot %d" % j] = functools.partial(cot_g.step, j)
    for name, gather in weights.items():
        for i in range(len(gather.by_chip)):
            steps["%s %d" % (name, i)] = functools.partial(gather.send, i)
        steps[name + " cross"] = gather.cross
        steps[name + " share"] = gather.share

    for name in ("cosine", "sine", "key_pos"):
        loads[name].start()
    greet(place)
    hid_g.start()
    cot_g.start()
    small_g.scatter()
    for name in GATHER_ORDER:
        steps[name]()
    weights["down a"].finish()
    weights["down b"].finish()
    for store in stores.values():
        store.wait()
    for gather in [hid_g, cot_g, small_g] + list(weights.values()):
        gather.drain()
    out_across.wait_send()
    out_swap.wait_send()


def gather_all(ctx_count, hid, cot, qkv, up, down, out, small, cosine, sine, key_pos):
    f32, b16 = jnp.float32, jnp.bfloat16
    chips = ctx_count // CORES
    rows = qkv.shape[0]
    groups = CORES * 2
    tokens = ctx_count * hid.shape[1]
    width = out.shape[1]
    head3, part = qkv.shape[1] // chips, up.shape[1] // chips
    head = head3 // 3
    qkv_s = ((chips, groups, rows, head3), b16)
    part_s = ((chips, groups, rows, part), b16)
    out_s = ((groups, rows, width), b16)
    small_s = ((chips, groups) + small.shape, f32)
    wide_s, narrow_s = ((tokens, width), b16), ((tokens, head), b16)
    results = [
        wide_s,
        wide_s,
        qkv_s,
        part_s,
        part_s,
        out_s,
        small_s,
        narrow_s,
        ((tokens, head3), b16),
        wide_s,
        ((tokens, part), b16),
        ((tokens, part), f32),
        qkv_s,
        part_s,
        out_s,
        ((8, width), f32),
        ((tokens, LANES), f32),
        ((8, head3), f32),
        ((8, width), f32),
    ]
    scratch = [
        wide_s,
        wide_s,
        qkv_s,
        part_s,
        out_s,
        small_s,
        ((tokens, LANES), f32),
        ((tokens, LANES), f32),
        ((8, tokens), f32),
        ((8, width), f32),
        ((3 * width // LANES, LANES), f32),
        ((8, head3), f32),
        ((8, part), f32),
        wide_s,
        wide_s,
        ((tokens, LANES), f32),
        narrow_s,
        narrow_s,
        narrow_s,
        ((tokens, head), f32),
        narrow_s,
        ((tokens, tokens), f32),
        ((tokens, tokens), b16),
        ((tokens, part), b16),
        ((tokens, part), f32),
        narrow_s,
        ((tokens, tokens), b16),
        ((tokens, head3), b16),
        out_s,
        ((8, head3), f32),
        ((8, width), f32),
    ]
    operands = (hid, cot, qkv, up, down, out, small, cosine, sine, key_pos)
    anywhere = pl.BlockSpec(memory_space=pl.ANY)
    return pl.pallas_call(
        lambda *refs: gather_kernel(ctx_count, *refs),
        out_shape=[jax.ShapeDtypeStruct(*shape) for shape in results],
        in_specs=[anywhere] * len(operands),
        out_specs=[anywhere] * len(results),
        scratch_shapes=[pltpu.VMEM(*shape) for shape in scratch]
        + [
            pltpu.SemaphoreType.DMA((112,)),
            pltpu.SemaphoreType.DMA((112,)),
            pltpu.SemaphoreType.DMA((48,)),
        ],
        compiler_params=pltpu.CompilerParams(
            collective_id=0, has_side_effects=True, vmem_limit_bytes=VMEM_BYTES
        ),
        name="gather_all",
    )(*operands)


def add_rows(total, other, count):
    step = 16
    per = total.shape[-2] // step

    @pl.loop(0, count * per)
    def _(i):
        k, at = i // per, tile(i % per, step)
        both = total[k, at, :].astype(jnp.float32) + other[k, at, :].astype(jnp.float32)
        total[k, at, :] = both.astype(total.dtype)


def add_tiles(total, other, pieces):
    rows = total.shape[-2]

    @pl.loop(0, pieces)
    def _(k):
        both = total[k].astype(jnp.float32) + other[k].astype(jnp.float32)
        total[k] = both.astype(total.dtype)


class GradScatter:
    def __init__(self, place, copies, partial, kept, from_core, from_plane, result, columns=None):
        self.place = place
        c, x, chip = place.c, place.x, place.chip
        self.kept, self.from_core, self.from_plane = kept, from_core, from_plane
        self.columns = cols = slice(0, kept.shape[3]) if columns is None else columns
        self.load = None
        given = partial.at[:, :, :, cols]
        if partial.shape != kept.shape:
            self.load = copies.inside(partial.at[:, pl.ds(2 * c, 2), :, cols], kept.at[:, :, :, cols])
            given = partial.at[:, pl.ds(2 * (1 - c), 2), :, cols]
        self.swap = copies.remote(given, from_core.at[:, :, :, cols], place.other_core())
        self.across = copies.remote(
            kept.at[:, 1 - x, :, cols], from_plane.at[:, :, cols], place.other_plane()
        )
        self.scattered = []
        for dz, dy in place.plane_offsets():
            z, y = place.shifted(dz, dy)
            self.scattered.append(
                copies.remote(
                    kept.at[z * LINE_Y + y, x, :, cols], result.at[chip, :, cols], place.at(z, y, c, x)
                )
            )
        self.own = copies.inside(kept.at[chip, x, :, cols], result.at[chip, :, cols])

    def start(self):
        if self.load is not None:
            self.load.start()
        self.swap.start()

    def cross(self):
        if self.load is not None:
            self.load.wait()
        self.swap.wait_recv()
        x = self.place.x
        self.add(1 - x, self.from_core.at[:, 1 - x])
        self.across.start()
        self.add(x, self.from_core.at[:, x])

    def add(self, x, other):
        step = 16
        per = self.kept.shape[2] // step
        cols = self.columns

        @pl.loop(0, self.kept.shape[0] * per)
        def _(i):
            k, at = i // per, tile(i % per, step)
            both = self.kept[k, x, at, cols].astype(jnp.float32) + other[k, at, cols].astype(jnp.float32)
            self.kept[k, x, at, cols] = both.astype(self.kept.dtype)

    def scatter(self):
        self.across.wait_recv()
        self.add(self.place.x, self.from_plane)
        for copy in self.scattered + [self.own]:
            copy.start()

    def finish(self):
        self.own.wait()
        for copy in self.scattered:
            copy.wait_recv()

    def drain(self):
        for copy in self.scattered + [self.swap, self.across]:
            copy.wait_send()


def weight_grads_by_core(place, tokens, grads, kept, given, columns):
    chips, half, rows = kept.shape[:3]
    step = 2 * half * rows

    @pl.loop(0, chips)
    def _(k):
        grad = contract_rows(tokens[:, tile(k, step)], grads[:, columns]).astype(jnp.bfloat16)
        grad = grad.reshape(2, half, rows, grad.shape[1])
        kept[k, :, :, columns] = jnp.where(place.c == 0, grad[0], grad[1])
        given[k, :, :, columns] = jnp.where(place.c == 0, grad[1], grad[0])


class TokenScatter:
    def __init__(self, place, copies, part, from_y, slots, total, result):
        self.place = place
        z, y, c, x = place.z, place.y, place.c, place.x
        self.part, self.from_y, self.slots, self.total = part, from_y, slots, total
        self.line = place.line
        last = self.line - 1
        self.last = last
        self.copies = copies
        self.over_base = copies.reserve(self.line)
        self.up_base = copies.reserve(self.line)
        self.down_base = copies.reserve(self.line)
        self.above = place.at(jnp.minimum(z + 1, last), y, c, x)
        self.below = place.at(jnp.maximum(z - 1, 0), y, c, x)
        self.swap = copies.remote(total.at[1 - c], result.at[c], place.other_core())
        self.own = copies.inside(total.at[c], result.at[c])

    def order(self, i):
        last = self.last
        chunk = 0
        for z in range(self.line):
            far = sorted(range(self.line), key=lambda k: (-abs(k - z), min(k, last - k)))
            chunk = jnp.where(self.place.z == z, far[i], chunk)
        return chunk

    def over(self, k):
        y = self.place.y
        return self.copies.remote_at(
            self.over_base + k, self.part.at[k, 1 - y], self.from_y.at[k], self.place.other_y()
        )

    def up(self, k):
        return self.copies.remote_at(
            self.up_base + k, self.part.at[k, self.place.y], self.slots.at[k], self.above
        )

    def down(self, k):
        slot = jnp.where(self.place.z - 1 == k, self.line, k)
        return self.copies.remote_at(
            self.down_base + k, self.part.at[k, self.place.y], self.slots.at[slot], self.below
        )

    def combine(self, k):
        self.over(k).wait_recv()
        add_rows(self.part.at[k, self.place.y], self.from_y.at[k], CORES)

    def step(self, i):
        z, y = self.place.z, self.place.y
        k = self.order(i)
        self.combine(k)

        @pl.when(k > z)
        def _():
            @pl.when(z > 0)
            def _():
                self.up(k).wait_recv()
                add_rows(self.part.at[k, y], self.slots.at[k], CORES)

            self.up(k).start()

        @pl.when(k < z)
        def _():
            @pl.when(z < self.last)
            def _():
                self.down(k).wait_recv()
                add_rows(self.part.at[k, y], self.slots.at[k], CORES)

            self.down(k).start()

    def reduce(self):
        z, y, last = self.place.z, self.place.y, self.last
        self.combine(z)
        pl.when(z > 0)(lambda: self.up(z).wait_recv())
        pl.when(z < last)(lambda: self.down(z).wait_recv())
        step = 16
        per = self.total.shape[1] // step

        @pl.loop(0, CORES * per)
        def _(i):
            k, at = i // per, tile(i % per, step)
            self.total[k, at, :] = self.part[z, y, k, at, :].astype(jnp.float32)

        def add(slot):
            @pl.loop(0, CORES * per)
            def _(i):
                k, at = i // per, tile(i % per, step)
                self.total[k, at, :] += self.slots[slot, k, at, :].astype(jnp.float32)

        pl.when(z > 0)(lambda: add(z))
        pl.when(z < last)(lambda: add(last + 1))
        self.swap.start()
        self.own.start()

    def finish(self):
        self.swap.wait_recv()

    def drain(self):
        z, last = self.place.z, self.last
        for k in range(self.line):
            self.over(k).wait_send()
            pl.when(z < k)(lambda: self.up(k).wait_send())
            pl.when(z > k)(lambda: self.down(k).wait_send())


def output_part(scatter, i, attended_low, activated, out_weight, down_weight):
    k = scatter.order(i)
    part = scatter.part
    size = part.shape[1] * part.shape[2] * part.shape[3]
    at = tile(k, size)
    rows = nn(attended_low[at, :], flat_rows(out_weight[...]))
    rows = rows + contract_cols(activated[at, :], flat_rows(down_weight[...]))
    part[k] = rows.astype(part.dtype).reshape(part.shape[1:])
    scatter.over(k).start()


def inner_grads(cot, down_weight, slope, slope_loads, inner_grad):
    step = slope.shape[1]
    for i, load in enumerate(slope_loads):
        load.wait()
        at = slice(i * step, (i + 1) * step)
        grad = nn(cot[at, :], flat_rows(down_weight[...])) * slope[i % 2]
        inner_grad[at, :] = grad.astype(jnp.bfloat16)
        if i + 2 < len(slope_loads):
            slope_loads[i + 2].start()


def hidden_part(scatter, i, inner_grad, up_weight, projected_grad, qkv_weight, hid, stats, vec, sums):
    def by_eight(values):
        return jnp.sum(values.reshape(-1, 8, values.shape[1]), axis=0)

    k = scatter.order(i)
    part = scatter.part
    size = part.shape[2] * part.shape[3]

    @pl.loop(0, LINE_Y)
    def _(y):
        at = tile(k * LINE_Y + y, size)
        one = contract_cols(projected_grad[at, :], flat_rows(qkv_weight[...]))
        two = contract_cols(inner_grad[at, :], flat_rows(up_weight[...]))
        xhat = (hid[at, :].astype(jnp.float32) - stats[at, 0:1]) * stats[at, 1:2]
        sums[0] += by_eight(one * xhat)
        sums[1] += by_eight(one)
        sums[2] += by_eight(two * xhat)
        sums[3] += by_eight(two)
        rows = one * vec[0:1, :] + two * vec[2:3, :]
        part[k, y] = rows.astype(part.dtype).reshape(part.shape[2:])

    scatter.over(k).start()


COT_SUM, UP_SUM, QKV_SUM = 4, 5, 7


def pack_small(place, sums, cot_sum, up_sum, qkv_sum, qkv_rows, tiles):
    chips, groups = tiles.shape[:2]
    tiles[...] = jnp.zeros_like(tiles)
    qkv_rows[...] = jnp.zeros_like(qkv_rows)
    third = qkv_rows.shape[0] // 3
    per_head = HEAD // LANES
    for k in range(3):
        for u in range(per_head):
            at = (k * per_head + u) * LANES
            qkv_rows[pl.ds(k * third + place.chip * per_head + u, 1), :] = qkv_sum[0:1, at : at + LANES]
    first = jnp.where(place.chip == 0, 1.0, 0.0)
    norm_sums = [jnp.sum(sums[row], axis=0, keepdims=True) for row in range(4)]
    norm_sums.append(cot_sum[0:1, :] * first)
    for pair in range(chips * groups // 2):
        chip, group = pair // (groups // 2), pair % (groups // 2) * 2
        at = slice(pair * LANES, (pair + 1) * LANES)
        for g in (group, group + 1):
            for row in range(5):
                tiles[chip, g, row : row + 1, :] = norm_sums[row][:, at]
            tiles[chip, g, QKV_SUM : QKV_SUM + 3, :] = qkv_rows[3 * pair : 3 * pair + 3, :]
    for group in range(groups):
        for u in range(2):
            at = (group * 2 + u) * LANES
            row = UP_SUM + u
            values = up_sum[0:1, at : at + LANES].reshape(1, 1, LANES)
            tiles[pl.ds(place.chip, 1), group, row : row + 1, :] = values


SCATTER_ORDER = (
    "outs tile 0",
    "qkv swap",
    "down a swap",
    "down b swap",
    "out swap",
    "outs tile 1",
    "qkv cross",
    "down a cross",
    "outs tile 2",
    "outs tile 3",
    "outs 0",
    "inner",
    "down b cross",
    "up a grad",
    "qkv scatter",
    "up sum",
    "up b grad",
    "outs 1",
    "outs 2",
    "up a swap",
    "hid tile 0",
    "hid tile 1",
    "up b swap",
    "down b scatter",
    "hid tile 2",
    "down a scatter",
    "hid tile 3",
    "out cross",
    "up b cross",
    "pack",
    "hid 0",
    "small swap",
    "hid 1",
    "small cross",
    "up b scatter",
    "small scatter",
    "up a cross",
    "out finish",
    "hid 2",
    "up a scatter",
    "outs reduce",
    "hid reduce",
)


def scatter_kernel(
    ctx_count,
    hid_in,
    cot_in,
    qkv_in,
    up_in,
    down_in,
    out_in,
    attended_low_in,
    projected_grad_in,
    norm_two_in,
    activated_in,
    slope_in,
    stats_in,
    vec_in,
    qkv_sum_in,
    cot_sum_in,
    qkv_grad,
    down_grad,
    out_grad,
    small_result,
    qkv_result,
    up_result,
    down_result,
    out_grad_result,
    out_result,
    hid_result,
    wide,
    weight,
    slope,
    act,
    attended_low,
    out_weight,
    qkv_weight,
    projected_grad,
    stats,
    vec,
    qkv_sum,
    cot_sum,
    up_sum,
    sums,
    qkv_rows,
    tiles,
    small_kept,
    small_core,
    small_plane,
    qkv_kept,
    qkv_core,
    qkv_plane,
    up_kept,
    up_core,
    up_plane,
    down_kept,
    down_core,
    down_plane,
    out_kept,
    out_core,
    out_plane,
    out_part,
    out_from_y,
    out_slots,
    hid_part,
    hid_from_y,
    hid_slots,
    total,
    send,
    recv,
    local,
):
    place = Place(ctx_count)
    copies = Copies(send, recv, local)
    c, x = place.c, place.x
    half = up_kept.shape[3] // 2
    halves = {" a": slice(0, half), " b": slice(half, 2 * half)}
    grads = {
        "qkv": GradScatter(place, copies, qkv_grad, qkv_kept, qkv_core, qkv_plane, qkv_result),
        "small": GradScatter(place, copies, tiles, small_kept, small_core, small_plane, small_result),
    }
    for name, cols in halves.items():
        grads["down" + name] = GradScatter(
            place, copies, down_grad, down_kept, down_core, down_plane, down_result, cols
        )
        grads["up" + name] = GradScatter(place, copies, down_core, up_kept, up_core, up_plane, up_result, cols)
    outs_s = TokenScatter(place, copies, out_part, out_from_y, out_slots, total, out_result)
    hid_s = TokenScatter(place, copies, hid_part, hid_from_y, hid_slots, total, hid_result)
    out_load = copies.inside(out_grad.at[pl.ds(2 * c, 2)], out_kept)
    out_swap = copies.remote(out_grad.at[pl.ds(2 * (1 - c), 2)], out_core, place.other_core())
    out_across = copies.remote(out_kept.at[1 - x], out_plane, place.other_plane())
    out_own = copies.inside(out_kept.at[x], out_grad_result)
    loads = {
        name: copies.inside(src, dst)
        for name, src, dst in (
            ("activated", activated_in, act),
            ("attended_low", attended_low_in, attended_low),
            ("out", out_in, out_weight),
            ("down", down_in, weight),
            ("cot", cot_in, wide),
            ("norm_two", norm_two_in, wide),
            ("qkv", qkv_in, qkv_weight),
            ("projected_grad", projected_grad_in, projected_grad),
            ("stats", stats_in, stats),
            ("vec", vec_in, vec),
            ("qkv_sum", qkv_sum_in, qkv_sum),
            ("cot_sum", cot_sum_in, cot_sum),
            ("up", up_in, weight),
            ("hid", hid_in, wide),
        )
    }
    early = ("activated", "attended_low", "out", "down", "cot", "qkv", "projected_grad")
    early += ("stats", "vec", "qkv_sum", "cot_sum")

    def out_cross():
        out_load.wait()
        out_swap.wait_recv()
        add_rows(out_kept, out_core, 2)
        out_across.start()

    def out_finish():
        out_across.wait_recv()
        step = 16

        @pl.loop(0, out_plane.shape[0] // step)
        def _(i):
            at = tile(i, step)
            both = out_kept[x, at, :].astype(jnp.float32) + out_plane[at, :].astype(jnp.float32)
            out_kept[x, at, :] = both.astype(out_kept.dtype)

        out_own.start()

    step = slope.shape[1]
    slope_loads = [
        copies.inside(slope_in.at[pl.ds(i * step, step)], slope.at[i % 2]) for i in range(slope_in.shape[0] // step)
    ]
    waited = set()

    def need(*names):
        for name in names:
            if name not in waited:
                waited.add(name)
                loads[name].wait()

    def output_tile(i):
        need("activated", "attended_low", "out", "down")
        output_part(outs_s, i, attended_low, act, out_weight, weight)

    def inner_all():
        need("cot")
        inner_grads(wide, weight, slope, slope_loads, act)
        loads["up"].start()
        loads["norm_two"].start()

    def up_half(name, last):
        need("norm_two")
        weight_grads_by_core(place, wide, act, up_kept, down_core, halves[name])
        if last:
            loads["hid"].start()

    def hidden_tile(i):
        if i == 0:
            need("qkv", "projected_grad", "stats", "vec", "up", "hid")
            sums[...] = jnp.zeros_like(sums)
        hidden_part(hid_s, i, act, weight, projected_grad, qkv_weight, wide, stats, vec, sums)

    def pack():
        need("qkv_sum", "cot_sum")
        pack_small(place, sums, cot_sum, up_sum, qkv_sum, qkv_rows, tiles)

    def out_start():
        out_load.start()
        out_swap.start()

    def hidden_reduce():
        outs_s.own.wait()
        outs_s.swap.wait_send()
        hid_s.reduce()

    steps = {
        "out swap": out_start,
        "out cross": out_cross,
        "out finish": out_finish,
        "inner": inner_all,
        "up a grad": functools.partial(up_half, " a", False),
        "up b grad": functools.partial(up_half, " b", True),
        "up sum": lambda: column_sums(act, up_sum),
        "pack": pack,
        "outs reduce": outs_s.reduce,
        "hid reduce": hidden_reduce,
    }
    for name, scatter in grads.items():
        steps[name + " swap"] = scatter.start
        steps[name + " cross"] = scatter.cross
        steps[name + " scatter"] = scatter.scatter
    for i in range(outs_s.line):
        steps["outs tile %d" % i] = functools.partial(output_tile, i)
        steps["hid tile %d" % i] = functools.partial(hidden_tile, i)
    for j in range(outs_s.last):
        steps["outs %d" % j] = functools.partial(outs_s.step, j)
        steps["hid %d" % j] = functools.partial(hid_s.step, j)

    for name in early:
        loads[name].start()
    slope_loads[0].start()
    slope_loads[1].start()
    greet(place)
    for name in SCATTER_ORDER:
        steps[name]()
    scatters = list(grads.values()) + [outs_s, hid_s]
    for scatter in scatters:
        scatter.finish()
    out_own.wait()
    hid_s.own.wait()
    hid_s.swap.wait_send()
    for scatter in scatters:
        scatter.drain()
    out_swap.wait_send()
    out_across.wait_send()


def scatter_all(ctx_count, local_rows, operands):
    f32, b16 = jnp.float32, jnp.bfloat16
    hid, _, w_qkv, w_up, _, w_out = operands[:6]
    chips, groups, rows, head3 = w_qkv.shape
    part = w_up.shape[3]
    tokens, width = hid.shape
    line = chips // LINE_Y
    small = (SMALL_ROWS, LANES)
    token = (CORES, local_rows, width)
    results = [
        ((chips,) + small, f32),
        ((chips, rows, head3), b16),
        ((chips, rows, part), b16),
        ((chips, rows, part), b16),
        ((rows, width), b16),
        (token, f32),
        (token, f32),
    ]
    scratch = [
        ((tokens, width), b16),
        (w_up.shape, b16),
        ((2, 256, part), f32),
        ((tokens, part), b16),
        ((tokens, head3 // 3), b16),
        (w_out.shape, b16),
        (w_qkv.shape, b16),
        ((tokens, head3), b16),
        ((tokens, LANES), f32),
        ((8, width), f32),
        ((8, head3), f32),
        ((8, width), f32),
        ((8, part), f32),
        ((4, 8, width), f32),
        ((3 * width // LANES, LANES), f32),
        ((chips, groups) + small, f32),
    ]
    for shape, dtype in ((small, f32), ((rows, head3), b16), ((rows, part), b16), ((rows, part), b16)):
        scratch += [((chips, 2) + shape, dtype)] * 2 + [((chips,) + shape, dtype)]
    scratch += [((2, rows, width), b16)] * 2 + [((rows, width), b16)]
    for _ in range(2):
        scratch += [
            ((line, LINE_Y) + token, b16),
            ((line,) + token, b16),
            ((line + 1,) + token, b16),
        ]
    scratch += [(token, f32)]
    anywhere = pl.BlockSpec(memory_space=pl.ANY)
    return pl.pallas_call(
        lambda *refs: scatter_kernel(ctx_count, *refs),
        out_shape=[jax.ShapeDtypeStruct(*shape) for shape in results],
        in_specs=[anywhere] * len(operands),
        out_specs=[anywhere] * len(results),
        scratch_shapes=[pltpu.VMEM(*shape) for shape in scratch]
        + [
            pltpu.SemaphoreType.DMA((96,)),
            pltpu.SemaphoreType.DMA((96,)),
            pltpu.SemaphoreType.DMA((48,)),
        ],
        compiler_params=pltpu.CompilerParams(
            collective_id=1, has_side_effects=True, vmem_limit_bytes=VMEM_BYTES
        ),
        name="scatter_all",
    )(*operands)


def small_tile(ln1_gain, ln1_bias, ln2_gain, ln2_bias, out_bias, down_bias, qkv_bias, up_bias):
    half = LANES // 2

    def put(values, row, lane):
        values = values.astype(jnp.float32).reshape(1, -1)
        return lax.pad(
            values,
            jnp.float32(0),
            ((row, SMALL_ROWS - 1 - row, 0), (lane, LANES - lane - values.shape[1], 0)),
        )

    total = jnp.zeros((SMALL_ROWS, LANES), jnp.float32)
    for row, values in (
        (GAIN_ONE, ln1_gain),
        (SHIFT_ONE, ln1_bias),
        (GAIN_TWO, ln2_gain),
        (SHIFT_TWO, ln2_bias),
        (OUT_BIAS, out_bias),
        (DOWN_BIAS, down_bias),
    ):
        total = total + put(values, row, 0) + put(values, row, half)
    total = total + put(qkv_bias[:LANES], QKV_BIAS, 0)
    total = total + put(qkv_bias[LANES:], QKV_BIAS + 1, 0) + put(qkv_bias[:half], QKV_BIAS + 1, half)
    total = total + put(qkv_bias[half:], QKV_BIAS + 2, 0)
    return total + put(up_bias[:LANES], UP_BIAS, 0) + put(up_bias[LANES:], UP_BIAS + 1, 0)


def rotation_tables(positions):
    half_rot = ROT // 2
    where = positions.astype(jnp.float32)[:, None]
    frequency = 1.0 / 10000.0 ** (jnp.arange(half_rot).astype(jnp.float32) * 2.0 / ROT)
    angles = where * frequency[None, :]
    cos, sin = jnp.cos(angles), jnp.sin(angles)
    rest = jnp.ones((positions.shape[0], LANES - ROT), jnp.float32)
    return (
        jnp.concatenate([cos, cos, rest], axis=1),
        jnp.concatenate([-sin, sin, rest * where], axis=1),
    )


def split_body(
    hidden,
    cotangent,
    pairing,
    ln1_gain,
    ln1_bias,
    qkv_weight,
    qkv_bias,
    out_weight,
    out_bias,
    ln2_gain,
    ln2_bias,
    up_weight,
    up_bias,
    down_weight,
    down_bias,
):
    local_rows, seq_count, width = hidden.shape
    ctx_count = lax.axis_size("ctx")
    chips = ctx_count // CORES
    total_rows = local_rows * ctx_count
    f32, b16 = jnp.float32, jnp.bfloat16
    head_id = lax.axis_index("ctx") // CORES
    owned = width // (ctx_count * 2)
    positions = row_positions(pairing, jnp.int32(0), total_rows, local_rows // 2, ctx_count)
    cosine, sine = rotation_tables(positions)
    key_pos = jnp.broadcast_to(positions.astype(f32)[None, :], (8, total_rows))

    (
        hid_all,
        cot_all,
        w_qkv,
        w_up,
        w_down,
        w_out,
        small_all,
        attended_low,
        projected_grad,
        norm_two,
        activated,
        slope,
        grad_qkv,
        grad_down,
        grad_out,
        vec,
        stats,
        qkv_sum,
        cot_sum,
    ) = gather_all(
        ctx_count,
        jnp.swapaxes(hidden, 0, 1),
        jnp.swapaxes(cotangent, 0, 1),
        qkv_weight,
        up_weight,
        down_weight,
        out_weight,
        small_tile(ln1_gain, ln1_bias, ln2_gain, ln2_bias, out_bias, down_bias, qkv_bias, up_bias),
        cosine,
        sine,
        key_pos,
    )
    smalls = small_all.reshape(ctx_count * 2, SMALL_ROWS, LANES)
    b_both = (smalls[:, OUT_BIAS, :owned] + smalls[:, DOWN_BIAS, :owned]).reshape(-1)
    small_sum, qkv_rows, up_rows, down_rows, out_sum, out_rows, hid_rows = scatter_all(
        ctx_count,
        local_rows,
        (
            hid_all,
            cot_all,
            w_qkv,
            w_up,
            w_down,
            w_out,
            attended_low,
            projected_grad,
            norm_two,
            activated,
            slope,
            stats,
            vec,
            qkv_sum,
            cot_sum,
            grad_qkv,
            grad_down,
            grad_out,
        ),
    )

    own = hidden.astype(f32)
    output = (own + jnp.swapaxes(out_rows, 0, 1) + b_both).astype(b16)
    average = jnp.mean(own, axis=-1, keepdims=True)
    spread = jnp.mean((own - average) ** 2, axis=-1, keepdims=True)
    scale = lax.rsqrt(spread + LN_EPSILON)
    xhat = (own - average) * scale
    e = jnp.swapaxes(hid_rows, 0, 1)
    grad_hidden = cotangent.astype(f32) + scale * (
        e - jnp.mean(e, axis=-1, keepdims=True) - xhat * jnp.mean(e * xhat, axis=-1, keepdims=True)
    )
    small = jnp.sum(small_sum, axis=0)
    odd = lax.axis_index("fsdp") == 1
    halves = jnp.where(odd, small[: COT_SUM + 1, owned:], small[: COT_SUM + 1, :owned])
    three = small[QKV_SUM : QKV_SUM + 3].reshape(-1)
    qkv_bias_sum = jnp.where(odd, three[3 * owned :], three[: 3 * owned])
    up_bias_sum = small[UP_SUM : UP_SUM + 2].reshape(-1)

    def columns(pieces, thirds):
        rows = pieces.shape[1]
        split = pieces.astype(f32).reshape(chips, rows, thirds, -1)
        return jnp.transpose(split, (1, 2, 0, 3)).reshape(rows, -1)

    return (
        output,
        grad_hidden,
        halves[0],
        halves[1],
        columns(qkv_rows, 3),
        qkv_bias_sum,
        out_sum.astype(f32),
        halves[COT_SUM],
        halves[2],
        halves[3],
        columns(up_rows, 1),
        up_bias_sum,
        columns(down_rows, 1),
        halves[COT_SUM],
    )


def solution(mesh):
    body = split_body if split_fits(mesh) else general_body
    return jax.shard_map(
        body,
        mesh=mesh,
        in_specs=(
            P("ctx", "fsdp", None),
            P("ctx", "fsdp", None),
            P(),
            P(("ctx", "fsdp")),
            P(("ctx", "fsdp")),
            P(("ctx", "fsdp"), None),
            P(("ctx", "fsdp")),
            P(("ctx", "fsdp"), None),
            P(("ctx", "fsdp")),
            P(("ctx", "fsdp")),
            P(("ctx", "fsdp")),
            P(("ctx", "fsdp"), None),
            P(("ctx", "fsdp")),
            P(("ctx", "fsdp"), None),
            P(("ctx", "fsdp")),
        ),
        out_specs=(
            P("ctx", "fsdp", None),
            P("ctx", "fsdp", None),
            P(("ctx", "fsdp")),
            P(("ctx", "fsdp")),
            P(("ctx", "fsdp"), None),
            P(("ctx", "fsdp")),
            P(("ctx", "fsdp"), None),
            P(("ctx", "fsdp")),
            P(("ctx", "fsdp")),
            P(("ctx", "fsdp")),
            P(("ctx", "fsdp"), None),
            P(("ctx", "fsdp")),
            P(("ctx", "fsdp"), None),
            P(("ctx", "fsdp")),
        ),
        check_vma=False,
    )
```

```python
import functools

import jax
import jax.numpy as jnp
from jax import lax
from jax.experimental import pallas as pl
from jax.experimental.pallas import tpu as pltpu
from jax.sharding import PartitionSpec as P

HEAD = 256
ROT = 64


LN_EPSILON = 1e-05
VERY_LOW = -1e30


def layer_norm(values, ln_gain, ln_shift):
    average = jnp.mean(values, axis=-1, keepdims=True)
    centered = values - average
    spread = jnp.mean(centered * centered, axis=-1, keepdims=True)
    return centered * lax.rsqrt(spread + LN_EPSILON) * ln_gain + ln_shift


def gelu_exact(values):
    return jax.nn.gelu(values, approximate=False)


def rotate(values, positions):
    half_rot = ROT // 2
    frequency = 1.0 / 10000.0 ** (jnp.arange(half_rot).astype(values.dtype) * 2.0 / ROT)
    angles = positions.astype(values.dtype)[:, None] * frequency[None, :]
    shape_out = (angles.shape[0],) + (1,) * (values.ndim - 2) + (ROT,)
    cosine = jnp.concatenate([jnp.cos(angles), jnp.cos(angles)], axis=-1).reshape(shape_out)
    sine_part = jnp.concatenate([jnp.sin(angles), jnp.sin(angles)], axis=-1).reshape(shape_out)
    rot_part = values[..., :ROT]
    turned = jnp.concatenate([-rot_part[..., half_rot:], rot_part[..., :half_rot]], axis=-1)
    return jnp.concatenate([rot_part * cosine + turned * sine_part, values[..., ROT:]], axis=-1)


def row_positions(pairing, first_row, row_count, block_rows, ctx_count):
    row_ids = first_row + jnp.arange(row_count, dtype=jnp.int32)
    device_ids = row_ids // (2 * block_rows)
    within = row_ids % (2 * block_rows)
    matches = device_ids[:, None] == jnp.arange(ctx_count, dtype=jnp.int32)[None, :]
    owned_block = jnp.sum(jnp.where(matches, pairing[None, :], 0), axis=1)
    blocks = jnp.where(within < block_rows, owned_block, 2 * ctx_count - 1 - owned_block)
    return blocks * block_rows + within % block_rows


def heads_view(values, row_total, seq_count):
    return values.reshape(row_total, seq_count, -1, HEAD)


def contract_rows(left, right):
    return lax.dot_general(
        left, right, (((0,), (0,)), ((), ())), preferred_element_type=jnp.float32
    )


def contract_cols(left, right):
    return lax.dot_general(
        left, right, (((1,), (1,)), ((), ())), preferred_element_type=jnp.float32
    )


def pair_grads(
    query_rows, grad_rows, log_rows, delta_rows, query_pos, key_heads, value_heads, key_pos, scaling
):
    scores = (
        jnp.einsum("qshd,kshd->shqk", query_rows, key_heads, preferred_element_type=jnp.float32)
        * scaling
    )
    allowed = key_pos[None, None, None, :] <= query_pos[None, None, :, None]
    probabilities = jnp.where(allowed, jnp.exp(scores - log_rows[..., None]), 0.0)
    prob_grad = jnp.einsum(
        "qshd,kshd->shqk", grad_rows, value_heads, preferred_element_type=jnp.float32
    )
    score_grad = (probabilities * (prob_grad - delta_rows[..., None])).astype(jnp.bfloat16)
    return (score_grad, probabilities.astype(jnp.bfloat16))


def general_body(
    hidden,
    cotangent,
    pairing,
    ln1_gain,
    ln1_bias,
    qkv_weight,
    qkv_bias,
    out_weight,
    out_bias,
    ln2_gain,
    ln2_bias,
    up_weight,
    up_bias,
    down_weight,
    down_bias,
):
    local_rows, seq_count, model_width = hidden.shape
    block_rows = local_rows // 2
    ctx_count = lax.axis_size("ctx")
    head_count = model_width // HEAD
    scaling = HEAD ** (-0.5)
    tokens = local_rows * seq_count
    total_rows = local_rows * ctx_count
    params = (
        lax.all_gather(ln1_gain, ("ctx", "fsdp"), axis=0, tiled=True),
        lax.all_gather(ln1_bias, ("ctx", "fsdp"), axis=0, tiled=True),
        lax.all_gather(qkv_weight, ("ctx", "fsdp"), axis=0, tiled=True),
        lax.all_gather(qkv_bias, ("ctx", "fsdp"), axis=0, tiled=True),
        lax.all_gather(out_weight, ("ctx", "fsdp"), axis=0, tiled=True),
        lax.all_gather(out_bias, ("ctx", "fsdp"), axis=0, tiled=True),
        lax.all_gather(ln2_gain, ("ctx", "fsdp"), axis=0, tiled=True),
        lax.all_gather(ln2_bias, ("ctx", "fsdp"), axis=0, tiled=True),
        lax.all_gather(up_weight, ("ctx", "fsdp"), axis=0, tiled=True),
        lax.all_gather(up_bias, ("ctx", "fsdp"), axis=0, tiled=True),
        lax.all_gather(down_weight, ("ctx", "fsdp"), axis=0, tiled=True),
        lax.all_gather(down_bias, ("ctx", "fsdp"), axis=0, tiled=True),
    )
    (
        gain_one,
        shift_one,
        w_qkv,
        b_qkv,
        w_out,
        b_out,
        gain_two,
        shift_two,
        w_up,
        b_up,
        w_down,
        b_down,
    ) = params
    ff_width = w_up.shape[1]
    hidden_f = hidden.astype(jnp.float32).reshape(tokens, model_width)
    own_pos = row_positions(
        pairing, lax.axis_index("ctx") * local_rows, local_rows, block_rows, ctx_count
    )
    normed_one, ln_one_pull = jax.vjp(
        layer_norm, hidden_f, gain_one.astype(jnp.float32), shift_one.astype(jnp.float32)
    )
    normed_one_low = normed_one.astype(jnp.bfloat16)
    projected = jnp.dot(normed_one_low, w_qkv, preferred_element_type=jnp.float32) + b_qkv.astype(
        jnp.float32
    )
    query_f, rotation_pull = jax.vjp(
        lambda values: rotate(values, own_pos),
        heads_view(projected[:, :model_width], local_rows, seq_count),
    )
    query_b = query_f.astype(jnp.bfloat16)
    key_b = (
        rotate(
            heads_view(projected[:, model_width : 2 * model_width], local_rows, seq_count), own_pos
        )
        .astype(jnp.bfloat16)
        .reshape(local_rows, seq_count, model_width)
    )
    value_b = (
        projected[:, 2 * model_width :]
        .astype(jnp.bfloat16)
        .reshape(local_rows, seq_count, model_width)
    )
    running_max = jnp.full((seq_count, head_count, local_rows), VERY_LOW, jnp.float32)
    key_piece = lax.all_gather(key_b, "ctx", axis=0, tiled=True)
    value_piece = lax.all_gather(value_b, "ctx", axis=0, tiled=True)
    row_total = key_piece.shape[0]
    key_pos = row_positions(pairing, jnp.int32(0), row_total, block_rows, ctx_count)
    scores = (
        jnp.einsum(
            "qshd,kshd->shqk",
            query_b,
            heads_view(key_piece, row_total, seq_count),
            preferred_element_type=jnp.float32,
        )
        * scaling
    )
    allowed = key_pos[None, None, None, :] <= own_pos[None, None, :, None]
    piece_max = jnp.max(jnp.where(allowed, scores, VERY_LOW), axis=-1)
    new_max = jnp.maximum(running_max, piece_max)
    weights = jnp.where(allowed, jnp.exp(scores - new_max[..., None]), 0.0)
    new_total = jnp.sum(weights, axis=-1)
    mixture = jnp.einsum(
        "shqk,kshd->qshd",
        weights.astype(jnp.bfloat16),
        heads_view(value_piece, row_total, seq_count),
        preferred_element_type=jnp.float32,
    )
    log_total = new_max + jnp.log(new_total)
    attended = mixture / jnp.transpose(new_total, (2, 0, 1))[..., None]
    attended_low = attended.astype(jnp.bfloat16).reshape(tokens, model_width)
    branch_attn = jnp.dot(attended_low, w_out, preferred_element_type=jnp.float32) + b_out.astype(
        jnp.float32
    )
    normed_two, ln_two_pull = jax.vjp(
        layer_norm, hidden_f, gain_two.astype(jnp.float32), shift_two.astype(jnp.float32)
    )
    normed_two_low = normed_two.astype(jnp.bfloat16)
    inner_act = jnp.dot(normed_two_low, w_up, preferred_element_type=jnp.float32) + b_up.astype(
        jnp.float32
    )
    activated_f, gelu_pull = jax.vjp(gelu_exact, inner_act)
    activated = activated_f.astype(jnp.bfloat16)
    branch_mlp = contract_cols(activated, w_down) + b_down.astype(jnp.float32)
    output = (
        (hidden_f + branch_attn + branch_mlp)
        .astype(jnp.bfloat16)
        .reshape(local_rows, seq_count, model_width)
    )
    back_qkv, back_out, back_up, back_down = (
        lax.all_gather(qkv_weight, ("ctx", "fsdp"), axis=0, tiled=True),
        lax.all_gather(out_weight, ("ctx", "fsdp"), axis=0, tiled=True),
        lax.all_gather(up_weight, ("ctx", "fsdp"), axis=0, tiled=True),
        lax.all_gather(down_weight, ("ctx", "fsdp"), axis=0, tiled=True),
    )
    grad_out = cotangent.reshape(tokens, model_width)
    grad_f = grad_out.astype(jnp.float32)
    bias_sum = jnp.sum(grad_f, axis=0)
    up_grad = jnp.dot(grad_out, back_down, preferred_element_type=jnp.float32)
    inner_grad = gelu_pull(up_grad)[0].astype(jnp.bfloat16)
    norm_two_grad = contract_cols(inner_grad, back_up)
    dx_two, dgain_two, dshift_two = ln_two_pull(norm_two_grad)
    up_bias_sum = jnp.sum(inner_grad, axis=0, dtype=jnp.float32)
    mlp_small = jnp.concatenate(
        [
            up_bias_sum.reshape(model_width, -1),
            jnp.stack([bias_sum, dgain_two, dshift_two], axis=1),
        ],
        axis=1,
    )
    up_w_sum, down_w_sum, mlp_small_sum = (
        lax.psum_scatter(
            contract_rows(normed_two_low, inner_grad),
            ("ctx", "fsdp"),
            scatter_dimension=0,
            tiled=True,
        ),
        lax.psum_scatter(
            contract_rows(grad_out, activated), ("ctx", "fsdp"), scatter_dimension=0, tiled=True
        ),
        lax.psum_scatter(mlp_small, ("ctx", "fsdp"), scatter_dimension=0, tiled=True),
    )
    ratio = ff_width // model_width
    attn_grad = contract_cols(grad_out, back_out).astype(jnp.bfloat16)
    out_w_grad = contract_rows(attended_low, grad_out)
    grad_heads = heads_view(attn_grad, local_rows, seq_count)
    row_delta = jnp.einsum("qshd,qshd->shq", grad_heads.astype(jnp.float32), attended)
    keys_all, values_all = (
        lax.all_gather(key_b, "ctx", axis=0, tiled=True),
        lax.all_gather(value_b, "ctx", axis=0, tiled=True),
    )
    key_block = 512
    block_count = total_rows // key_block
    starts = jnp.arange(block_count, dtype=jnp.int32) * key_block

    def query_step(query_grad, inputs):
        key_piece, value_piece, offset = inputs
        key_pos = row_positions(pairing, offset, key_block, block_rows, ctx_count)
        key_heads = heads_view(key_piece, key_block, seq_count)
        value_heads = heads_view(value_piece, key_block, seq_count)
        score_grad, unused = pair_grads(
            query_b,
            grad_heads,
            log_total,
            row_delta,
            own_pos,
            key_heads,
            value_heads,
            key_pos,
            scaling,
        )
        query_grad = (
            query_grad
            + jnp.einsum(
                "shqk,kshd->qshd", score_grad, key_heads, preferred_element_type=jnp.float32
            )
            * scaling
        )
        return (query_grad, None)

    query_grad, unused_out = lax.scan(
        query_step,
        jnp.zeros((local_rows, seq_count, head_count, HEAD), jnp.float32),
        (
            keys_all.reshape(block_count, key_block, seq_count, model_width),
            values_all.reshape(block_count, key_block, seq_count, model_width),
            starts,
        ),
    )
    queries_all, grads_all = (
        lax.all_gather(query_b, "ctx", axis=0, tiled=True),
        lax.all_gather(grad_heads, "ctx", axis=0, tiled=True),
    )
    logs_all, deltas_all = (
        lax.all_gather(log_total, "ctx", axis=2, tiled=True),
        lax.all_gather(row_delta, "ctx", axis=2, tiled=True),
    )
    own_keys = heads_view(key_b, local_rows, seq_count)
    own_values = heads_view(value_b, local_rows, seq_count)

    def key_step(carry, inputs):
        key_acc, value_acc = carry
        query_piece, grad_piece, log_piece, delta_piece, offset = inputs
        query_pos = row_positions(pairing, offset, key_block, block_rows, ctx_count)
        score_grad, probs_low = pair_grads(
            query_piece,
            grad_piece,
            log_piece,
            delta_piece,
            query_pos,
            own_keys,
            own_values,
            own_pos,
            scaling,
        )
        key_acc = (
            key_acc
            + jnp.einsum(
                "shqk,qshd->kshd", score_grad, query_piece, preferred_element_type=jnp.float32
            )
            * scaling
        )
        value_acc = value_acc + jnp.einsum(
            "shqk,qshd->kshd", probs_low, grad_piece, preferred_element_type=jnp.float32
        )
        return ((key_acc, value_acc), None)

    empty_acc = jnp.zeros((local_rows, seq_count, head_count, HEAD), jnp.float32)
    log_blocks = jnp.moveaxis(logs_all.reshape(seq_count, head_count, block_count, key_block), 2, 0)
    delta_blocks = jnp.moveaxis(
        deltas_all.reshape(seq_count, head_count, block_count, key_block), 2, 0
    )
    (key_sum, value_sum), unused_keys = lax.scan(
        key_step,
        (empty_acc, empty_acc),
        (
            queries_all.reshape(block_count, key_block, seq_count, head_count, HEAD),
            grads_all.reshape(block_count, key_block, seq_count, head_count, HEAD),
            log_blocks,
            delta_blocks,
            starts,
        ),
    )
    key_owned = key_sum.reshape(local_rows, seq_count, model_width)
    value_owned = value_sum.reshape(local_rows, seq_count, model_width)
    query_pre = rotation_pull(query_grad)[0].reshape(tokens, model_width)
    key_pre = rotation_pull(heads_view(key_owned, local_rows, seq_count))[0].reshape(
        tokens, model_width
    )
    value_pre = value_owned.reshape(tokens, model_width)
    projected_grad = jnp.concatenate([query_pre, key_pre, value_pre], axis=1).astype(jnp.bfloat16)
    norm_one_grad = contract_cols(projected_grad, back_qkv)
    dx_one, dgain_one, dshift_one = ln_one_pull(norm_one_grad)
    qkv_bias_sum = jnp.sum(projected_grad, axis=0, dtype=jnp.float32)
    attn_small = jnp.concatenate(
        [
            qkv_bias_sum.reshape(model_width, -1),
            jnp.stack([bias_sum, dgain_one, dshift_one], axis=1),
        ],
        axis=1,
    )
    qkv_w_sum, out_w_sum, attn_small_sum = (
        lax.psum_scatter(
            contract_rows(normed_one_low, projected_grad),
            ("ctx", "fsdp"),
            scatter_dimension=0,
            tiled=True,
        ),
        lax.psum_scatter(out_w_grad, ("ctx", "fsdp"), scatter_dimension=0, tiled=True),
        lax.psum_scatter(attn_small, ("ctx", "fsdp"), scatter_dimension=0, tiled=True),
    )
    grad_hidden = (grad_f + dx_one + dx_two).reshape(local_rows, seq_count, model_width)
    return (
        output,
        grad_hidden,
        attn_small_sum[:, 4],
        attn_small_sum[:, 5],
        qkv_w_sum,
        attn_small_sum[:, :3].reshape(-1),
        out_w_sum,
        attn_small_sum[:, 3],
        mlp_small_sum[:, ratio + 1],
        mlp_small_sum[:, ratio + 2],
        up_w_sum,
        mlp_small_sum[:, :ratio].reshape(-1),
        down_w_sum,
        mlp_small_sum[:, ratio],
    )


MESH = pl.DeviceIdType.MESH
CORES = 2
LINE_Y = 2
VMEM_BYTES = 60 * 2**20


def split_fits(mesh):
    return mesh.shape["ctx"] == 16 and mesh.shape["fsdp"] == 2


class Place:
    def __init__(self, ctx_count):
        self.chips = ctx_count // CORES
        self.line = self.chips // LINE_Y
        index = lax.axis_index("ctx")
        self.c = index % CORES
        self.chip = index // CORES
        self.y = self.chip % LINE_Y
        self.z = self.chip // LINE_Y
        self.x = lax.axis_index("fsdp")

    def at(self, z, y, c, x):
        return ((z * LINE_Y + y) * CORES + c, x)

    def other_core(self):
        return self.at(self.z, self.y, 1 - self.c, self.x)

    def other_plane(self):
        return self.at(self.z, self.y, self.c, 1 - self.x)

    def other_y(self):
        return self.at(self.z, 1 - self.y, self.c, self.x)

    def plane_offsets(self):
        return [(dz, dy) for dz in range(self.line) for dy in range(LINE_Y) if dz or dy]

    def shifted(self, dz, dy):
        return (self.z + dz) % self.line, (self.y + dy) % LINE_Y


class Copies:
    def __init__(self, send, recv, local):
        self.send, self.recv, self.local = send, recv, local
        self.remotes, self.locals = 0, 0

    def reserve(self, count):
        self.remotes += count
        return self.remotes - count

    def remote(self, src, dst, device):
        return self.remote_at(self.reserve(1), src, dst, device)

    def remote_at(self, i, src, dst, device):
        return pltpu.make_async_remote_copy(
            src_ref=src,
            dst_ref=dst,
            send_sem=self.send.at[i],
            recv_sem=self.recv.at[i],
            device_id=device,
            device_id_type=MESH,
        )

    def inside(self, src, dst):
        i = self.locals
        self.locals += 1
        return pltpu.make_async_copy(src, dst, self.local.at[i])


def greet(place):
    barrier = pltpu.get_barrier_semaphore()
    partners = [place.other_core(), place.other_plane()]
    for dz, dy in place.plane_offsets():
        z, y = place.shifted(dz, dy)
        partners.append(place.at(z, y, place.c, place.x))
    for partner in partners:
        pl.semaphore_signal(barrier, inc=1, device_id=partner, device_id_type=MESH)
    return lambda: pl.semaphore_wait(barrier, len(partners))


class TokenGather:
    def __init__(self, place, copies, own, whole):
        self.place = place
        self.whole = whole
        c, chip, z, y = place.c, place.chip, place.z, place.y
        rows = own.shape[1]
        block = whole.at[pl.ds(pl.multiple_of((chip * CORES + c) * rows, rows), rows)]
        self.first = copies.remote(own.at[1 - c], block, place.other_core())
        self.mine = copies.inside(own.at[c], block)
        last = place.line - 1
        up = place.at(jnp.minimum(z + 1, last), y, c, place.x)
        down = place.at(jnp.maximum(z - 1, 0), y, c, place.x)

        def pair(zz):
            first = (jnp.clip(zz, 0, last) * LINE_Y + y) * CORES * rows
            return whole.at[pl.ds(pl.multiple_of(first, CORES * rows), CORES * rows)]

        self.ups = [copies.remote(pair(z - j), pair(z - j), up) for j in range(last)]
        self.downs = [copies.remote(pair(z + j), pair(z + j), down) for j in range(last)]
        self.over_own = copies.remote(pair(z), pair(z), place.other_y())
        self.over_ups = [copies.remote(pair(z - 1 - j), pair(z - 1 - j), place.other_y()) for j in range(last)]
        self.over_downs = [copies.remote(pair(z + 1 + j), pair(z + 1 + j), place.other_y()) for j in range(last)]
        self.last = last

    def start(self):
        self.mine.start()
        self.first.start()

    def spread(self):
        self.mine.wait()
        self.first.wait_recv()
        z = self.place.z
        pl.when(z < self.last)(lambda: self.ups[0].start())
        pl.when(z > 0)(lambda: self.downs[0].start())
        self.over_own.start()

    def step(self, j):
        z, last = self.place.z, self.last

        @pl.when(z - 1 - j >= 0)
        def _():
            self.ups[j].wait_recv()
            if j + 1 < last:
                pl.when(z < last)(lambda: self.ups[j + 1].start())
            self.over_ups[j].start()

        @pl.when(z + 1 + j <= last)
        def _():
            self.downs[j].wait_recv()
            if j + 1 < last:
                pl.when(z > 0)(lambda: self.downs[j + 1].start())
            self.over_downs[j].start()

    def finish(self):
        z, last = self.place.z, self.last
        self.over_own.wait_recv()
        for j in range(last):
            pl.when(z - 1 - j >= 0)(lambda: self.over_ups[j].wait_recv())
            pl.when(z + 1 + j <= last)(lambda: self.over_downs[j].wait_recv())

    def drain(self):
        z, last = self.place.z, self.last
        self.first.wait_send()
        self.over_own.wait_send()
        for j in range(last):
            pl.when((z - j >= 0) & (z < last))(lambda: self.ups[j].wait_send())
            pl.when((z + j <= last) & (z > 0))(lambda: self.downs[j].wait_send())
            pl.when(z - 1 - j >= 0)(lambda: self.over_ups[j].wait_send())
            pl.when(z + 1 + j <= last)(lambda: self.over_downs[j].wait_send())


class WeightGather:
    def __init__(self, place, copies, pieces, whole, columns=slice(None)):
        self.place = place
        group = 2 * place.c + place.x
        self.by_chip = []
        for dz, dy in place.plane_offsets():
            z, y = place.shifted(dz, dy)
            device = place.at(z, y, place.c, place.x)
            self.by_chip.append(
                [copies.remote(src, dst, device) for src, dst in pieces(z * LINE_Y + y, place.chip, group)]
            )
        self.kept = [copies.inside(src, dst) for src, dst in pieces(place.chip, place.chip, group)]
        mine = whole.at[:, group, :, columns]
        self.across = copies.remote(mine, mine, place.other_plane())
        pair = whole.at[:, pl.ds(2 * place.c, 2), :, columns]
        self.swap = copies.remote(pair, pair, place.other_core())

    def send(self, i):
        for copy in self.by_chip[i] + (self.kept if i == 0 else []):
            copy.start()

    def scatter(self):
        for i in range(len(self.by_chip)):
            self.send(i)

    def cross(self):
        for copy in self.kept:
            copy.wait()
        for copies in self.by_chip:
            for copy in copies:
                copy.wait_recv()
        self.across.start()

    def share(self):
        self.across.wait_recv()
        self.swap.start()

    def finish(self):
        self.swap.wait_recv()

    def drain(self):
        for copy in sum(self.by_chip, []) + [self.across, self.swap]:
            copy.wait_send()


NORM_PARTS = 4
GATHER_ORDER = (
    "qkv 6",
    "hid spread",
    "up b 0",
    "up a 0",
    "out start",
    "qkv 1",
    "qkv 0",
    "tables",
    "hid 0",
    "small cross",
    "up a 1",
    "qkv 2",
    "small share",
    "down b 0",
    "up b 5",
    "up b 2",
    "hid 1",
    "up a 3",
    "small done",
    "up a 5",
    "out share",
    "qkv 5",
    "cot spread",
    "qkv 3",
    "qkv 4",
    "up a 4",
    "qkv cross",
    "hid 2",
    "down a 0",
    "up a 6",
    "up a 2",
    "up b 1",
    "up b 3",
    "cot 0",
    "up a cross",
    "hid done",
    "norm",
    "up b 4",
    "up b 6",
    "qkv share",
    "norm",
    "down a 2",
    "cot 1",
    "down a 1",
    "down a 4",
    "up b cross",
    "down a 5",
    "norm",
    "norm",
    "norm done",
    "up a share",
    "project",
    "down a 6",
    "down a 3",
    "cot 2",
    "up b share",
    "attend",
    "down a cross",
    "down b 3",
    "down b 2",
    "down b 5",
    "inner",
    "down b 4",
    "down b 6",
    "down b 1",
    "cot done",
    "out grads",
    "down b cross",
    "down grads",
    "attention back",
    "down a share",
    "down b share",
    "qkv grads",
)


def nn(left, right):
    return lax.dot_general(left, right, (((1,), (0,)), ((), ())), preferred_element_type=jnp.float32)


def tile(i, size):
    return pl.ds(pl.multiple_of(i * size, size), size)


def flat_rows(values):
    return values.reshape(-1, values.shape[-1])


GAIN_ONE, SHIFT_ONE, GAIN_TWO, SHIFT_TWO, OUT_BIAS, DOWN_BIAS, QKV_BIAS, UP_BIAS, SMALL_ROWS = (
    0,
    1,
    2,
    3,
    4,
    5,
    6,
    9,
    16,
)
LANES = 128


def lanes_of(shape):
    return lax.broadcasted_iota(jnp.int32, shape, len(shape) - 1)


def pack_parameters(vectors, tile_ref):
    half = LANES // 2
    ln1_gain, ln1_bias, ln2_gain, ln2_bias, out_bias, down_bias, qkv_bias, up_bias = [
        ref[...].astype(jnp.float32).reshape(1, -1) for ref in vectors
    ]
    tile_ref[...] = jnp.zeros_like(tile_ref)
    for row, values in (
        (GAIN_ONE, ln1_gain),
        (SHIFT_ONE, ln1_bias),
        (GAIN_TWO, ln2_gain),
        (SHIFT_TWO, ln2_bias),
        (OUT_BIAS, out_bias),
        (DOWN_BIAS, down_bias),
    ):
        tile_ref[row : row + 1, :half] = values
        tile_ref[row : row + 1, half:] = values
    tile_ref[QKV_BIAS : QKV_BIAS + 1, :] = qkv_bias[:, :LANES]
    tile_ref[QKV_BIAS + 1 : QKV_BIAS + 2, :half] = qkv_bias[:, LANES:]
    tile_ref[QKV_BIAS + 1 : QKV_BIAS + 2, half:] = qkv_bias[:, :half]
    tile_ref[QKV_BIAS + 2 : QKV_BIAS + 3, :] = qkv_bias[:, half:]
    tile_ref[UP_BIAS : UP_BIAS + 1, :] = up_bias[:, :LANES]
    tile_ref[UP_BIAS + 1 : UP_BIAS + 2, :] = up_bias[:, LANES:]


def position_tables(ctx_count, pairing, cosine, sine, key_pos):
    block_rows = cosine.shape[0] // (2 * ctx_count)
    half_rot = ROT // 2
    lane = lanes_of((block_rows, LANES))
    power = (lane % half_rot).astype(jnp.float32) * (2.0 / ROT)
    frequency = jnp.exp(power * -9.210340371976184)
    row = lax.broadcasted_iota(jnp.int32, (block_rows, LANES), 0)

    @pl.loop(0, ctx_count)
    def _(device):
        owned = pairing[device]
        for late in range(2):
            block = 2 * ctx_count - 1 - owned if late else owned
            where = (block * block_rows + row).astype(jnp.float32)
            angles = where * frequency
            at = tile(2 * device + late, block_rows)
            cosine[at, :] = jnp.where(lane < ROT, jnp.cos(angles), 1.0)
            sin = jnp.sin(angles)
            sine[at, :] = jnp.where(lane < half_rot, -sin, jnp.where(lane < ROT, sin, where))

    lane = lanes_of((8, LANES))
    per = LANES // (2 * block_rows)
    for first in range(0, ctx_count, per):
        block = jnp.zeros((8, LANES), jnp.int32)
        for device in range(per):
            owned = pairing[first + device]
            for late in range(2):
                value = 2 * ctx_count - 1 - owned if late else owned
                block = jnp.where(lane // block_rows == 2 * device + late, value, block)
        at = first * 2 * block_rows
        key_pos[:, at : at + LANES] = (block * block_rows + lane % block_rows).astype(jnp.float32)


def split_sequences(rows, own):
    for i in range(rows.shape[1]):
        own[i] = rows[:, i, :]


def assemble_small(place, small, vec, qkv_rows, qkv_bias, up_bias):
    chips, groups = small.shape[:2]
    low = lanes_of((1, LANES)) < LANES // 2
    for pair in range(chips * groups // 2):
        chip, group = pair // (groups // 2), pair % (groups // 2) * 2
        for row in range(6):
            a = small[chip, group, row : row + 1, :]
            b = small[chip, group + 1, row : row + 1, :]
            vec[row : row + 1, pair * LANES : (pair + 1) * LANES] = jnp.where(low, a, b)
        qkv_rows[3 * pair : 3 * pair + 1, :] = small[chip, group, QKV_BIAS : QKV_BIAS + 1, :]
        a = small[chip, group, QKV_BIAS + 1 : QKV_BIAS + 2, :]
        b = small[chip, group + 1, QKV_BIAS + 1 : QKV_BIAS + 2, :]
        qkv_rows[3 * pair + 1 : 3 * pair + 2, :] = jnp.where(low, a, b)
        qkv_rows[3 * pair + 2 : 3 * pair + 3, :] = small[chip, group + 1, QKV_BIAS + 2 : QKV_BIAS + 3, :]
    third = qkv_rows.shape[0] // 3
    per_head = HEAD // LANES
    for k in range(3):
        for u in range(per_head):
            at = (k * per_head + u) * LANES
            qkv_bias[0:1, at : at + LANES] = qkv_rows[pl.ds(k * third + place.chip * per_head + u, 1), :]
    for group in range(groups):
        for u in range(2):
            at = (group * 2 + u) * LANES
            row = UP_BIAS + u
            up_bias[0:1, at : at + LANES] = small[pl.ds(place.chip, 1), group, row : row + 1, :].reshape(1, LANES)


def norm_rows(start, count, hid, vec, norm_one, norm_two, stats):
    step = 16

    @pl.loop(0, count // step)
    def _(i):
        at = pl.ds(pl.multiple_of(start + i * step, step), step)
        x = hid[at, :].astype(jnp.float32)
        average = jnp.mean(x, axis=1, keepdims=True)
        centered = x - average
        scale = lax.rsqrt(jnp.mean(centered * centered, axis=1, keepdims=True) + LN_EPSILON)
        stats[at, 0:1] = average
        stats[at, 1:2] = scale
        xhat = centered * scale
        norm_one[at, :] = (xhat * vec[0:1, :] + vec[1:2, :]).astype(jnp.bfloat16)
        norm_two[at, :] = (xhat * vec[2:3, :] + vec[3:4, :]).astype(jnp.bfloat16)


def turned_half(values):
    half_rot = ROT // 2
    lane = lanes_of(values.shape)
    width = values.shape[-1]
    return jnp.where(
        lane < half_rot,
        pltpu.roll(values, width - half_rot, 1),
        jnp.where(lane < ROT, pltpu.roll(values, half_rot, 1), 0.0),
    )


def project(norm_one, weight, bias, cosine, sine, query, key, value):
    step = 256

    @pl.loop(0, norm_one.shape[0] // step)
    def _(i):
        at = tile(i, step)
        both = nn(norm_one[at, :], flat_rows(weight[...])) + bias[0:1, :]
        cos, sin = cosine[at, :], sine[at, :]
        for k, target in enumerate((query, key)):
            first = both[:, k * HEAD : k * HEAD + LANES]
            target[at, 0:LANES] = (first * cos + turned_half(first) * sin).astype(jnp.bfloat16)
            target[at, LANES:HEAD] = both[:, k * HEAD + LANES : (k + 1) * HEAD].astype(jnp.bfloat16)
        value[at, :] = both[:, 2 * HEAD :].astype(jnp.bfloat16)


def attend(query, key, value, sine, key_pos, attended, attended_low, probs, probs_low):
    step = 256

    @pl.loop(0, query.shape[0] // step)
    def _(i):
        at = tile(i, step)
        scores = contract_cols(query[at, :], key[...]) * HEAD**-0.5
        allowed = key_pos[0:1, :] <= sine[at, ROT : ROT + 1]
        scores = jnp.where(allowed, scores, VERY_LOW)
        highest = jnp.max(scores, axis=1, keepdims=True)
        weights = jnp.where(allowed, jnp.exp(scores - highest), 0.0)
        weights = weights / jnp.sum(weights, axis=1, keepdims=True)
        low = weights.astype(jnp.bfloat16)
        probs[at, :] = weights
        probs_low[at, :] = low
        total = nn(low, value[...])
        attended[at, :] = total
        attended_low[at, :] = total.astype(jnp.bfloat16)


def feed_inner(norm_two, weight, bias, activated, slope):
    step = 128

    @pl.loop(0, norm_two.shape[0] // step)
    def _(i):
        at = tile(i, step)
        inner = nn(norm_two[at, :], flat_rows(weight[...])) + bias[0:1, :]
        normal = 0.5 + 0.5 * lax.erf(inner * 0.5**0.5)
        activated[at, :] = (inner * normal).astype(jnp.bfloat16)
        density = (2.0 * jnp.pi) ** -0.5 * jnp.exp(-0.5 * inner * inner)
        slope[at, :] = normal + inner * density


def attended_grads(cot, weight, attended_low, attended_grad, weight_grad):
    @pl.loop(0, cot.shape[0] // 256)
    def _(i):
        at = tile(i, 256)
        attended_grad[at, :] = contract_cols(cot[at, :], flat_rows(weight[...])).astype(jnp.bfloat16)

    @pl.loop(0, cot.shape[1] // 512)
    def _(i):
        at = tile(i, 512)
        grad = contract_rows(attended_low[...], cot[:, at]).astype(jnp.bfloat16)
        weight_grad[:, :, at] = grad.reshape(weight_grad.shape[0], weight_grad.shape[1], 512)


def attention_grads(
    query, key, value, cosine, sine, attended, attended_grad, probs, probs_low, score_grad, projected_grad
):
    step = 256
    scaling = HEAD**-0.5

    def put(at, k, grad):
        first = grad[:, 0:LANES]
        back = first * cosine[at, :] - turned_half(first) * sine[at, :]
        projected_grad[at, k * HEAD : k * HEAD + LANES] = back.astype(jnp.bfloat16)
        projected_grad[at, k * HEAD + LANES : (k + 1) * HEAD] = grad[:, LANES:].astype(jnp.bfloat16)

    @pl.loop(0, query.shape[0] // step)
    def _(i):
        at = tile(i, step)
        own = attended_grad[at, :]
        row_delta = jnp.sum(own.astype(jnp.float32) * attended[at, :], axis=1, keepdims=True)
        grad = (probs[at, :] * (contract_cols(own, value[...]) - row_delta)).astype(jnp.bfloat16)
        score_grad[at, :] = grad
        put(at, 0, nn(grad, key[...]) * scaling)

    @pl.loop(0, query.shape[0] // step)
    def _(i):
        at = tile(i, step)
        put(at, 1, contract_rows(score_grad[:, at], query[...]) * scaling)
        projected_grad[at, 2 * HEAD :] = contract_rows(probs_low[:, at], attended_grad[...]).astype(jnp.bfloat16)


def weight_grads(tokens, grads, result):
    chips, groups, rows = result.shape[:3]
    step = groups * rows

    @pl.loop(0, chips)
    def _(k):
        grad = contract_rows(tokens[:, tile(k, step)], grads[...]).astype(jnp.bfloat16)
        result[k] = grad.reshape(result.shape[1:])


def column_sums(values, result):
    step = 16

    def add(i, total):
        return total + values[tile(i, step), :].astype(jnp.float32)

    total = lax.fori_loop(0, values.shape[0] // step, add, jnp.zeros((step, values.shape[1]), jnp.float32))
    result[0:1, :] = jnp.sum(total, axis=0, keepdims=True)


def gather_kernel(
    ctx_count,
    hid_in,
    cot_in,
    ln1_gain_in,
    ln1_bias_in,
    ln2_gain_in,
    ln2_bias_in,
    out_bias_in,
    down_bias_in,
    qkv_bias_in,
    up_bias_in,
    qkv,
    up,
    down,
    out,
    pairing,
    hid_all,
    cot_all,
    qkv_all,
    up_all,
    down_all,
    out_all,
    small_all,
    attended_low_out,
    projected_grad_out,
    norm_two_out,
    activated_out,
    slope_out,
    qkv_grad_out,
    down_grad_out,
    out_grad_out,
    vec_out,
    stats_out,
    qkv_sum_out,
    cot_sum_out,
    hid_rows,
    cot_rows,
    hid,
    cot,
    ln1_gain,
    ln1_bias,
    ln2_gain,
    ln2_bias,
    out_bias,
    down_bias,
    qkv_bias_own,
    up_bias_own,
    small,
    hid_v,
    cot_v,
    qkv_v,
    up_v,
    out_v,
    small_v,
    cosine,
    sine,
    key_pos,
    vec,
    qkv_rows,
    qkv_bias,
    up_bias,
    norm_one,
    norm_two,
    stats,
    query,
    key,
    value,
    attended,
    attended_low,
    probs,
    probs_low,
    activated,
    slope,
    attended_grad,
    score_grad,
    projected_grad,
    out_grad,
    qkv_sum,
    cot_sum,
    send,
    recv,
    local,
):
    place = Place(ctx_count)
    copies = Copies(send, recv, local)
    width = out.shape[1]
    head = qkv_all.shape[3] // 3
    part = up_all.shape[3]

    def qkv_pieces(to, row, group):
        return [
            (
                qkv.at[:, pl.ds(pl.multiple_of(k * width + to * head, head), head)],
                qkv_all.at[row, group, :, pl.ds(k * head, head)],
            )
            for k in range(3)
        ]

    half = part // 2

    def half_gather(source, whole, first):
        columns = pl.ds(first, half)

        def pieces(to, row, group):
            given = pl.ds(pl.multiple_of(to * part + first, half), half)
            return [(source.at[:, given], whole.at[row, group, :, columns])]

        return WeightGather(place, copies, pieces, whole, columns)

    hid_g = TokenGather(place, copies, hid, hid_all)
    cot_g = TokenGather(place, copies, cot, cot_all)
    small_g = WeightGather(place, copies, lambda to, row, group: [(small, small_all.at[row, group])], small_all)
    qkv_g = WeightGather(place, copies, qkv_pieces, qkv_all)
    weights = {"qkv": qkv_g}
    for name, source, whole in (("up", up, up_all), ("down", down, down_all)):
        weights[name + " a"] = half_gather(source, whole, 0)
        weights[name + " b"] = half_gather(source, whole, half)
    group = 2 * place.c + place.x
    out_mine = copies.inside(out, out_all.at[group])
    out_across = copies.remote(out, out_all.at[group], place.other_plane())
    out_pair = out_all.at[pl.ds(2 * place.c, 2)]
    out_swap = copies.remote(out_pair, out_pair, place.other_core())
    loads = {
        name: copies.inside(src, dst)
        for name, src, dst in (
            ("hid rows", hid_in, hid_rows),
            ("cot rows", cot_in, cot_rows),
            ("small", small_all, small_v),
            ("hid", hid_all, hid_v),
            ("cot", cot_all, cot_v),
            ("qkv", qkv_all, qkv_v),
            ("up", up_all, up_v),
            ("out", out_all, out_v),
        )
    }
    stores = {
        name: copies.inside(src, dst)
        for name, src, dst in (
            ("vec", vec, vec_out),
            ("stats", stats, stats_out),
            ("attended_low", attended_low, attended_low_out),
            ("norm_two", norm_two, norm_two_out),
            ("activated", activated, activated_out),
            ("slope", slope, slope_out),
            ("out_grad", out_grad, out_grad_out),
            ("projected_grad", projected_grad, projected_grad_out),
            ("qkv_grad", qkv_v, qkv_grad_out),
            ("down_grad", up_v, down_grad_out),
            ("qkv_sum", qkv_sum, qkv_sum_out),
            ("cot_sum", cot_sum, cot_sum_out),
        )
    }

    def fetch(name):
        loads[name].start()
        loads[name].wait()

    rows = hid_v.shape[0]
    normed = iter(range(NORM_PARTS))

    def norm_next():
        part_rows = rows // NORM_PARTS
        norm_rows(next(normed) * part_rows, part_rows, hid_v, vec, norm_one, norm_two, stats)

    def norm_done():
        stores["norm_two"].start()
        stores["stats"].start()

    def small_done():
        small_g.finish()
        fetch("small")
        assemble_small(place, small_v, vec, qkv_rows, qkv_bias, up_bias)
        stores["vec"].start()

    def hid_done():
        hid_g.finish()
        fetch("hid")

    def project_all():
        qkv_g.finish()
        fetch("qkv")
        project(norm_one, qkv_v, qkv_bias, cosine, sine, query, key, value)

    def attend_all():
        attend(query, key, value, sine, key_pos, attended, attended_low, probs, probs_low)
        stores["attended_low"].start()

    def inner_all():
        weights["up a"].finish()
        weights["up b"].finish()
        fetch("up")
        feed_inner(norm_two, up_v, up_bias, activated, slope)
        stores["activated"].start()
        stores["slope"].start()

    def out_start():
        out_mine.start()
        out_across.start()

    def out_share():
        out_mine.wait()
        out_across.wait_recv()
        out_swap.start()

    def cot_done():
        cot_g.finish()
        loads["cot"].start()
        out_swap.wait_recv()
        fetch("out")
        loads["cot"].wait()

    def out_grads():
        attended_grads(cot_v, out_v, attended_low, attended_grad, out_grad)
        stores["out_grad"].start()

    def down_grads():
        weight_grads(cot_v, activated, up_v)
        stores["down_grad"].start()
        column_sums(cot_v, cot_sum)
        stores["cot_sum"].start()

    def attention_back():
        attention_grads(
            query, key, value, cosine, sine, attended, attended_grad, probs, probs_low, score_grad, projected_grad
        )
        stores["projected_grad"].start()

    def qkv_grads():
        weight_grads(norm_one, projected_grad, qkv_v)
        stores["qkv_grad"].start()
        column_sums(projected_grad, qkv_sum)
        stores["qkv_sum"].start()

    steps = {
        "tables": lambda: position_tables(ctx_count, pairing, cosine, sine, key_pos),
        "hid spread": hid_g.spread,
        "cot spread": cot_g.spread,
        "small cross": small_g.cross,
        "small share": small_g.share,
        "small done": small_done,
        "out start": out_start,
        "out share": out_share,
        "hid done": hid_done,
        "norm": norm_next,
        "norm done": norm_done,
        "project": project_all,
        "attend": attend_all,
        "inner": inner_all,
        "cot done": cot_done,
        "out grads": out_grads,
        "down grads": down_grads,
        "attention back": attention_back,
        "qkv grads": qkv_grads,
    }
    for j in range(place.line - 1):
        steps["hid %d" % j] = functools.partial(hid_g.step, j)
        steps["cot %d" % j] = functools.partial(cot_g.step, j)
    for name, gather in weights.items():
        for i in range(len(gather.by_chip)):
            steps["%s %d" % (name, i)] = functools.partial(gather.send, i)
        steps[name + " cross"] = gather.cross
        steps[name + " share"] = gather.share

    vectors = (ln1_gain, ln1_bias, ln2_gain, ln2_bias, out_bias, down_bias, qkv_bias_own, up_bias_own)
    vectors_in = (
        ln1_gain_in,
        ln1_bias_in,
        ln2_gain_in,
        ln2_bias_in,
        out_bias_in,
        down_bias_in,
        qkv_bias_in,
        up_bias_in,
    )
    vector_loads = [copies.inside(src, dst) for src, dst in zip(vectors_in, vectors)]
    loads["hid rows"].start()
    for load in vector_loads:
        load.start()
    loads["cot rows"].start()
    answered = greet(place)
    loads["hid rows"].wait()
    split_sequences(hid_rows, hid)
    for load in vector_loads:
        load.wait()
    pack_parameters(vectors, small)
    answered()
    hid_g.start()
    small_g.scatter()
    loads["cot rows"].wait()
    split_sequences(cot_rows, cot)
    cot_g.start()
    for name in GATHER_ORDER:
        steps[name]()
    weights["down a"].finish()
    weights["down b"].finish()
    for store in stores.values():
        store.wait()
    for gather in [hid_g, cot_g, small_g] + list(weights.values()):
        gather.drain()
    out_across.wait_send()
    out_swap.wait_send()


def gather_all(ctx_count, hid, cot, vectors, qkv, up, down, out, pairing):
    f32, b16 = jnp.float32, jnp.bfloat16
    chips = ctx_count // CORES
    rows = qkv.shape[0]
    groups = CORES * 2
    tokens = ctx_count * hid.shape[0]
    width = out.shape[1]
    head3, part = qkv.shape[1] // chips, up.shape[1] // chips
    head = head3 // 3
    qkv_s = ((chips, groups, rows, head3), b16)
    part_s = ((chips, groups, rows, part), b16)
    out_s = ((groups, rows, width), b16)
    small = (SMALL_ROWS, LANES)
    small_s = ((chips, groups) + small, f32)
    wide_s, narrow_s = ((tokens, width), b16), ((tokens, head), b16)
    own_s = ((hid.shape[1], hid.shape[0], width), b16)
    results = [
        wide_s,
        wide_s,
        qkv_s,
        part_s,
        part_s,
        out_s,
        small_s,
        narrow_s,
        ((tokens, head3), b16),
        wide_s,
        ((tokens, part), b16),
        ((tokens, part), f32),
        qkv_s,
        part_s,
        out_s,
        ((8, width), f32),
        ((tokens, LANES), f32),
        ((8, head3), f32),
        ((8, width), f32),
    ]
    scratch = [
        (hid.shape, b16),
        (cot.shape, b16),
        own_s,
        own_s,
    ]
    scratch += [(vector.shape, b16) for vector in vectors]
    scratch += [
        (small, f32),
        wide_s,
        wide_s,
        qkv_s,
        part_s,
        out_s,
        small_s,
        ((tokens, LANES), f32),
        ((tokens, LANES), f32),
        ((8, tokens), f32),
        ((8, width), f32),
        ((3 * width // LANES, LANES), f32),
        ((8, head3), f32),
        ((8, part), f32),
        wide_s,
        wide_s,
        ((tokens, LANES), f32),
        narrow_s,
        narrow_s,
        narrow_s,
        ((tokens, head), f32),
        narrow_s,
        ((tokens, tokens), f32),
        ((tokens, tokens), b16),
        ((tokens, part), b16),
        ((tokens, part), f32),
        narrow_s,
        ((tokens, tokens), b16),
        ((tokens, head3), b16),
        out_s,
        ((8, head3), f32),
        ((8, width), f32),
    ]
    operands = (hid, cot, *vectors, qkv, up, down, out, pairing)
    anywhere = pl.BlockSpec(memory_space=pl.ANY)
    return pl.pallas_call(
        lambda *refs: gather_kernel(ctx_count, *refs),
        out_shape=[jax.ShapeDtypeStruct(*shape) for shape in results],
        in_specs=[anywhere] * (len(operands) - 1) + [pl.BlockSpec(memory_space=pltpu.SMEM)],
        out_specs=[anywhere] * len(results),
        scratch_shapes=[pltpu.VMEM(*shape) for shape in scratch]
        + [
            pltpu.SemaphoreType.DMA((112,)),
            pltpu.SemaphoreType.DMA((112,)),
            pltpu.SemaphoreType.DMA((48,)),
        ],
        compiler_params=pltpu.CompilerParams(
            collective_id=0, has_side_effects=True, vmem_limit_bytes=VMEM_BYTES
        ),
        name="gather_all",
    )(*operands)


def add_rows(total, other, count):
    step = 16
    per = total.shape[-2] // step

    @pl.loop(0, count * per)
    def _(i):
        k, at = i // per, tile(i % per, step)
        both = total[k, at, :].astype(jnp.float32) + other[k, at, :].astype(jnp.float32)
        total[k, at, :] = both.astype(total.dtype)


def add_tiles(total, other, pieces):
    rows = total.shape[-2]

    @pl.loop(0, pieces)
    def _(k):
        both = total[k].astype(jnp.float32) + other[k].astype(jnp.float32)
        total[k] = both.astype(total.dtype)


class GradScatter:
    def __init__(self, place, copies, partial, kept, from_core, from_plane, result, columns=None):
        self.place = place
        c, x, chip = place.c, place.x, place.chip
        self.kept, self.from_core, self.from_plane = kept, from_core, from_plane
        self.columns = cols = slice(0, kept.shape[3]) if columns is None else columns
        self.load = None
        given = partial.at[:, :, :, cols]
        if partial.shape != kept.shape:
            self.load = copies.inside(partial.at[:, pl.ds(2 * c, 2), :, cols], kept.at[:, :, :, cols])
            given = partial.at[:, pl.ds(2 * (1 - c), 2), :, cols]
        self.swap = copies.remote(given, from_core.at[:, :, :, cols], place.other_core())
        self.across = copies.remote(
            kept.at[:, 1 - x, :, cols], from_plane.at[:, :, cols], place.other_plane()
        )
        self.scattered = []
        for dz, dy in place.plane_offsets():
            z, y = place.shifted(dz, dy)
            self.scattered.append(
                copies.remote(
                    kept.at[z * LINE_Y + y, x, :, cols], result.at[chip, :, cols], place.at(z, y, c, x)
                )
            )
        self.own = copies.inside(kept.at[chip, x, :, cols], result.at[chip, :, cols])

    def start(self):
        if self.load is not None:
            self.load.start()
        self.swap.start()

    def cross(self):
        if self.load is not None:
            self.load.wait()
        self.swap.wait_recv()
        x = self.place.x
        self.add(1 - x, self.from_core.at[:, 1 - x])
        self.across.start()
        self.add(x, self.from_core.at[:, x])

    def add(self, x, other):
        step = 16
        per = self.kept.shape[2] // step
        cols = self.columns

        @pl.loop(0, self.kept.shape[0] * per)
        def _(i):
            k, at = i // per, tile(i % per, step)
            both = self.kept[k, x, at, cols].astype(jnp.float32) + other[k, at, cols].astype(jnp.float32)
            self.kept[k, x, at, cols] = both.astype(self.kept.dtype)

    def scatter(self):
        self.across.wait_recv()
        self.add(self.place.x, self.from_plane)
        for copy in self.scattered + [self.own]:
            copy.start()

    def finish(self):
        self.own.wait()
        for copy in self.scattered:
            copy.wait_recv()

    def drain(self):
        for copy in self.scattered + [self.swap, self.across]:
            copy.wait_send()


def weight_grads_by_core(place, tokens, grads, kept, given, columns):
    chips, half, rows = kept.shape[:3]
    step = 2 * half * rows

    @pl.loop(0, chips)
    def _(k):
        grad = contract_rows(tokens[:, tile(k, step)], grads[:, columns]).astype(jnp.bfloat16)
        grad = grad.reshape(2, half, rows, grad.shape[1])
        kept[k, :, :, columns] = jnp.where(place.c == 0, grad[0], grad[1])
        given[k, :, :, columns] = jnp.where(place.c == 0, grad[1], grad[0])


class TokenScatter:
    def __init__(self, place, copies, part, from_y, slots, total, result):
        self.place = place
        z, y, c, x = place.z, place.y, place.c, place.x
        self.part, self.from_y, self.slots, self.total = part, from_y, slots, total
        self.line = place.line
        last = self.line - 1
        self.last = last
        self.copies = copies
        self.over_base = copies.reserve(self.line)
        self.up_base = copies.reserve(self.line)
        self.down_base = copies.reserve(self.line)
        self.above = place.at(jnp.minimum(z + 1, last), y, c, x)
        self.below = place.at(jnp.maximum(z - 1, 0), y, c, x)
        self.swap = copies.remote(total.at[1 - c], result.at[c], place.other_core())
        self.own = copies.inside(total.at[c], result.at[c])

    def order(self, i):
        last = self.last
        chunk = 0
        for z in range(self.line):
            far = sorted(range(self.line), key=lambda k: (-abs(k - z), min(k, last - k)))
            chunk = jnp.where(self.place.z == z, far[i], chunk)
        return chunk

    def over(self, k):
        y = self.place.y
        return self.copies.remote_at(
            self.over_base + k, self.part.at[k, 1 - y], self.from_y.at[k], self.place.other_y()
        )

    def up(self, k):
        return self.copies.remote_at(
            self.up_base + k, self.part.at[k, self.place.y], self.slots.at[k], self.above
        )

    def down(self, k):
        slot = jnp.where(self.place.z - 1 == k, self.line, k)
        return self.copies.remote_at(
            self.down_base + k, self.part.at[k, self.place.y], self.slots.at[slot], self.below
        )

    def combine(self, k):
        self.over(k).wait_recv()
        add_rows(self.part.at[k, self.place.y], self.from_y.at[k], CORES)

    def step(self, i):
        z, y = self.place.z, self.place.y
        k = self.order(i)
        self.combine(k)

        @pl.when(k > z)
        def _():
            @pl.when(z > 0)
            def _():
                self.up(k).wait_recv()
                add_rows(self.part.at[k, y], self.slots.at[k], CORES)

            self.up(k).start()

        @pl.when(k < z)
        def _():
            @pl.when(z < self.last)
            def _():
                self.down(k).wait_recv()
                add_rows(self.part.at[k, y], self.slots.at[k], CORES)

            self.down(k).start()

    def reduce(self):
        z, y, last = self.place.z, self.place.y, self.last
        self.combine(z)
        pl.when(z > 0)(lambda: self.up(z).wait_recv())
        pl.when(z < last)(lambda: self.down(z).wait_recv())
        step = 16
        per = self.total.shape[1] // step

        @pl.loop(0, CORES * per)
        def _(i):
            k, at = i // per, tile(i % per, step)
            self.total[k, at, :] = self.part[z, y, k, at, :].astype(jnp.float32)

        def add(slot):
            @pl.loop(0, CORES * per)
            def _(i):
                k, at = i // per, tile(i % per, step)
                self.total[k, at, :] += self.slots[slot, k, at, :].astype(jnp.float32)

        pl.when(z > 0)(lambda: add(z))
        pl.when(z < last)(lambda: add(last + 1))
        self.swap.start()
        self.own.start()

    def finish(self):
        self.swap.wait_recv()

    def drain(self):
        z, last = self.place.z, self.last
        for k in range(self.line):
            self.over(k).wait_send()
            pl.when(z < k)(lambda: self.up(k).wait_send())
            pl.when(z > k)(lambda: self.down(k).wait_send())


def output_part(scatter, i, attended_low, activated, out_weight, down_weight):
    k = scatter.order(i)
    part = scatter.part
    size = part.shape[1] * part.shape[2] * part.shape[3]
    at = tile(k, size)
    rows = nn(attended_low[at, :], flat_rows(out_weight[...]))
    rows = rows + contract_cols(activated[at, :], flat_rows(down_weight[...]))
    part[k] = rows.astype(part.dtype).reshape(part.shape[1:])
    scatter.over(k).start()


def inner_grads(cot, down_weight, slope, slope_loads, inner_grad):
    step = slope.shape[1]
    for i, load in enumerate(slope_loads):
        load.wait()
        at = slice(i * step, (i + 1) * step)
        grad = nn(cot[at, :], flat_rows(down_weight[...])) * slope[i % 2]
        inner_grad[at, :] = grad.astype(jnp.bfloat16)
        if i + 2 < len(slope_loads):
            slope_loads[i + 2].start()


def hidden_part(scatter, i, inner_grad, up_weight, projected_grad, qkv_weight, hid, stats, vec, sums):
    def by_eight(values):
        return jnp.sum(values.reshape(-1, 8, values.shape[1]), axis=0)

    k = scatter.order(i)
    part = scatter.part
    size = part.shape[2] * part.shape[3]

    @pl.loop(0, LINE_Y)
    def _(y):
        at = tile(k * LINE_Y + y, size)
        one = contract_cols(projected_grad[at, :], flat_rows(qkv_weight[...]))
        two = contract_cols(inner_grad[at, :], flat_rows(up_weight[...]))
        xhat = (hid[at, :].astype(jnp.float32) - stats[at, 0:1]) * stats[at, 1:2]
        sums[0] += by_eight(one * xhat)
        sums[1] += by_eight(one)
        sums[2] += by_eight(two * xhat)
        sums[3] += by_eight(two)
        rows = one * vec[0:1, :] + two * vec[2:3, :]
        part[k, y] = rows.astype(part.dtype).reshape(part.shape[2:])

    scatter.over(k).start()


COT_SUM, UP_SUM, QKV_SUM = 4, 5, 7


def pack_small(place, sums, cot_sum, up_sum, qkv_sum, qkv_rows, tiles):
    chips, groups = tiles.shape[:2]
    tiles[...] = jnp.zeros_like(tiles)
    qkv_rows[...] = jnp.zeros_like(qkv_rows)
    third = qkv_rows.shape[0] // 3
    per_head = HEAD // LANES
    for k in range(3):
        for u in range(per_head):
            at = (k * per_head + u) * LANES
            qkv_rows[pl.ds(k * third + place.chip * per_head + u, 1), :] = qkv_sum[0:1, at : at + LANES]
    first = jnp.where(place.chip == 0, 1.0, 0.0)
    norm_sums = [jnp.sum(sums[row], axis=0, keepdims=True) for row in range(4)]
    norm_sums.append(cot_sum[0:1, :] * first)
    for pair in range(chips * groups // 2):
        chip, group = pair // (groups // 2), pair % (groups // 2) * 2
        at = slice(pair * LANES, (pair + 1) * LANES)
        for g in (group, group + 1):
            for row in range(5):
                tiles[chip, g, row : row + 1, :] = norm_sums[row][:, at]
            tiles[chip, g, QKV_SUM : QKV_SUM + 3, :] = qkv_rows[3 * pair : 3 * pair + 3, :]
    for group in range(groups):
        for u in range(2):
            at = (group * 2 + u) * LANES
            row = UP_SUM + u
            values = up_sum[0:1, at : at + LANES].reshape(1, 1, LANES)
            tiles[pl.ds(place.chip, 1), group, row : row + 1, :] = values


SCATTER_ORDER = (
    "outs tile 0",
    "qkv swap",
    "down a swap",
    "down b swap",
    "out swap",
    "outs tile 1",
    "qkv cross",
    "down a cross",
    "outs tile 2",
    "outs tile 3",
    "outs 0",
    "inner",
    "down b cross",
    "up a grad",
    "qkv scatter",
    "up sum",
    "up b grad",
    "outs 1",
    "outs 2",
    "up a swap",
    "hid tile 0",
    "hid tile 1",
    "up b swap",
    "down b scatter",
    "hid tile 2",
    "down a scatter",
    "hid tile 3",
    "out cross",
    "up b cross",
    "pack",
    "hid 0",
    "small swap",
    "hid 1",
    "small cross",
    "up b scatter",
    "small scatter",
    "up a cross",
    "out finish",
    "hid 2",
    "up a scatter",
    "outs reduce",
    "hid reduce",
)


def scatter_kernel(
    ctx_count,
    hid_in,
    cot_in,
    qkv_in,
    up_in,
    down_in,
    out_in,
    attended_low_in,
    projected_grad_in,
    norm_two_in,
    activated_in,
    slope_in,
    stats_in,
    vec_in,
    qkv_sum_in,
    cot_sum_in,
    qkv_grad,
    down_grad,
    out_grad,
    small_result,
    qkv_result,
    up_result,
    down_result,
    out_grad_result,
    out_result,
    hid_result,
    wide,
    weight,
    slope,
    act,
    attended_low,
    out_weight,
    qkv_weight,
    projected_grad,
    stats,
    vec,
    qkv_sum,
    cot_sum,
    up_sum,
    sums,
    qkv_rows,
    tiles,
    small_kept,
    small_core,
    small_plane,
    qkv_kept,
    qkv_core,
    qkv_plane,
    up_kept,
    up_core,
    up_plane,
    down_kept,
    down_core,
    down_plane,
    out_kept,
    out_core,
    out_plane,
    out_part,
    out_from_y,
    out_slots,
    hid_part,
    hid_from_y,
    hid_slots,
    total,
    send,
    recv,
    local,
):
    place = Place(ctx_count)
    copies = Copies(send, recv, local)
    c, x = place.c, place.x
    half = up_kept.shape[3] // 2
    halves = {" a": slice(0, half), " b": slice(half, 2 * half)}
    grads = {
        "qkv": GradScatter(place, copies, qkv_grad, qkv_kept, qkv_core, qkv_plane, qkv_result),
        "small": GradScatter(place, copies, tiles, small_kept, small_core, small_plane, small_result),
    }
    for name, cols in halves.items():
        grads["down" + name] = GradScatter(
            place, copies, down_grad, down_kept, down_core, down_plane, down_result, cols
        )
        grads["up" + name] = GradScatter(place, copies, down_core, up_kept, up_core, up_plane, up_result, cols)
    outs_s = TokenScatter(place, copies, out_part, out_from_y, out_slots, total, out_result)
    hid_s = TokenScatter(place, copies, hid_part, hid_from_y, hid_slots, total, hid_result)
    out_load = copies.inside(out_grad.at[pl.ds(2 * c, 2)], out_kept)
    out_swap = copies.remote(out_grad.at[pl.ds(2 * (1 - c), 2)], out_core, place.other_core())
    out_across = copies.remote(out_kept.at[1 - x], out_plane, place.other_plane())
    out_own = copies.inside(out_kept.at[x], out_grad_result)
    loads = {
        name: copies.inside(src, dst)
        for name, src, dst in (
            ("activated", activated_in, act),
            ("attended_low", attended_low_in, attended_low),
            ("out", out_in, out_weight),
            ("down", down_in, weight),
            ("cot", cot_in, wide),
            ("norm_two", norm_two_in, wide),
            ("qkv", qkv_in, qkv_weight),
            ("projected_grad", projected_grad_in, projected_grad),
            ("stats", stats_in, stats),
            ("vec", vec_in, vec),
            ("qkv_sum", qkv_sum_in, qkv_sum),
            ("cot_sum", cot_sum_in, cot_sum),
            ("up", up_in, weight),
            ("hid", hid_in, wide),
        )
    }
    early = ("activated", "attended_low", "out", "down", "cot", "qkv", "projected_grad")
    early += ("stats", "vec", "qkv_sum", "cot_sum")

    def out_cross():
        out_load.wait()
        out_swap.wait_recv()
        add_rows(out_kept, out_core, 2)
        out_across.start()

    def out_finish():
        out_across.wait_recv()
        step = 16

        @pl.loop(0, out_plane.shape[0] // step)
        def _(i):
            at = tile(i, step)
            both = out_kept[x, at, :].astype(jnp.float32) + out_plane[at, :].astype(jnp.float32)
            out_kept[x, at, :] = both.astype(out_kept.dtype)

        out_own.start()

    step = slope.shape[1]
    slope_loads = [
        copies.inside(slope_in.at[pl.ds(i * step, step)], slope.at[i % 2]) for i in range(slope_in.shape[0] // step)
    ]
    waited = set()

    def need(*names):
        for name in names:
            if name not in waited:
                waited.add(name)
                loads[name].wait()

    def output_tile(i):
        need("activated", "attended_low", "out", "down")
        output_part(outs_s, i, attended_low, act, out_weight, weight)

    def inner_all():
        need("cot")
        inner_grads(wide, weight, slope, slope_loads, act)
        loads["up"].start()
        loads["norm_two"].start()

    def up_half(name, last):
        need("norm_two")
        weight_grads_by_core(place, wide, act, up_kept, down_core, halves[name])
        if last:
            loads["hid"].start()

    def hidden_tile(i):
        if i == 0:
            need("qkv", "projected_grad", "stats", "vec", "up", "hid")
            sums[...] = jnp.zeros_like(sums)
        hidden_part(hid_s, i, act, weight, projected_grad, qkv_weight, wide, stats, vec, sums)

    def pack():
        need("qkv_sum", "cot_sum")
        pack_small(place, sums, cot_sum, up_sum, qkv_sum, qkv_rows, tiles)

    def out_start():
        out_load.start()
        out_swap.start()

    def hidden_reduce():
        outs_s.own.wait()
        outs_s.swap.wait_send()
        hid_s.reduce()

    steps = {
        "out swap": out_start,
        "out cross": out_cross,
        "out finish": out_finish,
        "inner": inner_all,
        "up a grad": functools.partial(up_half, " a", False),
        "up b grad": functools.partial(up_half, " b", True),
        "up sum": lambda: column_sums(act, up_sum),
        "pack": pack,
        "outs reduce": outs_s.reduce,
        "hid reduce": hidden_reduce,
    }
    for name, scatter in grads.items():
        steps[name + " swap"] = scatter.start
        steps[name + " cross"] = scatter.cross
        steps[name + " scatter"] = scatter.scatter
    for i in range(outs_s.line):
        steps["outs tile %d" % i] = functools.partial(output_tile, i)
        steps["hid tile %d" % i] = functools.partial(hidden_tile, i)
    for j in range(outs_s.last):
        steps["outs %d" % j] = functools.partial(outs_s.step, j)
        steps["hid %d" % j] = functools.partial(hid_s.step, j)

    for name in early:
        loads[name].start()
    slope_loads[0].start()
    slope_loads[1].start()
    greet(place)()
    for name in SCATTER_ORDER:
        steps[name]()
    scatters = list(grads.values()) + [outs_s, hid_s]
    for scatter in scatters:
        scatter.finish()
    out_own.wait()
    hid_s.own.wait()
    hid_s.swap.wait_send()
    for scatter in scatters:
        scatter.drain()
    out_swap.wait_send()
    out_across.wait_send()


def scatter_all(ctx_count, local_rows, operands):
    f32, b16 = jnp.float32, jnp.bfloat16
    hid, _, w_qkv, w_up, _, w_out = operands[:6]
    chips, groups, rows, head3 = w_qkv.shape
    part = w_up.shape[3]
    tokens, width = hid.shape
    line = chips // LINE_Y
    small = (SMALL_ROWS, LANES)
    token = (CORES, local_rows, width)
    results = [
        ((chips,) + small, f32),
        ((chips, rows, head3), b16),
        ((chips, rows, part), b16),
        ((chips, rows, part), b16),
        ((rows, width), b16),
        (token, f32),
        (token, f32),
    ]
    scratch = [
        ((tokens, width), b16),
        (w_up.shape, b16),
        ((2, 256, part), f32),
        ((tokens, part), b16),
        ((tokens, head3 // 3), b16),
        (w_out.shape, b16),
        (w_qkv.shape, b16),
        ((tokens, head3), b16),
        ((tokens, LANES), f32),
        ((8, width), f32),
        ((8, head3), f32),
        ((8, width), f32),
        ((8, part), f32),
        ((4, 8, width), f32),
        ((3 * width // LANES, LANES), f32),
        ((chips, groups) + small, f32),
    ]
    for shape, dtype in ((small, f32), ((rows, head3), b16), ((rows, part), b16), ((rows, part), b16)):
        scratch += [((chips, 2) + shape, dtype)] * 2 + [((chips,) + shape, dtype)]
    scratch += [((2, rows, width), b16)] * 2 + [((rows, width), b16)]
    for _ in range(2):
        scratch += [
            ((line, LINE_Y) + token, b16),
            ((line,) + token, b16),
            ((line + 1,) + token, b16),
        ]
    scratch += [(token, f32)]
    anywhere = pl.BlockSpec(memory_space=pl.ANY)
    return pl.pallas_call(
        lambda *refs: scatter_kernel(ctx_count, *refs),
        out_shape=[jax.ShapeDtypeStruct(*shape) for shape in results],
        in_specs=[anywhere] * len(operands),
        out_specs=[anywhere] * len(results),
        scratch_shapes=[pltpu.VMEM(*shape) for shape in scratch]
        + [
            pltpu.SemaphoreType.DMA((96,)),
            pltpu.SemaphoreType.DMA((96,)),
            pltpu.SemaphoreType.DMA((48,)),
        ],
        compiler_params=pltpu.CompilerParams(
            collective_id=1, has_side_effects=True, vmem_limit_bytes=VMEM_BYTES
        ),
        name="scatter_all",
    )(*operands)


def finish_kernel(
    qkv_in,
    up_in,
    down_in,
    out_in,
    out_rows_in,
    hid_rows_in,
    hidden_in,
    cotangent_in,
    small,
    vec,
    ln1_gain,
    ln1_bias,
    qkv_bias,
    out_bias,
    ln2_gain,
    ln2_bias,
    up_bias,
    down_bias,
    output_out,
    grad_hidden_out,
    qkv_out,
    out_out,
    up_out,
    down_out,
    qkv_rows,
    up_rows,
    down_rows,
    out_piece,
    out_rows,
    hid_rows,
    hidden,
    cotangent,
    output,
    grad_hidden,
    qkv,
    out,
    up,
    down,
    load_sems,
    store_sems,
):
    f32 = jnp.float32
    given = (up_in, down_in, qkv_in, out_in, out_rows_in, hid_rows_in, hidden_in, cotangent_in)
    held = (up_rows, down_rows, qkv_rows, out_piece, out_rows, hid_rows, hidden, cotangent)
    loads = [pltpu.make_async_copy(src, dst, load_sems.at[i]) for i, (src, dst) in enumerate(zip(given, held))]
    made = (up, down, qkv, out, output, grad_hidden)
    asked = (up_out, down_out, qkv_out, out_out, output_out, grad_hidden_out)
    stores = [pltpu.make_async_copy(src, dst, store_sems.at[i]) for i, (src, dst) in enumerate(zip(made, asked))]
    for load in loads:
        load.start()

    total = jnp.sum(small[...], axis=0)
    half = LANES // 2
    odd = lax.axis_index("fsdp") == 1
    halves = jnp.where(odd, total[: COT_SUM + 1, half:], total[: COT_SUM + 1, :half])
    for row, ref in enumerate((ln1_gain, ln1_bias, ln2_gain, ln2_bias, out_bias)):
        ref[...] = halves[row]
    down_bias[...] = halves[COT_SUM]
    for u in range(2):
        up_bias[u * LANES : (u + 1) * LANES] = total[UP_SUM + u]
    first, middle, last = [total[QKV_SUM + u : QKV_SUM + u + 1] for u in range(3)]
    even_row = jnp.concatenate([first, middle[:, :half]], axis=1)
    odd_row = jnp.concatenate([middle[:, half:], last], axis=1)
    qkv_bias[...] = jnp.where(odd, odd_row, even_row)[0]

    chips = up_rows.shape[0]
    for i, rows, made_ref in ((0, up_rows, up), (1, down_rows, down)):
        loads[i].wait()
        size = rows.shape[2]
        for k in range(chips):
            made_ref[:, k * size : (k + 1) * size] = rows[k].astype(f32)
        stores[i].start()
    loads[2].wait()
    third = qkv.shape[1] // 3
    for k in range(chips):
        for t in range(3):
            at = t * third + k * HEAD
            qkv[:, at : at + HEAD] = qkv_rows[k, :, t * HEAD : (t + 1) * HEAD].astype(f32)
    stores[2].start()
    loads[3].wait()
    out[...] = out_piece[...].astype(f32)
    stores[3].start()

    for load in loads[4:]:
        load.wait()
    bias = vec[OUT_BIAS : OUT_BIAS + 1, :] + vec[DOWN_BIAS : DOWN_BIAS + 1, :]
    step = 16

    @pl.loop(0, hidden.shape[0] // step)
    def _(i):
        at = tile(i, step)
        both, grads = [], []
        for s in range(hidden.shape[1]):
            x = hidden[at, s, :].astype(f32)
            both.append(x + out_rows[s, at, :] + bias)
            average = jnp.mean(x, axis=1, keepdims=True)
            centered = x - average
            scale = lax.rsqrt(jnp.mean(centered * centered, axis=1, keepdims=True) + LN_EPSILON)
            xhat = centered * scale
            e = hid_rows[s, at, :]
            slope = jnp.mean(e * xhat, axis=1, keepdims=True)
            back = scale * (e - jnp.mean(e, axis=1, keepdims=True) - xhat * slope)
            grads.append(cotangent[at, s, :].astype(f32) + back)
        output[at] = jnp.stack(both, axis=1).astype(output.dtype)
        grad_hidden[at] = jnp.stack(grads, axis=1)

    stores[4].start()
    stores[5].start()
    for store in stores:
        store.wait()


def finish_all(qkv_rows, up_rows, down_rows, out_sum, out_rows, hid_rows, hidden, cotangent, small, vec):
    f32 = jnp.float32
    rows, width = out_sum.shape
    part, head3 = up_rows.shape[0] * up_rows.shape[2], qkv_rows.shape[0] * qkv_rows.shape[2]
    vectors = [rows, rows, 3 * rows, rows, rows, rows, part // width * rows, rows]
    big = [
        (hidden.shape, hidden.dtype),
        (hidden.shape, f32),
        ((rows, head3), f32),
        ((rows, width), f32),
        ((rows, part), f32),
        ((rows, part), f32),
    ]
    operands = (qkv_rows, up_rows, down_rows, out_sum, out_rows, hid_rows, hidden, cotangent)
    anywhere, held = pl.BlockSpec(memory_space=pl.ANY), pl.BlockSpec(memory_space=pltpu.VMEM)
    return pl.pallas_call(
        finish_kernel,
        out_shape=[jax.ShapeDtypeStruct((n,), f32) for n in vectors]
        + [jax.ShapeDtypeStruct(*shape) for shape in big],
        in_specs=[anywhere] * len(operands) + [held, held],
        out_specs=[held] * len(vectors) + [anywhere] * len(big),
        scratch_shapes=[pltpu.VMEM(o.shape, o.dtype) for o in operands]
        + [pltpu.VMEM(*shape) for shape in big]
        + [pltpu.SemaphoreType.DMA((8,)), pltpu.SemaphoreType.DMA((8,))],
        compiler_params=pltpu.CompilerParams(vmem_limit_bytes=VMEM_BYTES),
        name="finish_all",
    )(*operands, small, vec)


def split_body(
    hidden,
    cotangent,
    pairing,
    ln1_gain,
    ln1_bias,
    qkv_weight,
    qkv_bias,
    out_weight,
    out_bias,
    ln2_gain,
    ln2_bias,
    up_weight,
    up_bias,
    down_weight,
    down_bias,
):
    ctx_count = lax.axis_size("ctx")
    (
        hid_all,
        cot_all,
        w_qkv,
        w_up,
        w_down,
        w_out,
        _,
        attended_low,
        projected_grad,
        norm_two,
        activated,
        slope,
        grad_qkv,
        grad_down,
        grad_out,
        vec,
        stats,
        qkv_sum,
        cot_sum,
    ) = gather_all(
        ctx_count,
        hidden,
        cotangent,
        (ln1_gain, ln1_bias, ln2_gain, ln2_bias, out_bias, down_bias, qkv_bias, up_bias),
        qkv_weight,
        up_weight,
        down_weight,
        out_weight,
        pairing,
    )
    small_sum, qkv_rows, up_rows, down_rows, out_sum, out_rows, hid_rows = scatter_all(
        ctx_count,
        hidden.shape[0],
        (
            hid_all,
            cot_all,
            w_qkv,
            w_up,
            w_down,
            w_out,
            attended_low,
            projected_grad,
            norm_two,
            activated,
            slope,
            stats,
            vec,
            qkv_sum,
            cot_sum,
            grad_qkv,
            grad_down,
            grad_out,
        ),
    )
    (
        grad_ln1_gain,
        grad_ln1_bias,
        grad_qkv_bias,
        grad_out_bias,
        grad_ln2_gain,
        grad_ln2_bias,
        grad_up_bias,
        grad_down_bias,
        output,
        grad_hidden,
        grad_qkv_weight,
        grad_out_weight,
        grad_up_weight,
        grad_down_weight,
    ) = finish_all(
        qkv_rows, up_rows, down_rows, out_sum, out_rows, hid_rows, hidden, cotangent, small_sum, vec
    )
    return (
        output,
        grad_hidden,
        grad_ln1_gain,
        grad_ln1_bias,
        grad_qkv_weight,
        grad_qkv_bias,
        grad_out_weight,
        grad_out_bias,
        grad_ln2_gain,
        grad_ln2_bias,
        grad_up_weight,
        grad_up_bias,
        grad_down_weight,
        grad_down_bias,
    )


def solution(mesh):
    body = split_body if split_fits(mesh) else general_body
    return jax.shard_map(
        body,
        mesh=mesh,
        in_specs=(
            P("ctx", "fsdp", None),
            P("ctx", "fsdp", None),
            P(),
            P(("ctx", "fsdp")),
            P(("ctx", "fsdp")),
            P(("ctx", "fsdp"), None),
            P(("ctx", "fsdp")),
            P(("ctx", "fsdp"), None),
            P(("ctx", "fsdp")),
            P(("ctx", "fsdp")),
            P(("ctx", "fsdp")),
            P(("ctx", "fsdp"), None),
            P(("ctx", "fsdp")),
            P(("ctx", "fsdp"), None),
            P(("ctx", "fsdp")),
        ),
        out_specs=(
            P("ctx", "fsdp", None),
            P("ctx", "fsdp", None),
            P(("ctx", "fsdp")),
            P(("ctx", "fsdp")),
            P(("ctx", "fsdp"), None),
            P(("ctx", "fsdp")),
            P(("ctx", "fsdp"), None),
            P(("ctx", "fsdp")),
            P(("ctx", "fsdp")),
            P(("ctx", "fsdp")),
            P(("ctx", "fsdp"), None),
            P(("ctx", "fsdp")),
            P(("ctx", "fsdp"), None),
            P(("ctx", "fsdp")),
        ),
        check_vma=False,
    )
```

```python
import functools

import jax
import jax.numpy as jnp
from jax import lax
from jax.experimental import pallas as pl
from jax.experimental.pallas import tpu as pltpu
from jax.sharding import PartitionSpec as P

HEAD = 256
ROT = 64


LN_EPSILON = 1e-05
VERY_LOW = -1e30


def layer_norm(values, ln_gain, ln_shift):
    average = jnp.mean(values, axis=-1, keepdims=True)
    centered = values - average
    spread = jnp.mean(centered * centered, axis=-1, keepdims=True)
    return centered * lax.rsqrt(spread + LN_EPSILON) * ln_gain + ln_shift


def gelu_exact(values):
    return jax.nn.gelu(values, approximate=False)


def rotate(values, positions):
    half_rot = ROT // 2
    frequency = 1.0 / 10000.0 ** (jnp.arange(half_rot).astype(values.dtype) * 2.0 / ROT)
    angles = positions.astype(values.dtype)[:, None] * frequency[None, :]
    shape_out = (angles.shape[0],) + (1,) * (values.ndim - 2) + (ROT,)
    cosine = jnp.concatenate([jnp.cos(angles), jnp.cos(angles)], axis=-1).reshape(shape_out)
    sine_part = jnp.concatenate([jnp.sin(angles), jnp.sin(angles)], axis=-1).reshape(shape_out)
    rot_part = values[..., :ROT]
    turned = jnp.concatenate([-rot_part[..., half_rot:], rot_part[..., :half_rot]], axis=-1)
    return jnp.concatenate([rot_part * cosine + turned * sine_part, values[..., ROT:]], axis=-1)


def row_positions(pairing, first_row, row_count, block_rows, ctx_count):
    row_ids = first_row + jnp.arange(row_count, dtype=jnp.int32)
    device_ids = row_ids // (2 * block_rows)
    within = row_ids % (2 * block_rows)
    matches = device_ids[:, None] == jnp.arange(ctx_count, dtype=jnp.int32)[None, :]
    owned_block = jnp.sum(jnp.where(matches, pairing[None, :], 0), axis=1)
    blocks = jnp.where(within < block_rows, owned_block, 2 * ctx_count - 1 - owned_block)
    return blocks * block_rows + within % block_rows


def heads_view(values, row_total, seq_count):
    return values.reshape(row_total, seq_count, -1, HEAD)


def contract_rows(left, right):
    return lax.dot_general(
        left, right, (((0,), (0,)), ((), ())), preferred_element_type=jnp.float32
    )


def contract_cols(left, right):
    return lax.dot_general(
        left, right, (((1,), (1,)), ((), ())), preferred_element_type=jnp.float32
    )


def pair_grads(
    query_rows, grad_rows, log_rows, delta_rows, query_pos, key_heads, value_heads, key_pos, scaling
):
    scores = (
        jnp.einsum("qshd,kshd->shqk", query_rows, key_heads, preferred_element_type=jnp.float32)
        * scaling
    )
    allowed = key_pos[None, None, None, :] <= query_pos[None, None, :, None]
    probabilities = jnp.where(allowed, jnp.exp(scores - log_rows[..., None]), 0.0)
    prob_grad = jnp.einsum(
        "qshd,kshd->shqk", grad_rows, value_heads, preferred_element_type=jnp.float32
    )
    score_grad = (probabilities * (prob_grad - delta_rows[..., None])).astype(jnp.bfloat16)
    return (score_grad, probabilities.astype(jnp.bfloat16))


def general_body(
    hidden,
    cotangent,
    pairing,
    ln1_gain,
    ln1_bias,
    qkv_weight,
    qkv_bias,
    out_weight,
    out_bias,
    ln2_gain,
    ln2_bias,
    up_weight,
    up_bias,
    down_weight,
    down_bias,
):
    local_rows, seq_count, model_width = hidden.shape
    block_rows = local_rows // 2
    ctx_count = lax.axis_size("ctx")
    head_count = model_width // HEAD
    scaling = HEAD ** (-0.5)
    tokens = local_rows * seq_count
    total_rows = local_rows * ctx_count
    params = (
        lax.all_gather(ln1_gain, ("ctx", "fsdp"), axis=0, tiled=True),
        lax.all_gather(ln1_bias, ("ctx", "fsdp"), axis=0, tiled=True),
        lax.all_gather(qkv_weight, ("ctx", "fsdp"), axis=0, tiled=True),
        lax.all_gather(qkv_bias, ("ctx", "fsdp"), axis=0, tiled=True),
        lax.all_gather(out_weight, ("ctx", "fsdp"), axis=0, tiled=True),
        lax.all_gather(out_bias, ("ctx", "fsdp"), axis=0, tiled=True),
        lax.all_gather(ln2_gain, ("ctx", "fsdp"), axis=0, tiled=True),
        lax.all_gather(ln2_bias, ("ctx", "fsdp"), axis=0, tiled=True),
        lax.all_gather(up_weight, ("ctx", "fsdp"), axis=0, tiled=True),
        lax.all_gather(up_bias, ("ctx", "fsdp"), axis=0, tiled=True),
        lax.all_gather(down_weight, ("ctx", "fsdp"), axis=0, tiled=True),
        lax.all_gather(down_bias, ("ctx", "fsdp"), axis=0, tiled=True),
    )
    (
        gain_one,
        shift_one,
        w_qkv,
        b_qkv,
        w_out,
        b_out,
        gain_two,
        shift_two,
        w_up,
        b_up,
        w_down,
        b_down,
    ) = params
    ff_width = w_up.shape[1]
    hidden_f = hidden.astype(jnp.float32).reshape(tokens, model_width)
    own_pos = row_positions(
        pairing, lax.axis_index("ctx") * local_rows, local_rows, block_rows, ctx_count
    )
    normed_one, ln_one_pull = jax.vjp(
        layer_norm, hidden_f, gain_one.astype(jnp.float32), shift_one.astype(jnp.float32)
    )
    normed_one_low = normed_one.astype(jnp.bfloat16)
    projected = jnp.dot(normed_one_low, w_qkv, preferred_element_type=jnp.float32) + b_qkv.astype(
        jnp.float32
    )
    query_f, rotation_pull = jax.vjp(
        lambda values: rotate(values, own_pos),
        heads_view(projected[:, :model_width], local_rows, seq_count),
    )
    query_b = query_f.astype(jnp.bfloat16)
    key_b = (
        rotate(
            heads_view(projected[:, model_width : 2 * model_width], local_rows, seq_count), own_pos
        )
        .astype(jnp.bfloat16)
        .reshape(local_rows, seq_count, model_width)
    )
    value_b = (
        projected[:, 2 * model_width :]
        .astype(jnp.bfloat16)
        .reshape(local_rows, seq_count, model_width)
    )
    running_max = jnp.full((seq_count, head_count, local_rows), VERY_LOW, jnp.float32)
    key_piece = lax.all_gather(key_b, "ctx", axis=0, tiled=True)
    value_piece = lax.all_gather(value_b, "ctx", axis=0, tiled=True)
    row_total = key_piece.shape[0]
    key_pos = row_positions(pairing, jnp.int32(0), row_total, block_rows, ctx_count)
    scores = (
        jnp.einsum(
            "qshd,kshd->shqk",
            query_b,
            heads_view(key_piece, row_total, seq_count),
            preferred_element_type=jnp.float32,
        )
        * scaling
    )
    allowed = key_pos[None, None, None, :] <= own_pos[None, None, :, None]
    piece_max = jnp.max(jnp.where(allowed, scores, VERY_LOW), axis=-1)
    new_max = jnp.maximum(running_max, piece_max)
    weights = jnp.where(allowed, jnp.exp(scores - new_max[..., None]), 0.0)
    new_total = jnp.sum(weights, axis=-1)
    mixture = jnp.einsum(
        "shqk,kshd->qshd",
        weights.astype(jnp.bfloat16),
        heads_view(value_piece, row_total, seq_count),
        preferred_element_type=jnp.float32,
    )
    log_total = new_max + jnp.log(new_total)
    attended = mixture / jnp.transpose(new_total, (2, 0, 1))[..., None]
    attended_low = attended.astype(jnp.bfloat16).reshape(tokens, model_width)
    branch_attn = jnp.dot(attended_low, w_out, preferred_element_type=jnp.float32) + b_out.astype(
        jnp.float32
    )
    normed_two, ln_two_pull = jax.vjp(
        layer_norm, hidden_f, gain_two.astype(jnp.float32), shift_two.astype(jnp.float32)
    )
    normed_two_low = normed_two.astype(jnp.bfloat16)
    inner_act = jnp.dot(normed_two_low, w_up, preferred_element_type=jnp.float32) + b_up.astype(
        jnp.float32
    )
    activated_f, gelu_pull = jax.vjp(gelu_exact, inner_act)
    activated = activated_f.astype(jnp.bfloat16)
    branch_mlp = contract_cols(activated, w_down) + b_down.astype(jnp.float32)
    output = (
        (hidden_f + branch_attn + branch_mlp)
        .astype(jnp.bfloat16)
        .reshape(local_rows, seq_count, model_width)
    )
    back_qkv, back_out, back_up, back_down = (
        lax.all_gather(qkv_weight, ("ctx", "fsdp"), axis=0, tiled=True),
        lax.all_gather(out_weight, ("ctx", "fsdp"), axis=0, tiled=True),
        lax.all_gather(up_weight, ("ctx", "fsdp"), axis=0, tiled=True),
        lax.all_gather(down_weight, ("ctx", "fsdp"), axis=0, tiled=True),
    )
    grad_out = cotangent.reshape(tokens, model_width)
    grad_f = grad_out.astype(jnp.float32)
    bias_sum = jnp.sum(grad_f, axis=0)
    up_grad = jnp.dot(grad_out, back_down, preferred_element_type=jnp.float32)
    inner_grad = gelu_pull(up_grad)[0].astype(jnp.bfloat16)
    norm_two_grad = contract_cols(inner_grad, back_up)
    dx_two, dgain_two, dshift_two = ln_two_pull(norm_two_grad)
    up_bias_sum = jnp.sum(inner_grad, axis=0, dtype=jnp.float32)
    mlp_small = jnp.concatenate(
        [
            up_bias_sum.reshape(model_width, -1),
            jnp.stack([bias_sum, dgain_two, dshift_two], axis=1),
        ],
        axis=1,
    )
    up_w_sum, down_w_sum, mlp_small_sum = (
        lax.psum_scatter(
            contract_rows(normed_two_low, inner_grad),
            ("ctx", "fsdp"),
            scatter_dimension=0,
            tiled=True,
        ),
        lax.psum_scatter(
            contract_rows(grad_out, activated), ("ctx", "fsdp"), scatter_dimension=0, tiled=True
        ),
        lax.psum_scatter(mlp_small, ("ctx", "fsdp"), scatter_dimension=0, tiled=True),
    )
    ratio = ff_width // model_width
    attn_grad = contract_cols(grad_out, back_out).astype(jnp.bfloat16)
    out_w_grad = contract_rows(attended_low, grad_out)
    grad_heads = heads_view(attn_grad, local_rows, seq_count)
    row_delta = jnp.einsum("qshd,qshd->shq", grad_heads.astype(jnp.float32), attended)
    keys_all, values_all = (
        lax.all_gather(key_b, "ctx", axis=0, tiled=True),
        lax.all_gather(value_b, "ctx", axis=0, tiled=True),
    )
    key_block = 512
    block_count = total_rows // key_block
    starts = jnp.arange(block_count, dtype=jnp.int32) * key_block

    def query_step(query_grad, inputs):
        key_piece, value_piece, offset = inputs
        key_pos = row_positions(pairing, offset, key_block, block_rows, ctx_count)
        key_heads = heads_view(key_piece, key_block, seq_count)
        value_heads = heads_view(value_piece, key_block, seq_count)
        score_grad, unused = pair_grads(
            query_b,
            grad_heads,
            log_total,
            row_delta,
            own_pos,
            key_heads,
            value_heads,
            key_pos,
            scaling,
        )
        query_grad = (
            query_grad
            + jnp.einsum(
                "shqk,kshd->qshd", score_grad, key_heads, preferred_element_type=jnp.float32
            )
            * scaling
        )
        return (query_grad, None)

    query_grad, unused_out = lax.scan(
        query_step,
        jnp.zeros((local_rows, seq_count, head_count, HEAD), jnp.float32),
        (
            keys_all.reshape(block_count, key_block, seq_count, model_width),
            values_all.reshape(block_count, key_block, seq_count, model_width),
            starts,
        ),
    )
    queries_all, grads_all = (
        lax.all_gather(query_b, "ctx", axis=0, tiled=True),
        lax.all_gather(grad_heads, "ctx", axis=0, tiled=True),
    )
    logs_all, deltas_all = (
        lax.all_gather(log_total, "ctx", axis=2, tiled=True),
        lax.all_gather(row_delta, "ctx", axis=2, tiled=True),
    )
    own_keys = heads_view(key_b, local_rows, seq_count)
    own_values = heads_view(value_b, local_rows, seq_count)

    def key_step(carry, inputs):
        key_acc, value_acc = carry
        query_piece, grad_piece, log_piece, delta_piece, offset = inputs
        query_pos = row_positions(pairing, offset, key_block, block_rows, ctx_count)
        score_grad, probs_low = pair_grads(
            query_piece,
            grad_piece,
            log_piece,
            delta_piece,
            query_pos,
            own_keys,
            own_values,
            own_pos,
            scaling,
        )
        key_acc = (
            key_acc
            + jnp.einsum(
                "shqk,qshd->kshd", score_grad, query_piece, preferred_element_type=jnp.float32
            )
            * scaling
        )
        value_acc = value_acc + jnp.einsum(
            "shqk,qshd->kshd", probs_low, grad_piece, preferred_element_type=jnp.float32
        )
        return ((key_acc, value_acc), None)

    empty_acc = jnp.zeros((local_rows, seq_count, head_count, HEAD), jnp.float32)
    log_blocks = jnp.moveaxis(logs_all.reshape(seq_count, head_count, block_count, key_block), 2, 0)
    delta_blocks = jnp.moveaxis(
        deltas_all.reshape(seq_count, head_count, block_count, key_block), 2, 0
    )
    (key_sum, value_sum), unused_keys = lax.scan(
        key_step,
        (empty_acc, empty_acc),
        (
            queries_all.reshape(block_count, key_block, seq_count, head_count, HEAD),
            grads_all.reshape(block_count, key_block, seq_count, head_count, HEAD),
            log_blocks,
            delta_blocks,
            starts,
        ),
    )
    key_owned = key_sum.reshape(local_rows, seq_count, model_width)
    value_owned = value_sum.reshape(local_rows, seq_count, model_width)
    query_pre = rotation_pull(query_grad)[0].reshape(tokens, model_width)
    key_pre = rotation_pull(heads_view(key_owned, local_rows, seq_count))[0].reshape(
        tokens, model_width
    )
    value_pre = value_owned.reshape(tokens, model_width)
    projected_grad = jnp.concatenate([query_pre, key_pre, value_pre], axis=1).astype(jnp.bfloat16)
    norm_one_grad = contract_cols(projected_grad, back_qkv)
    dx_one, dgain_one, dshift_one = ln_one_pull(norm_one_grad)
    qkv_bias_sum = jnp.sum(projected_grad, axis=0, dtype=jnp.float32)
    attn_small = jnp.concatenate(
        [
            qkv_bias_sum.reshape(model_width, -1),
            jnp.stack([bias_sum, dgain_one, dshift_one], axis=1),
        ],
        axis=1,
    )
    qkv_w_sum, out_w_sum, attn_small_sum = (
        lax.psum_scatter(
            contract_rows(normed_one_low, projected_grad),
            ("ctx", "fsdp"),
            scatter_dimension=0,
            tiled=True,
        ),
        lax.psum_scatter(out_w_grad, ("ctx", "fsdp"), scatter_dimension=0, tiled=True),
        lax.psum_scatter(attn_small, ("ctx", "fsdp"), scatter_dimension=0, tiled=True),
    )
    grad_hidden = (grad_f + dx_one + dx_two).reshape(local_rows, seq_count, model_width)
    return (
        output,
        grad_hidden,
        attn_small_sum[:, 4],
        attn_small_sum[:, 5],
        qkv_w_sum,
        attn_small_sum[:, :3].reshape(-1),
        out_w_sum,
        attn_small_sum[:, 3],
        mlp_small_sum[:, ratio + 1],
        mlp_small_sum[:, ratio + 2],
        up_w_sum,
        mlp_small_sum[:, :ratio].reshape(-1),
        down_w_sum,
        mlp_small_sum[:, ratio],
    )


MESH = pl.DeviceIdType.MESH
CORES = 2
LINE_Y = 2
VMEM_BYTES = 60 * 2**20


def split_fits(mesh):
    return mesh.shape["ctx"] == 16 and mesh.shape["fsdp"] == 2


class Place:
    def __init__(self, ctx_count):
        self.chips = ctx_count // CORES
        self.line = self.chips // LINE_Y
        index = lax.axis_index("ctx")
        self.c = index % CORES
        self.chip = index // CORES
        self.y = self.chip % LINE_Y
        self.z = self.chip // LINE_Y
        self.x = lax.axis_index("fsdp")

    def at(self, z, y, c, x):
        return ((z * LINE_Y + y) * CORES + c, x)

    def other_core(self):
        return self.at(self.z, self.y, 1 - self.c, self.x)

    def other_plane(self):
        return self.at(self.z, self.y, self.c, 1 - self.x)

    def other_y(self):
        return self.at(self.z, 1 - self.y, self.c, self.x)

    def plane_offsets(self):
        return [(dz, dy) for dz in range(self.line) for dy in range(LINE_Y) if dz or dy]

    def shifted(self, dz, dy):
        return (self.z + dz) % self.line, (self.y + dy) % LINE_Y


class Copies:
    def __init__(self, send, recv, local):
        self.send, self.recv, self.local = send, recv, local
        self.remotes, self.locals = 0, 0

    def reserve(self, count):
        self.remotes += count
        return self.remotes - count

    def remote(self, src, dst, device):
        return self.remote_at(self.reserve(1), src, dst, device)

    def remote_at(self, i, src, dst, device):
        return pltpu.make_async_remote_copy(
            src_ref=src,
            dst_ref=dst,
            send_sem=self.send.at[i],
            recv_sem=self.recv.at[i],
            device_id=device,
            device_id_type=MESH,
        )

    def inside(self, src, dst):
        i = self.locals
        self.locals += 1
        return pltpu.make_async_copy(src, dst, self.local.at[i])


def greet(place):
    barrier = pltpu.get_barrier_semaphore()
    partners = [place.other_core(), place.other_plane()]
    for dz, dy in place.plane_offsets():
        z, y = place.shifted(dz, dy)
        partners.append(place.at(z, y, place.c, place.x))
    for partner in partners:
        pl.semaphore_signal(barrier, inc=1, device_id=partner, device_id_type=MESH)
    return lambda: pl.semaphore_wait(barrier, len(partners))


TOKEN_CHUNKS = 2


class TokenGather:
    def __init__(self, place, copies, own, whole):
        self.place, self.copies, self.whole = place, copies, whole
        c, chip, z, y = place.c, place.chip, place.z, place.y
        rows = own.shape[1]
        block = whole.at[tile(chip * CORES + c, rows)]
        self.first = copies.remote(own.at[1 - c], block, place.other_core())
        self.mine = copies.inside(own.at[c], block)
        self.size = CORES * rows // TOKEN_CHUNKS
        self.last = last = place.line - 1
        up = place.at(jnp.minimum(z + 1, last), y, c, place.x)
        down = place.at(jnp.maximum(z - 1, 0), y, c, place.x)
        over = place.other_y()
        chunks = range(TOKEN_CHUNKS)
        self.ups = [[self.copy(z - j, ch, up) for ch in chunks] for j in range(last)]
        self.downs = [[self.copy(z + j, ch, down) for ch in chunks] for j in range(last)]
        self.over_own = [self.copy(z, ch, over) for ch in chunks]
        self.over_ups = [[self.copy(z - 1 - j, ch, over) for ch in chunks] for j in range(last)]
        self.over_downs = [[self.copy(z + 1 + j, ch, over) for ch in chunks] for j in range(last)]

    def copy(self, z, ch, device):
        chip = jnp.clip(z, 0, self.last) * LINE_Y + self.place.y
        chunk = self.whole.at[tile(chip * TOKEN_CHUNKS + ch, self.size)]
        return self.copies.remote(chunk, chunk, device)

    def start(self):
        self.mine.start()
        self.first.start()

    def spread(self, ch):
        if ch == 0:
            self.mine.wait()
            self.first.wait_recv()
        z = self.place.z
        pl.when(z < self.last)(lambda: self.ups[0][ch].start())
        pl.when(z > 0)(lambda: self.downs[0][ch].start())
        self.over_own[ch].start()

    def step(self, j, ch):
        z, last = self.place.z, self.last

        @pl.when(z - 1 - j >= 0)
        def _():
            self.ups[j][ch].wait_recv()
            if j + 1 < last:
                pl.when(z < last)(lambda: self.ups[j + 1][ch].start())
            self.over_ups[j][ch].start()

        @pl.when(z + 1 + j <= last)
        def _():
            self.downs[j][ch].wait_recv()
            if j + 1 < last:
                pl.when(z > 0)(lambda: self.downs[j + 1][ch].start())
            self.over_downs[j][ch].start()

    def finish(self):
        z, last = self.place.z, self.last
        for ch in range(TOKEN_CHUNKS):
            self.over_own[ch].wait_recv()
            for j in range(last):
                pl.when(z - 1 - j >= 0)(lambda: self.over_ups[j][ch].wait_recv())
                pl.when(z + 1 + j <= last)(lambda: self.over_downs[j][ch].wait_recv())

    def drain(self):
        z, last = self.place.z, self.last
        self.first.wait_send()
        for ch in range(TOKEN_CHUNKS):
            self.over_own[ch].wait_send()
            for j in range(last):
                pl.when((z - j >= 0) & (z < last))(lambda: self.ups[j][ch].wait_send())
                pl.when((z + j <= last) & (z > 0))(lambda: self.downs[j][ch].wait_send())
                pl.when(z - 1 - j >= 0)(lambda: self.over_ups[j][ch].wait_send())
                pl.when(z + 1 + j <= last)(lambda: self.over_downs[j][ch].wait_send())


class WeightGather:
    def __init__(self, place, copies, pieces, whole, columns=slice(None)):
        self.place = place
        group = 2 * place.c + place.x
        self.by_chip = []
        for dz, dy in place.plane_offsets():
            z, y = place.shifted(dz, dy)
            device = place.at(z, y, place.c, place.x)
            self.by_chip.append(
                [copies.remote(src, dst, device) for src, dst in pieces(z * LINE_Y + y, place.chip, group)]
            )
        self.kept = [copies.inside(src, dst) for src, dst in pieces(place.chip, place.chip, group)]
        mine = whole.at[:, group, :, columns]
        self.across = copies.remote(mine, mine, place.other_plane())
        pair = whole.at[:, pl.ds(2 * place.c, 2), :, columns]
        self.swap = copies.remote(pair, pair, place.other_core())

    def send(self, i):
        for copy in self.by_chip[i] + (self.kept if i == 0 else []):
            copy.start()

    def scatter(self):
        for i in range(len(self.by_chip)):
            self.send(i)

    def cross(self):
        for copy in self.kept:
            copy.wait()
        for copies in self.by_chip:
            for copy in copies:
                copy.wait_recv()
        self.across.start()

    def share(self):
        self.across.wait_recv()
        self.swap.start()

    def finish(self):
        self.swap.wait_recv()

    def drain(self):
        for copy in sum(self.by_chip, []) + [self.across, self.swap]:
            copy.wait_send()


NORM_PARTS = 4
GATHER_ORDER = (
    "qkv 2",
    "hid spread 0",
    "qkv 4",
    "up b 6",
    "down a 0",
    "qkv 0",
    "cot spread 0",
    "down b 0",
    "hid 0 0",
    "hid spread 1",
    "hid 1 0",
    "up a 0",
    "hid 0 1",
    "qkv 1",
    "qkv 3",
    "tables",
    "small cross",
    "qkv 5",
    "up a 6",
    "up b 2",
    "qkv 6",
    "hid 1 1",
    "up a 2",
    "up a 4",
    "up b 5",
    "small share",
    "up b 4",
    "up a 5",
    "up b 3",
    "down b 6",
    "down a 5",
    "out start",
    "down b 1",
    "up a 1",
    "down b 5",
    "qkv cross",
    "hid 2 0",
    "small done",
    "up b 0",
    "hid 2 1",
    "up b 1",
    "cot spread 1",
    "hid done",
    "cot 0 0",
    "cot 0 1",
    "up b cross",
    "norm",
    "qkv share",
    "down b 4",
    "up a 3",
    "norm",
    "cot 1 0",
    "norm",
    "up a cross",
    "down b 2",
    "norm",
    "norm done",
    "cot 1 1",
    "up b share",
    "project",
    "down b 3",
    "cot 2 0",
    "down a 1",
    "attend",
    "down a 2",
    "up a share",
    "down b cross",
    "out share",
    "down a 6",
    "down a 3",
    "cot 2 1",
    "down a 4",
    "inner",
    "down a cross",
    "cot done",
    "down grads",
    "attended grads",
    "down b share",
    "down a share",
    "attention back",
)


def nn(left, right):
    return lax.dot_general(left, right, (((1,), (0,)), ((), ())), preferred_element_type=jnp.float32)


def tile(i, size):
    return pl.ds(pl.multiple_of(i * size, size), size)


def flat_rows(values):
    return values.reshape(-1, values.shape[-1])


GAIN_ONE, SHIFT_ONE, GAIN_TWO, SHIFT_TWO, OUT_BIAS, DOWN_BIAS, QKV_BIAS, UP_BIAS, SMALL_ROWS = (
    0,
    1,
    2,
    3,
    4,
    5,
    6,
    9,
    16,
)
LANES = 128


def lanes_of(shape):
    return lax.broadcasted_iota(jnp.int32, shape, len(shape) - 1)


def pack_parameters(vectors, tile_ref):
    half = LANES // 2
    ln1_gain, ln1_bias, ln2_gain, ln2_bias, out_bias, down_bias, qkv_bias, up_bias = [
        ref[...].astype(jnp.float32).reshape(1, -1) for ref in vectors
    ]
    tile_ref[...] = jnp.zeros_like(tile_ref)
    for row, values in (
        (GAIN_ONE, ln1_gain),
        (SHIFT_ONE, ln1_bias),
        (GAIN_TWO, ln2_gain),
        (SHIFT_TWO, ln2_bias),
        (OUT_BIAS, out_bias),
        (DOWN_BIAS, down_bias),
    ):
        tile_ref[row : row + 1, :half] = values
        tile_ref[row : row + 1, half:] = values
    tile_ref[QKV_BIAS : QKV_BIAS + 1, :] = qkv_bias[:, :LANES]
    tile_ref[QKV_BIAS + 1 : QKV_BIAS + 2, :half] = qkv_bias[:, LANES:]
    tile_ref[QKV_BIAS + 1 : QKV_BIAS + 2, half:] = qkv_bias[:, :half]
    tile_ref[QKV_BIAS + 2 : QKV_BIAS + 3, :] = qkv_bias[:, half:]
    tile_ref[UP_BIAS : UP_BIAS + 1, :] = up_bias[:, :LANES]
    tile_ref[UP_BIAS + 1 : UP_BIAS + 2, :] = up_bias[:, LANES:]


def position_tables(ctx_count, pairing, cosine, sine, key_pos):
    block_rows = cosine.shape[0] // (2 * ctx_count)
    half_rot = ROT // 2
    lane = lanes_of((block_rows, LANES))
    power = (lane % half_rot).astype(jnp.float32) * (2.0 / ROT)
    frequency = jnp.exp(power * -9.210340371976184)
    row = lax.broadcasted_iota(jnp.int32, (block_rows, LANES), 0)

    @pl.loop(0, ctx_count)
    def _(device):
        owned = pairing[device]
        for late in range(2):
            block = 2 * ctx_count - 1 - owned if late else owned
            where = (block * block_rows + row).astype(jnp.float32)
            angles = where * frequency
            at = tile(2 * device + late, block_rows)
            cosine[at, :] = jnp.where(lane < ROT, jnp.cos(angles), 1.0)
            sin = jnp.sin(angles)
            sine[at, :] = jnp.where(lane < half_rot, -sin, jnp.where(lane < ROT, sin, where))

    lane = lanes_of((8, LANES))
    per = LANES // (2 * block_rows)
    for first in range(0, ctx_count, per):
        block = jnp.zeros((8, LANES), jnp.int32)
        for device in range(per):
            owned = pairing[first + device]
            for late in range(2):
                value = 2 * ctx_count - 1 - owned if late else owned
                block = jnp.where(lane // block_rows == 2 * device + late, value, block)
        at = first * 2 * block_rows
        key_pos[:, at : at + LANES] = (block * block_rows + lane % block_rows).astype(jnp.float32)


def split_sequences(rows, own):
    for i in range(rows.shape[1]):
        own[i] = rows[:, i, :]


def assemble_small(place, small, vec, qkv_rows, qkv_bias, up_bias):
    chips, groups = small.shape[:2]
    low = lanes_of((1, LANES)) < LANES // 2
    for pair in range(chips * groups // 2):
        chip, group = pair // (groups // 2), pair % (groups // 2) * 2
        for row in range(6):
            a = small[chip, group, row : row + 1, :]
            b = small[chip, group + 1, row : row + 1, :]
            vec[row : row + 1, pair * LANES : (pair + 1) * LANES] = jnp.where(low, a, b)
        qkv_rows[3 * pair : 3 * pair + 1, :] = small[chip, group, QKV_BIAS : QKV_BIAS + 1, :]
        a = small[chip, group, QKV_BIAS + 1 : QKV_BIAS + 2, :]
        b = small[chip, group + 1, QKV_BIAS + 1 : QKV_BIAS + 2, :]
        qkv_rows[3 * pair + 1 : 3 * pair + 2, :] = jnp.where(low, a, b)
        qkv_rows[3 * pair + 2 : 3 * pair + 3, :] = small[chip, group + 1, QKV_BIAS + 2 : QKV_BIAS + 3, :]
    third = qkv_rows.shape[0] // 3
    per_head = HEAD // LANES
    for k in range(3):
        for u in range(per_head):
            at = (k * per_head + u) * LANES
            qkv_bias[0:1, at : at + LANES] = qkv_rows[pl.ds(k * third + place.chip * per_head + u, 1), :]
    for group in range(groups):
        for u in range(2):
            at = (group * 2 + u) * LANES
            row = UP_BIAS + u
            up_bias[0:1, at : at + LANES] = small[pl.ds(place.chip, 1), group, row : row + 1, :].reshape(1, LANES)


def norm_rows(start, count, hid, vec, norm_one, norm_two, stats):
    step = 16

    @pl.loop(0, count // step)
    def _(i):
        at = pl.ds(pl.multiple_of(start + i * step, step), step)
        x = hid[at, :].astype(jnp.float32)
        average = jnp.mean(x, axis=1, keepdims=True)
        centered = x - average
        scale = lax.rsqrt(jnp.mean(centered * centered, axis=1, keepdims=True) + LN_EPSILON)
        stats[at, 0:1] = average
        stats[at, 1:2] = scale
        xhat = centered * scale
        norm_one[at, :] = (xhat * vec[0:1, :] + vec[1:2, :]).astype(jnp.bfloat16)
        norm_two[at, :] = (xhat * vec[2:3, :] + vec[3:4, :]).astype(jnp.bfloat16)


def turned_half(values):
    half_rot = ROT // 2
    lane = lanes_of(values.shape)
    width = values.shape[-1]
    return jnp.where(
        lane < half_rot,
        pltpu.roll(values, width - half_rot, 1),
        jnp.where(lane < ROT, pltpu.roll(values, half_rot, 1), 0.0),
    )


def project(norm_one, weight, bias, cosine, sine, query, key, value):
    step = 256

    @pl.loop(0, norm_one.shape[0] // step)
    def _(i):
        at = tile(i, step)
        both = nn(norm_one[at, :], flat_rows(weight[...])) + bias[0:1, :]
        cos, sin = cosine[at, :], sine[at, :]
        for k, target in enumerate((query, key)):
            first = both[:, k * HEAD : k * HEAD + LANES]
            target[at, 0:LANES] = (first * cos + turned_half(first) * sin).astype(jnp.bfloat16)
            target[at, LANES:HEAD] = both[:, k * HEAD + LANES : (k + 1) * HEAD].astype(jnp.bfloat16)
        value[at, :] = both[:, 2 * HEAD :].astype(jnp.bfloat16)


def attend(query, key, value, sine, key_pos, attended, attended_low, probs, probs_low):
    step = 256

    @pl.loop(0, query.shape[0] // step)
    def _(i):
        at = tile(i, step)
        scores = contract_cols(query[at, :], key[...]) * HEAD**-0.5
        allowed = key_pos[0:1, :] <= sine[at, ROT : ROT + 1]
        scores = jnp.where(allowed, scores, VERY_LOW)
        highest = jnp.max(scores, axis=1, keepdims=True)
        weights = jnp.where(allowed, jnp.exp(scores - highest), 0.0)
        weights = weights / jnp.sum(weights, axis=1, keepdims=True)
        low = weights.astype(jnp.bfloat16)
        probs[at, :] = weights
        probs_low[at, :] = low
        total = nn(low, value[...])
        attended[at, :] = total
        attended_low[at, :] = total.astype(jnp.bfloat16)


def feed_inner(norm_two, weight, bias, activated, slope):
    step = 128

    @pl.loop(0, norm_two.shape[0] // step)
    def _(i):
        at = tile(i, step)
        inner = nn(norm_two[at, :], flat_rows(weight[...])) + bias[0:1, :]
        normal = 0.5 + 0.5 * lax.erf(inner * 0.5**0.5)
        activated[at, :] = (inner * normal).astype(jnp.bfloat16)
        density = (2.0 * jnp.pi) ** -0.5 * jnp.exp(-0.5 * inner * inner)
        slope[at, :] = normal + inner * density


def attended_grads(cot, weight, attended_grad):
    step = 256

    @pl.loop(0, cot.shape[0] // step)
    def _(i):
        at = tile(i, step)
        attended_grad[at, :] = contract_cols(cot[at, :], flat_rows(weight[...])).astype(jnp.bfloat16)


def attention_grads(
    query, key, value, cosine, sine, attended, attended_grad, probs, probs_low, score_grad, projected_grad
):
    step = 256
    scaling = HEAD**-0.5

    def put(at, k, grad):
        first = grad[:, 0:LANES]
        back = first * cosine[at, :] - turned_half(first) * sine[at, :]
        projected_grad[at, k * HEAD : k * HEAD + LANES] = back.astype(jnp.bfloat16)
        projected_grad[at, k * HEAD + LANES : (k + 1) * HEAD] = grad[:, LANES:].astype(jnp.bfloat16)

    @pl.loop(0, query.shape[0] // step)
    def _(i):
        at = tile(i, step)
        own = attended_grad[at, :]
        row_delta = jnp.sum(own.astype(jnp.float32) * attended[at, :], axis=1, keepdims=True)
        grad = (probs[at, :] * (contract_cols(own, value[...]) - row_delta)).astype(jnp.bfloat16)
        score_grad[at, :] = grad
        put(at, 0, nn(grad, key[...]) * scaling)

    @pl.loop(0, query.shape[0] // step)
    def _(i):
        at = tile(i, step)
        put(at, 1, contract_rows(score_grad[:, at], query[...]) * scaling)
        projected_grad[at, 2 * HEAD :] = contract_rows(probs_low[:, at], attended_grad[...]).astype(jnp.bfloat16)


def weight_grads(tokens, grads, result):
    chips, groups, rows = result.shape[:3]
    step = groups * rows

    @pl.loop(0, chips)
    def _(k):
        grad = contract_rows(tokens[:, tile(k, step)], grads[...]).astype(jnp.bfloat16)
        result[k] = grad.reshape(result.shape[1:])


def column_sums(values, result):
    step = 16

    def add(i, total):
        return total + values[tile(i, step), :].astype(jnp.float32)

    total = lax.fori_loop(0, values.shape[0] // step, add, jnp.zeros((step, values.shape[1]), jnp.float32))
    result[0:1, :] = jnp.sum(total, axis=0, keepdims=True)


def gather_kernel(
    ctx_count,
    hid_in,
    cot_in,
    ln1_gain_in,
    ln1_bias_in,
    ln2_gain_in,
    ln2_bias_in,
    out_bias_in,
    down_bias_in,
    qkv_bias_in,
    up_bias_in,
    qkv,
    up,
    down,
    out,
    pairing,
    hid_all,
    cot_all,
    qkv_all,
    up_all,
    down_all,
    out_all,
    small_all,
    attended_low_out,
    projected_grad_out,
    norm_two_out,
    activated_out,
    slope_out,
    norm_one_out,
    down_grad_out,
    vec_out,
    stats_out,
    hid_rows,
    cot_rows,
    hid,
    cot,
    ln1_gain,
    ln1_bias,
    ln2_gain,
    ln2_bias,
    out_bias,
    down_bias,
    qkv_bias_own,
    up_bias_own,
    small,
    hid_v,
    cot_v,
    qkv_v,
    up_v,
    out_v,
    small_v,
    cosine,
    sine,
    key_pos,
    vec,
    qkv_rows,
    qkv_bias,
    up_bias,
    norm_one,
    norm_two,
    stats,
    query,
    key,
    value,
    attended,
    attended_low,
    probs,
    probs_low,
    activated,
    slope,
    attended_grad,
    score_grad,
    projected_grad,
    send,
    recv,
    local,
):
    place = Place(ctx_count)
    copies = Copies(send, recv, local)
    width = out.shape[1]
    head = qkv_all.shape[3] // 3
    part = up_all.shape[3]

    def qkv_pieces(to, row, group):
        return [
            (
                qkv.at[:, pl.ds(pl.multiple_of(k * width + to * head, head), head)],
                qkv_all.at[row, group, :, pl.ds(k * head, head)],
            )
            for k in range(3)
        ]

    half = part // 2

    def half_gather(source, whole, first):
        columns = pl.ds(first, half)

        def pieces(to, row, group):
            given = pl.ds(pl.multiple_of(to * part + first, half), half)
            return [(source.at[:, given], whole.at[row, group, :, columns])]

        return WeightGather(place, copies, pieces, whole, columns)

    hid_g = TokenGather(place, copies, hid, hid_all)
    cot_g = TokenGather(place, copies, cot, cot_all)
    small_g = WeightGather(place, copies, lambda to, row, group: [(small, small_all.at[row, group])], small_all)
    qkv_g = WeightGather(place, copies, qkv_pieces, qkv_all)
    weights = {"qkv": qkv_g}
    for name, source, whole in (("up", up, up_all), ("down", down, down_all)):
        weights[name + " a"] = half_gather(source, whole, 0)
        weights[name + " b"] = half_gather(source, whole, half)
    group = 2 * place.c + place.x
    out_mine = copies.inside(out, out_all.at[group])
    out_across = copies.remote(out, out_all.at[group], place.other_plane())
    out_pair = out_all.at[pl.ds(2 * place.c, 2)]
    out_swap = copies.remote(out_pair, out_pair, place.other_core())
    loads = {
        name: copies.inside(src, dst)
        for name, src, dst in (
            ("hid rows", hid_in, hid_rows),
            ("cot rows", cot_in, cot_rows),
            ("small", small_all, small_v),
            ("hid", hid_all, hid_v),
            ("cot", cot_all, cot_v),
            ("qkv", qkv_all, qkv_v),
            ("up", up_all, up_v),
            ("out", out_all, out_v),
        )
    }
    stores = {
        name: copies.inside(src, dst)
        for name, src, dst in (
            ("vec", vec, vec_out),
            ("stats", stats, stats_out),
            ("attended_low", attended_low, attended_low_out),
            ("norm_two", norm_two, norm_two_out),
            ("activated", activated, activated_out),
            ("slope", slope, slope_out),
            ("projected_grad", projected_grad, projected_grad_out),
            ("norm_one", norm_one, norm_one_out),
            ("down_grad", up_v, down_grad_out),
        )
    }

    def fetch(name):
        loads[name].start()
        loads[name].wait()

    rows = hid_v.shape[0]
    normed = iter(range(NORM_PARTS))

    def norm_next():
        part_rows = rows // NORM_PARTS
        norm_rows(next(normed) * part_rows, part_rows, hid_v, vec, norm_one, norm_two, stats)

    def norm_done():
        stores["norm_one"].start()
        stores["norm_two"].start()
        stores["stats"].start()

    def small_done():
        small_g.finish()
        fetch("small")
        assemble_small(place, small_v, vec, qkv_rows, qkv_bias, up_bias)
        stores["vec"].start()

    def hid_done():
        hid_g.finish()
        fetch("hid")

    def project_all():
        qkv_g.finish()
        fetch("qkv")
        project(norm_one, qkv_v, qkv_bias, cosine, sine, query, key, value)

    def attend_all():
        attend(query, key, value, sine, key_pos, attended, attended_low, probs, probs_low)
        stores["attended_low"].start()

    def inner_all():
        weights["up a"].finish()
        weights["up b"].finish()
        fetch("up")
        feed_inner(norm_two, up_v, up_bias, activated, slope)
        stores["activated"].start()
        stores["slope"].start()

    def out_start():
        out_mine.start()
        out_across.start()

    def out_share():
        out_mine.wait()
        out_across.wait_recv()
        out_swap.start()

    def cot_done():
        cot_g.finish()
        loads["cot"].start()
        out_swap.wait_recv()
        fetch("out")
        loads["cot"].wait()

    def out_grads():
        attended_grads(cot_v, out_v, attended_grad)

    def down_grads():
        weight_grads(cot_v, activated, up_v)
        stores["down_grad"].start()

    def attention_back():
        attention_grads(
            query, key, value, cosine, sine, attended, attended_grad, probs, probs_low, score_grad, projected_grad
        )
        stores["projected_grad"].start()

    steps = {
        "tables": lambda: position_tables(ctx_count, pairing, cosine, sine, key_pos),
        "small cross": small_g.cross,
        "small share": small_g.share,
        "small done": small_done,
        "out start": out_start,
        "out share": out_share,
        "hid done": hid_done,
        "norm": norm_next,
        "norm done": norm_done,
        "project": project_all,
        "attend": attend_all,
        "inner": inner_all,
        "cot done": cot_done,
        "attended grads": out_grads,
        "down grads": down_grads,
        "attention back": attention_back,
    }
    for ch in range(TOKEN_CHUNKS):
        for name, gather in (("hid", hid_g), ("cot", cot_g)):
            steps["%s spread %d" % (name, ch)] = functools.partial(gather.spread, ch)
            for j in range(place.line - 1):
                steps["%s %d %d" % (name, j, ch)] = functools.partial(gather.step, j, ch)
    for name, gather in weights.items():
        for i in range(len(gather.by_chip)):
            steps["%s %d" % (name, i)] = functools.partial(gather.send, i)
        steps[name + " cross"] = gather.cross
        steps[name + " share"] = gather.share

    vectors = (ln1_gain, ln1_bias, ln2_gain, ln2_bias, out_bias, down_bias, qkv_bias_own, up_bias_own)
    vectors_in = (
        ln1_gain_in,
        ln1_bias_in,
        ln2_gain_in,
        ln2_bias_in,
        out_bias_in,
        down_bias_in,
        qkv_bias_in,
        up_bias_in,
    )
    vector_loads = [copies.inside(src, dst) for src, dst in zip(vectors_in, vectors)]
    loads["hid rows"].start()
    for load in vector_loads:
        load.start()
    loads["cot rows"].start()
    answered = greet(place)
    loads["hid rows"].wait()
    split_sequences(hid_rows, hid)
    for load in vector_loads:
        load.wait()
    pack_parameters(vectors, small)
    answered()
    hid_g.start()
    small_g.scatter()
    loads["cot rows"].wait()
    split_sequences(cot_rows, cot)
    cot_g.start()
    for name in GATHER_ORDER:
        steps[name]()
    weights["down a"].finish()
    weights["down b"].finish()
    for store in stores.values():
        store.wait()
    for gather in [hid_g, cot_g, small_g] + list(weights.values()):
        gather.drain()
    out_across.wait_send()
    out_swap.wait_send()


def gather_all(ctx_count, hid, cot, vectors, qkv, up, down, out, pairing):
    f32, b16 = jnp.float32, jnp.bfloat16
    chips = ctx_count // CORES
    rows = qkv.shape[0]
    groups = CORES * 2
    tokens = ctx_count * hid.shape[0]
    width = out.shape[1]
    head3, part = qkv.shape[1] // chips, up.shape[1] // chips
    head = head3 // 3
    qkv_s = ((chips, groups, rows, head3), b16)
    part_s = ((chips, groups, rows, part), b16)
    out_s = ((groups, rows, width), b16)
    small = (SMALL_ROWS, LANES)
    small_s = ((chips, groups) + small, f32)
    wide_s, narrow_s = ((tokens, width), b16), ((tokens, head), b16)
    own_s = ((hid.shape[1], hid.shape[0], width), b16)
    results = [
        wide_s,
        wide_s,
        qkv_s,
        part_s,
        part_s,
        out_s,
        small_s,
        narrow_s,
        ((tokens, head3), b16),
        wide_s,
        ((tokens, part), b16),
        ((tokens, part), f32),
        wide_s,
        part_s,
        ((8, width), f32),
        ((tokens, LANES), f32),
    ]
    scratch = [
        (hid.shape, b16),
        (cot.shape, b16),
        own_s,
        own_s,
    ]
    scratch += [(vector.shape, b16) for vector in vectors]
    scratch += [
        (small, f32),
        wide_s,
        wide_s,
        qkv_s,
        part_s,
        out_s,
        small_s,
        ((tokens, LANES), f32),
        ((tokens, LANES), f32),
        ((8, tokens), f32),
        ((8, width), f32),
        ((3 * width // LANES, LANES), f32),
        ((8, head3), f32),
        ((8, part), f32),
        wide_s,
        wide_s,
        ((tokens, LANES), f32),
        narrow_s,
        narrow_s,
        narrow_s,
        ((tokens, head), f32),
        narrow_s,
        ((tokens, tokens), f32),
        ((tokens, tokens), b16),
        ((tokens, part), b16),
        ((tokens, part), f32),
        narrow_s,
        ((tokens, tokens), b16),
        ((tokens, head3), b16),
    ]
    operands = (hid, cot, *vectors, qkv, up, down, out, pairing)
    anywhere = pl.BlockSpec(memory_space=pl.ANY)
    return pl.pallas_call(
        lambda *refs: gather_kernel(ctx_count, *refs),
        out_shape=[jax.ShapeDtypeStruct(*shape) for shape in results],
        in_specs=[anywhere] * (len(operands) - 1) + [pl.BlockSpec(memory_space=pltpu.SMEM)],
        out_specs=[anywhere] * len(results),
        scratch_shapes=[pltpu.VMEM(*shape) for shape in scratch]
        + [
            pltpu.SemaphoreType.DMA((160,)),
            pltpu.SemaphoreType.DMA((160,)),
            pltpu.SemaphoreType.DMA((48,)),
        ],
        compiler_params=pltpu.CompilerParams(
            collective_id=0, has_side_effects=True, vmem_limit_bytes=VMEM_BYTES
        ),
        name="gather_all",
    )(*operands)


def add_rows(total, other):
    step = 16

    @pl.loop(0, total.shape[0] // step)
    def _(i):
        at = tile(i, step)
        both = total[at, :].astype(jnp.float32) + other[at, :].astype(jnp.float32)
        total[at, :] = both.astype(total.dtype)


class GradScatter:
    def __init__(self, place, copies, partial, kept, from_core, from_plane, result, columns=None):
        self.place = place
        c, x, chip = place.c, place.x, place.chip
        self.kept, self.from_core, self.from_plane = kept, from_core, from_plane
        self.columns = cols = slice(0, kept.shape[3]) if columns is None else columns
        self.load = None
        given = partial.at[:, :, :, cols]
        if partial.shape != kept.shape:
            self.load = copies.inside(partial.at[:, pl.ds(2 * c, 2), :, cols], kept.at[:, :, :, cols])
            given = partial.at[:, pl.ds(2 * (1 - c), 2), :, cols]
        self.swap = copies.remote(given, from_core.at[:, :, :, cols], place.other_core())
        self.across = copies.remote(
            kept.at[:, 1 - x, :, cols], from_plane.at[:, :, cols], place.other_plane()
        )
        self.scattered = []
        for dz, dy in place.plane_offsets():
            z, y = place.shifted(dz, dy)
            self.scattered.append(
                copies.remote(
                    kept.at[z * LINE_Y + y, x, :, cols], result.at[chip, :, cols], place.at(z, y, c, x)
                )
            )
        self.own = copies.inside(kept.at[chip, x, :, cols], result.at[chip, :, cols])

    def start(self):
        if self.load is not None:
            self.load.start()
        self.swap.start()

    def cross(self):
        if self.load is not None:
            self.load.wait()
        self.swap.wait_recv()
        x = self.place.x
        self.add(1 - x, self.from_core.at[:, 1 - x])
        self.across.start()
        self.add(x, self.from_core.at[:, x])

    def add(self, x, other):
        step = 16
        per = self.kept.shape[2] // step
        cols = self.columns

        @pl.loop(0, self.kept.shape[0] * per)
        def _(i):
            k, at = i // per, tile(i % per, step)
            both = self.kept[k, x, at, cols].astype(jnp.float32) + other[k, at, cols].astype(jnp.float32)
            self.kept[k, x, at, cols] = both.astype(self.kept.dtype)

    def scatter(self):
        self.across.wait_recv()
        self.add(self.place.x, self.from_plane)
        for copy in self.scattered + [self.own]:
            copy.start()

    def finish(self):
        self.own.wait()
        for copy in self.scattered:
            copy.wait_recv()

    def drain(self, swapped=False):
        for copy in self.scattered + [self.across] + ([] if swapped else [self.swap]):
            copy.wait_send()


def out_weight_grads(place, attended_low, cot, kept, given):
    step = 512

    @pl.loop(0, cot.shape[1] // step)
    def _(i):
        at = tile(i, step)
        grad = contract_rows(attended_low[...], cot[:, at]).astype(jnp.bfloat16)
        grad = grad.reshape((2,) + kept.shape[:2] + (step,))
        kept[:, :, at] = jnp.where(place.c == 0, grad[0], grad[1])
        given[:, :, at] = jnp.where(place.c == 0, grad[1], grad[0])


def weight_grads_by_core(place, tokens, grads, kept, given, columns):
    chips, half, rows = kept.shape[:3]
    step = 2 * half * rows

    @pl.loop(0, chips)
    def _(k):
        grad = contract_rows(tokens[:, tile(k, step)], grads[:, columns]).astype(jnp.bfloat16)
        grad = grad.reshape(2, half, rows, grad.shape[1])
        kept[k, :, :, columns] = jnp.where(place.c == 0, grad[0], grad[1])
        given[k, :, :, columns] = jnp.where(place.c == 0, grad[1], grad[0])


class TokenScatter:
    def __init__(self, place, copies, part, from_y, slots, total, result):
        self.place, self.copies = place, copies
        z, y, c, x = place.z, place.y, place.c, place.x
        self.part, self.from_y, self.slots, self.total = part, from_y, slots, total
        self.line = place.line
        self.last = last = self.line - 1
        self.rows = total.shape[0]
        self.size = self.rows // TOKEN_CHUNKS
        count = self.line * TOKEN_CHUNKS
        self.over_base = copies.reserve(count)
        self.up_base = copies.reserve(count)
        self.down_base = copies.reserve(count)
        self.above = place.at(jnp.minimum(z + 1, last), y, c, x)
        self.below = place.at(jnp.maximum(z - 1, 0), y, c, x)
        half = self.rows // CORES
        self.swap = copies.remote(total.at[tile(1 - c, half)], result.at[c], place.other_core())
        self.own = copies.inside(total.at[tile(c, half)], result.at[c])

    def order(self, i):
        last = self.last
        chosen = 0
        for z in range(self.line):
            far = sorted(range(self.line), key=lambda k: (-abs(k - z), min(k, last - k)))
            chosen = jnp.where(self.place.z == z, far[i], chosen)
        return chosen

    def chunk(self, ref, k, ch):
        return ref.at[tile(k * TOKEN_CHUNKS + ch, self.size)]

    def held(self, k, ch):
        return self.chunk(self.part, k * LINE_Y + self.place.y, ch)

    def copy(self, base, k, ch, src, dst, device):
        return self.copies.remote_at(base + k * TOKEN_CHUNKS + ch, src, dst, device)

    def over(self, k, ch):
        src = self.chunk(self.part, k * LINE_Y + 1 - self.place.y, ch)
        return self.copy(self.over_base, k, ch, src, self.chunk(self.from_y, k, ch), self.place.other_y())

    def up(self, k, ch):
        return self.copy(self.up_base, k, ch, self.held(k, ch), self.chunk(self.slots, k, ch), self.above)

    def down(self, k, ch):
        slot = jnp.where(self.place.z - 1 == k, self.line, k)
        return self.copy(self.down_base, k, ch, self.held(k, ch), self.chunk(self.slots, slot, ch), self.below)

    def send_over(self, k):
        for ch in range(TOKEN_CHUNKS):
            self.over(k, ch).start()

    def combine(self, k, ch):
        self.over(k, ch).wait_recv()
        add_rows(self.held(k, ch), self.chunk(self.from_y, k, ch))

    def step(self, i, ch):
        z = self.place.z
        k = self.order(i)
        self.combine(k, ch)

        @pl.when(k > z)
        def _():
            @pl.when(z > 0)
            def _():
                self.up(k, ch).wait_recv()
                add_rows(self.held(k, ch), self.chunk(self.slots, k, ch))

            self.up(k, ch).start()

        @pl.when(k < z)
        def _():
            @pl.when(z < self.last)
            def _():
                self.down(k, ch).wait_recv()
                add_rows(self.held(k, ch), self.chunk(self.slots, k, ch))

            self.down(k, ch).start()

    def reduce(self):
        z, y, last = self.place.z, self.place.y, self.last
        step = 16
        for ch in range(TOKEN_CHUNKS):
            self.combine(z, ch)
            pl.when(z > 0)(lambda: self.up(z, ch).wait_recv())
            pl.when(z < last)(lambda: self.down(z, ch).wait_recv())

        @pl.loop(0, self.rows // step)
        def _(i):
            at = tile((z * LINE_Y + y) * (self.rows // step) + i, step)
            self.total[tile(i, step), :] = self.part[at, :].astype(jnp.float32)

        def add(slot):
            @pl.loop(0, self.rows // step)
            def _(i):
                at = tile(slot * (self.rows // step) + i, step)
                self.total[tile(i, step), :] += self.slots[at, :].astype(jnp.float32)

        pl.when(z > 0)(lambda: add(z))
        pl.when(z < last)(lambda: add(last + 1))
        self.swap.start()
        self.own.start()

    def finish(self):
        self.swap.wait_recv()

    def drain(self):
        z = self.place.z
        for k in range(self.line):
            for ch in range(TOKEN_CHUNKS):
                self.over(k, ch).wait_send()
                pl.when(z < k)(lambda: self.up(k, ch).wait_send())
                pl.when(z > k)(lambda: self.down(k, ch).wait_send())


def output_part(scatter, i, attended_low, activated, out_weight, down_weight):
    k = scatter.order(i)
    at = tile(k, LINE_Y * scatter.rows)
    rows = nn(attended_low[at, :], flat_rows(out_weight[...]))
    rows = rows + contract_cols(activated[at, :], flat_rows(down_weight[...]))
    scatter.part[at, :] = rows.astype(scatter.part.dtype)
    scatter.send_over(k)


def inner_grads(cot, down_weight, slope, slope_loads, inner_grad):
    step = slope.shape[1]
    for i, load in enumerate(slope_loads):
        load.wait()
        at = slice(i * step, (i + 1) * step)
        grad = nn(cot[at, :], flat_rows(down_weight[...])) * slope[i % 2]
        inner_grad[at, :] = grad.astype(jnp.bfloat16)
        if i + 2 < len(slope_loads):
            slope_loads[i + 2].start()


def hidden_part(scatter, i, inner_grad, up_weight, projected_grad, qkv_weight, hid, stats, vec, sums):
    def by_eight(values):
        return jnp.sum(values.reshape(-1, 8, values.shape[1]), axis=0)

    k = scatter.order(i)

    @pl.loop(0, LINE_Y)
    def _(y):
        at = tile(k * LINE_Y + y, scatter.rows)
        one = contract_cols(projected_grad[at, :], flat_rows(qkv_weight[...]))
        two = contract_cols(inner_grad[at, :], flat_rows(up_weight[...]))
        xhat = (hid[at, :].astype(jnp.float32) - stats[at, 0:1]) * stats[at, 1:2]
        sums[0] += by_eight(one * xhat)
        sums[1] += by_eight(one)
        sums[2] += by_eight(two * xhat)
        sums[3] += by_eight(two)
        rows = one * vec[0:1, :] + two * vec[2:3, :]
        scatter.part[at, :] = rows.astype(scatter.part.dtype)

    scatter.send_over(k)


COT_SUM, UP_SUM, QKV_SUM = 4, 5, 7


def pack_small(place, sums, cot_sum, up_sum, qkv_sum, qkv_rows, tiles):
    chips, groups = tiles.shape[:2]
    tiles[...] = jnp.zeros_like(tiles)
    qkv_rows[...] = jnp.zeros_like(qkv_rows)
    third = qkv_rows.shape[0] // 3
    per_head = HEAD // LANES
    for k in range(3):
        for u in range(per_head):
            at = (k * per_head + u) * LANES
            qkv_rows[pl.ds(k * third + place.chip * per_head + u, 1), :] = qkv_sum[0:1, at : at + LANES]
    first = jnp.where(place.chip == 0, 1.0, 0.0)
    norm_sums = [jnp.sum(sums[row], axis=0, keepdims=True) for row in range(4)]
    norm_sums.append(cot_sum[0:1, :] * first)
    for pair in range(chips * groups // 2):
        chip, group = pair // (groups // 2), pair % (groups // 2) * 2
        at = slice(pair * LANES, (pair + 1) * LANES)
        for g in (group, group + 1):
            for row in range(5):
                tiles[chip, g, row : row + 1, :] = norm_sums[row][:, at]
            tiles[chip, g, QKV_SUM : QKV_SUM + 3, :] = qkv_rows[3 * pair : 3 * pair + 3, :]
    for group in range(groups):
        for u in range(2):
            at = (group * 2 + u) * LANES
            row = UP_SUM + u
            values = up_sum[0:1, at : at + LANES].reshape(1, 1, LANES)
            tiles[pl.ds(place.chip, 1), group, row : row + 1, :] = values


SCATTER_ORDER = (
    "down a swap",
    "outs tile 0",
    "outs tile 1",
    "qkv grads",
    "outs 0 0",
    "down a cross",
    "outs tile 2",
    "down b swap",
    "outs 0 1",
    "out grads",
    "outs 1 0",
    "down b cross",
    "qkv swap",
    "down a scatter",
    "outs tile 3",
    "out swap",
    "inner",
    "outs 1 1",
    "outs 2 0",
    "qkv cross",
    "up a grad",
    "down b scatter",
    "up b grad",
    "hid tile 0",
    "up b swap",
    "outs 2 1",
    "out cross",
    "hid tile 1",
    "hid tile 2",
    "qkv scatter",
    "hid 0 0",
    "up a swap",
    "up b cross",
    "up sum",
    "hid 0 1",
    "hid tile 3",
    "pack",
    "hid 1 0",
    "small swap",
    "out finish",
    "small cross",
    "up b scatter",
    "hid 1 1",
    "hid 2 0",
    "outs reduce",
    "up a cross",
    "hid 2 1",
    "small scatter",
    "up a scatter",
    "hid reduce",
)


def scatter_kernel(
    ctx_count,
    hid_in,
    cot_in,
    qkv_in,
    up_in,
    down_in,
    out_in,
    attended_low_in,
    projected_grad_in,
    norm_two_in,
    activated_in,
    slope_in,
    stats_in,
    vec_in,
    norm_one_in,
    down_grad,
    small_result,
    qkv_result,
    up_result,
    down_result,
    out_grad_result,
    out_result,
    hid_result,
    wide,
    weight,
    slope,
    act,
    attended_low,
    out_weight,
    qkv_weight,
    projected_grad,
    stats,
    vec,
    qkv_sum,
    cot_sum,
    up_sum,
    sums,
    qkv_rows,
    tiles,
    small_kept,
    small_core,
    small_plane,
    qkv_kept,
    qkv_core,
    qkv_plane,
    up_kept,
    up_core,
    up_plane,
    down_kept,
    down_core,
    down_plane,
    out_kept,
    out_core,
    out_plane,
    out_part,
    out_from_y,
    out_slots,
    hid_part,
    hid_from_y,
    hid_slots,
    total,
    out_given,
    send,
    recv,
    local,
):
    place = Place(ctx_count)
    copies = Copies(send, recv, local)
    c, x = place.c, place.x
    qkv_given = up_kept.at[:, :, :, : qkv_kept.shape[3]]
    half = up_kept.shape[3] // 2
    halves = {" a": slice(0, half), " b": slice(half, 2 * half)}
    grads = {
        "qkv": GradScatter(place, copies, qkv_given, qkv_kept, qkv_core, qkv_plane, qkv_result),
        "small": GradScatter(place, copies, tiles, small_kept, small_core, small_plane, small_result),
    }
    for name, cols in halves.items():
        grads["down" + name] = GradScatter(
            place, copies, down_grad, down_kept, down_core, down_plane, down_result, cols
        )
        grads["up" + name] = GradScatter(place, copies, down_core, up_kept, up_core, up_plane, up_result, cols)
    outs_s = TokenScatter(place, copies, out_part, out_from_y, out_slots, total, out_result)
    hid_s = TokenScatter(place, copies, hid_part, hid_from_y, hid_slots, total, hid_result)
    out_swap = copies.remote(out_given, out_core, place.other_core())
    out_across = copies.remote(out_kept.at[1 - x], out_plane, place.other_plane())
    out_own = copies.inside(out_kept.at[x], out_grad_result)
    loads = {
        name: copies.inside(src, dst)
        for name, src, dst in (
            ("activated", activated_in, act),
            ("attended_low", attended_low_in, attended_low),
            ("out", out_in, out_weight),
            ("down", down_in, weight),
            ("cot", cot_in, wide),
            ("norm_two", norm_two_in, wide),
            ("qkv", qkv_in, qkv_weight),
            ("projected_grad", projected_grad_in, projected_grad),
            ("stats", stats_in, stats),
            ("vec", vec_in, vec),
            ("norm_one", norm_one_in, wide),
            ("up", up_in, weight),
            ("hid", hid_in, wide),
        )
    }
    early = ("activated", "attended_low", "out", "down", "projected_grad", "norm_one", "qkv", "stats", "vec")

    def out_cross():
        out_swap.wait_recv()
        for k in range(2):
            add_rows(out_kept.at[k], out_core.at[k])
        out_across.start()

    def out_finish():
        out_across.wait_recv()
        step = 16

        @pl.loop(0, out_plane.shape[0] // step)
        def _(i):
            at = tile(i, step)
            both = out_kept[x, at, :].astype(jnp.float32) + out_plane[at, :].astype(jnp.float32)
            out_kept[x, at, :] = both.astype(out_kept.dtype)

        out_own.start()

    step = slope.shape[1]
    slope_loads = [
        copies.inside(slope_in.at[pl.ds(i * step, step)], slope.at[i % 2]) for i in range(slope_in.shape[0] // step)
    ]
    waited = set()

    def need(*names):
        for name in names:
            if name not in waited:
                waited.add(name)
                loads[name].wait()

    def output_tile(i):
        need("activated", "attended_low", "out", "down")
        output_part(outs_s, i, attended_low, act, out_weight, weight)

    def inner_all():
        need("cot")
        inner_grads(wide, weight, slope, slope_loads, act)
        loads["up"].start()
        loads["norm_two"].start()

    def qkv_grads():
        need("projected_grad", "norm_one")
        columns = slice(0, qkv_kept.shape[3])
        weight_grads_by_core(place, wide, projected_grad, qkv_kept, qkv_given, columns)
        loads["cot"].start()
        column_sums(projected_grad, qkv_sum)

    def out_grads():
        need("attended_low", "cot")
        out_weight_grads(place, attended_low, wide, out_kept, out_given)
        column_sums(wide, cot_sum)

    def up_half(name, last):
        if not last:
            grads["qkv"].swap.wait_send()
        need("norm_two")
        weight_grads_by_core(place, wide, act, up_kept, down_core, halves[name])
        if last:
            loads["hid"].start()

    def hidden_tile(i):
        if i == 0:
            need("qkv", "projected_grad", "stats", "vec", "up", "hid")
            sums[...] = jnp.zeros_like(sums)
        hidden_part(hid_s, i, act, weight, projected_grad, qkv_weight, wide, stats, vec, sums)

    def pack():
        pack_small(place, sums, cot_sum, up_sum, qkv_sum, qkv_rows, tiles)

    def hidden_reduce():
        outs_s.own.wait()
        outs_s.swap.wait_send()
        hid_s.reduce()

    steps = {
        "qkv grads": qkv_grads,
        "out grads": out_grads,
        "out swap": out_swap.start,
        "out cross": out_cross,
        "out finish": out_finish,
        "inner": inner_all,
        "up a grad": functools.partial(up_half, " a", False),
        "up b grad": functools.partial(up_half, " b", True),
        "up sum": lambda: column_sums(act, up_sum),
        "pack": pack,
        "outs reduce": outs_s.reduce,
        "hid reduce": hidden_reduce,
    }
    for name, scatter in grads.items():
        steps[name + " swap"] = scatter.start
        steps[name + " cross"] = scatter.cross
        steps[name + " scatter"] = scatter.scatter
    for i in range(outs_s.line):
        steps["outs tile %d" % i] = functools.partial(output_tile, i)
        steps["hid tile %d" % i] = functools.partial(hidden_tile, i)
    for j in range(outs_s.last):
        for ch in range(TOKEN_CHUNKS):
            steps["outs %d %d" % (j, ch)] = functools.partial(outs_s.step, j, ch)
            steps["hid %d %d" % (j, ch)] = functools.partial(hid_s.step, j, ch)

    for name in early:
        loads[name].start()
    slope_loads[0].start()
    slope_loads[1].start()
    greet(place)()
    for name in SCATTER_ORDER:
        steps[name]()
    for scatter in list(grads.values()) + [outs_s, hid_s]:
        scatter.finish()
    out_own.wait()
    hid_s.own.wait()
    hid_s.swap.wait_send()
    for name, scatter in grads.items():
        scatter.drain(name == "qkv")
    outs_s.drain()
    hid_s.drain()
    out_swap.wait_send()
    out_across.wait_send()


def scatter_all(ctx_count, local_rows, operands):
    f32, b16 = jnp.float32, jnp.bfloat16
    hid, _, w_qkv, w_up, _, w_out = operands[:6]
    chips, groups, rows, head3 = w_qkv.shape
    part = w_up.shape[3]
    tokens, width = hid.shape
    line = chips // LINE_Y
    small = (SMALL_ROWS, LANES)
    token = (CORES, local_rows, width)
    results = [
        ((chips,) + small, f32),
        ((chips, rows, head3), b16),
        ((chips, rows, part), b16),
        ((chips, rows, part), b16),
        ((rows, width), b16),
        (token, f32),
        (token, f32),
    ]
    scratch = [
        ((tokens, width), b16),
        (w_up.shape, b16),
        ((2, 256, part), f32),
        ((tokens, part), b16),
        ((tokens, head3 // 3), b16),
        (w_out.shape, b16),
        (w_qkv.shape, b16),
        ((tokens, head3), b16),
        ((tokens, LANES), f32),
        ((8, width), f32),
        ((8, head3), f32),
        ((8, width), f32),
        ((8, part), f32),
        ((4, 8, width), f32),
        ((3 * width // LANES, LANES), f32),
        ((chips, groups) + small, f32),
    ]
    for shape, dtype in ((small, f32), ((rows, head3), b16), ((rows, part), b16), ((rows, part), b16)):
        scratch += [((chips, 2) + shape, dtype)] * 2 + [((chips,) + shape, dtype)]
    scratch += [((2, rows, width), b16)] * 2 + [((rows, width), b16)]
    chip_rows = CORES * local_rows
    for _ in range(2):
        scratch += [
            ((tokens, width), b16),
            ((line * chip_rows, width), b16),
            (((line + 1) * chip_rows, width), b16),
        ]
    scratch += [((chip_rows, width), f32), ((2, rows, width), b16)]
    anywhere = pl.BlockSpec(memory_space=pl.ANY)
    return pl.pallas_call(
        lambda *refs: scatter_kernel(ctx_count, *refs),
        out_shape=[jax.ShapeDtypeStruct(*shape) for shape in results],
        in_specs=[anywhere] * len(operands),
        out_specs=[anywhere] * len(results),
        scratch_shapes=[pltpu.VMEM(*shape) for shape in scratch]
        + [
            pltpu.SemaphoreType.DMA((128,)),
            pltpu.SemaphoreType.DMA((128,)),
            pltpu.SemaphoreType.DMA((48,)),
        ],
        compiler_params=pltpu.CompilerParams(
            collective_id=1, has_side_effects=True, vmem_limit_bytes=VMEM_BYTES
        ),
        name="scatter_all",
    )(*operands)


def finish_kernel(
    qkv_in,
    up_in,
    down_in,
    out_in,
    out_rows_in,
    hid_rows_in,
    hidden_in,
    cotangent_in,
    small,
    vec,
    ln1_gain,
    ln1_bias,
    qkv_bias,
    out_bias,
    ln2_gain,
    ln2_bias,
    up_bias,
    down_bias,
    output_out,
    grad_hidden_out,
    qkv_out,
    out_out,
    up_out,
    down_out,
    qkv_rows,
    up_rows,
    down_rows,
    out_piece,
    out_rows,
    hid_rows,
    hidden,
    cotangent,
    output,
    grad_hidden,
    qkv,
    out,
    up,
    down,
    load_sems,
    store_sems,
):
    f32 = jnp.float32
    given = (up_in, down_in, qkv_in, out_in, out_rows_in, hid_rows_in, hidden_in, cotangent_in)
    held = (up_rows, down_rows, qkv_rows, out_piece, out_rows, hid_rows, hidden, cotangent)
    loads = [pltpu.make_async_copy(src, dst, load_sems.at[i]) for i, (src, dst) in enumerate(zip(given, held))]
    made = (up, down, qkv, out, output, grad_hidden)
    asked = (up_out, down_out, qkv_out, out_out, output_out, grad_hidden_out)
    stores = [pltpu.make_async_copy(src, dst, store_sems.at[i]) for i, (src, dst) in enumerate(zip(made, asked))]
    for load in loads:
        load.start()

    total = jnp.sum(small[...], axis=0)
    half = LANES // 2
    odd = lax.axis_index("fsdp") == 1
    halves = jnp.where(odd, total[: COT_SUM + 1, half:], total[: COT_SUM + 1, :half])
    for row, ref in enumerate((ln1_gain, ln1_bias, ln2_gain, ln2_bias, out_bias)):
        ref[...] = halves[row]
    down_bias[...] = halves[COT_SUM]
    for u in range(2):
        up_bias[u * LANES : (u + 1) * LANES] = total[UP_SUM + u]
    first, middle, last = [total[QKV_SUM + u : QKV_SUM + u + 1] for u in range(3)]
    even_row = jnp.concatenate([first, middle[:, :half]], axis=1)
    odd_row = jnp.concatenate([middle[:, half:], last], axis=1)
    qkv_bias[...] = jnp.where(odd, odd_row, even_row)[0]

    chips = up_rows.shape[0]
    for i, rows, made_ref in ((0, up_rows, up), (1, down_rows, down)):
        loads[i].wait()
        size = rows.shape[2]
        for k in range(chips):
            made_ref[:, k * size : (k + 1) * size] = rows[k].astype(f32)
        stores[i].start()
    loads[2].wait()
    third = qkv.shape[1] // 3
    for k in range(chips):
        for t in range(3):
            at = t * third + k * HEAD
            qkv[:, at : at + HEAD] = qkv_rows[k, :, t * HEAD : (t + 1) * HEAD].astype(f32)
    stores[2].start()
    loads[3].wait()
    out[...] = out_piece[...].astype(f32)
    stores[3].start()

    for load in loads[4:]:
        load.wait()
    bias = vec[OUT_BIAS : OUT_BIAS + 1, :] + vec[DOWN_BIAS : DOWN_BIAS + 1, :]
    step = 16

    @pl.loop(0, hidden.shape[0] // step)
    def _(i):
        at = tile(i, step)
        both, grads = [], []
        for s in range(hidden.shape[1]):
            x = hidden[at, s, :].astype(f32)
            both.append(x + out_rows[s, at, :] + bias)
            average = jnp.mean(x, axis=1, keepdims=True)
            centered = x - average
            scale = lax.rsqrt(jnp.mean(centered * centered, axis=1, keepdims=True) + LN_EPSILON)
            xhat = centered * scale
            e = hid_rows[s, at, :]
            slope = jnp.mean(e * xhat, axis=1, keepdims=True)
            back = scale * (e - jnp.mean(e, axis=1, keepdims=True) - xhat * slope)
            grads.append(cotangent[at, s, :].astype(f32) + back)
        output[at] = jnp.stack(both, axis=1).astype(output.dtype)
        grad_hidden[at] = jnp.stack(grads, axis=1)

    stores[4].start()
    stores[5].start()
    for store in stores:
        store.wait()


def finish_all(qkv_rows, up_rows, down_rows, out_sum, out_rows, hid_rows, hidden, cotangent, small, vec):
    f32 = jnp.float32
    rows, width = out_sum.shape
    part, head3 = up_rows.shape[0] * up_rows.shape[2], qkv_rows.shape[0] * qkv_rows.shape[2]
    vectors = [rows, rows, 3 * rows, rows, rows, rows, part // width * rows, rows]
    big = [
        (hidden.shape, hidden.dtype),
        (hidden.shape, f32),
        ((rows, head3), f32),
        ((rows, width), f32),
        ((rows, part), f32),
        ((rows, part), f32),
    ]
    operands = (qkv_rows, up_rows, down_rows, out_sum, out_rows, hid_rows, hidden, cotangent)
    anywhere, held = pl.BlockSpec(memory_space=pl.ANY), pl.BlockSpec(memory_space=pltpu.VMEM)
    return pl.pallas_call(
        finish_kernel,
        out_shape=[jax.ShapeDtypeStruct((n,), f32) for n in vectors]
        + [jax.ShapeDtypeStruct(*shape) for shape in big],
        in_specs=[anywhere] * len(operands) + [held, held],
        out_specs=[held] * len(vectors) + [anywhere] * len(big),
        scratch_shapes=[pltpu.VMEM(o.shape, o.dtype) for o in operands]
        + [pltpu.VMEM(*shape) for shape in big]
        + [pltpu.SemaphoreType.DMA((8,)), pltpu.SemaphoreType.DMA((8,))],
        compiler_params=pltpu.CompilerParams(vmem_limit_bytes=VMEM_BYTES),
        name="finish_all",
    )(*operands, small, vec)


def split_body(
    hidden,
    cotangent,
    pairing,
    ln1_gain,
    ln1_bias,
    qkv_weight,
    qkv_bias,
    out_weight,
    out_bias,
    ln2_gain,
    ln2_bias,
    up_weight,
    up_bias,
    down_weight,
    down_bias,
):
    ctx_count = lax.axis_size("ctx")
    (
        hid_all,
        cot_all,
        w_qkv,
        w_up,
        w_down,
        w_out,
        _,
        attended_low,
        projected_grad,
        norm_two,
        activated,
        slope,
        norm_one,
        grad_down,
        vec,
        stats,
    ) = gather_all(
        ctx_count,
        hidden,
        cotangent,
        (ln1_gain, ln1_bias, ln2_gain, ln2_bias, out_bias, down_bias, qkv_bias, up_bias),
        qkv_weight,
        up_weight,
        down_weight,
        out_weight,
        pairing,
    )
    small_sum, qkv_rows, up_rows, down_rows, out_sum, out_rows, hid_rows = scatter_all(
        ctx_count,
        hidden.shape[0],
        (
            hid_all,
            cot_all,
            w_qkv,
            w_up,
            w_down,
            w_out,
            attended_low,
            projected_grad,
            norm_two,
            activated,
            slope,
            stats,
            vec,
            norm_one,
            grad_down,
        ),
    )
    (
        grad_ln1_gain,
        grad_ln1_bias,
        grad_qkv_bias,
        grad_out_bias,
        grad_ln2_gain,
        grad_ln2_bias,
        grad_up_bias,
        grad_down_bias,
        output,
        grad_hidden,
        grad_qkv_weight,
        grad_out_weight,
        grad_up_weight,
        grad_down_weight,
    ) = finish_all(
        qkv_rows, up_rows, down_rows, out_sum, out_rows, hid_rows, hidden, cotangent, small_sum, vec
    )
    return (
        output,
        grad_hidden,
        grad_ln1_gain,
        grad_ln1_bias,
        grad_qkv_weight,
        grad_qkv_bias,
        grad_out_weight,
        grad_out_bias,
        grad_ln2_gain,
        grad_ln2_bias,
        grad_up_weight,
        grad_up_bias,
        grad_down_weight,
        grad_down_bias,
    )


def solution(mesh):
    body = split_body if split_fits(mesh) else general_body
    return jax.shard_map(
        body,
        mesh=mesh,
        in_specs=(
            P("ctx", "fsdp", None),
            P("ctx", "fsdp", None),
            P(),
            P(("ctx", "fsdp")),
            P(("ctx", "fsdp")),
            P(("ctx", "fsdp"), None),
            P(("ctx", "fsdp")),
            P(("ctx", "fsdp"), None),
            P(("ctx", "fsdp")),
            P(("ctx", "fsdp")),
            P(("ctx", "fsdp")),
            P(("ctx", "fsdp"), None),
            P(("ctx", "fsdp")),
            P(("ctx", "fsdp"), None),
            P(("ctx", "fsdp")),
        ),
        out_specs=(
            P("ctx", "fsdp", None),
            P("ctx", "fsdp", None),
            P(("ctx", "fsdp")),
            P(("ctx", "fsdp")),
            P(("ctx", "fsdp"), None),
            P(("ctx", "fsdp")),
            P(("ctx", "fsdp"), None),
            P(("ctx", "fsdp")),
            P(("ctx", "fsdp")),
            P(("ctx", "fsdp")),
            P(("ctx", "fsdp"), None),
            P(("ctx", "fsdp")),
            P(("ctx", "fsdp"), None),
            P(("ctx", "fsdp")),
        ),
        check_vma=False,
    )
```

```python
import functools

import jax
import jax.numpy as jnp
from jax import lax
from jax.experimental import pallas as pl
from jax.experimental.pallas import tpu as pltpu
from jax.sharding import PartitionSpec as P

HEAD = 256
ROT = 64


LN_EPSILON = 1e-05
VERY_LOW = -1e30


def layer_norm(values, ln_gain, ln_shift):
    average = jnp.mean(values, axis=-1, keepdims=True)
    centered = values - average
    spread = jnp.mean(centered * centered, axis=-1, keepdims=True)
    return centered * lax.rsqrt(spread + LN_EPSILON) * ln_gain + ln_shift


def gelu_exact(values):
    return jax.nn.gelu(values, approximate=False)


def rotate(values, positions):
    half_rot = ROT // 2
    frequency = 1.0 / 10000.0 ** (jnp.arange(half_rot).astype(values.dtype) * 2.0 / ROT)
    angles = positions.astype(values.dtype)[:, None] * frequency[None, :]
    shape_out = (angles.shape[0],) + (1,) * (values.ndim - 2) + (ROT,)
    cosine = jnp.concatenate([jnp.cos(angles), jnp.cos(angles)], axis=-1).reshape(shape_out)
    sine_part = jnp.concatenate([jnp.sin(angles), jnp.sin(angles)], axis=-1).reshape(shape_out)
    rot_part = values[..., :ROT]
    turned = jnp.concatenate([-rot_part[..., half_rot:], rot_part[..., :half_rot]], axis=-1)
    return jnp.concatenate([rot_part * cosine + turned * sine_part, values[..., ROT:]], axis=-1)


def row_positions(pairing, first_row, row_count, block_rows, ctx_count):
    row_ids = first_row + jnp.arange(row_count, dtype=jnp.int32)
    device_ids = row_ids // (2 * block_rows)
    within = row_ids % (2 * block_rows)
    matches = device_ids[:, None] == jnp.arange(ctx_count, dtype=jnp.int32)[None, :]
    owned_block = jnp.sum(jnp.where(matches, pairing[None, :], 0), axis=1)
    blocks = jnp.where(within < block_rows, owned_block, 2 * ctx_count - 1 - owned_block)
    return blocks * block_rows + within % block_rows


def heads_view(values, row_total, seq_count):
    return values.reshape(row_total, seq_count, -1, HEAD)


def contract_rows(left, right):
    return lax.dot_general(
        left, right, (((0,), (0,)), ((), ())), preferred_element_type=jnp.float32
    )


def contract_cols(left, right):
    return lax.dot_general(
        left, right, (((1,), (1,)), ((), ())), preferred_element_type=jnp.float32
    )


def pair_grads(
    query_rows, grad_rows, log_rows, delta_rows, query_pos, key_heads, value_heads, key_pos, scaling
):
    scores = (
        jnp.einsum("qshd,kshd->shqk", query_rows, key_heads, preferred_element_type=jnp.float32)
        * scaling
    )
    allowed = key_pos[None, None, None, :] <= query_pos[None, None, :, None]
    probabilities = jnp.where(allowed, jnp.exp(scores - log_rows[..., None]), 0.0)
    prob_grad = jnp.einsum(
        "qshd,kshd->shqk", grad_rows, value_heads, preferred_element_type=jnp.float32
    )
    score_grad = (probabilities * (prob_grad - delta_rows[..., None])).astype(jnp.bfloat16)
    return (score_grad, probabilities.astype(jnp.bfloat16))


def general_body(
    hidden,
    cotangent,
    pairing,
    ln1_gain,
    ln1_bias,
    qkv_weight,
    qkv_bias,
    out_weight,
    out_bias,
    ln2_gain,
    ln2_bias,
    up_weight,
    up_bias,
    down_weight,
    down_bias,
):
    local_rows, seq_count, model_width = hidden.shape
    block_rows = local_rows // 2
    ctx_count = lax.axis_size("ctx")
    head_count = model_width // HEAD
    scaling = HEAD ** (-0.5)
    tokens = local_rows * seq_count
    total_rows = local_rows * ctx_count
    params = (
        lax.all_gather(ln1_gain, ("ctx", "fsdp"), axis=0, tiled=True),
        lax.all_gather(ln1_bias, ("ctx", "fsdp"), axis=0, tiled=True),
        lax.all_gather(qkv_weight, ("ctx", "fsdp"), axis=0, tiled=True),
        lax.all_gather(qkv_bias, ("ctx", "fsdp"), axis=0, tiled=True),
        lax.all_gather(out_weight, ("ctx", "fsdp"), axis=0, tiled=True),
        lax.all_gather(out_bias, ("ctx", "fsdp"), axis=0, tiled=True),
        lax.all_gather(ln2_gain, ("ctx", "fsdp"), axis=0, tiled=True),
        lax.all_gather(ln2_bias, ("ctx", "fsdp"), axis=0, tiled=True),
        lax.all_gather(up_weight, ("ctx", "fsdp"), axis=0, tiled=True),
        lax.all_gather(up_bias, ("ctx", "fsdp"), axis=0, tiled=True),
        lax.all_gather(down_weight, ("ctx", "fsdp"), axis=0, tiled=True),
        lax.all_gather(down_bias, ("ctx", "fsdp"), axis=0, tiled=True),
    )
    (
        gain_one,
        shift_one,
        w_qkv,
        b_qkv,
        w_out,
        b_out,
        gain_two,
        shift_two,
        w_up,
        b_up,
        w_down,
        b_down,
    ) = params
    ff_width = w_up.shape[1]
    hidden_f = hidden.astype(jnp.float32).reshape(tokens, model_width)
    own_pos = row_positions(
        pairing, lax.axis_index("ctx") * local_rows, local_rows, block_rows, ctx_count
    )
    normed_one, ln_one_pull = jax.vjp(
        layer_norm, hidden_f, gain_one.astype(jnp.float32), shift_one.astype(jnp.float32)
    )
    normed_one_low = normed_one.astype(jnp.bfloat16)
    projected = jnp.dot(normed_one_low, w_qkv, preferred_element_type=jnp.float32) + b_qkv.astype(
        jnp.float32
    )
    query_f, rotation_pull = jax.vjp(
        lambda values: rotate(values, own_pos),
        heads_view(projected[:, :model_width], local_rows, seq_count),
    )
    query_b = query_f.astype(jnp.bfloat16)
    key_b = (
        rotate(
            heads_view(projected[:, model_width : 2 * model_width], local_rows, seq_count), own_pos
        )
        .astype(jnp.bfloat16)
        .reshape(local_rows, seq_count, model_width)
    )
    value_b = (
        projected[:, 2 * model_width :]
        .astype(jnp.bfloat16)
        .reshape(local_rows, seq_count, model_width)
    )
    running_max = jnp.full((seq_count, head_count, local_rows), VERY_LOW, jnp.float32)
    key_piece = lax.all_gather(key_b, "ctx", axis=0, tiled=True)
    value_piece = lax.all_gather(value_b, "ctx", axis=0, tiled=True)
    row_total = key_piece.shape[0]
    key_pos = row_positions(pairing, jnp.int32(0), row_total, block_rows, ctx_count)
    scores = (
        jnp.einsum(
            "qshd,kshd->shqk",
            query_b,
            heads_view(key_piece, row_total, seq_count),
            preferred_element_type=jnp.float32,
        )
        * scaling
    )
    allowed = key_pos[None, None, None, :] <= own_pos[None, None, :, None]
    piece_max = jnp.max(jnp.where(allowed, scores, VERY_LOW), axis=-1)
    new_max = jnp.maximum(running_max, piece_max)
    weights = jnp.where(allowed, jnp.exp(scores - new_max[..., None]), 0.0)
    new_total = jnp.sum(weights, axis=-1)
    mixture = jnp.einsum(
        "shqk,kshd->qshd",
        weights.astype(jnp.bfloat16),
        heads_view(value_piece, row_total, seq_count),
        preferred_element_type=jnp.float32,
    )
    log_total = new_max + jnp.log(new_total)
    attended = mixture / jnp.transpose(new_total, (2, 0, 1))[..., None]
    attended_low = attended.astype(jnp.bfloat16).reshape(tokens, model_width)
    branch_attn = jnp.dot(attended_low, w_out, preferred_element_type=jnp.float32) + b_out.astype(
        jnp.float32
    )
    normed_two, ln_two_pull = jax.vjp(
        layer_norm, hidden_f, gain_two.astype(jnp.float32), shift_two.astype(jnp.float32)
    )
    normed_two_low = normed_two.astype(jnp.bfloat16)
    inner_act = jnp.dot(normed_two_low, w_up, preferred_element_type=jnp.float32) + b_up.astype(
        jnp.float32
    )
    activated_f, gelu_pull = jax.vjp(gelu_exact, inner_act)
    activated = activated_f.astype(jnp.bfloat16)
    branch_mlp = contract_cols(activated, w_down) + b_down.astype(jnp.float32)
    output = (
        (hidden_f + branch_attn + branch_mlp)
        .astype(jnp.bfloat16)
        .reshape(local_rows, seq_count, model_width)
    )
    back_qkv, back_out, back_up, back_down = (
        lax.all_gather(qkv_weight, ("ctx", "fsdp"), axis=0, tiled=True),
        lax.all_gather(out_weight, ("ctx", "fsdp"), axis=0, tiled=True),
        lax.all_gather(up_weight, ("ctx", "fsdp"), axis=0, tiled=True),
        lax.all_gather(down_weight, ("ctx", "fsdp"), axis=0, tiled=True),
    )
    grad_out = cotangent.reshape(tokens, model_width)
    grad_f = grad_out.astype(jnp.float32)
    bias_sum = jnp.sum(grad_f, axis=0)
    up_grad = jnp.dot(grad_out, back_down, preferred_element_type=jnp.float32)
    inner_grad = gelu_pull(up_grad)[0].astype(jnp.bfloat16)
    norm_two_grad = contract_cols(inner_grad, back_up)
    dx_two, dgain_two, dshift_two = ln_two_pull(norm_two_grad)
    up_bias_sum = jnp.sum(inner_grad, axis=0, dtype=jnp.float32)
    mlp_small = jnp.concatenate(
        [
            up_bias_sum.reshape(model_width, -1),
            jnp.stack([bias_sum, dgain_two, dshift_two], axis=1),
        ],
        axis=1,
    )
    up_w_sum, down_w_sum, mlp_small_sum = (
        lax.psum_scatter(
            contract_rows(normed_two_low, inner_grad),
            ("ctx", "fsdp"),
            scatter_dimension=0,
            tiled=True,
        ),
        lax.psum_scatter(
            contract_rows(grad_out, activated), ("ctx", "fsdp"), scatter_dimension=0, tiled=True
        ),
        lax.psum_scatter(mlp_small, ("ctx", "fsdp"), scatter_dimension=0, tiled=True),
    )
    ratio = ff_width // model_width
    attn_grad = contract_cols(grad_out, back_out).astype(jnp.bfloat16)
    out_w_grad = contract_rows(attended_low, grad_out)
    grad_heads = heads_view(attn_grad, local_rows, seq_count)
    row_delta = jnp.einsum("qshd,qshd->shq", grad_heads.astype(jnp.float32), attended)
    keys_all, values_all = (
        lax.all_gather(key_b, "ctx", axis=0, tiled=True),
        lax.all_gather(value_b, "ctx", axis=0, tiled=True),
    )
    key_block = 512
    block_count = total_rows // key_block
    starts = jnp.arange(block_count, dtype=jnp.int32) * key_block

    def query_step(query_grad, inputs):
        key_piece, value_piece, offset = inputs
        key_pos = row_positions(pairing, offset, key_block, block_rows, ctx_count)
        key_heads = heads_view(key_piece, key_block, seq_count)
        value_heads = heads_view(value_piece, key_block, seq_count)
        score_grad, unused = pair_grads(
            query_b,
            grad_heads,
            log_total,
            row_delta,
            own_pos,
            key_heads,
            value_heads,
            key_pos,
            scaling,
        )
        query_grad = (
            query_grad
            + jnp.einsum(
                "shqk,kshd->qshd", score_grad, key_heads, preferred_element_type=jnp.float32
            )
            * scaling
        )
        return (query_grad, None)

    query_grad, unused_out = lax.scan(
        query_step,
        jnp.zeros((local_rows, seq_count, head_count, HEAD), jnp.float32),
        (
            keys_all.reshape(block_count, key_block, seq_count, model_width),
            values_all.reshape(block_count, key_block, seq_count, model_width),
            starts,
        ),
    )
    queries_all, grads_all = (
        lax.all_gather(query_b, "ctx", axis=0, tiled=True),
        lax.all_gather(grad_heads, "ctx", axis=0, tiled=True),
    )
    logs_all, deltas_all = (
        lax.all_gather(log_total, "ctx", axis=2, tiled=True),
        lax.all_gather(row_delta, "ctx", axis=2, tiled=True),
    )
    own_keys = heads_view(key_b, local_rows, seq_count)
    own_values = heads_view(value_b, local_rows, seq_count)

    def key_step(carry, inputs):
        key_acc, value_acc = carry
        query_piece, grad_piece, log_piece, delta_piece, offset = inputs
        query_pos = row_positions(pairing, offset, key_block, block_rows, ctx_count)
        score_grad, probs_low = pair_grads(
            query_piece,
            grad_piece,
            log_piece,
            delta_piece,
            query_pos,
            own_keys,
            own_values,
            own_pos,
            scaling,
        )
        key_acc = (
            key_acc
            + jnp.einsum(
                "shqk,qshd->kshd", score_grad, query_piece, preferred_element_type=jnp.float32
            )
            * scaling
        )
        value_acc = value_acc + jnp.einsum(
            "shqk,qshd->kshd", probs_low, grad_piece, preferred_element_type=jnp.float32
        )
        return ((key_acc, value_acc), None)

    empty_acc = jnp.zeros((local_rows, seq_count, head_count, HEAD), jnp.float32)
    log_blocks = jnp.moveaxis(logs_all.reshape(seq_count, head_count, block_count, key_block), 2, 0)
    delta_blocks = jnp.moveaxis(
        deltas_all.reshape(seq_count, head_count, block_count, key_block), 2, 0
    )
    (key_sum, value_sum), unused_keys = lax.scan(
        key_step,
        (empty_acc, empty_acc),
        (
            queries_all.reshape(block_count, key_block, seq_count, head_count, HEAD),
            grads_all.reshape(block_count, key_block, seq_count, head_count, HEAD),
            log_blocks,
            delta_blocks,
            starts,
        ),
    )
    key_owned = key_sum.reshape(local_rows, seq_count, model_width)
    value_owned = value_sum.reshape(local_rows, seq_count, model_width)
    query_pre = rotation_pull(query_grad)[0].reshape(tokens, model_width)
    key_pre = rotation_pull(heads_view(key_owned, local_rows, seq_count))[0].reshape(
        tokens, model_width
    )
    value_pre = value_owned.reshape(tokens, model_width)
    projected_grad = jnp.concatenate([query_pre, key_pre, value_pre], axis=1).astype(jnp.bfloat16)
    norm_one_grad = contract_cols(projected_grad, back_qkv)
    dx_one, dgain_one, dshift_one = ln_one_pull(norm_one_grad)
    qkv_bias_sum = jnp.sum(projected_grad, axis=0, dtype=jnp.float32)
    attn_small = jnp.concatenate(
        [
            qkv_bias_sum.reshape(model_width, -1),
            jnp.stack([bias_sum, dgain_one, dshift_one], axis=1),
        ],
        axis=1,
    )
    qkv_w_sum, out_w_sum, attn_small_sum = (
        lax.psum_scatter(
            contract_rows(normed_one_low, projected_grad),
            ("ctx", "fsdp"),
            scatter_dimension=0,
            tiled=True,
        ),
        lax.psum_scatter(out_w_grad, ("ctx", "fsdp"), scatter_dimension=0, tiled=True),
        lax.psum_scatter(attn_small, ("ctx", "fsdp"), scatter_dimension=0, tiled=True),
    )
    grad_hidden = (grad_f + dx_one + dx_two).reshape(local_rows, seq_count, model_width)
    return (
        output,
        grad_hidden,
        attn_small_sum[:, 4],
        attn_small_sum[:, 5],
        qkv_w_sum,
        attn_small_sum[:, :3].reshape(-1),
        out_w_sum,
        attn_small_sum[:, 3],
        mlp_small_sum[:, ratio + 1],
        mlp_small_sum[:, ratio + 2],
        up_w_sum,
        mlp_small_sum[:, :ratio].reshape(-1),
        down_w_sum,
        mlp_small_sum[:, ratio],
    )


MESH = pl.DeviceIdType.MESH
CORES = 2
LINE_Y = 2
VMEM_BYTES = 60 * 2**20


def split_fits(mesh):
    return mesh.shape["ctx"] == 16 and mesh.shape["fsdp"] == 2


class Place:
    def __init__(self, ctx_count):
        self.chips = ctx_count // CORES
        self.line = self.chips // LINE_Y
        index = lax.axis_index("ctx")
        self.c = index % CORES
        self.chip = index // CORES
        self.y = self.chip % LINE_Y
        self.z = self.chip // LINE_Y
        self.x = lax.axis_index("fsdp")

    def at(self, z, y, c, x):
        return ((z * LINE_Y + y) * CORES + c, x)

    def other_core(self):
        return self.at(self.z, self.y, 1 - self.c, self.x)

    def other_plane(self):
        return self.at(self.z, self.y, self.c, 1 - self.x)

    def other_y(self):
        return self.at(self.z, 1 - self.y, self.c, self.x)

    def plane_offsets(self):
        return [(dz, dy) for dz in range(self.line) for dy in range(LINE_Y) if dz or dy]

    def shifted(self, dz, dy):
        return (self.z + dz) % self.line, (self.y + dy) % LINE_Y


class Copies:
    def __init__(self, send, recv, local):
        self.send, self.recv, self.local = send, recv, local
        self.remotes, self.locals = 0, 0

    def reserve(self, count):
        self.remotes += count
        return self.remotes - count

    def remote(self, src, dst, device):
        return self.remote_at(self.reserve(1), src, dst, device)

    def remote_at(self, i, src, dst, device):
        return pltpu.make_async_remote_copy(
            src_ref=src,
            dst_ref=dst,
            send_sem=self.send.at[i],
            recv_sem=self.recv.at[i],
            device_id=device,
            device_id_type=MESH,
        )

    def inside(self, src, dst):
        i = self.locals
        self.locals += 1
        return pltpu.make_async_copy(src, dst, self.local.at[i])


def greet(place):
    barrier = pltpu.get_barrier_semaphore()
    partners = [place.other_core(), place.other_plane()]
    for dz, dy in place.plane_offsets():
        z, y = place.shifted(dz, dy)
        partners.append(place.at(z, y, place.c, place.x))
    for partner in partners:
        pl.semaphore_signal(barrier, inc=1, device_id=partner, device_id_type=MESH)
    pl.semaphore_wait(barrier, len(partners))


TOKEN_CHUNKS = 2


class TokenGather:
    def __init__(self, place, copies, own, whole):
        self.place, self.copies, self.whole = place, copies, whole
        c, chip, z, y = place.c, place.chip, place.z, place.y
        rows = own.shape[1]
        block = whole.at[tile(chip * CORES + c, rows)]
        self.first = copies.remote(own.at[1 - c], block, place.other_core())
        self.mine = copies.inside(own.at[c], block)
        self.size = CORES * rows // TOKEN_CHUNKS
        self.last = last = place.line - 1
        up = place.at(jnp.minimum(z + 1, last), y, c, place.x)
        down = place.at(jnp.maximum(z - 1, 0), y, c, place.x)
        over = place.other_y()
        chunks = range(TOKEN_CHUNKS)
        self.ups = [[self.copy(z - j, ch, up) for ch in chunks] for j in range(last)]
        self.downs = [[self.copy(z + j, ch, down) for ch in chunks] for j in range(last)]
        self.over_own = [self.copy(z, ch, over) for ch in chunks]
        self.over_ups = [[self.copy(z - 1 - j, ch, over) for ch in chunks] for j in range(last)]
        self.over_downs = [[self.copy(z + 1 + j, ch, over) for ch in chunks] for j in range(last)]

    def copy(self, z, ch, device):
        chip = jnp.clip(z, 0, self.last) * LINE_Y + self.place.y
        chunk = self.whole.at[tile(chip * TOKEN_CHUNKS + ch, self.size)]
        return self.copies.remote(chunk, chunk, device)

    def start(self):
        self.mine.start()
        self.first.start()

    def spread(self, ch):
        if ch == 0:
            self.mine.wait()
            self.first.wait_recv()
        z = self.place.z
        pl.when(z < self.last)(lambda: self.ups[0][ch].start())
        pl.when(z > 0)(lambda: self.downs[0][ch].start())
        self.over_own[ch].start()

    def step(self, j, ch):
        z, last = self.place.z, self.last

        @pl.when(z - 1 - j >= 0)
        def _():
            self.ups[j][ch].wait_recv()
            if j + 1 < last:
                pl.when(z < last)(lambda: self.ups[j + 1][ch].start())
            self.over_ups[j][ch].start()

        @pl.when(z + 1 + j <= last)
        def _():
            self.downs[j][ch].wait_recv()
            if j + 1 < last:
                pl.when(z > 0)(lambda: self.downs[j + 1][ch].start())
            self.over_downs[j][ch].start()

    def finish(self):
        z, last = self.place.z, self.last
        for ch in range(TOKEN_CHUNKS):
            self.over_own[ch].wait_recv()
            for j in range(last):
                pl.when(z - 1 - j >= 0)(lambda: self.over_ups[j][ch].wait_recv())
                pl.when(z + 1 + j <= last)(lambda: self.over_downs[j][ch].wait_recv())

    def drain(self):
        z, last = self.place.z, self.last
        self.first.wait_send()
        for ch in range(TOKEN_CHUNKS):
            self.over_own[ch].wait_send()
            for j in range(last):
                pl.when((z - j >= 0) & (z < last))(lambda: self.ups[j][ch].wait_send())
                pl.when((z + j <= last) & (z > 0))(lambda: self.downs[j][ch].wait_send())
                pl.when(z - 1 - j >= 0)(lambda: self.over_ups[j][ch].wait_send())
                pl.when(z + 1 + j <= last)(lambda: self.over_downs[j][ch].wait_send())


class WeightGather:
    def __init__(self, place, copies, pieces, whole, columns=slice(None)):
        self.place = place
        group = 2 * place.c + place.x
        self.by_chip = []
        for dz, dy in place.plane_offsets():
            z, y = place.shifted(dz, dy)
            device = place.at(z, y, place.c, place.x)
            self.by_chip.append(
                [copies.remote(src, dst, device) for src, dst in pieces(z * LINE_Y + y, place.chip, group)]
            )
        self.kept = [copies.inside(src, dst) for src, dst in pieces(place.chip, place.chip, group)]
        mine = whole.at[:, group, :, columns]
        self.across = copies.remote(mine, mine, place.other_plane())
        pair = whole.at[:, pl.ds(2 * place.c, 2), :, columns]
        self.swap = copies.remote(pair, pair, place.other_core())

    def send(self, i):
        for copy in self.by_chip[i] + (self.kept if i == 0 else []):
            copy.start()

    def scatter(self):
        for i in range(len(self.by_chip)):
            self.send(i)

    def cross(self):
        for copy in self.kept:
            copy.wait()
        for copies in self.by_chip:
            for copy in copies:
                copy.wait_recv()
        self.across.start()

    def share(self):
        self.across.wait_recv()
        self.swap.start()

    def finish(self):
        self.swap.wait_recv()

    def drain(self):
        for copy in sum(self.by_chip, []) + [self.across, self.swap]:
            copy.wait_send()


NORM_PARTS = 2
DOWN_PARTS = "ab"
GATHER_ORDER = (
    "qkv 6",
    "up a 0",
    "up a 3",
    "qkv 0",
    "up b 2",
    "prepare hid",
    "up b 0",
    "small scatter",
    "hid spread 0",
    "qkv 5",
    "tables",
    "qkv 2",
    "small cross",
    "hid spread 1",
    "prepare cot",
    "hid 0 0",
    "hid 0 1",
    "small share",
    "up a 2",
    "down a 0",
    "out start",
    "hid 1 0",
    "small done",
    "up b 6",
    "down b 5",
    "qkv 1",
    "down a 3",
    "qkv 3",
    "up b 1",
    "hid 1 1",
    "hid 2 0",
    "qkv 4",
    "up a 4",
    "up b 3",
    "cot spread 0",
    "qkv cross",
    "down a 1",
    "hid 2 1",
    "down a 6",
    "up b 4",
    "up b 5",
    "down a 5",
    "down a 4",
    "cot 0 0",
    "up b cross",
    "hid done",
    "up a 5",
    "up a 1",
    "up a 6",
    "norm",
    "qkv share",
    "out share",
    "cot spread 1",
    "cot 1 0",
    "norm",
    "norm done",
    "up a cross",
    "cot 0 1",
    "down a 2",
    "down b 0",
    "project",
    "up a share",
    "up b share",
    "down b 4",
    "down b 6",
    "down b 1",
    "cot 2 0",
    "down a cross",
    "attend",
    "cot 1 1",
    "down b 2",
    "down b 3",
    "inner",
    "down a share",
    "cot 2 1",
    "down b cross",
    "cot done",
    "attended grads",
    "attention back",
    "down b share",
    "down grads",
)


def nn(left, right):
    return lax.dot_general(left, right, (((1,), (0,)), ((), ())), preferred_element_type=jnp.float32)


def tile(i, size):
    return pl.ds(pl.multiple_of(i * size, size), size)


def flat_rows(values):
    return values.reshape(-1, values.shape[-1])


GAIN_ONE, SHIFT_ONE, GAIN_TWO, SHIFT_TWO, OUT_BIAS, DOWN_BIAS, QKV_BIAS, UP_BIAS, SMALL_ROWS = (
    0,
    1,
    2,
    3,
    4,
    5,
    6,
    9,
    16,
)
LANES = 128


def lanes_of(shape):
    return lax.broadcasted_iota(jnp.int32, shape, len(shape) - 1)


def pack_parameters(vectors, tile_ref):
    half = LANES // 2
    ln1_gain, ln1_bias, ln2_gain, ln2_bias, out_bias, down_bias, qkv_bias, up_bias = [
        ref[...].astype(jnp.float32).reshape(1, -1) for ref in vectors
    ]
    tile_ref[...] = jnp.zeros_like(tile_ref)
    for row, values in (
        (GAIN_ONE, ln1_gain),
        (SHIFT_ONE, ln1_bias),
        (GAIN_TWO, ln2_gain),
        (SHIFT_TWO, ln2_bias),
        (OUT_BIAS, out_bias),
        (DOWN_BIAS, down_bias),
    ):
        tile_ref[row : row + 1, :half] = values
        tile_ref[row : row + 1, half:] = values
    tile_ref[QKV_BIAS : QKV_BIAS + 1, :] = qkv_bias[:, :LANES]
    tile_ref[QKV_BIAS + 1 : QKV_BIAS + 2, :half] = qkv_bias[:, LANES:]
    tile_ref[QKV_BIAS + 1 : QKV_BIAS + 2, half:] = qkv_bias[:, :half]
    tile_ref[QKV_BIAS + 2 : QKV_BIAS + 3, :] = qkv_bias[:, half:]
    tile_ref[UP_BIAS : UP_BIAS + 1, :] = up_bias[:, :LANES]
    tile_ref[UP_BIAS + 1 : UP_BIAS + 2, :] = up_bias[:, LANES:]


def position_tables(ctx_count, pairing, cosine, sine, key_pos):
    block_rows = cosine.shape[0] // (2 * ctx_count)
    half_rot = ROT // 2
    lane = lanes_of((block_rows, LANES))
    power = (lane % half_rot).astype(jnp.float32) * (2.0 / ROT)
    frequency = jnp.exp(power * -9.210340371976184)
    row = lax.broadcasted_iota(jnp.int32, (block_rows, LANES), 0)

    @pl.loop(0, ctx_count)
    def _(device):
        owned = pairing[device]
        for late in range(2):
            block = 2 * ctx_count - 1 - owned if late else owned
            where = (block * block_rows + row).astype(jnp.float32)
            angles = where * frequency
            at = tile(2 * device + late, block_rows)
            cosine[at, :] = jnp.where(lane < ROT, jnp.cos(angles), 1.0)
            sin = jnp.sin(angles)
            sine[at, :] = jnp.where(lane < half_rot, -sin, jnp.where(lane < ROT, sin, where))

    lane = lanes_of((8, LANES))
    per = LANES // (2 * block_rows)
    for first in range(0, ctx_count, per):
        block = jnp.zeros((8, LANES), jnp.int32)
        for device in range(per):
            owned = pairing[first + device]
            for late in range(2):
                value = 2 * ctx_count - 1 - owned if late else owned
                block = jnp.where(lane // block_rows == 2 * device + late, value, block)
        at = first * 2 * block_rows
        key_pos[:, at : at + LANES] = (block * block_rows + lane % block_rows).astype(jnp.float32)


def split_sequences(rows, own):
    for i in range(rows.shape[1]):
        own[i] = rows[:, i, :]


def assemble_small(place, small, vec, qkv_rows, qkv_bias, up_bias):
    chips, groups = small.shape[:2]
    low = lanes_of((1, LANES)) < LANES // 2
    for pair in range(chips * groups // 2):
        chip, group = pair // (groups // 2), pair % (groups // 2) * 2
        for row in range(6):
            a = small[chip, group, row : row + 1, :]
            b = small[chip, group + 1, row : row + 1, :]
            vec[row : row + 1, pair * LANES : (pair + 1) * LANES] = jnp.where(low, a, b)
        qkv_rows[3 * pair : 3 * pair + 1, :] = small[chip, group, QKV_BIAS : QKV_BIAS + 1, :]
        a = small[chip, group, QKV_BIAS + 1 : QKV_BIAS + 2, :]
        b = small[chip, group + 1, QKV_BIAS + 1 : QKV_BIAS + 2, :]
        qkv_rows[3 * pair + 1 : 3 * pair + 2, :] = jnp.where(low, a, b)
        qkv_rows[3 * pair + 2 : 3 * pair + 3, :] = small[chip, group + 1, QKV_BIAS + 2 : QKV_BIAS + 3, :]
    third = qkv_rows.shape[0] // 3
    per_head = HEAD // LANES
    for k in range(3):
        for u in range(per_head):
            at = (k * per_head + u) * LANES
            qkv_bias[0:1, at : at + LANES] = qkv_rows[pl.ds(k * third + place.chip * per_head + u, 1), :]
    for group in range(groups):
        for u in range(2):
            at = (group * 2 + u) * LANES
            row = UP_BIAS + u
            up_bias[0:1, at : at + LANES] = small[pl.ds(place.chip, 1), group, row : row + 1, :].reshape(1, LANES)


def norm_rows(start, count, hid, vec, norm_one, norm_two, stats):
    step = 128

    @pl.loop(0, count // step)
    def _(i):
        at = pl.ds(pl.multiple_of(start + i * step, step), step)
        x = hid[at, :].astype(jnp.float32)
        average = jnp.mean(x, axis=1, keepdims=True)
        centered = x - average
        scale = lax.rsqrt(jnp.mean(centered * centered, axis=1, keepdims=True) + LN_EPSILON)
        stats[at, 0:1] = average
        stats[at, 1:2] = scale
        xhat = centered * scale
        norm_one[at, :] = (xhat * vec[0:1, :] + vec[1:2, :]).astype(jnp.bfloat16)
        norm_two[at, :] = (xhat * vec[2:3, :] + vec[3:4, :]).astype(jnp.bfloat16)


def turned_half(values):
    half_rot = ROT // 2
    lane = lanes_of(values.shape)
    width = values.shape[-1]
    return jnp.where(
        lane < half_rot,
        pltpu.roll(values, width - half_rot, 1),
        jnp.where(lane < ROT, pltpu.roll(values, half_rot, 1), 0.0),
    )


def project(norm_one, weight, bias, cosine, sine, query, key, value):
    step = 256

    @pl.loop(0, norm_one.shape[0] // step)
    def _(i):
        at = tile(i, step)
        both = nn(norm_one[at, :], flat_rows(weight[...])) + bias[0:1, :]
        cos, sin = cosine[at, :], sine[at, :]
        for k, target in enumerate((query, key)):
            first = both[:, k * HEAD : k * HEAD + LANES]
            target[at, 0:LANES] = (first * cos + turned_half(first) * sin).astype(jnp.bfloat16)
            target[at, LANES:HEAD] = both[:, k * HEAD + LANES : (k + 1) * HEAD].astype(jnp.bfloat16)
        value[at, :] = both[:, 2 * HEAD :].astype(jnp.bfloat16)


def attend(query, key, value, sine, key_pos, attended, attended_low, probs, probs_low):
    step = 256

    @pl.loop(0, query.shape[0] // step)
    def _(i):
        at = tile(i, step)
        scores = contract_cols(query[at, :], key[...]) * HEAD**-0.5
        allowed = key_pos[0:1, :] <= sine[at, ROT : ROT + 1]
        scores = jnp.where(allowed, scores, VERY_LOW)
        highest = jnp.max(scores, axis=1, keepdims=True)
        weights = jnp.where(allowed, jnp.exp(scores - highest), 0.0)
        weights = weights / jnp.sum(weights, axis=1, keepdims=True)
        low = weights.astype(jnp.bfloat16)
        probs[at, :] = weights
        probs_low[at, :] = low
        total = nn(low, value[...])
        attended[at, :] = total
        attended_low[at, :] = total.astype(jnp.bfloat16)


def feed_inner(norm_two, weight, bias, activated, slope):
    step = 128

    @pl.loop(0, norm_two.shape[0] // step)
    def _(i):
        at = tile(i, step)
        inner = nn(norm_two[at, :], flat_rows(weight[...])) + bias[0:1, :]
        normal = 0.5 + 0.5 * lax.erf(inner * 0.5**0.5)
        activated[at, :] = (inner * normal).astype(jnp.bfloat16)
        density = (2.0 * jnp.pi) ** -0.5 * jnp.exp(-0.5 * inner * inner)
        slope[at, :] = normal + inner * density


def attended_grads(cot, weight, attended_grad):
    step = 256

    @pl.loop(0, cot.shape[0] // step)
    def _(i):
        at = tile(i, step)
        attended_grad[at, :] = contract_cols(cot[at, :], flat_rows(weight[...])).astype(jnp.bfloat16)


def attention_grads(
    query, key, value, cosine, sine, attended, attended_grad, probs, probs_low, score_grad, projected_grad
):
    step = 256
    scaling = HEAD**-0.5

    def put(at, k, grad):
        first = grad[:, 0:LANES]
        back = first * cosine[at, :] - turned_half(first) * sine[at, :]
        projected_grad[at, k * HEAD : k * HEAD + LANES] = back.astype(jnp.bfloat16)
        projected_grad[at, k * HEAD + LANES : (k + 1) * HEAD] = grad[:, LANES:].astype(jnp.bfloat16)

    @pl.loop(0, query.shape[0] // step)
    def _(i):
        at = tile(i, step)
        own = attended_grad[at, :]
        row_delta = jnp.sum(own.astype(jnp.float32) * attended[at, :], axis=1, keepdims=True)
        grad = (probs[at, :] * (contract_cols(own, value[...]) - row_delta)).astype(jnp.bfloat16)
        score_grad[at, :] = grad
        put(at, 0, nn(grad, key[...]) * scaling)

    @pl.loop(0, query.shape[0] // step)
    def _(i):
        at = tile(i, step)
        put(at, 1, contract_rows(score_grad[:, at], query[...]) * scaling)
        projected_grad[at, 2 * HEAD :] = contract_rows(probs_low[:, at], attended_grad[...]).astype(jnp.bfloat16)


def weight_grads(tokens, grads, result):
    chips, groups, rows = result.shape[:3]
    step = groups * rows

    @pl.loop(0, chips)
    def _(k):
        grad = contract_rows(tokens[:, tile(k, step)], grads[...]).astype(jnp.bfloat16)
        result[k] = grad.reshape(result.shape[1:])


def column_sums(values, result):
    step = 128
    result[...] = jnp.zeros_like(result)

    @pl.loop(0, values.shape[0] // step)
    def _(i):
        part = values[tile(i, step), :].astype(jnp.float32)
        result[...] += jnp.sum(part.reshape(-1, 8, values.shape[1]), axis=0)


def gather_kernel(
    ctx_count,
    hid_in,
    cot_in,
    ln1_gain_in,
    ln1_bias_in,
    ln2_gain_in,
    ln2_bias_in,
    out_bias_in,
    down_bias_in,
    qkv_bias_in,
    up_bias_in,
    qkv,
    up,
    down,
    out,
    pairing,
    hid_all,
    cot_all,
    qkv_all,
    up_all,
    down_all,
    out_all,
    small_all,
    attended_low_out,
    projected_grad_out,
    norm_two_out,
    activated_out,
    slope_out,
    norm_one_out,
    down_grad_out,
    vec_out,
    stats_out,
    hid_rows,
    cot_rows,
    hid,
    cot,
    ln1_gain,
    ln1_bias,
    ln2_gain,
    ln2_bias,
    out_bias,
    down_bias,
    qkv_bias_own,
    up_bias_own,
    small,
    hid_v,
    cot_v,
    qkv_v,
    up_v,
    out_v,
    small_v,
    cosine,
    sine,
    key_pos,
    vec,
    qkv_rows,
    qkv_bias,
    up_bias,
    norm_one,
    norm_two,
    stats,
    query,
    key,
    value,
    attended,
    attended_low,
    probs,
    probs_low,
    activated,
    slope,
    attended_grad,
    score_grad,
    projected_grad,
    send,
    recv,
    local,
):
    place = Place(ctx_count)
    copies = Copies(send, recv, local)
    width = out.shape[1]
    head = qkv_all.shape[3] // 3
    part = up_all.shape[3]

    def qkv_pieces(to, row, group):
        return [
            (
                qkv.at[:, pl.ds(pl.multiple_of(k * width + to * head, head), head)],
                qkv_all.at[row, group, :, pl.ds(k * head, head)],
            )
            for k in range(3)
        ]

    def part_gather(source, whole, first, size):
        columns = pl.ds(first, size)

        def pieces(to, row, group):
            given = pl.ds(pl.multiple_of(to * part + first, size), size)
            return [(source.at[:, given], whole.at[row, group, :, columns])]

        return WeightGather(place, copies, pieces, whole, columns)

    hid_g = TokenGather(place, copies, hid, hid_all)
    cot_g = TokenGather(place, copies, cot, cot_all)
    small_g = WeightGather(place, copies, lambda to, row, group: [(small, small_all.at[row, group])], small_all)
    qkv_g = WeightGather(place, copies, qkv_pieces, qkv_all)
    weights = {"qkv": qkv_g}
    for name, source, whole, letters in (("up", up, up_all, "ab"), ("down", down, down_all, DOWN_PARTS)):
        size = part // len(letters)
        for i, letter in enumerate(letters):
            weights[name + " " + letter] = part_gather(source, whole, i * size, size)
    group = 2 * place.c + place.x
    out_mine = copies.inside(out, out_all.at[group])
    out_across = copies.remote(out, out_all.at[group], place.other_plane())
    out_pair = out_all.at[pl.ds(2 * place.c, 2)]
    out_swap = copies.remote(out_pair, out_pair, place.other_core())
    loads = {
        name: copies.inside(src, dst)
        for name, src, dst in (
            ("hid rows", hid_in, hid_rows),
            ("cot rows", cot_in, cot_rows),
            ("small", small_all, small_v),
            ("hid", hid_all, hid_v),
            ("cot", cot_all, cot_v),
            ("qkv", qkv_all, qkv_v),
            ("up", up_all, up_v),
            ("out", out_all, out_v),
        )
    }
    stores = {
        name: copies.inside(src, dst)
        for name, src, dst in (
            ("vec", vec, vec_out),
            ("stats", stats, stats_out),
            ("attended_low", attended_low, attended_low_out),
            ("norm_two", norm_two, norm_two_out),
            ("activated", activated, activated_out),
            ("slope", slope, slope_out),
            ("projected_grad", projected_grad, projected_grad_out),
            ("norm_one", norm_one, norm_one_out),
            ("down_grad", up_v, down_grad_out),
        )
    }

    def fetch(name):
        loads[name].start()
        loads[name].wait()

    rows = hid_v.shape[0]
    normed = iter(range(NORM_PARTS))

    def norm_next():
        part_rows = rows // NORM_PARTS
        norm_rows(next(normed) * part_rows, part_rows, hid_v, vec, norm_one, norm_two, stats)

    def norm_done():
        stores["norm_one"].start()
        stores["norm_two"].start()
        stores["stats"].start()

    def small_done():
        small_g.finish()
        fetch("small")
        assemble_small(place, small_v, vec, qkv_rows, qkv_bias, up_bias)
        stores["vec"].start()

    def hid_done():
        hid_g.finish()
        fetch("hid")

    def project_all():
        qkv_g.finish()
        fetch("qkv")
        project(norm_one, qkv_v, qkv_bias, cosine, sine, query, key, value)

    def attend_all():
        attend(query, key, value, sine, key_pos, attended, attended_low, probs, probs_low)
        stores["attended_low"].start()

    def inner_all():
        weights["up a"].finish()
        weights["up b"].finish()
        fetch("up")
        feed_inner(norm_two, up_v, up_bias, activated, slope)
        stores["activated"].start()
        stores["slope"].start()

    def out_start():
        out_mine.start()
        out_across.start()

    def out_share():
        out_mine.wait()
        out_across.wait_recv()
        out_swap.start()

    def cot_done():
        cot_g.finish()
        loads["cot"].start()
        out_swap.wait_recv()
        fetch("out")
        loads["cot"].wait()

    def out_grads():
        attended_grads(cot_v, out_v, attended_grad)

    def down_grads():
        weight_grads(cot_v, activated, up_v)
        stores["down_grad"].start()

    def attention_back():
        attention_grads(
            query, key, value, cosine, sine, attended, attended_grad, probs, probs_low, score_grad, projected_grad
        )
        stores["projected_grad"].start()

    steps = {
        "tables": lambda: position_tables(ctx_count, pairing, cosine, sine, key_pos),
        "small cross": small_g.cross,
        "small share": small_g.share,
        "small done": small_done,
        "out start": out_start,
        "out share": out_share,
        "hid done": hid_done,
        "norm": norm_next,
        "norm done": norm_done,
        "project": project_all,
        "attend": attend_all,
        "inner": inner_all,
        "cot done": cot_done,
        "attended grads": out_grads,
        "down grads": down_grads,
        "attention back": attention_back,
    }
    for ch in range(TOKEN_CHUNKS):
        for name, gather in (("hid", hid_g), ("cot", cot_g)):
            steps["%s spread %d" % (name, ch)] = functools.partial(gather.spread, ch)
            for j in range(place.line - 1):
                steps["%s %d %d" % (name, j, ch)] = functools.partial(gather.step, j, ch)
    for name, gather in weights.items():
        for i in range(len(gather.by_chip)):
            steps["%s %d" % (name, i)] = functools.partial(gather.send, i)
        steps[name + " cross"] = gather.cross
        steps[name + " share"] = gather.share

    vectors = (ln1_gain, ln1_bias, ln2_gain, ln2_bias, out_bias, down_bias, qkv_bias_own, up_bias_own)
    vectors_in = (
        ln1_gain_in,
        ln1_bias_in,
        ln2_gain_in,
        ln2_bias_in,
        out_bias_in,
        down_bias_in,
        qkv_bias_in,
        up_bias_in,
    )
    vector_loads = [copies.inside(src, dst) for src, dst in zip(vectors_in, vectors)]
    loads["hid rows"].start()
    for load in vector_loads:
        load.start()
    loads["cot rows"].start()
    greet(place)

    def prepare_hid():
        loads["hid rows"].wait()
        split_sequences(hid_rows, hid)
        hid_g.start()

    def prepare_cot():
        loads["cot rows"].wait()
        split_sequences(cot_rows, cot)
        cot_g.start()

    def prepare_small():
        for load in vector_loads:
            load.wait()
        pack_parameters(vectors, small)
        small_g.scatter()

    steps["prepare hid"] = prepare_hid
    steps["prepare cot"] = prepare_cot
    steps["small scatter"] = prepare_small
    for name in GATHER_ORDER:
        steps[name]()
    for letter in DOWN_PARTS:
        weights["down " + letter].finish()
    for store in stores.values():
        store.wait()
    for gather in [hid_g, cot_g, small_g] + list(weights.values()):
        gather.drain()
    out_across.wait_send()
    out_swap.wait_send()


def gather_all(ctx_count, hid, cot, vectors, qkv, up, down, out, pairing):
    f32, b16 = jnp.float32, jnp.bfloat16
    chips = ctx_count // CORES
    rows = qkv.shape[0]
    groups = CORES * 2
    tokens = ctx_count * hid.shape[0]
    width = out.shape[1]
    head3, part = qkv.shape[1] // chips, up.shape[1] // chips
    head = head3 // 3
    qkv_s = ((chips, groups, rows, head3), b16)
    part_s = ((chips, groups, rows, part), b16)
    out_s = ((groups, rows, width), b16)
    small = (SMALL_ROWS, LANES)
    small_s = ((chips, groups) + small, f32)
    wide_s, narrow_s = ((tokens, width), b16), ((tokens, head), b16)
    own_s = ((hid.shape[1], hid.shape[0], width), b16)
    results = [
        wide_s,
        wide_s,
        qkv_s,
        part_s,
        part_s,
        out_s,
        small_s,
        narrow_s,
        ((tokens, head3), b16),
        wide_s,
        ((tokens, part), b16),
        ((tokens, part), f32),
        wide_s,
        part_s,
        ((8, width), f32),
        ((tokens, LANES), f32),
    ]
    scratch = [
        (hid.shape, b16),
        (cot.shape, b16),
        own_s,
        own_s,
    ]
    scratch += [(vector.shape, b16) for vector in vectors]
    scratch += [
        (small, f32),
        wide_s,
        wide_s,
        qkv_s,
        part_s,
        out_s,
        small_s,
        ((tokens, LANES), f32),
        ((tokens, LANES), f32),
        ((8, tokens), f32),
        ((8, width), f32),
        ((3 * width // LANES, LANES), f32),
        ((8, head3), f32),
        ((8, part), f32),
        wide_s,
        wide_s,
        ((tokens, LANES), f32),
        narrow_s,
        narrow_s,
        narrow_s,
        ((tokens, head), f32),
        narrow_s,
        ((tokens, tokens), f32),
        ((tokens, tokens), b16),
        ((tokens, part), b16),
        ((tokens, part), f32),
        narrow_s,
        ((tokens, tokens), b16),
        ((tokens, head3), b16),
    ]
    operands = (hid, cot, *vectors, qkv, up, down, out, pairing)
    anywhere = pl.BlockSpec(memory_space=pl.ANY)
    return pl.pallas_call(
        lambda *refs: gather_kernel(ctx_count, *refs),
        out_shape=[jax.ShapeDtypeStruct(*shape) for shape in results],
        in_specs=[anywhere] * (len(operands) - 1) + [pl.BlockSpec(memory_space=pltpu.SMEM)],
        out_specs=[anywhere] * len(results),
        scratch_shapes=[pltpu.VMEM(*shape) for shape in scratch]
        + [
            pltpu.SemaphoreType.DMA((176,)),
            pltpu.SemaphoreType.DMA((176,)),
            pltpu.SemaphoreType.DMA((48,)),
        ],
        compiler_params=pltpu.CompilerParams(
            collective_id=0, has_side_effects=True, vmem_limit_bytes=VMEM_BYTES
        ),
        name="gather_all",
    )(*operands)


def add_rows(total, other):
    step = 64

    @pl.loop(0, total.shape[0] // step)
    def _(i):
        at = tile(i, step)
        both = total[at, :].astype(jnp.float32) + other[at, :].astype(jnp.float32)
        total[at, :] = both.astype(total.dtype)


class GradScatter:
    def __init__(self, place, copies, partial, kept, from_core, from_plane, result, columns=None):
        self.place = place
        c, x, chip = place.c, place.x, place.chip
        self.kept, self.from_core, self.from_plane = kept, from_core, from_plane
        self.columns = cols = slice(0, kept.shape[3]) if columns is None else columns
        self.load = None
        given = partial.at[:, :, :, cols]
        if partial.shape != kept.shape:
            self.load = copies.inside(partial.at[:, pl.ds(2 * c, 2), :, cols], kept.at[:, :, :, cols])
            given = partial.at[:, pl.ds(2 * (1 - c), 2), :, cols]
        self.swap = copies.remote(given, from_core.at[:, :, :, cols], place.other_core())
        self.across = copies.remote(
            kept.at[:, 1 - x, :, cols], from_plane.at[:, :, cols], place.other_plane()
        )
        self.scattered = []
        for dz, dy in place.plane_offsets():
            z, y = place.shifted(dz, dy)
            self.scattered.append(
                copies.remote(
                    kept.at[z * LINE_Y + y, x, :, cols], result.at[chip, :, cols], place.at(z, y, c, x)
                )
            )
        self.own = copies.inside(kept.at[chip, x, :, cols], result.at[chip, :, cols])

    def start(self):
        if self.load is not None:
            self.load.start()
        self.swap.start()

    def cross(self):
        if self.load is not None:
            self.load.wait()
        self.swap.wait_recv()
        x = self.place.x
        self.add(1 - x, self.from_core.at[:, 1 - x])
        self.across.start()
        self.add(x, self.from_core.at[:, x])

    def add(self, x, other):
        cols = self.columns

        @pl.loop(0, self.kept.shape[0])
        def _(k):
            both = self.kept[k, x, :, cols].astype(jnp.float32) + other[k, :, cols].astype(jnp.float32)
            self.kept[k, x, :, cols] = both.astype(self.kept.dtype)

    def scatter(self):
        self.across.wait_recv()
        self.add(self.place.x, self.from_plane)
        for copy in self.scattered + [self.own]:
            copy.start()

    def finish(self):
        self.own.wait()
        for copy in self.scattered:
            copy.wait_recv()

    def drain(self, swapped=False):
        for copy in self.scattered + [self.across] + ([] if swapped else [self.swap]):
            copy.wait_send()


def out_weight_grads(place, attended_low, cot, kept, given):
    step = 512

    @pl.loop(0, cot.shape[1] // step)
    def _(i):
        at = tile(i, step)
        grad = contract_rows(attended_low[...], cot[:, at]).astype(jnp.bfloat16)
        grad = grad.reshape((2,) + kept.shape[:2] + (step,))
        kept[:, :, at] = jnp.where(place.c == 0, grad[0], grad[1])
        given[:, :, at] = jnp.where(place.c == 0, grad[1], grad[0])


def weight_grads_by_core(place, tokens, grads, kept, given, columns):
    chips, half, rows = kept.shape[:3]
    step = 2 * half * rows

    @pl.loop(0, chips)
    def _(k):
        grad = contract_rows(tokens[:, tile(k, step)], grads[:, columns]).astype(jnp.bfloat16)
        grad = grad.reshape(2, half, rows, grad.shape[1])
        kept[k, :, :, columns] = jnp.where(place.c == 0, grad[0], grad[1])
        given[k, :, :, columns] = jnp.where(place.c == 0, grad[1], grad[0])


class TokenScatter:
    def __init__(self, place, copies, part, from_y, slots, total, result):
        self.place, self.copies = place, copies
        z, y, c, x = place.z, place.y, place.c, place.x
        self.part, self.from_y, self.slots, self.total = part, from_y, slots, total
        self.line = place.line
        self.last = last = self.line - 1
        self.rows = total.shape[0]
        self.size = self.rows // TOKEN_CHUNKS
        count = self.line * TOKEN_CHUNKS
        self.over_base = copies.reserve(count)
        self.up_base = copies.reserve(count)
        self.down_base = copies.reserve(count)
        self.above = place.at(jnp.minimum(z + 1, last), y, c, x)
        self.below = place.at(jnp.maximum(z - 1, 0), y, c, x)
        half = self.rows // CORES
        self.swap = copies.remote(total.at[tile(1 - c, half)], result.at[c], place.other_core())
        self.own = copies.inside(total.at[tile(c, half)], result.at[c])

    def order(self, i):
        last = self.last
        chosen = 0
        for z in range(self.line):
            far = sorted(range(self.line), key=lambda k: (-abs(k - z), min(k, last - k)))
            chosen = jnp.where(self.place.z == z, far[i], chosen)
        return chosen

    def chunk(self, ref, k, ch):
        return ref.at[tile(k * TOKEN_CHUNKS + ch, self.size)]

    def held(self, k, ch):
        return self.chunk(self.part, k * LINE_Y + self.place.y, ch)

    def copy(self, base, k, ch, src, dst, device):
        return self.copies.remote_at(base + k * TOKEN_CHUNKS + ch, src, dst, device)

    def over(self, k, ch):
        src = self.chunk(self.part, k * LINE_Y + 1 - self.place.y, ch)
        return self.copy(self.over_base, k, ch, src, self.chunk(self.from_y, k, ch), self.place.other_y())

    def up(self, k, ch):
        return self.copy(self.up_base, k, ch, self.held(k, ch), self.chunk(self.slots, k, ch), self.above)

    def down(self, k, ch):
        slot = jnp.where(self.place.z - 1 == k, self.line, k)
        return self.copy(self.down_base, k, ch, self.held(k, ch), self.chunk(self.slots, slot, ch), self.below)

    def send_over(self, k):
        for ch in range(TOKEN_CHUNKS):
            self.over(k, ch).start()

    def combine(self, k, ch):
        self.over(k, ch).wait_recv()
        add_rows(self.held(k, ch), self.chunk(self.from_y, k, ch))

    def step(self, i, ch):
        z = self.place.z
        k = self.order(i)
        self.combine(k, ch)

        @pl.when(k > z)
        def _():
            @pl.when(z > 0)
            def _():
                self.up(k, ch).wait_recv()
                add_rows(self.held(k, ch), self.chunk(self.slots, k, ch))

            self.up(k, ch).start()

        @pl.when(k < z)
        def _():
            @pl.when(z < self.last)
            def _():
                self.down(k, ch).wait_recv()
                add_rows(self.held(k, ch), self.chunk(self.slots, k, ch))

            self.down(k, ch).start()

    def reduce(self):
        z, y, last = self.place.z, self.place.y, self.last
        step = 64
        for ch in range(TOKEN_CHUNKS):
            self.combine(z, ch)
            pl.when(z > 0)(lambda: self.up(z, ch).wait_recv())
            pl.when(z < last)(lambda: self.down(z, ch).wait_recv())

        @pl.loop(0, self.rows // step)
        def _(i):
            at = tile((z * LINE_Y + y) * (self.rows // step) + i, step)
            self.total[tile(i, step), :] = self.part[at, :].astype(jnp.float32)

        def add(slot):
            @pl.loop(0, self.rows // step)
            def _(i):
                at = tile(slot * (self.rows // step) + i, step)
                self.total[tile(i, step), :] += self.slots[at, :].astype(jnp.float32)

        pl.when(z > 0)(lambda: add(z))
        pl.when(z < last)(lambda: add(last + 1))
        self.swap.start()
        self.own.start()

    def finish(self):
        self.swap.wait_recv()

    def drain(self):
        z = self.place.z
        for k in range(self.line):
            for ch in range(TOKEN_CHUNKS):
                self.over(k, ch).wait_send()
                pl.when(z < k)(lambda: self.up(k, ch).wait_send())
                pl.when(z > k)(lambda: self.down(k, ch).wait_send())


def output_part(scatter, i, attended_low, activated, out_weight, down_weight):
    k = scatter.order(i)
    at = tile(k, LINE_Y * scatter.rows)
    rows = nn(attended_low[at, :], flat_rows(out_weight[...]))
    rows = rows + contract_cols(activated[at, :], flat_rows(down_weight[...]))
    scatter.part[at, :] = rows.astype(scatter.part.dtype)
    scatter.send_over(k)


def inner_grads(cot, down_weight, slope, slope_loads, inner_grad):
    step = slope.shape[1]
    for i, load in enumerate(slope_loads):
        load.wait()
        at = slice(i * step, (i + 1) * step)
        grad = nn(cot[at, :], flat_rows(down_weight[...])) * slope[i % 2]
        inner_grad[at, :] = grad.astype(jnp.bfloat16)
        if i + 2 < len(slope_loads):
            slope_loads[i + 2].start()


def hidden_part(scatter, i, inner_grad, up_weight, projected_grad, qkv_weight, hid, stats, vec, sums):
    def by_eight(values):
        return jnp.sum(values.reshape(-1, 8, values.shape[1]), axis=0)

    k = scatter.order(i)

    @pl.loop(0, LINE_Y)
    def _(y):
        at = tile(k * LINE_Y + y, scatter.rows)
        one = contract_cols(projected_grad[at, :], flat_rows(qkv_weight[...]))
        two = contract_cols(inner_grad[at, :], flat_rows(up_weight[...]))
        xhat = (hid[at, :].astype(jnp.float32) - stats[at, 0:1]) * stats[at, 1:2]
        sums[0] += by_eight(one * xhat)
        sums[1] += by_eight(one)
        sums[2] += by_eight(two * xhat)
        sums[3] += by_eight(two)
        rows = one * vec[0:1, :] + two * vec[2:3, :]
        scatter.part[at, :] = rows.astype(scatter.part.dtype)

    scatter.send_over(k)


COT_SUM, UP_SUM, QKV_SUM = 4, 5, 7


def pack_small(place, sums, cot_sum, up_sum, qkv_sum, qkv_rows, tiles):
    chips, groups = tiles.shape[:2]
    tiles[...] = jnp.zeros_like(tiles)
    qkv_rows[...] = jnp.zeros_like(qkv_rows)
    qkv_total = jnp.sum(qkv_sum[...], axis=0, keepdims=True)
    up_total = jnp.sum(up_sum[...], axis=0, keepdims=True)
    third = qkv_rows.shape[0] // 3
    per_head = HEAD // LANES
    for k in range(3):
        for u in range(per_head):
            at = (k * per_head + u) * LANES
            qkv_rows[pl.ds(k * third + place.chip * per_head + u, 1), :] = qkv_total[:, at : at + LANES]
    first = jnp.where(place.chip == 0, 1.0, 0.0)
    norm_sums = [jnp.sum(sums[row], axis=0, keepdims=True) for row in range(4)]
    norm_sums.append(jnp.sum(cot_sum[...], axis=0, keepdims=True) * first)
    for pair in range(chips * groups // 2):
        chip, group = pair // (groups // 2), pair % (groups // 2) * 2
        at = slice(pair * LANES, (pair + 1) * LANES)
        for g in (group, group + 1):
            for row in range(5):
                tiles[chip, g, row : row + 1, :] = norm_sums[row][:, at]
            tiles[chip, g, QKV_SUM : QKV_SUM + 3, :] = qkv_rows[3 * pair : 3 * pair + 3, :]
    for group in range(groups):
        for u in range(2):
            at = (group * 2 + u) * LANES
            row = UP_SUM + u
            values = up_total[:, at : at + LANES].reshape(1, 1, LANES)
            tiles[pl.ds(place.chip, 1), group, row : row + 1, :] = values


SCATTER_ORDER = (
    "down a swap",
    "outs tile 0",
    "outs tile 1",
    "qkv grads",
    "outs 0 0",
    "down a cross",
    "outs tile 2",
    "down b swap",
    "outs 0 1",
    "out grads",
    "outs 1 0",
    "down b cross",
    "qkv swap",
    "down a scatter",
    "outs tile 3",
    "out swap",
    "inner",
    "outs 1 1",
    "outs 2 0",
    "qkv cross",
    "up a grad",
    "down b scatter",
    "up b grad",
    "hid tile 0",
    "up b swap",
    "outs 2 1",
    "out cross",
    "hid tile 1",
    "hid tile 2",
    "qkv scatter",
    "hid 0 0",
    "up a swap",
    "up b cross",
    "up sum",
    "hid 0 1",
    "hid tile 3",
    "pack",
    "hid 1 0",
    "small swap",
    "out finish",
    "small cross",
    "up b scatter",
    "hid 1 1",
    "hid 2 0",
    "outs reduce",
    "up a cross",
    "hid 2 1",
    "small scatter",
    "up a scatter",
    "hid reduce",
)


def scatter_kernel(
    ctx_count,
    hid_in,
    cot_in,
    qkv_in,
    up_in,
    down_in,
    out_in,
    attended_low_in,
    projected_grad_in,
    norm_two_in,
    activated_in,
    slope_in,
    stats_in,
    vec_in,
    norm_one_in,
    down_grad,
    small_result,
    qkv_result,
    up_result,
    down_result,
    out_grad_result,
    out_result,
    hid_result,
    wide,
    weight,
    slope,
    act,
    attended_low,
    out_weight,
    qkv_weight,
    projected_grad,
    stats,
    vec,
    qkv_sum,
    cot_sum,
    up_sum,
    sums,
    qkv_rows,
    tiles,
    small_kept,
    small_core,
    small_plane,
    qkv_kept,
    qkv_core,
    qkv_plane,
    up_kept,
    up_core,
    up_plane,
    down_kept,
    down_core,
    down_plane,
    out_kept,
    out_core,
    out_plane,
    out_part,
    out_from_y,
    out_slots,
    hid_part,
    hid_from_y,
    hid_slots,
    total,
    out_given,
    send,
    recv,
    local,
):
    place = Place(ctx_count)
    copies = Copies(send, recv, local)
    c, x = place.c, place.x
    qkv_given = up_kept.at[:, :, :, : qkv_kept.shape[3]]
    half = up_kept.shape[3] // 2
    halves = {" a": slice(0, half), " b": slice(half, 2 * half)}
    grads = {
        "qkv": GradScatter(place, copies, qkv_given, qkv_kept, qkv_core, qkv_plane, qkv_result),
        "small": GradScatter(place, copies, tiles, small_kept, small_core, small_plane, small_result),
    }
    for name, cols in halves.items():
        grads["down" + name] = GradScatter(
            place, copies, down_grad, down_kept, down_core, down_plane, down_result, cols
        )
        grads["up" + name] = GradScatter(place, copies, down_core, up_kept, up_core, up_plane, up_result, cols)
    outs_s = TokenScatter(place, copies, out_part, out_from_y, out_slots, total, out_result)
    hid_s = TokenScatter(place, copies, hid_part, hid_from_y, hid_slots, total, hid_result)
    out_swap = copies.remote(out_given, out_core, place.other_core())
    out_across = copies.remote(out_kept.at[1 - x], out_plane, place.other_plane())
    out_own = copies.inside(out_kept.at[x], out_grad_result)
    loads = {
        name: copies.inside(src, dst)
        for name, src, dst in (
            ("activated", activated_in, act),
            ("attended_low", attended_low_in, attended_low),
            ("out", out_in, out_weight),
            ("down", down_in, weight),
            ("cot", cot_in, wide),
            ("norm_two", norm_two_in, wide),
            ("qkv", qkv_in, qkv_weight),
            ("projected_grad", projected_grad_in, projected_grad),
            ("stats", stats_in, stats),
            ("vec", vec_in, vec),
            ("norm_one", norm_one_in, wide),
            ("up", up_in, weight),
            ("hid", hid_in, wide),
        )
    }
    early = ("activated", "attended_low", "out", "down", "projected_grad", "norm_one", "qkv", "stats", "vec")

    def out_cross():
        out_swap.wait_recv()
        for k in range(2):
            add_rows(out_kept.at[k], out_core.at[k])
        out_across.start()

    def out_finish():
        out_across.wait_recv()
        add_rows(out_kept.at[x], out_plane)
        out_own.start()

    step = slope.shape[1]
    slope_loads = [
        copies.inside(slope_in.at[pl.ds(i * step, step)], slope.at[i % 2]) for i in range(slope_in.shape[0] // step)
    ]
    waited = set()

    def need(*names):
        for name in names:
            if name not in waited:
                waited.add(name)
                loads[name].wait()

    def output_tile(i):
        need("activated", "attended_low", "out", "down")
        output_part(outs_s, i, attended_low, act, out_weight, weight)

    def inner_all():
        need("cot")
        inner_grads(wide, weight, slope, slope_loads, act)
        loads["up"].start()
        loads["norm_two"].start()

    def qkv_grads():
        need("projected_grad", "norm_one")
        columns = slice(0, qkv_kept.shape[3])
        weight_grads_by_core(place, wide, projected_grad, qkv_kept, qkv_given, columns)
        loads["cot"].start()
        column_sums(projected_grad, qkv_sum)

    def out_grads():
        need("attended_low", "cot")
        out_weight_grads(place, attended_low, wide, out_kept, out_given)
        column_sums(wide, cot_sum)

    def up_half(name, last):
        if not last:
            grads["qkv"].swap.wait_send()
        need("norm_two")
        weight_grads_by_core(place, wide, act, up_kept, down_core, halves[name])
        if last:
            loads["hid"].start()

    def hidden_tile(i):
        if i == 0:
            need("qkv", "projected_grad", "stats", "vec", "up", "hid")
            sums[...] = jnp.zeros_like(sums)
        hidden_part(hid_s, i, act, weight, projected_grad, qkv_weight, wide, stats, vec, sums)

    def pack():
        pack_small(place, sums, cot_sum, up_sum, qkv_sum, qkv_rows, tiles)

    def hidden_reduce():
        outs_s.own.wait()
        outs_s.swap.wait_send()
        hid_s.reduce()

    steps = {
        "qkv grads": qkv_grads,
        "out grads": out_grads,
        "out swap": out_swap.start,
        "out cross": out_cross,
        "out finish": out_finish,
        "inner": inner_all,
        "up a grad": functools.partial(up_half, " a", False),
        "up b grad": functools.partial(up_half, " b", True),
        "up sum": lambda: column_sums(act, up_sum),
        "pack": pack,
        "outs reduce": outs_s.reduce,
        "hid reduce": hidden_reduce,
    }
    for name, scatter in grads.items():
        steps[name + " swap"] = scatter.start
        steps[name + " cross"] = scatter.cross
        steps[name + " scatter"] = scatter.scatter
    for i in range(outs_s.line):
        steps["outs tile %d" % i] = functools.partial(output_tile, i)
        steps["hid tile %d" % i] = functools.partial(hidden_tile, i)
    for j in range(outs_s.last):
        for ch in range(TOKEN_CHUNKS):
            steps["outs %d %d" % (j, ch)] = functools.partial(outs_s.step, j, ch)
            steps["hid %d %d" % (j, ch)] = functools.partial(hid_s.step, j, ch)

    for name in early:
        loads[name].start()
    slope_loads[0].start()
    slope_loads[1].start()
    greet(place)
    for name in SCATTER_ORDER:
        steps[name]()
    for scatter in list(grads.values()) + [outs_s, hid_s]:
        scatter.finish()
    out_own.wait()
    hid_s.own.wait()
    hid_s.swap.wait_send()
    for name, scatter in grads.items():
        scatter.drain(name == "qkv")
    outs_s.drain()
    hid_s.drain()
    out_swap.wait_send()
    out_across.wait_send()


def scatter_all(ctx_count, local_rows, operands):
    f32, b16 = jnp.float32, jnp.bfloat16
    hid, _, w_qkv, w_up, _, w_out = operands[:6]
    chips, groups, rows, head3 = w_qkv.shape
    part = w_up.shape[3]
    tokens, width = hid.shape
    line = chips // LINE_Y
    small = (SMALL_ROWS, LANES)
    token = (CORES, local_rows, width)
    results = [
        ((chips,) + small, f32),
        ((chips, rows, head3), b16),
        ((chips, rows, part), b16),
        ((chips, rows, part), b16),
        ((rows, width), b16),
        (token, f32),
        (token, f32),
    ]
    scratch = [
        ((tokens, width), b16),
        (w_up.shape, b16),
        ((2, 256, part), f32),
        ((tokens, part), b16),
        ((tokens, head3 // 3), b16),
        (w_out.shape, b16),
        (w_qkv.shape, b16),
        ((tokens, head3), b16),
        ((tokens, LANES), f32),
        ((8, width), f32),
        ((8, head3), f32),
        ((8, width), f32),
        ((8, part), f32),
        ((4, 8, width), f32),
        ((3 * width // LANES, LANES), f32),
        ((chips, groups) + small, f32),
    ]
    for shape, dtype in ((small, f32), ((rows, head3), b16), ((rows, part), b16), ((rows, part), b16)):
        scratch += [((chips, 2) + shape, dtype)] * 2 + [((chips,) + shape, dtype)]
    scratch += [((2, rows, width), b16)] * 2 + [((rows, width), b16)]
    chip_rows = CORES * local_rows
    for _ in range(2):
        scratch += [
            ((tokens, width), b16),
            ((line * chip_rows, width), b16),
            (((line + 1) * chip_rows, width), b16),
        ]
    scratch += [((chip_rows, width), f32), ((2, rows, width), b16)]
    anywhere = pl.BlockSpec(memory_space=pl.ANY)
    return pl.pallas_call(
        lambda *refs: scatter_kernel(ctx_count, *refs),
        out_shape=[jax.ShapeDtypeStruct(*shape) for shape in results],
        in_specs=[anywhere] * len(operands),
        out_specs=[anywhere] * len(results),
        scratch_shapes=[pltpu.VMEM(*shape) for shape in scratch]
        + [
            pltpu.SemaphoreType.DMA((128,)),
            pltpu.SemaphoreType.DMA((128,)),
            pltpu.SemaphoreType.DMA((48,)),
        ],
        compiler_params=pltpu.CompilerParams(
            collective_id=1, has_side_effects=True, vmem_limit_bytes=VMEM_BYTES
        ),
        name="scatter_all",
    )(*operands)


def finish_kernel(
    qkv_in,
    up_in,
    down_in,
    out_in,
    out_rows_in,
    hid_rows_in,
    hidden_in,
    cotangent_in,
    small,
    vec,
    ln1_gain,
    ln1_bias,
    qkv_bias,
    out_bias,
    ln2_gain,
    ln2_bias,
    up_bias,
    down_bias,
    output_out,
    grad_hidden_out,
    qkv_out,
    out_out,
    up_out,
    down_out,
    qkv_rows,
    up_rows,
    down_rows,
    out_piece,
    out_rows,
    hid_rows,
    hidden,
    cotangent,
    output,
    grad_hidden,
    qkv,
    out,
    up,
    down,
    load_sems,
    store_sems,
):
    f32 = jnp.float32
    given = (up_in, down_in, qkv_in, out_in, out_rows_in, hid_rows_in, hidden_in, cotangent_in)
    held = (up_rows, down_rows, qkv_rows, out_piece, out_rows, hid_rows, hidden, cotangent)
    loads = [pltpu.make_async_copy(src, dst, load_sems.at[i]) for i, (src, dst) in enumerate(zip(given, held))]
    made = (up, down, qkv, out, output, grad_hidden)
    asked = (up_out, down_out, qkv_out, out_out, output_out, grad_hidden_out)
    stores = [pltpu.make_async_copy(src, dst, store_sems.at[i]) for i, (src, dst) in enumerate(zip(made, asked))]
    for load in loads:
        load.start()

    total = jnp.sum(small[...], axis=0)
    half = LANES // 2
    odd = lax.axis_index("fsdp") == 1
    halves = jnp.where(odd, total[: COT_SUM + 1, half:], total[: COT_SUM + 1, :half])
    for row, ref in enumerate((ln1_gain, ln1_bias, ln2_gain, ln2_bias, out_bias)):
        ref[...] = halves[row]
    down_bias[...] = halves[COT_SUM]
    for u in range(2):
        up_bias[u * LANES : (u + 1) * LANES] = total[UP_SUM + u]
    first, middle, last = [total[QKV_SUM + u : QKV_SUM + u + 1] for u in range(3)]
    even_row = jnp.concatenate([first, middle[:, :half]], axis=1)
    odd_row = jnp.concatenate([middle[:, half:], last], axis=1)
    qkv_bias[...] = jnp.where(odd, odd_row, even_row)[0]

    chips = up_rows.shape[0]
    for i, rows, made_ref in ((0, up_rows, up), (1, down_rows, down)):
        loads[i].wait()
        size = rows.shape[2]
        for k in range(chips):
            made_ref[:, k * size : (k + 1) * size] = rows[k].astype(f32)
        stores[i].start()
    loads[2].wait()
    third = qkv.shape[1] // 3
    for k in range(chips):
        for t in range(3):
            at = t * third + k * HEAD
            qkv[:, at : at + HEAD] = qkv_rows[k, :, t * HEAD : (t + 1) * HEAD].astype(f32)
    stores[2].start()
    loads[3].wait()
    out[...] = out_piece[...].astype(f32)
    stores[3].start()

    for load in loads[4:]:
        load.wait()
    bias = vec[OUT_BIAS : OUT_BIAS + 1, :] + vec[DOWN_BIAS : DOWN_BIAS + 1, :]
    step = 32

    @pl.loop(0, hidden.shape[0] // step)
    def _(i):
        at = tile(i, step)
        both, grads = [], []
        for s in range(hidden.shape[1]):
            x = hidden[at, s, :].astype(f32)
            both.append(x + out_rows[s, at, :] + bias)
            average = jnp.mean(x, axis=1, keepdims=True)
            centered = x - average
            scale = lax.rsqrt(jnp.mean(centered * centered, axis=1, keepdims=True) + LN_EPSILON)
            xhat = centered * scale
            e = hid_rows[s, at, :]
            slope = jnp.mean(e * xhat, axis=1, keepdims=True)
            back = scale * (e - jnp.mean(e, axis=1, keepdims=True) - xhat * slope)
            grads.append(cotangent[at, s, :].astype(f32) + back)
        output[at] = jnp.stack(both, axis=1).astype(output.dtype)
        grad_hidden[at] = jnp.stack(grads, axis=1)

    stores[4].start()
    stores[5].start()
    for store in stores:
        store.wait()


def finish_all(qkv_rows, up_rows, down_rows, out_sum, out_rows, hid_rows, hidden, cotangent, small, vec):
    f32 = jnp.float32
    rows, width = out_sum.shape
    part, head3 = up_rows.shape[0] * up_rows.shape[2], qkv_rows.shape[0] * qkv_rows.shape[2]
    vectors = [rows, rows, 3 * rows, rows, rows, rows, part // width * rows, rows]
    big = [
        (hidden.shape, hidden.dtype),
        (hidden.shape, f32),
        ((rows, head3), f32),
        ((rows, width), f32),
        ((rows, part), f32),
        ((rows, part), f32),
    ]
    operands = (qkv_rows, up_rows, down_rows, out_sum, out_rows, hid_rows, hidden, cotangent)
    anywhere, held = pl.BlockSpec(memory_space=pl.ANY), pl.BlockSpec(memory_space=pltpu.VMEM)
    return pl.pallas_call(
        finish_kernel,
        out_shape=[jax.ShapeDtypeStruct((n,), f32) for n in vectors]
        + [jax.ShapeDtypeStruct(*shape) for shape in big],
        in_specs=[anywhere] * len(operands) + [held, held],
        out_specs=[held] * len(vectors) + [anywhere] * len(big),
        scratch_shapes=[pltpu.VMEM(o.shape, o.dtype) for o in operands]
        + [pltpu.VMEM(*shape) for shape in big]
        + [pltpu.SemaphoreType.DMA((8,)), pltpu.SemaphoreType.DMA((8,))],
        compiler_params=pltpu.CompilerParams(vmem_limit_bytes=VMEM_BYTES),
        name="finish_all",
    )(*operands, small, vec)


def split_body(
    hidden,
    cotangent,
    pairing,
    ln1_gain,
    ln1_bias,
    qkv_weight,
    qkv_bias,
    out_weight,
    out_bias,
    ln2_gain,
    ln2_bias,
    up_weight,
    up_bias,
    down_weight,
    down_bias,
):
    ctx_count = lax.axis_size("ctx")
    (
        hid_all,
        cot_all,
        w_qkv,
        w_up,
        w_down,
        w_out,
        _,
        attended_low,
        projected_grad,
        norm_two,
        activated,
        slope,
        norm_one,
        grad_down,
        vec,
        stats,
    ) = gather_all(
        ctx_count,
        hidden,
        cotangent,
        (ln1_gain, ln1_bias, ln2_gain, ln2_bias, out_bias, down_bias, qkv_bias, up_bias),
        qkv_weight,
        up_weight,
        down_weight,
        out_weight,
        pairing,
    )
    small_sum, qkv_rows, up_rows, down_rows, out_sum, out_rows, hid_rows = scatter_all(
        ctx_count,
        hidden.shape[0],
        (
            hid_all,
            cot_all,
            w_qkv,
            w_up,
            w_down,
            w_out,
            attended_low,
            projected_grad,
            norm_two,
            activated,
            slope,
            stats,
            vec,
            norm_one,
            grad_down,
        ),
    )
    (
        grad_ln1_gain,
        grad_ln1_bias,
        grad_qkv_bias,
        grad_out_bias,
        grad_ln2_gain,
        grad_ln2_bias,
        grad_up_bias,
        grad_down_bias,
        output,
        grad_hidden,
        grad_qkv_weight,
        grad_out_weight,
        grad_up_weight,
        grad_down_weight,
    ) = finish_all(
        qkv_rows, up_rows, down_rows, out_sum, out_rows, hid_rows, hidden, cotangent, small_sum, vec
    )
    return (
        output,
        grad_hidden,
        grad_ln1_gain,
        grad_ln1_bias,
        grad_qkv_weight,
        grad_qkv_bias,
        grad_out_weight,
        grad_out_bias,
        grad_ln2_gain,
        grad_ln2_bias,
        grad_up_weight,
        grad_up_bias,
        grad_down_weight,
        grad_down_bias,
    )


def solution(mesh):
    body = split_body if split_fits(mesh) else general_body
    return jax.shard_map(
        body,
        mesh=mesh,
        in_specs=(
            P("ctx", "fsdp", None),
            P("ctx", "fsdp", None),
            P(),
            P(("ctx", "fsdp")),
            P(("ctx", "fsdp")),
            P(("ctx", "fsdp"), None),
            P(("ctx", "fsdp")),
            P(("ctx", "fsdp"), None),
            P(("ctx", "fsdp")),
            P(("ctx", "fsdp")),
            P(("ctx", "fsdp")),
            P(("ctx", "fsdp"), None),
            P(("ctx", "fsdp")),
            P(("ctx", "fsdp"), None),
            P(("ctx", "fsdp")),
        ),
        out_specs=(
            P("ctx", "fsdp", None),
            P("ctx", "fsdp", None),
            P(("ctx", "fsdp")),
            P(("ctx", "fsdp")),
            P(("ctx", "fsdp"), None),
            P(("ctx", "fsdp")),
            P(("ctx", "fsdp"), None),
            P(("ctx", "fsdp")),
            P(("ctx", "fsdp")),
            P(("ctx", "fsdp")),
            P(("ctx", "fsdp"), None),
            P(("ctx", "fsdp")),
            P(("ctx", "fsdp"), None),
            P(("ctx", "fsdp")),
        ),
        check_vma=False,
    )
```

```python
import functools

import jax
import jax.numpy as jnp
from jax import lax
from jax.experimental import pallas as pl
from jax.experimental.pallas import tpu as pltpu
from jax.sharding import PartitionSpec as P

HEAD = 256
ROT = 64


LN_EPSILON = 1e-05
VERY_LOW = -1e30


def layer_norm(values, ln_gain, ln_shift):
    average = jnp.mean(values, axis=-1, keepdims=True)
    centered = values - average
    spread = jnp.mean(centered * centered, axis=-1, keepdims=True)
    return centered * lax.rsqrt(spread + LN_EPSILON) * ln_gain + ln_shift


def gelu_exact(values):
    return jax.nn.gelu(values, approximate=False)


def rotate(values, positions):
    half_rot = ROT // 2
    frequency = 1.0 / 10000.0 ** (jnp.arange(half_rot).astype(values.dtype) * 2.0 / ROT)
    angles = positions.astype(values.dtype)[:, None] * frequency[None, :]
    shape_out = (angles.shape[0],) + (1,) * (values.ndim - 2) + (ROT,)
    cosine = jnp.concatenate([jnp.cos(angles), jnp.cos(angles)], axis=-1).reshape(shape_out)
    sine_part = jnp.concatenate([jnp.sin(angles), jnp.sin(angles)], axis=-1).reshape(shape_out)
    rot_part = values[..., :ROT]
    turned = jnp.concatenate([-rot_part[..., half_rot:], rot_part[..., :half_rot]], axis=-1)
    return jnp.concatenate([rot_part * cosine + turned * sine_part, values[..., ROT:]], axis=-1)


def row_positions(pairing, first_row, row_count, block_rows, ctx_count):
    row_ids = first_row + jnp.arange(row_count, dtype=jnp.int32)
    device_ids = row_ids // (2 * block_rows)
    within = row_ids % (2 * block_rows)
    matches = device_ids[:, None] == jnp.arange(ctx_count, dtype=jnp.int32)[None, :]
    owned_block = jnp.sum(jnp.where(matches, pairing[None, :], 0), axis=1)
    blocks = jnp.where(within < block_rows, owned_block, 2 * ctx_count - 1 - owned_block)
    return blocks * block_rows + within % block_rows


def heads_view(values, row_total, seq_count):
    return values.reshape(row_total, seq_count, -1, HEAD)


def contract_rows(left, right):
    return lax.dot_general(
        left, right, (((0,), (0,)), ((), ())), preferred_element_type=jnp.float32
    )


def contract_cols(left, right):
    return lax.dot_general(
        left, right, (((1,), (1,)), ((), ())), preferred_element_type=jnp.float32
    )


def pair_grads(
    query_rows, grad_rows, log_rows, delta_rows, query_pos, key_heads, value_heads, key_pos, scaling
):
    scores = (
        jnp.einsum("qshd,kshd->shqk", query_rows, key_heads, preferred_element_type=jnp.float32)
        * scaling
    )
    allowed = key_pos[None, None, None, :] <= query_pos[None, None, :, None]
    probabilities = jnp.where(allowed, jnp.exp(scores - log_rows[..., None]), 0.0)
    prob_grad = jnp.einsum(
        "qshd,kshd->shqk", grad_rows, value_heads, preferred_element_type=jnp.float32
    )
    score_grad = (probabilities * (prob_grad - delta_rows[..., None])).astype(jnp.bfloat16)
    return (score_grad, probabilities.astype(jnp.bfloat16))


def general_body(
    hidden,
    cotangent,
    pairing,
    ln1_gain,
    ln1_bias,
    qkv_weight,
    qkv_bias,
    out_weight,
    out_bias,
    ln2_gain,
    ln2_bias,
    up_weight,
    up_bias,
    down_weight,
    down_bias,
):
    local_rows, seq_count, model_width = hidden.shape
    block_rows = local_rows // 2
    ctx_count = lax.axis_size("ctx")
    head_count = model_width // HEAD
    scaling = HEAD ** (-0.5)
    tokens = local_rows * seq_count
    total_rows = local_rows * ctx_count
    params = (
        lax.all_gather(ln1_gain, ("ctx", "fsdp"), axis=0, tiled=True),
        lax.all_gather(ln1_bias, ("ctx", "fsdp"), axis=0, tiled=True),
        lax.all_gather(qkv_weight, ("ctx", "fsdp"), axis=0, tiled=True),
        lax.all_gather(qkv_bias, ("ctx", "fsdp"), axis=0, tiled=True),
        lax.all_gather(out_weight, ("ctx", "fsdp"), axis=0, tiled=True),
        lax.all_gather(out_bias, ("ctx", "fsdp"), axis=0, tiled=True),
        lax.all_gather(ln2_gain, ("ctx", "fsdp"), axis=0, tiled=True),
        lax.all_gather(ln2_bias, ("ctx", "fsdp"), axis=0, tiled=True),
        lax.all_gather(up_weight, ("ctx", "fsdp"), axis=0, tiled=True),
        lax.all_gather(up_bias, ("ctx", "fsdp"), axis=0, tiled=True),
        lax.all_gather(down_weight, ("ctx", "fsdp"), axis=0, tiled=True),
        lax.all_gather(down_bias, ("ctx", "fsdp"), axis=0, tiled=True),
    )
    (
        gain_one,
        shift_one,
        w_qkv,
        b_qkv,
        w_out,
        b_out,
        gain_two,
        shift_two,
        w_up,
        b_up,
        w_down,
        b_down,
    ) = params
    ff_width = w_up.shape[1]
    hidden_f = hidden.astype(jnp.float32).reshape(tokens, model_width)
    own_pos = row_positions(
        pairing, lax.axis_index("ctx") * local_rows, local_rows, block_rows, ctx_count
    )
    normed_one, ln_one_pull = jax.vjp(
        layer_norm, hidden_f, gain_one.astype(jnp.float32), shift_one.astype(jnp.float32)
    )
    normed_one_low = normed_one.astype(jnp.bfloat16)
    projected = jnp.dot(normed_one_low, w_qkv, preferred_element_type=jnp.float32) + b_qkv.astype(
        jnp.float32
    )
    query_f, rotation_pull = jax.vjp(
        lambda values: rotate(values, own_pos),
        heads_view(projected[:, :model_width], local_rows, seq_count),
    )
    query_b = query_f.astype(jnp.bfloat16)
    key_b = (
        rotate(
            heads_view(projected[:, model_width : 2 * model_width], local_rows, seq_count), own_pos
        )
        .astype(jnp.bfloat16)
        .reshape(local_rows, seq_count, model_width)
    )
    value_b = (
        projected[:, 2 * model_width :]
        .astype(jnp.bfloat16)
        .reshape(local_rows, seq_count, model_width)
    )
    running_max = jnp.full((seq_count, head_count, local_rows), VERY_LOW, jnp.float32)
    key_piece = lax.all_gather(key_b, "ctx", axis=0, tiled=True)
    value_piece = lax.all_gather(value_b, "ctx", axis=0, tiled=True)
    row_total = key_piece.shape[0]
    key_pos = row_positions(pairing, jnp.int32(0), row_total, block_rows, ctx_count)
    scores = (
        jnp.einsum(
            "qshd,kshd->shqk",
            query_b,
            heads_view(key_piece, row_total, seq_count),
            preferred_element_type=jnp.float32,
        )
        * scaling
    )
    allowed = key_pos[None, None, None, :] <= own_pos[None, None, :, None]
    piece_max = jnp.max(jnp.where(allowed, scores, VERY_LOW), axis=-1)
    new_max = jnp.maximum(running_max, piece_max)
    weights = jnp.where(allowed, jnp.exp(scores - new_max[..., None]), 0.0)
    new_total = jnp.sum(weights, axis=-1)
    mixture = jnp.einsum(
        "shqk,kshd->qshd",
        weights.astype(jnp.bfloat16),
        heads_view(value_piece, row_total, seq_count),
        preferred_element_type=jnp.float32,
    )
    log_total = new_max + jnp.log(new_total)
    attended = mixture / jnp.transpose(new_total, (2, 0, 1))[..., None]
    attended_low = attended.astype(jnp.bfloat16).reshape(tokens, model_width)
    branch_attn = jnp.dot(attended_low, w_out, preferred_element_type=jnp.float32) + b_out.astype(
        jnp.float32
    )
    normed_two, ln_two_pull = jax.vjp(
        layer_norm, hidden_f, gain_two.astype(jnp.float32), shift_two.astype(jnp.float32)
    )
    normed_two_low = normed_two.astype(jnp.bfloat16)
    inner_act = jnp.dot(normed_two_low, w_up, preferred_element_type=jnp.float32) + b_up.astype(
        jnp.float32
    )
    activated_f, gelu_pull = jax.vjp(gelu_exact, inner_act)
    activated = activated_f.astype(jnp.bfloat16)
    branch_mlp = contract_cols(activated, w_down) + b_down.astype(jnp.float32)
    output = (
        (hidden_f + branch_attn + branch_mlp)
        .astype(jnp.bfloat16)
        .reshape(local_rows, seq_count, model_width)
    )
    back_qkv, back_out, back_up, back_down = (
        lax.all_gather(qkv_weight, ("ctx", "fsdp"), axis=0, tiled=True),
        lax.all_gather(out_weight, ("ctx", "fsdp"), axis=0, tiled=True),
        lax.all_gather(up_weight, ("ctx", "fsdp"), axis=0, tiled=True),
        lax.all_gather(down_weight, ("ctx", "fsdp"), axis=0, tiled=True),
    )
    grad_out = cotangent.reshape(tokens, model_width)
    grad_f = grad_out.astype(jnp.float32)
    bias_sum = jnp.sum(grad_f, axis=0)
    up_grad = jnp.dot(grad_out, back_down, preferred_element_type=jnp.float32)
    inner_grad = gelu_pull(up_grad)[0].astype(jnp.bfloat16)
    norm_two_grad = contract_cols(inner_grad, back_up)
    dx_two, dgain_two, dshift_two = ln_two_pull(norm_two_grad)
    up_bias_sum = jnp.sum(inner_grad, axis=0, dtype=jnp.float32)
    mlp_small = jnp.concatenate(
        [
            up_bias_sum.reshape(model_width, -1),
            jnp.stack([bias_sum, dgain_two, dshift_two], axis=1),
        ],
        axis=1,
    )
    up_w_sum, down_w_sum, mlp_small_sum = (
        lax.psum_scatter(
            contract_rows(normed_two_low, inner_grad),
            ("ctx", "fsdp"),
            scatter_dimension=0,
            tiled=True,
        ),
        lax.psum_scatter(
            contract_rows(grad_out, activated), ("ctx", "fsdp"), scatter_dimension=0, tiled=True
        ),
        lax.psum_scatter(mlp_small, ("ctx", "fsdp"), scatter_dimension=0, tiled=True),
    )
    ratio = ff_width // model_width
    attn_grad = contract_cols(grad_out, back_out).astype(jnp.bfloat16)
    out_w_grad = contract_rows(attended_low, grad_out)
    grad_heads = heads_view(attn_grad, local_rows, seq_count)
    row_delta = jnp.einsum("qshd,qshd->shq", grad_heads.astype(jnp.float32), attended)
    keys_all, values_all = (
        lax.all_gather(key_b, "ctx", axis=0, tiled=True),
        lax.all_gather(value_b, "ctx", axis=0, tiled=True),
    )
    key_block = 512
    block_count = total_rows // key_block
    starts = jnp.arange(block_count, dtype=jnp.int32) * key_block

    def query_step(query_grad, inputs):
        key_piece, value_piece, offset = inputs
        key_pos = row_positions(pairing, offset, key_block, block_rows, ctx_count)
        key_heads = heads_view(key_piece, key_block, seq_count)
        value_heads = heads_view(value_piece, key_block, seq_count)
        score_grad, unused = pair_grads(
            query_b,
            grad_heads,
            log_total,
            row_delta,
            own_pos,
            key_heads,
            value_heads,
            key_pos,
            scaling,
        )
        query_grad = (
            query_grad
            + jnp.einsum(
                "shqk,kshd->qshd", score_grad, key_heads, preferred_element_type=jnp.float32
            )
            * scaling
        )
        return (query_grad, None)

    query_grad, unused_out = lax.scan(
        query_step,
        jnp.zeros((local_rows, seq_count, head_count, HEAD), jnp.float32),
        (
            keys_all.reshape(block_count, key_block, seq_count, model_width),
            values_all.reshape(block_count, key_block, seq_count, model_width),
            starts,
        ),
    )
    queries_all, grads_all = (
        lax.all_gather(query_b, "ctx", axis=0, tiled=True),
        lax.all_gather(grad_heads, "ctx", axis=0, tiled=True),
    )
    logs_all, deltas_all = (
        lax.all_gather(log_total, "ctx", axis=2, tiled=True),
        lax.all_gather(row_delta, "ctx", axis=2, tiled=True),
    )
    own_keys = heads_view(key_b, local_rows, seq_count)
    own_values = heads_view(value_b, local_rows, seq_count)

    def key_step(carry, inputs):
        key_acc, value_acc = carry
        query_piece, grad_piece, log_piece, delta_piece, offset = inputs
        query_pos = row_positions(pairing, offset, key_block, block_rows, ctx_count)
        score_grad, probs_low = pair_grads(
            query_piece,
            grad_piece,
            log_piece,
            delta_piece,
            query_pos,
            own_keys,
            own_values,
            own_pos,
            scaling,
        )
        key_acc = (
            key_acc
            + jnp.einsum(
                "shqk,qshd->kshd", score_grad, query_piece, preferred_element_type=jnp.float32
            )
            * scaling
        )
        value_acc = value_acc + jnp.einsum(
            "shqk,qshd->kshd", probs_low, grad_piece, preferred_element_type=jnp.float32
        )
        return ((key_acc, value_acc), None)

    empty_acc = jnp.zeros((local_rows, seq_count, head_count, HEAD), jnp.float32)
    log_blocks = jnp.moveaxis(logs_all.reshape(seq_count, head_count, block_count, key_block), 2, 0)
    delta_blocks = jnp.moveaxis(
        deltas_all.reshape(seq_count, head_count, block_count, key_block), 2, 0
    )
    (key_sum, value_sum), unused_keys = lax.scan(
        key_step,
        (empty_acc, empty_acc),
        (
            queries_all.reshape(block_count, key_block, seq_count, head_count, HEAD),
            grads_all.reshape(block_count, key_block, seq_count, head_count, HEAD),
            log_blocks,
            delta_blocks,
            starts,
        ),
    )
    key_owned = key_sum.reshape(local_rows, seq_count, model_width)
    value_owned = value_sum.reshape(local_rows, seq_count, model_width)
    query_pre = rotation_pull(query_grad)[0].reshape(tokens, model_width)
    key_pre = rotation_pull(heads_view(key_owned, local_rows, seq_count))[0].reshape(
        tokens, model_width
    )
    value_pre = value_owned.reshape(tokens, model_width)
    projected_grad = jnp.concatenate([query_pre, key_pre, value_pre], axis=1).astype(jnp.bfloat16)
    norm_one_grad = contract_cols(projected_grad, back_qkv)
    dx_one, dgain_one, dshift_one = ln_one_pull(norm_one_grad)
    qkv_bias_sum = jnp.sum(projected_grad, axis=0, dtype=jnp.float32)
    attn_small = jnp.concatenate(
        [
            qkv_bias_sum.reshape(model_width, -1),
            jnp.stack([bias_sum, dgain_one, dshift_one], axis=1),
        ],
        axis=1,
    )
    qkv_w_sum, out_w_sum, attn_small_sum = (
        lax.psum_scatter(
            contract_rows(normed_one_low, projected_grad),
            ("ctx", "fsdp"),
            scatter_dimension=0,
            tiled=True,
        ),
        lax.psum_scatter(out_w_grad, ("ctx", "fsdp"), scatter_dimension=0, tiled=True),
        lax.psum_scatter(attn_small, ("ctx", "fsdp"), scatter_dimension=0, tiled=True),
    )
    grad_hidden = (grad_f + dx_one + dx_two).reshape(local_rows, seq_count, model_width)
    return (
        output,
        grad_hidden,
        attn_small_sum[:, 4],
        attn_small_sum[:, 5],
        qkv_w_sum,
        attn_small_sum[:, :3].reshape(-1),
        out_w_sum,
        attn_small_sum[:, 3],
        mlp_small_sum[:, ratio + 1],
        mlp_small_sum[:, ratio + 2],
        up_w_sum,
        mlp_small_sum[:, :ratio].reshape(-1),
        down_w_sum,
        mlp_small_sum[:, ratio],
    )


MESH = pl.DeviceIdType.MESH
CORES = 2
LINE_Y = 2
VMEM_BYTES = 60 * 2**20


def split_fits(mesh):
    return mesh.shape["ctx"] == 16 and mesh.shape["fsdp"] == 2


class Place:
    def __init__(self, ctx_count):
        self.chips = ctx_count // CORES
        self.line = self.chips // LINE_Y
        index = lax.axis_index("ctx")
        self.c = index % CORES
        self.chip = index // CORES
        self.y = self.chip % LINE_Y
        self.z = self.chip // LINE_Y
        self.x = lax.axis_index("fsdp")

    def at(self, z, y, c, x):
        return ((z * LINE_Y + y) * CORES + c, x)

    def other_core(self):
        return self.at(self.z, self.y, 1 - self.c, self.x)

    def other_plane(self):
        return self.at(self.z, self.y, self.c, 1 - self.x)

    def other_y(self):
        return self.at(self.z, 1 - self.y, self.c, self.x)

    def plane_offsets(self):
        return [(dz, dy) for dz in range(self.line) for dy in range(LINE_Y) if dz or dy]

    def shifted(self, dz, dy):
        return (self.z + dz) % self.line, (self.y + dy) % LINE_Y


class Copies:
    def __init__(self, send, recv, local):
        self.send, self.recv, self.local = send, recv, local
        self.remotes, self.locals = 0, 0

    def reserve(self, count):
        self.remotes += count
        return self.remotes - count

    def remote(self, src, dst, device):
        return self.remote_at(self.reserve(1), src, dst, device)

    def remote_at(self, i, src, dst, device):
        return pltpu.make_async_remote_copy(
            src_ref=src,
            dst_ref=dst,
            send_sem=self.send.at[i],
            recv_sem=self.recv.at[i],
            device_id=device,
            device_id_type=MESH,
        )

    def inside(self, src, dst):
        i = self.locals
        self.locals += 1
        return pltpu.make_async_copy(src, dst, self.local.at[i])


def greet(place):
    barrier = pltpu.get_barrier_semaphore()
    partners = [place.other_core(), place.other_plane()]
    for dz, dy in place.plane_offsets():
        z, y = place.shifted(dz, dy)
        partners.append(place.at(z, y, place.c, place.x))
    for partner in partners:
        pl.semaphore_signal(barrier, inc=1, device_id=partner, device_id_type=MESH)
    pl.semaphore_wait(barrier, len(partners))


TOKEN_CHUNKS = 2


class TokenGather:
    def __init__(self, place, copies, own, whole):
        self.place, self.copies, self.whole = place, copies, whole
        c, chip, z, y = place.c, place.chip, place.z, place.y
        rows = own.shape[1]
        block = whole.at[tile(chip * CORES + c, rows)]
        self.first = copies.remote(own.at[1 - c], block, place.other_core())
        self.mine = copies.inside(own.at[c], block)
        self.size = CORES * rows // TOKEN_CHUNKS
        self.last = last = place.line - 1
        up = place.at(jnp.minimum(z + 1, last), y, c, place.x)
        down = place.at(jnp.maximum(z - 1, 0), y, c, place.x)
        over = place.other_y()
        chunks = range(TOKEN_CHUNKS)
        self.ups = [[self.copy(z - j, ch, up) for ch in chunks] for j in range(last)]
        self.downs = [[self.copy(z + j, ch, down) for ch in chunks] for j in range(last)]
        self.over_own = [self.copy(z, ch, over) for ch in chunks]
        self.over_ups = [[self.copy(z - 1 - j, ch, over) for ch in chunks] for j in range(last)]
        self.over_downs = [[self.copy(z + 1 + j, ch, over) for ch in chunks] for j in range(last)]

    def copy(self, z, ch, device):
        chip = jnp.clip(z, 0, self.last) * LINE_Y + self.place.y
        chunk = self.whole.at[tile(chip * TOKEN_CHUNKS + ch, self.size)]
        return self.copies.remote(chunk, chunk, device)

    def start(self):
        self.mine.start()
        self.first.start()

    def spread(self, ch):
        if ch == 0:
            self.mine.wait()
            self.first.wait_recv()
        z = self.place.z
        pl.when(z < self.last)(lambda: self.ups[0][ch].start())
        pl.when(z > 0)(lambda: self.downs[0][ch].start())
        self.over_own[ch].start()

    def step(self, j, ch):
        z, last = self.place.z, self.last

        @pl.when(z - 1 - j >= 0)
        def _():
            self.ups[j][ch].wait_recv()
            if j + 1 < last:
                pl.when(z < last)(lambda: self.ups[j + 1][ch].start())
            self.over_ups[j][ch].start()

        @pl.when(z + 1 + j <= last)
        def _():
            self.downs[j][ch].wait_recv()
            if j + 1 < last:
                pl.when(z > 0)(lambda: self.downs[j + 1][ch].start())
            self.over_downs[j][ch].start()

    def finish(self):
        z, last = self.place.z, self.last
        for ch in range(TOKEN_CHUNKS):
            self.over_own[ch].wait_recv()
            for j in range(last):
                pl.when(z - 1 - j >= 0)(lambda: self.over_ups[j][ch].wait_recv())
                pl.when(z + 1 + j <= last)(lambda: self.over_downs[j][ch].wait_recv())

    def drain(self):
        z, last = self.place.z, self.last
        self.first.wait_send()
        for ch in range(TOKEN_CHUNKS):
            self.over_own[ch].wait_send()
            for j in range(last):
                pl.when((z - j >= 0) & (z < last))(lambda: self.ups[j][ch].wait_send())
                pl.when((z + j <= last) & (z > 0))(lambda: self.downs[j][ch].wait_send())
                pl.when(z - 1 - j >= 0)(lambda: self.over_ups[j][ch].wait_send())
                pl.when(z + 1 + j <= last)(lambda: self.over_downs[j][ch].wait_send())


class WeightGather:
    def __init__(self, place, copies, pieces, whole, columns=slice(None)):
        self.place = place
        group = 2 * place.c + place.x
        self.by_chip = []
        for dz, dy in place.plane_offsets():
            z, y = place.shifted(dz, dy)
            device = place.at(z, y, place.c, place.x)
            self.by_chip.append(
                [copies.remote(src, dst, device) for src, dst in pieces(z * LINE_Y + y, place.chip, group)]
            )
        self.kept = [copies.inside(src, dst) for src, dst in pieces(place.chip, place.chip, group)]
        mine = whole.at[:, group, :, columns]
        self.across = copies.remote(mine, mine, place.other_plane())
        pair = whole.at[:, pl.ds(2 * place.c, 2), :, columns]
        self.swap = copies.remote(pair, pair, place.other_core())

    def send(self, i):
        for copy in self.by_chip[i] + (self.kept if i == 0 else []):
            copy.start()

    def scatter(self):
        for i in range(len(self.by_chip)):
            self.send(i)

    def cross(self):
        for copy in self.kept:
            copy.wait()
        for copies in self.by_chip:
            for copy in copies:
                copy.wait_recv()
        self.across.start()

    def share(self):
        self.across.wait_recv()
        self.swap.start()

    def finish(self):
        self.swap.wait_recv()

    def drain(self):
        for copy in sum(self.by_chip, []) + [self.across, self.swap]:
            copy.wait_send()


NORM_PARTS = 2
DOWN_PARTS = "ab"
GATHER_ORDER = (
    "qkv 6",
    "up a 0",
    "up a 3",
    "qkv 0",
    "up b 2",
    "prepare hid",
    "up b 0",
    "small scatter",
    "hid spread 0",
    "qkv 5",
    "tables",
    "qkv 2",
    "small cross",
    "hid spread 1",
    "prepare cot",
    "hid 0 0",
    "hid 0 1",
    "small share",
    "up a 2",
    "down a 0",
    "out start",
    "hid 1 0",
    "small done",
    "up b 6",
    "down b 5",
    "qkv 1",
    "down a 3",
    "qkv 3",
    "up b 1",
    "hid 1 1",
    "hid 2 0",
    "qkv 4",
    "up a 4",
    "up b 3",
    "cot spread 0",
    "qkv cross",
    "down a 1",
    "hid 2 1",
    "down a 6",
    "up b 4",
    "up b 5",
    "down a 5",
    "down a 4",
    "cot 0 0",
    "up b cross",
    "hid done",
    "up a 5",
    "up a 1",
    "up a 6",
    "norm",
    "qkv share",
    "out share",
    "cot spread 1",
    "cot 1 0",
    "norm",
    "norm done",
    "up a cross",
    "cot 0 1",
    "down a 2",
    "down b 0",
    "project",
    "up a share",
    "up b share",
    "down b 4",
    "down b 6",
    "down b 1",
    "cot 2 0",
    "down a cross",
    "attend",
    "cot 1 1",
    "down b 2",
    "down b 3",
    "inner",
    "down a share",
    "cot 2 1",
    "down b cross",
    "cot done",
    "attended grads",
    "attention back",
    "down b share",
    "down grads",
)


def nn(left, right):
    return lax.dot_general(left, right, (((1,), (0,)), ((), ())), preferred_element_type=jnp.float32)


def tile(i, size):
    return pl.ds(pl.multiple_of(i * size, size), size)


def flat_rows(values):
    return values.reshape(-1, values.shape[-1])


GAIN_ONE, SHIFT_ONE, GAIN_TWO, SHIFT_TWO, OUT_BIAS, DOWN_BIAS, QKV_BIAS, UP_BIAS, SMALL_ROWS = (
    0,
    1,
    2,
    3,
    4,
    5,
    6,
    9,
    16,
)
LANES = 128


def lanes_of(shape):
    return lax.broadcasted_iota(jnp.int32, shape, len(shape) - 1)


def pack_parameters(vectors, tile_ref):
    half = LANES // 2
    ln1_gain, ln1_bias, ln2_gain, ln2_bias, out_bias, down_bias, qkv_bias, up_bias = [
        ref[...].astype(jnp.float32).reshape(1, -1) for ref in vectors
    ]
    tile_ref[...] = jnp.zeros_like(tile_ref)
    for row, values in (
        (GAIN_ONE, ln1_gain),
        (SHIFT_ONE, ln1_bias),
        (GAIN_TWO, ln2_gain),
        (SHIFT_TWO, ln2_bias),
        (OUT_BIAS, out_bias),
        (DOWN_BIAS, down_bias),
    ):
        tile_ref[row : row + 1, :half] = values
        tile_ref[row : row + 1, half:] = values
    tile_ref[QKV_BIAS : QKV_BIAS + 1, :] = qkv_bias[:, :LANES]
    tile_ref[QKV_BIAS + 1 : QKV_BIAS + 2, :half] = qkv_bias[:, LANES:]
    tile_ref[QKV_BIAS + 1 : QKV_BIAS + 2, half:] = qkv_bias[:, :half]
    tile_ref[QKV_BIAS + 2 : QKV_BIAS + 3, :] = qkv_bias[:, half:]
    tile_ref[UP_BIAS : UP_BIAS + 1, :] = up_bias[:, :LANES]
    tile_ref[UP_BIAS + 1 : UP_BIAS + 2, :] = up_bias[:, LANES:]


def position_tables(ctx_count, pairing, cosine, sine, key_pos):
    block_rows = cosine.shape[0] // (2 * ctx_count)
    half_rot = ROT // 2
    lane = lanes_of((block_rows, LANES))
    power = (lane % half_rot).astype(jnp.float32) * (2.0 / ROT)
    frequency = jnp.exp(power * -9.210340371976184)
    row = lax.broadcasted_iota(jnp.int32, (block_rows, LANES), 0)

    @pl.loop(0, ctx_count)
    def _(device):
        owned = pairing[device]
        for late in range(2):
            block = 2 * ctx_count - 1 - owned if late else owned
            where = (block * block_rows + row).astype(jnp.float32)
            angles = where * frequency
            at = tile(2 * device + late, block_rows)
            cosine[at, :] = jnp.where(lane < ROT, jnp.cos(angles), 1.0)
            sin = jnp.sin(angles)
            sine[at, :] = jnp.where(lane < half_rot, -sin, jnp.where(lane < ROT, sin, where))

    lane = lanes_of((8, LANES))
    per = LANES // (2 * block_rows)
    for first in range(0, ctx_count, per):
        block = jnp.zeros((8, LANES), jnp.int32)
        for device in range(per):
            owned = pairing[first + device]
            for late in range(2):
                value = 2 * ctx_count - 1 - owned if late else owned
                block = jnp.where(lane // block_rows == 2 * device + late, value, block)
        at = first * 2 * block_rows
        key_pos[:, at : at + LANES] = (block * block_rows + lane % block_rows).astype(jnp.float32)


def split_sequences(rows, own):
    for i in range(rows.shape[1]):
        own[i] = rows[:, i, :]


def assemble_small(place, small, vec, qkv_rows, qkv_bias, up_bias):
    chips, groups = small.shape[:2]
    low = lanes_of((1, LANES)) < LANES // 2
    for pair in range(chips * groups // 2):
        chip, group = pair // (groups // 2), pair % (groups // 2) * 2
        for row in range(6):
            a = small[chip, group, row : row + 1, :]
            b = small[chip, group + 1, row : row + 1, :]
            vec[row : row + 1, pair * LANES : (pair + 1) * LANES] = jnp.where(low, a, b)
        qkv_rows[3 * pair : 3 * pair + 1, :] = small[chip, group, QKV_BIAS : QKV_BIAS + 1, :]
        a = small[chip, group, QKV_BIAS + 1 : QKV_BIAS + 2, :]
        b = small[chip, group + 1, QKV_BIAS + 1 : QKV_BIAS + 2, :]
        qkv_rows[3 * pair + 1 : 3 * pair + 2, :] = jnp.where(low, a, b)
        qkv_rows[3 * pair + 2 : 3 * pair + 3, :] = small[chip, group + 1, QKV_BIAS + 2 : QKV_BIAS + 3, :]
    third = qkv_rows.shape[0] // 3
    per_head = HEAD // LANES
    for k in range(3):
        for u in range(per_head):
            at = (k * per_head + u) * LANES
            qkv_bias[0:1, at : at + LANES] = qkv_rows[pl.ds(k * third + place.chip * per_head + u, 1), :]
    for group in range(groups):
        for u in range(2):
            at = (group * 2 + u) * LANES
            row = UP_BIAS + u
            up_bias[0:1, at : at + LANES] = small[pl.ds(place.chip, 1), group, row : row + 1, :].reshape(1, LANES)


def norm_rows(start, count, hid, vec, norm_one, norm_two, stats):
    step = 128

    @pl.loop(0, count // step)
    def _(i):
        at = pl.ds(pl.multiple_of(start + i * step, step), step)
        x = hid[at, :].astype(jnp.float32)
        average = jnp.mean(x, axis=1, keepdims=True)
        centered = x - average
        scale = lax.rsqrt(jnp.mean(centered * centered, axis=1, keepdims=True) + LN_EPSILON)
        stats[at, 0:1] = average
        stats[at, 1:2] = scale
        xhat = centered * scale
        norm_one[at, :] = (xhat * vec[0:1, :] + vec[1:2, :]).astype(jnp.bfloat16)
        norm_two[at, :] = (xhat * vec[2:3, :] + vec[3:4, :]).astype(jnp.bfloat16)


def turned_half(values):
    half_rot = ROT // 2
    lane = lanes_of(values.shape)
    width = values.shape[-1]
    return jnp.where(
        lane < half_rot,
        pltpu.roll(values, width - half_rot, 1),
        jnp.where(lane < ROT, pltpu.roll(values, half_rot, 1), 0.0),
    )


def project(norm_one, weight, bias, cosine, sine, query, key, value):
    step = 256

    @pl.loop(0, norm_one.shape[0] // step)
    def _(i):
        at = tile(i, step)
        both = nn(norm_one[at, :], flat_rows(weight[...])) + bias[0:1, :]
        cos, sin = cosine[at, :], sine[at, :]
        for k, target in enumerate((query, key)):
            first = both[:, k * HEAD : k * HEAD + LANES]
            target[at, 0:LANES] = (first * cos + turned_half(first) * sin).astype(jnp.bfloat16)
            target[at, LANES:HEAD] = both[:, k * HEAD + LANES : (k + 1) * HEAD].astype(jnp.bfloat16)
        value[at, :] = both[:, 2 * HEAD :].astype(jnp.bfloat16)


def attend(query, key, value, sine, key_pos, attended, attended_low, probs, probs_low):
    step = 256

    @pl.loop(0, query.shape[0] // step)
    def _(i):
        at = tile(i, step)
        scores = contract_cols(query[at, :], key[...]) * HEAD**-0.5
        allowed = key_pos[0:1, :] <= sine[at, ROT : ROT + 1]
        scores = jnp.where(allowed, scores, VERY_LOW)
        highest = jnp.max(scores, axis=1, keepdims=True)
        weights = jnp.where(allowed, jnp.exp(scores - highest), 0.0)
        weights = weights / jnp.sum(weights, axis=1, keepdims=True)
        low = weights.astype(jnp.bfloat16)
        probs[at, :] = weights
        probs_low[at, :] = low
        total = nn(low, value[...])
        attended[at, :] = total
        attended_low[at, :] = total.astype(jnp.bfloat16)


def feed_inner(norm_two, weight, bias, activated, slope):
    step = 128

    @pl.loop(0, norm_two.shape[0] // step)
    def _(i):
        at = tile(i, step)
        inner = nn(norm_two[at, :], flat_rows(weight[...])) + bias[0:1, :]
        normal = 0.5 + 0.5 * lax.erf(inner * 0.5**0.5)
        activated[at, :] = (inner * normal).astype(jnp.bfloat16)
        density = (2.0 * jnp.pi) ** -0.5 * jnp.exp(-0.5 * inner * inner)
        slope[at, :] = normal + inner * density


def attended_grads(cot, weight, attended_grad):
    step = 256

    @pl.loop(0, cot.shape[0] // step)
    def _(i):
        at = tile(i, step)
        attended_grad[at, :] = contract_cols(cot[at, :], flat_rows(weight[...])).astype(jnp.bfloat16)


def attention_grads(
    query, key, value, cosine, sine, attended, attended_grad, probs, probs_low, score_grad, projected_grad
):
    step = 256
    scaling = HEAD**-0.5

    def put(at, k, grad):
        first = grad[:, 0:LANES]
        back = first * cosine[at, :] - turned_half(first) * sine[at, :]
        projected_grad[at, k * HEAD : k * HEAD + LANES] = back.astype(jnp.bfloat16)
        projected_grad[at, k * HEAD + LANES : (k + 1) * HEAD] = grad[:, LANES:].astype(jnp.bfloat16)

    @pl.loop(0, query.shape[0] // step)
    def _(i):
        at = tile(i, step)
        own = attended_grad[at, :]
        row_delta = jnp.sum(own.astype(jnp.float32) * attended[at, :], axis=1, keepdims=True)
        grad = (probs[at, :] * (contract_cols(own, value[...]) - row_delta)).astype(jnp.bfloat16)
        score_grad[at, :] = grad
        put(at, 0, nn(grad, key[...]) * scaling)

    @pl.loop(0, query.shape[0] // step)
    def _(i):
        at = tile(i, step)
        put(at, 1, contract_rows(score_grad[:, at], query[...]) * scaling)
        projected_grad[at, 2 * HEAD :] = contract_rows(probs_low[:, at], attended_grad[...]).astype(jnp.bfloat16)


def weight_grads(tokens, grads, result):
    chips, groups, rows = result.shape[:3]
    step = groups * rows

    @pl.loop(0, chips)
    def _(k):
        grad = contract_rows(tokens[:, tile(k, step)], grads[...]).astype(jnp.bfloat16)
        result[k] = grad.reshape(result.shape[1:])


def column_sums(values, result):
    step = 128
    result[...] = jnp.zeros_like(result)

    @pl.loop(0, values.shape[0] // step)
    def _(i):
        part = values[tile(i, step), :].astype(jnp.float32)
        result[...] += jnp.sum(part.reshape(-1, 8, values.shape[1]), axis=0)


def gather_kernel(
    ctx_count,
    hid_in,
    cot_in,
    ln1_gain_in,
    ln1_bias_in,
    ln2_gain_in,
    ln2_bias_in,
    out_bias_in,
    down_bias_in,
    qkv_bias_in,
    up_bias_in,
    qkv,
    up,
    down,
    out,
    pairing,
    hid_all,
    cot_all,
    qkv_all,
    up_all,
    down_all,
    out_all,
    attended_low_out,
    projected_grad_out,
    norm_two_out,
    activated_out,
    slope_out,
    norm_one_out,
    down_grad_out,
    vec_out,
    stats_out,
    hid_rows,
    cot_rows,
    hid,
    cot,
    ln1_gain,
    ln1_bias,
    ln2_gain,
    ln2_bias,
    out_bias,
    down_bias,
    qkv_bias_own,
    up_bias_own,
    small,
    hid_v,
    cot_v,
    qkv_v,
    up_v,
    out_v,
    small_v,
    cosine,
    sine,
    key_pos,
    vec,
    qkv_rows,
    qkv_bias,
    up_bias,
    norm_one,
    norm_two,
    stats,
    query,
    key,
    value,
    attended,
    attended_low,
    probs,
    probs_low,
    activated,
    slope,
    attended_grad,
    score_grad,
    projected_grad,
    send,
    recv,
    local,
):
    place = Place(ctx_count)
    copies = Copies(send, recv, local)
    width = out.shape[1]
    head = qkv_all.shape[3] // 3
    part = up_all.shape[3]

    def qkv_pieces(to, row, group):
        return [
            (
                qkv.at[:, pl.ds(pl.multiple_of(k * width + to * head, head), head)],
                qkv_v.at[row, group, :, pl.ds(k * head, head)],
            )
            for k in range(3)
        ]

    def part_gather(source, whole, first, size):
        columns = pl.ds(first, size)

        def pieces(to, row, group):
            given = pl.ds(pl.multiple_of(to * part + first, size), size)
            return [(source.at[:, given], whole.at[row, group, :, columns])]

        return WeightGather(place, copies, pieces, whole, columns)

    hid_g = TokenGather(place, copies, hid, hid_v)
    cot_g = TokenGather(place, copies, cot, cot_v)
    small_g = WeightGather(place, copies, lambda to, row, group: [(small, small_v.at[row, group])], small_v)
    qkv_g = WeightGather(place, copies, qkv_pieces, qkv_v)
    weights = {"qkv": qkv_g}
    for name, source, whole, letters in (("up", up, up_v, "ab"), ("down", down, down_all, DOWN_PARTS)):
        size = part // len(letters)
        for i, letter in enumerate(letters):
            weights[name + " " + letter] = part_gather(source, whole, i * size, size)
    group = 2 * place.c + place.x
    out_mine = copies.inside(out, out_v.at[group])
    out_across = copies.remote(out, out_v.at[group], place.other_plane())
    out_pair = out_v.at[pl.ds(2 * place.c, 2)]
    out_swap = copies.remote(out_pair, out_pair, place.other_core())
    loads = {
        name: copies.inside(src, dst)
        for name, src, dst in (
            ("hid rows", hid_in, hid_rows),
            ("cot rows", cot_in, cot_rows),
        )
    }
    stores = {
        name: copies.inside(src, dst)
        for name, src, dst in (
            ("hid", hid_v, hid_all),
            ("cot", cot_v, cot_all),
            ("qkv", qkv_v, qkv_all),
            ("up", up_v, up_all),
            ("out", out_v, out_all),
            ("vec", vec, vec_out),
            ("stats", stats, stats_out),
            ("attended_low", attended_low, attended_low_out),
            ("norm_two", norm_two, norm_two_out),
            ("activated", activated, activated_out),
            ("slope", slope, slope_out),
            ("projected_grad", projected_grad, projected_grad_out),
            ("norm_one", norm_one, norm_one_out),
            ("down_grad", up_v, down_grad_out),
        )
    }

    rows = hid_v.shape[0]
    normed = iter(range(NORM_PARTS))

    def norm_next():
        part_rows = rows // NORM_PARTS
        norm_rows(next(normed) * part_rows, part_rows, hid_v, vec, norm_one, norm_two, stats)

    def norm_done():
        stores["norm_one"].start()
        stores["norm_two"].start()
        stores["stats"].start()

    def small_done():
        small_g.finish()
        assemble_small(place, small_v, vec, qkv_rows, qkv_bias, up_bias)
        stores["vec"].start()

    def hid_done():
        hid_g.finish()
        stores["hid"].start()

    def project_all():
        qkv_g.finish()
        stores["qkv"].start()
        project(norm_one, qkv_v, qkv_bias, cosine, sine, query, key, value)

    def attend_all():
        attend(query, key, value, sine, key_pos, attended, attended_low, probs, probs_low)
        stores["attended_low"].start()

    def inner_all():
        weights["up a"].finish()
        weights["up b"].finish()
        stores["up"].start()
        feed_inner(norm_two, up_v, up_bias, activated, slope)
        stores["activated"].start()
        stores["slope"].start()

    def out_start():
        out_mine.start()
        out_across.start()

    def out_share():
        out_mine.wait()
        out_across.wait_recv()
        out_swap.start()

    def cot_done():
        cot_g.finish()
        stores["cot"].start()
        out_swap.wait_recv()
        stores["out"].start()

    def out_grads():
        attended_grads(cot_v, out_v, attended_grad)

    def down_grads():
        stores["up"].wait()
        weights["up a"].drain()
        weights["up b"].drain()
        weight_grads(cot_v, activated, up_v)
        stores["down_grad"].start()

    def attention_back():
        attention_grads(
            query, key, value, cosine, sine, attended, attended_grad, probs, probs_low, score_grad, projected_grad
        )
        stores["projected_grad"].start()

    steps = {
        "tables": lambda: position_tables(ctx_count, pairing, cosine, sine, key_pos),
        "small cross": small_g.cross,
        "small share": small_g.share,
        "small done": small_done,
        "out start": out_start,
        "out share": out_share,
        "hid done": hid_done,
        "norm": norm_next,
        "norm done": norm_done,
        "project": project_all,
        "attend": attend_all,
        "inner": inner_all,
        "cot done": cot_done,
        "attended grads": out_grads,
        "down grads": down_grads,
        "attention back": attention_back,
    }
    for ch in range(TOKEN_CHUNKS):
        for name, gather in (("hid", hid_g), ("cot", cot_g)):
            steps["%s spread %d" % (name, ch)] = functools.partial(gather.spread, ch)
            for j in range(place.line - 1):
                steps["%s %d %d" % (name, j, ch)] = functools.partial(gather.step, j, ch)
    for name, gather in weights.items():
        for i in range(len(gather.by_chip)):
            steps["%s %d" % (name, i)] = functools.partial(gather.send, i)
        steps[name + " cross"] = gather.cross
        steps[name + " share"] = gather.share

    vectors = (ln1_gain, ln1_bias, ln2_gain, ln2_bias, out_bias, down_bias, qkv_bias_own, up_bias_own)
    vectors_in = (
        ln1_gain_in,
        ln1_bias_in,
        ln2_gain_in,
        ln2_bias_in,
        out_bias_in,
        down_bias_in,
        qkv_bias_in,
        up_bias_in,
    )
    vector_loads = [copies.inside(src, dst) for src, dst in zip(vectors_in, vectors)]
    loads["hid rows"].start()
    for load in vector_loads:
        load.start()
    loads["cot rows"].start()
    greet(place)

    def prepare_hid():
        loads["hid rows"].wait()
        split_sequences(hid_rows, hid)
        hid_g.start()

    def prepare_cot():
        loads["cot rows"].wait()
        split_sequences(cot_rows, cot)
        cot_g.start()

    def prepare_small():
        for load in vector_loads:
            load.wait()
        pack_parameters(vectors, small)
        small_g.scatter()

    steps["prepare hid"] = prepare_hid
    steps["prepare cot"] = prepare_cot
    steps["small scatter"] = prepare_small
    for name in GATHER_ORDER:
        steps[name]()
    for letter in DOWN_PARTS:
        weights["down " + letter].finish()
    for name, store in stores.items():
        if name != "up":
            store.wait()
    for gather in [hid_g, cot_g, small_g] + [weights[name] for name in weights if name[:2] != "up"]:
        gather.drain()
    out_across.wait_send()
    out_swap.wait_send()


def gather_all(ctx_count, hid, cot, vectors, qkv, up, down, out, pairing):
    f32, b16 = jnp.float32, jnp.bfloat16
    chips = ctx_count // CORES
    rows = qkv.shape[0]
    groups = CORES * 2
    tokens = ctx_count * hid.shape[0]
    width = out.shape[1]
    head3, part = qkv.shape[1] // chips, up.shape[1] // chips
    head = head3 // 3
    qkv_s = ((chips, groups, rows, head3), b16)
    part_s = ((chips, groups, rows, part), b16)
    out_s = ((groups, rows, width), b16)
    small = (SMALL_ROWS, LANES)
    small_s = ((chips, groups) + small, f32)
    wide_s, narrow_s = ((tokens, width), b16), ((tokens, head), b16)
    own_s = ((hid.shape[1], hid.shape[0], width), b16)
    results = [
        wide_s,
        wide_s,
        qkv_s,
        part_s,
        part_s,
        out_s,
        narrow_s,
        ((tokens, head3), b16),
        wide_s,
        ((tokens, part), b16),
        ((tokens, part), f32),
        wide_s,
        part_s,
        ((8, width), f32),
        ((tokens, LANES), f32),
    ]
    scratch = [
        (hid.shape, b16),
        (cot.shape, b16),
        own_s,
        own_s,
    ]
    scratch += [(vector.shape, b16) for vector in vectors]
    scratch += [
        (small, f32),
        wide_s,
        wide_s,
        qkv_s,
        part_s,
        out_s,
        small_s,
        ((tokens, LANES), f32),
        ((tokens, LANES), f32),
        ((8, tokens), f32),
        ((8, width), f32),
        ((3 * width // LANES, LANES), f32),
        ((8, head3), f32),
        ((8, part), f32),
        wide_s,
        wide_s,
        ((tokens, LANES), f32),
        narrow_s,
        narrow_s,
        narrow_s,
        ((tokens, head), f32),
        narrow_s,
        ((tokens, tokens), f32),
        ((tokens, tokens), b16),
        ((tokens, part), b16),
        ((tokens, part), f32),
        narrow_s,
        ((tokens, tokens), b16),
        ((tokens, head3), b16),
    ]
    operands = (hid, cot, *vectors, qkv, up, down, out, pairing)
    anywhere = pl.BlockSpec(memory_space=pl.ANY)
    return pl.pallas_call(
        lambda *refs: gather_kernel(ctx_count, *refs),
        out_shape=[jax.ShapeDtypeStruct(*shape) for shape in results],
        in_specs=[anywhere] * (len(operands) - 1) + [pl.BlockSpec(memory_space=pltpu.SMEM)],
        out_specs=[anywhere] * len(results),
        scratch_shapes=[pltpu.VMEM(*shape) for shape in scratch]
        + [
            pltpu.SemaphoreType.DMA((176,)),
            pltpu.SemaphoreType.DMA((176,)),
            pltpu.SemaphoreType.DMA((48,)),
        ],
        compiler_params=pltpu.CompilerParams(
            collective_id=0, has_side_effects=True, vmem_limit_bytes=VMEM_BYTES
        ),
        name="gather_all",
    )(*operands)


def add_rows(total, other):
    step = 64

    @pl.loop(0, total.shape[0] // step)
    def _(i):
        at = tile(i, step)
        both = total[at, :].astype(jnp.float32) + other[at, :].astype(jnp.float32)
        total[at, :] = both.astype(total.dtype)


class GradScatter:
    def __init__(self, place, copies, partial, kept, from_core, from_plane, result, columns=None):
        self.place = place
        c, x, chip = place.c, place.x, place.chip
        self.kept, self.from_core, self.from_plane = kept, from_core, from_plane
        self.columns = cols = slice(0, kept.shape[3]) if columns is None else columns
        self.load = None
        given = partial.at[:, :, :, cols]
        if partial.shape != kept.shape:
            self.load = copies.inside(partial.at[:, pl.ds(2 * c, 2), :, cols], kept.at[:, :, :, cols])
            given = partial.at[:, pl.ds(2 * (1 - c), 2), :, cols]
        self.swap = copies.remote(given, from_core.at[:, :, :, cols], place.other_core())
        self.across = copies.remote(
            kept.at[:, 1 - x, :, cols], from_plane.at[:, :, cols], place.other_plane()
        )
        self.scattered = []
        for dz, dy in place.plane_offsets():
            z, y = place.shifted(dz, dy)
            self.scattered.append(
                copies.remote(
                    kept.at[z * LINE_Y + y, x, :, cols], result.at[chip, :, cols], place.at(z, y, c, x)
                )
            )
        self.own = copies.inside(kept.at[chip, x, :, cols], result.at[chip, :, cols])

    def start(self):
        if self.load is not None:
            self.load.start()
        self.swap.start()

    def cross(self):
        if self.load is not None:
            self.load.wait()
        self.swap.wait_recv()
        x = self.place.x
        self.add(1 - x, self.from_core.at[:, 1 - x])
        self.across.start()
        self.add(x, self.from_core.at[:, x])

    def add(self, x, other):
        cols = self.columns

        @pl.loop(0, self.kept.shape[0])
        def _(k):
            both = self.kept[k, x, :, cols].astype(jnp.float32) + other[k, :, cols].astype(jnp.float32)
            self.kept[k, x, :, cols] = both.astype(self.kept.dtype)

    def scatter(self):
        self.across.wait_recv()
        self.add(self.place.x, self.from_plane)
        for copy in self.scattered + [self.own]:
            copy.start()

    def finish(self):
        self.own.wait()
        for copy in self.scattered:
            copy.wait_recv()

    def drain(self, swapped=False):
        for copy in self.scattered + [self.across] + ([] if swapped else [self.swap]):
            copy.wait_send()


def out_weight_grads(place, attended_low, cot, kept, given):
    step = 512

    @pl.loop(0, cot.shape[1] // step)
    def _(i):
        at = tile(i, step)
        grad = contract_rows(attended_low[...], cot[:, at]).astype(jnp.bfloat16)
        grad = grad.reshape((2,) + kept.shape[:2] + (step,))
        kept[:, :, at] = jnp.where(place.c == 0, grad[0], grad[1])
        given[:, :, at] = jnp.where(place.c == 0, grad[1], grad[0])


def weight_grads_by_core(place, tokens, grads, kept, given, columns):
    chips, half, rows = kept.shape[:3]
    step = 2 * half * rows

    @pl.loop(0, chips)
    def _(k):
        grad = contract_rows(tokens[:, tile(k, step)], grads[:, columns]).astype(jnp.bfloat16)
        grad = grad.reshape(2, half, rows, grad.shape[1])
        kept[k, :, :, columns] = jnp.where(place.c == 0, grad[0], grad[1])
        given[k, :, :, columns] = jnp.where(place.c == 0, grad[1], grad[0])


class TokenScatter:
    def __init__(self, place, copies, part, from_y, slots, total, result):
        self.place, self.copies = place, copies
        z, y, c, x = place.z, place.y, place.c, place.x
        self.part, self.from_y, self.slots, self.total = part, from_y, slots, total
        self.line = place.line
        self.last = last = self.line - 1
        self.rows = total.shape[0]
        self.size = self.rows // TOKEN_CHUNKS
        count = self.line * TOKEN_CHUNKS
        self.over_base = copies.reserve(count)
        self.up_base = copies.reserve(count)
        self.down_base = copies.reserve(count)
        self.above = place.at(jnp.minimum(z + 1, last), y, c, x)
        self.below = place.at(jnp.maximum(z - 1, 0), y, c, x)
        half = self.rows // CORES
        self.swap = copies.remote(total.at[tile(1 - c, half)], result.at[c], place.other_core())
        self.own = copies.inside(total.at[tile(c, half)], result.at[c])

    def order(self, i):
        last = self.last
        chosen = 0
        for z in range(self.line):
            far = sorted(range(self.line), key=lambda k: (-abs(k - z), min(k, last - k)))
            chosen = jnp.where(self.place.z == z, far[i], chosen)
        return chosen

    def chunk(self, ref, k, ch):
        return ref.at[tile(k * TOKEN_CHUNKS + ch, self.size)]

    def held(self, k, ch):
        return self.chunk(self.part, k * LINE_Y + self.place.y, ch)

    def copy(self, base, k, ch, src, dst, device):
        return self.copies.remote_at(base + k * TOKEN_CHUNKS + ch, src, dst, device)

    def over(self, k, ch):
        src = self.chunk(self.part, k * LINE_Y + 1 - self.place.y, ch)
        return self.copy(self.over_base, k, ch, src, self.chunk(self.from_y, k, ch), self.place.other_y())

    def up(self, k, ch):
        return self.copy(self.up_base, k, ch, self.held(k, ch), self.chunk(self.slots, k, ch), self.above)

    def down(self, k, ch):
        slot = jnp.where(self.place.z - 1 == k, self.line, k)
        return self.copy(self.down_base, k, ch, self.held(k, ch), self.chunk(self.slots, slot, ch), self.below)

    def send_over(self, k):
        for ch in range(TOKEN_CHUNKS):
            self.over(k, ch).start()

    def combine(self, k, ch):
        self.over(k, ch).wait_recv()
        add_rows(self.held(k, ch), self.chunk(self.from_y, k, ch))

    def step(self, i, ch):
        z = self.place.z
        k = self.order(i)
        self.combine(k, ch)

        @pl.when(k > z)
        def _():
            @pl.when(z > 0)
            def _():
                self.up(k, ch).wait_recv()
                add_rows(self.held(k, ch), self.chunk(self.slots, k, ch))

            self.up(k, ch).start()

        @pl.when(k < z)
        def _():
            @pl.when(z < self.last)
            def _():
                self.down(k, ch).wait_recv()
                add_rows(self.held(k, ch), self.chunk(self.slots, k, ch))

            self.down(k, ch).start()

    def reduce(self):
        z, y, last = self.place.z, self.place.y, self.last
        step = 64
        for ch in range(TOKEN_CHUNKS):
            self.combine(z, ch)
            pl.when(z > 0)(lambda: self.up(z, ch).wait_recv())
            pl.when(z < last)(lambda: self.down(z, ch).wait_recv())

        @pl.loop(0, self.rows // step)
        def _(i):
            at = tile((z * LINE_Y + y) * (self.rows // step) + i, step)
            self.total[tile(i, step), :] = self.part[at, :].astype(jnp.float32)

        def add(slot):
            @pl.loop(0, self.rows // step)
            def _(i):
                at = tile(slot * (self.rows // step) + i, step)
                self.total[tile(i, step), :] += self.slots[at, :].astype(jnp.float32)

        pl.when(z > 0)(lambda: add(z))
        pl.when(z < last)(lambda: add(last + 1))
        self.swap.start()
        self.own.start()

    def finish(self):
        self.swap.wait_recv()

    def drain(self):
        z = self.place.z
        for k in range(self.line):
            for ch in range(TOKEN_CHUNKS):
                self.over(k, ch).wait_send()
                pl.when(z < k)(lambda: self.up(k, ch).wait_send())
                pl.when(z > k)(lambda: self.down(k, ch).wait_send())


def output_part(scatter, i, attended_low, activated, out_weight, down_weight):
    k = scatter.order(i)
    at = tile(k, LINE_Y * scatter.rows)
    rows = nn(attended_low[at, :], flat_rows(out_weight[...]))
    rows = rows + contract_cols(activated[at, :], flat_rows(down_weight[...]))
    scatter.part[at, :] = rows.astype(scatter.part.dtype)
    scatter.send_over(k)


def inner_grads(cot, down_weight, slope, slope_loads, inner_grad):
    step = slope.shape[1]
    for i, load in enumerate(slope_loads):
        load.wait()
        at = slice(i * step, (i + 1) * step)
        grad = nn(cot[at, :], flat_rows(down_weight[...])) * slope[i % 2]
        inner_grad[at, :] = grad.astype(jnp.bfloat16)
        if i + 2 < len(slope_loads):
            slope_loads[i + 2].start()


def hidden_part(scatter, i, inner_grad, up_weight, projected_grad, qkv_weight, hid, stats, vec, sums):
    def by_eight(values):
        return jnp.sum(values.reshape(-1, 8, values.shape[1]), axis=0)

    k = scatter.order(i)

    @pl.loop(0, LINE_Y)
    def _(y):
        at = tile(k * LINE_Y + y, scatter.rows)
        one = contract_cols(projected_grad[at, :], flat_rows(qkv_weight[...]))
        two = contract_cols(inner_grad[at, :], flat_rows(up_weight[...]))
        xhat = (hid[at, :].astype(jnp.float32) - stats[at, 0:1]) * stats[at, 1:2]
        sums[0] += by_eight(one * xhat)
        sums[1] += by_eight(one)
        sums[2] += by_eight(two * xhat)
        sums[3] += by_eight(two)
        rows = one * vec[0:1, :] + two * vec[2:3, :]
        scatter.part[at, :] = rows.astype(scatter.part.dtype)

    scatter.send_over(k)


COT_SUM, UP_SUM, QKV_SUM = 4, 5, 7


def pack_small(place, sums, cot_sum, up_sum, qkv_sum, qkv_rows, tiles):
    chips, groups = tiles.shape[:2]
    tiles[...] = jnp.zeros_like(tiles)
    qkv_rows[...] = jnp.zeros_like(qkv_rows)
    qkv_total = jnp.sum(qkv_sum[...], axis=0, keepdims=True)
    up_total = jnp.sum(up_sum[...], axis=0, keepdims=True)
    third = qkv_rows.shape[0] // 3
    per_head = HEAD // LANES
    for k in range(3):
        for u in range(per_head):
            at = (k * per_head + u) * LANES
            qkv_rows[pl.ds(k * third + place.chip * per_head + u, 1), :] = qkv_total[:, at : at + LANES]
    first = jnp.where(place.chip == 0, 1.0, 0.0)
    norm_sums = [jnp.sum(sums[row], axis=0, keepdims=True) for row in range(4)]
    norm_sums.append(jnp.sum(cot_sum[...], axis=0, keepdims=True) * first)
    for pair in range(chips * groups // 2):
        chip, group = pair // (groups // 2), pair % (groups // 2) * 2
        at = slice(pair * LANES, (pair + 1) * LANES)
        for g in (group, group + 1):
            for row in range(5):
                tiles[chip, g, row : row + 1, :] = norm_sums[row][:, at]
            tiles[chip, g, QKV_SUM : QKV_SUM + 3, :] = qkv_rows[3 * pair : 3 * pair + 3, :]
    for group in range(groups):
        for u in range(2):
            at = (group * 2 + u) * LANES
            row = UP_SUM + u
            values = up_total[:, at : at + LANES].reshape(1, 1, LANES)
            tiles[pl.ds(place.chip, 1), group, row : row + 1, :] = values


SCATTER_ORDER = (
    "down a swap",
    "outs tile 0",
    "outs tile 1",
    "qkv grads",
    "outs 0 0",
    "down a cross",
    "outs tile 2",
    "down b swap",
    "outs 0 1",
    "out grads",
    "outs 1 0",
    "down b cross",
    "qkv swap",
    "down a scatter",
    "outs tile 3",
    "out swap",
    "inner",
    "outs 1 1",
    "outs 2 0",
    "qkv cross",
    "up a grad",
    "down b scatter",
    "up b grad",
    "hid tile 0",
    "up b swap",
    "outs 2 1",
    "out cross",
    "hid tile 1",
    "hid tile 2",
    "qkv scatter",
    "hid 0 0",
    "up a swap",
    "up b cross",
    "up sum",
    "hid 0 1",
    "hid tile 3",
    "pack",
    "hid 1 0",
    "small swap",
    "out finish",
    "small cross",
    "up b scatter",
    "hid 1 1",
    "hid 2 0",
    "outs reduce",
    "up a cross",
    "hid 2 1",
    "small scatter",
    "up a scatter",
    "hid reduce",
)


def scatter_kernel(
    ctx_count,
    hid_in,
    cot_in,
    qkv_in,
    up_in,
    down_in,
    out_in,
    attended_low_in,
    projected_grad_in,
    norm_two_in,
    activated_in,
    slope_in,
    stats_in,
    vec_in,
    norm_one_in,
    down_grad,
    small_result,
    qkv_result,
    up_result,
    down_result,
    out_grad_result,
    out_result,
    hid_result,
    wide,
    weight,
    slope,
    act,
    attended_low,
    out_weight,
    qkv_weight,
    projected_grad,
    stats,
    vec,
    qkv_sum,
    cot_sum,
    up_sum,
    sums,
    qkv_rows,
    tiles,
    small_kept,
    small_core,
    small_plane,
    qkv_kept,
    qkv_core,
    qkv_plane,
    up_kept,
    up_core,
    up_plane,
    down_kept,
    down_core,
    down_plane,
    out_kept,
    out_core,
    out_plane,
    out_part,
    out_from_y,
    out_slots,
    hid_part,
    hid_from_y,
    hid_slots,
    total,
    out_given,
    send,
    recv,
    local,
):
    place = Place(ctx_count)
    copies = Copies(send, recv, local)
    c, x = place.c, place.x
    qkv_given = up_kept.at[:, :, :, : qkv_kept.shape[3]]
    half = up_kept.shape[3] // 2
    halves = {" a": slice(0, half), " b": slice(half, 2 * half)}
    grads = {
        "qkv": GradScatter(place, copies, qkv_given, qkv_kept, qkv_core, qkv_plane, qkv_result),
        "small": GradScatter(place, copies, tiles, small_kept, small_core, small_plane, small_result),
    }
    for name, cols in halves.items():
        grads["down" + name] = GradScatter(
            place, copies, down_grad, down_kept, down_core, down_plane, down_result, cols
        )
        grads["up" + name] = GradScatter(place, copies, down_core, up_kept, up_core, up_plane, up_result, cols)
    outs_s = TokenScatter(place, copies, out_part, out_from_y, out_slots, total, out_result)
    hid_s = TokenScatter(place, copies, hid_part, hid_from_y, hid_slots, total, hid_result)
    out_swap = copies.remote(out_given, out_core, place.other_core())
    out_across = copies.remote(out_kept.at[1 - x], out_plane, place.other_plane())
    out_own = copies.inside(out_kept.at[x], out_grad_result)
    loads = {
        name: copies.inside(src, dst)
        for name, src, dst in (
            ("activated", activated_in, act),
            ("attended_low", attended_low_in, attended_low),
            ("out", out_in, out_weight),
            ("down", down_in, weight),
            ("cot", cot_in, wide),
            ("norm_two", norm_two_in, wide),
            ("qkv", qkv_in, qkv_weight),
            ("projected_grad", projected_grad_in, projected_grad),
            ("stats", stats_in, stats),
            ("vec", vec_in, vec),
            ("norm_one", norm_one_in, wide),
            ("up", up_in, weight),
            ("hid", hid_in, wide),
        )
    }
    early = ("activated", "attended_low", "out", "down", "projected_grad", "norm_one", "qkv", "stats", "vec")

    def out_cross():
        out_swap.wait_recv()
        for k in range(2):
            add_rows(out_kept.at[k], out_core.at[k])
        out_across.start()

    def out_finish():
        out_across.wait_recv()
        add_rows(out_kept.at[x], out_plane)
        out_own.start()

    step = slope.shape[1]
    slope_loads = [
        copies.inside(slope_in.at[pl.ds(i * step, step)], slope.at[i % 2]) for i in range(slope_in.shape[0] // step)
    ]
    waited = set()

    def need(*names):
        for name in names:
            if name not in waited:
                waited.add(name)
                loads[name].wait()

    def output_tile(i):
        need("activated", "attended_low", "out", "down")
        output_part(outs_s, i, attended_low, act, out_weight, weight)

    def inner_all():
        need("cot")
        inner_grads(wide, weight, slope, slope_loads, act)
        loads["up"].start()
        loads["norm_two"].start()

    def qkv_grads():
        need("projected_grad", "norm_one")
        columns = slice(0, qkv_kept.shape[3])
        weight_grads_by_core(place, wide, projected_grad, qkv_kept, qkv_given, columns)
        loads["cot"].start()
        column_sums(projected_grad, qkv_sum)

    def out_grads():
        need("attended_low", "cot")
        out_weight_grads(place, attended_low, wide, out_kept, out_given)
        column_sums(wide, cot_sum)

    def up_half(name, last):
        if not last:
            grads["qkv"].swap.wait_send()
        need("norm_two")
        weight_grads_by_core(place, wide, act, up_kept, down_core, halves[name])
        if last:
            loads["hid"].start()

    def hidden_tile(i):
        if i == 0:
            need("qkv", "projected_grad", "stats", "vec", "up", "hid")
            sums[...] = jnp.zeros_like(sums)
        hidden_part(hid_s, i, act, weight, projected_grad, qkv_weight, wide, stats, vec, sums)

    def pack():
        pack_small(place, sums, cot_sum, up_sum, qkv_sum, qkv_rows, tiles)

    def hidden_reduce():
        outs_s.own.wait()
        outs_s.swap.wait_send()
        hid_s.reduce()

    steps = {
        "qkv grads": qkv_grads,
        "out grads": out_grads,
        "out swap": out_swap.start,
        "out cross": out_cross,
        "out finish": out_finish,
        "inner": inner_all,
        "up a grad": functools.partial(up_half, " a", False),
        "up b grad": functools.partial(up_half, " b", True),
        "up sum": lambda: column_sums(act, up_sum),
        "pack": pack,
        "outs reduce": outs_s.reduce,
        "hid reduce": hidden_reduce,
    }
    for name, scatter in grads.items():
        steps[name + " swap"] = scatter.start
        steps[name + " cross"] = scatter.cross
        steps[name + " scatter"] = scatter.scatter
    for i in range(outs_s.line):
        steps["outs tile %d" % i] = functools.partial(output_tile, i)
        steps["hid tile %d" % i] = functools.partial(hidden_tile, i)
    for j in range(outs_s.last):
        for ch in range(TOKEN_CHUNKS):
            steps["outs %d %d" % (j, ch)] = functools.partial(outs_s.step, j, ch)
            steps["hid %d %d" % (j, ch)] = functools.partial(hid_s.step, j, ch)

    for name in early:
        loads[name].start()
    slope_loads[0].start()
    slope_loads[1].start()
    greet(place)
    for name in SCATTER_ORDER:
        steps[name]()
    for scatter in list(grads.values()) + [outs_s, hid_s]:
        scatter.finish()
    out_own.wait()
    hid_s.own.wait()
    hid_s.swap.wait_send()
    for name, scatter in grads.items():
        scatter.drain(name == "qkv")
    outs_s.drain()
    hid_s.drain()
    out_swap.wait_send()
    out_across.wait_send()


def scatter_all(ctx_count, local_rows, operands):
    f32, b16 = jnp.float32, jnp.bfloat16
    hid, _, w_qkv, w_up, _, w_out = operands[:6]
    chips, groups, rows, head3 = w_qkv.shape
    part = w_up.shape[3]
    tokens, width = hid.shape
    line = chips // LINE_Y
    small = (SMALL_ROWS, LANES)
    token = (CORES, local_rows, width)
    results = [
        ((chips,) + small, f32),
        ((chips, rows, head3), b16),
        ((chips, rows, part), b16),
        ((chips, rows, part), b16),
        ((rows, width), b16),
        (token, f32),
        (token, f32),
    ]
    scratch = [
        ((tokens, width), b16),
        (w_up.shape, b16),
        ((2, 256, part), f32),
        ((tokens, part), b16),
        ((tokens, head3 // 3), b16),
        (w_out.shape, b16),
        (w_qkv.shape, b16),
        ((tokens, head3), b16),
        ((tokens, LANES), f32),
        ((8, width), f32),
        ((8, head3), f32),
        ((8, width), f32),
        ((8, part), f32),
        ((4, 8, width), f32),
        ((3 * width // LANES, LANES), f32),
        ((chips, groups) + small, f32),
    ]
    for shape, dtype in ((small, f32), ((rows, head3), b16), ((rows, part), b16), ((rows, part), b16)):
        scratch += [((chips, 2) + shape, dtype)] * 2 + [((chips,) + shape, dtype)]
    scratch += [((2, rows, width), b16)] * 2 + [((rows, width), b16)]
    chip_rows = CORES * local_rows
    for _ in range(2):
        scratch += [
            ((tokens, width), b16),
            ((line * chip_rows, width), b16),
            (((line + 1) * chip_rows, width), b16),
        ]
    scratch += [((chip_rows, width), f32), ((2, rows, width), b16)]
    anywhere = pl.BlockSpec(memory_space=pl.ANY)
    return pl.pallas_call(
        lambda *refs: scatter_kernel(ctx_count, *refs),
        out_shape=[jax.ShapeDtypeStruct(*shape) for shape in results],
        in_specs=[anywhere] * len(operands),
        out_specs=[anywhere] * len(results),
        scratch_shapes=[pltpu.VMEM(*shape) for shape in scratch]
        + [
            pltpu.SemaphoreType.DMA((128,)),
            pltpu.SemaphoreType.DMA((128,)),
            pltpu.SemaphoreType.DMA((48,)),
        ],
        compiler_params=pltpu.CompilerParams(
            collective_id=1, has_side_effects=True, vmem_limit_bytes=VMEM_BYTES
        ),
        name="scatter_all",
    )(*operands)


def finish_kernel(
    qkv_in,
    up_in,
    down_in,
    out_in,
    out_rows_in,
    hid_rows_in,
    hidden_in,
    cotangent_in,
    small,
    vec,
    ln1_gain,
    ln1_bias,
    qkv_bias,
    out_bias,
    ln2_gain,
    ln2_bias,
    up_bias,
    down_bias,
    output_out,
    grad_hidden_out,
    qkv_out,
    out_out,
    up_out,
    down_out,
    qkv_rows,
    up_rows,
    down_rows,
    out_piece,
    out_rows,
    hid_rows,
    hidden,
    cotangent,
    output,
    grad_hidden,
    qkv,
    out,
    up,
    down,
    load_sems,
    store_sems,
):
    f32 = jnp.float32
    given = (up_in, down_in, qkv_in, out_in, out_rows_in, hid_rows_in, hidden_in, cotangent_in)
    held = (up_rows, down_rows, qkv_rows, out_piece, out_rows, hid_rows, hidden, cotangent)
    loads = [pltpu.make_async_copy(src, dst, load_sems.at[i]) for i, (src, dst) in enumerate(zip(given, held))]
    made = (up, down, qkv, out, output, grad_hidden)
    asked = (up_out, down_out, qkv_out, out_out, output_out, grad_hidden_out)
    stores = [pltpu.make_async_copy(src, dst, store_sems.at[i]) for i, (src, dst) in enumerate(zip(made, asked))]
    for load in loads:
        load.start()

    total = jnp.sum(small[...], axis=0)
    half = LANES // 2
    odd = lax.axis_index("fsdp") == 1
    halves = jnp.where(odd, total[: COT_SUM + 1, half:], total[: COT_SUM + 1, :half])
    for row, ref in enumerate((ln1_gain, ln1_bias, ln2_gain, ln2_bias, out_bias)):
        ref[...] = halves[row]
    down_bias[...] = halves[COT_SUM]
    for u in range(2):
        up_bias[u * LANES : (u + 1) * LANES] = total[UP_SUM + u]
    first, middle, last = [total[QKV_SUM + u : QKV_SUM + u + 1] for u in range(3)]
    even_row = jnp.concatenate([first, middle[:, :half]], axis=1)
    odd_row = jnp.concatenate([middle[:, half:], last], axis=1)
    qkv_bias[...] = jnp.where(odd, odd_row, even_row)[0]

    chips = up_rows.shape[0]
    for i, rows, made_ref in ((0, up_rows, up), (1, down_rows, down)):
        loads[i].wait()
        size = rows.shape[2]
        for k in range(chips):
            made_ref[:, k * size : (k + 1) * size] = rows[k].astype(f32)
        stores[i].start()
    loads[2].wait()
    third = qkv.shape[1] // 3
    for k in range(chips):
        for t in range(3):
            at = t * third + k * HEAD
            qkv[:, at : at + HEAD] = qkv_rows[k, :, t * HEAD : (t + 1) * HEAD].astype(f32)
    stores[2].start()
    loads[3].wait()
    out[...] = out_piece[...].astype(f32)
    stores[3].start()

    for load in loads[4:]:
        load.wait()
    bias = vec[OUT_BIAS : OUT_BIAS + 1, :] + vec[DOWN_BIAS : DOWN_BIAS + 1, :]
    step = 32

    @pl.loop(0, hidden.shape[0] // step)
    def _(i):
        at = tile(i, step)
        both, grads = [], []
        for s in range(hidden.shape[1]):
            x = hidden[at, s, :].astype(f32)
            both.append(x + out_rows[s, at, :] + bias)
            average = jnp.mean(x, axis=1, keepdims=True)
            centered = x - average
            scale = lax.rsqrt(jnp.mean(centered * centered, axis=1, keepdims=True) + LN_EPSILON)
            xhat = centered * scale
            e = hid_rows[s, at, :]
            slope = jnp.mean(e * xhat, axis=1, keepdims=True)
            back = scale * (e - jnp.mean(e, axis=1, keepdims=True) - xhat * slope)
            grads.append(cotangent[at, s, :].astype(f32) + back)
        output[at] = jnp.stack(both, axis=1).astype(output.dtype)
        grad_hidden[at] = jnp.stack(grads, axis=1)

    stores[4].start()
    stores[5].start()
    for store in stores:
        store.wait()


def finish_all(qkv_rows, up_rows, down_rows, out_sum, out_rows, hid_rows, hidden, cotangent, small, vec):
    f32 = jnp.float32
    rows, width = out_sum.shape
    part, head3 = up_rows.shape[0] * up_rows.shape[2], qkv_rows.shape[0] * qkv_rows.shape[2]
    vectors = [rows, rows, 3 * rows, rows, rows, rows, part // width * rows, rows]
    big = [
        (hidden.shape, hidden.dtype),
        (hidden.shape, f32),
        ((rows, head3), f32),
        ((rows, width), f32),
        ((rows, part), f32),
        ((rows, part), f32),
    ]
    operands = (qkv_rows, up_rows, down_rows, out_sum, out_rows, hid_rows, hidden, cotangent)
    anywhere, held = pl.BlockSpec(memory_space=pl.ANY), pl.BlockSpec(memory_space=pltpu.VMEM)
    return pl.pallas_call(
        finish_kernel,
        out_shape=[jax.ShapeDtypeStruct((n,), f32) for n in vectors]
        + [jax.ShapeDtypeStruct(*shape) for shape in big],
        in_specs=[anywhere] * len(operands) + [held, held],
        out_specs=[held] * len(vectors) + [anywhere] * len(big),
        scratch_shapes=[pltpu.VMEM(o.shape, o.dtype) for o in operands]
        + [pltpu.VMEM(*shape) for shape in big]
        + [pltpu.SemaphoreType.DMA((8,)), pltpu.SemaphoreType.DMA((8,))],
        compiler_params=pltpu.CompilerParams(vmem_limit_bytes=VMEM_BYTES),
        name="finish_all",
    )(*operands, small, vec)


def split_body(
    hidden,
    cotangent,
    pairing,
    ln1_gain,
    ln1_bias,
    qkv_weight,
    qkv_bias,
    out_weight,
    out_bias,
    ln2_gain,
    ln2_bias,
    up_weight,
    up_bias,
    down_weight,
    down_bias,
):
    ctx_count = lax.axis_size("ctx")
    (
        hid_all,
        cot_all,
        w_qkv,
        w_up,
        w_down,
        w_out,
        attended_low,
        projected_grad,
        norm_two,
        activated,
        slope,
        norm_one,
        grad_down,
        vec,
        stats,
    ) = gather_all(
        ctx_count,
        hidden,
        cotangent,
        (ln1_gain, ln1_bias, ln2_gain, ln2_bias, out_bias, down_bias, qkv_bias, up_bias),
        qkv_weight,
        up_weight,
        down_weight,
        out_weight,
        pairing,
    )
    small_sum, qkv_rows, up_rows, down_rows, out_sum, out_rows, hid_rows = scatter_all(
        ctx_count,
        hidden.shape[0],
        (
            hid_all,
            cot_all,
            w_qkv,
            w_up,
            w_down,
            w_out,
            attended_low,
            projected_grad,
            norm_two,
            activated,
            slope,
            stats,
            vec,
            norm_one,
            grad_down,
        ),
    )
    (
        grad_ln1_gain,
        grad_ln1_bias,
        grad_qkv_bias,
        grad_out_bias,
        grad_ln2_gain,
        grad_ln2_bias,
        grad_up_bias,
        grad_down_bias,
        output,
        grad_hidden,
        grad_qkv_weight,
        grad_out_weight,
        grad_up_weight,
        grad_down_weight,
    ) = finish_all(
        qkv_rows, up_rows, down_rows, out_sum, out_rows, hid_rows, hidden, cotangent, small_sum, vec
    )
    return (
        output,
        grad_hidden,
        grad_ln1_gain,
        grad_ln1_bias,
        grad_qkv_weight,
        grad_qkv_bias,
        grad_out_weight,
        grad_out_bias,
        grad_ln2_gain,
        grad_ln2_bias,
        grad_up_weight,
        grad_up_bias,
        grad_down_weight,
        grad_down_bias,
    )


def solution(mesh):
    body = split_body if split_fits(mesh) else general_body
    return jax.shard_map(
        body,
        mesh=mesh,
        in_specs=(
            P("ctx", "fsdp", None),
            P("ctx", "fsdp", None),
            P(),
            P(("ctx", "fsdp")),
            P(("ctx", "fsdp")),
            P(("ctx", "fsdp"), None),
            P(("ctx", "fsdp")),
            P(("ctx", "fsdp"), None),
            P(("ctx", "fsdp")),
            P(("ctx", "fsdp")),
            P(("ctx", "fsdp")),
            P(("ctx", "fsdp"), None),
            P(("ctx", "fsdp")),
            P(("ctx", "fsdp"), None),
            P(("ctx", "fsdp")),
        ),
        out_specs=(
            P("ctx", "fsdp", None),
            P("ctx", "fsdp", None),
            P(("ctx", "fsdp")),
            P(("ctx", "fsdp")),
            P(("ctx", "fsdp"), None),
            P(("ctx", "fsdp")),
            P(("ctx", "fsdp"), None),
            P(("ctx", "fsdp")),
            P(("ctx", "fsdp")),
            P(("ctx", "fsdp")),
            P(("ctx", "fsdp"), None),
            P(("ctx", "fsdp")),
            P(("ctx", "fsdp"), None),
            P(("ctx", "fsdp")),
        ),
        check_vma=False,
    )
```

```python
import functools

import jax
import jax.numpy as jnp
from jax import lax
from jax.experimental import pallas as pl
from jax.experimental.pallas import tpu as pltpu
from jax.sharding import PartitionSpec as P

HEAD = 256
ROT = 64


LN_EPSILON = 1e-05
VERY_LOW = -1e30


def layer_norm(values, ln_gain, ln_shift):
    average = jnp.mean(values, axis=-1, keepdims=True)
    centered = values - average
    spread = jnp.mean(centered * centered, axis=-1, keepdims=True)
    return centered * lax.rsqrt(spread + LN_EPSILON) * ln_gain + ln_shift


def gelu_exact(values):
    return jax.nn.gelu(values, approximate=False)


def rotate(values, positions):
    half_rot = ROT // 2
    frequency = 1.0 / 10000.0 ** (jnp.arange(half_rot).astype(values.dtype) * 2.0 / ROT)
    angles = positions.astype(values.dtype)[:, None] * frequency[None, :]
    shape_out = (angles.shape[0],) + (1,) * (values.ndim - 2) + (ROT,)
    cosine = jnp.concatenate([jnp.cos(angles), jnp.cos(angles)], axis=-1).reshape(shape_out)
    sine_part = jnp.concatenate([jnp.sin(angles), jnp.sin(angles)], axis=-1).reshape(shape_out)
    rot_part = values[..., :ROT]
    turned = jnp.concatenate([-rot_part[..., half_rot:], rot_part[..., :half_rot]], axis=-1)
    return jnp.concatenate([rot_part * cosine + turned * sine_part, values[..., ROT:]], axis=-1)


def row_positions(pairing, first_row, row_count, block_rows, ctx_count):
    row_ids = first_row + jnp.arange(row_count, dtype=jnp.int32)
    device_ids = row_ids // (2 * block_rows)
    within = row_ids % (2 * block_rows)
    matches = device_ids[:, None] == jnp.arange(ctx_count, dtype=jnp.int32)[None, :]
    owned_block = jnp.sum(jnp.where(matches, pairing[None, :], 0), axis=1)
    blocks = jnp.where(within < block_rows, owned_block, 2 * ctx_count - 1 - owned_block)
    return blocks * block_rows + within % block_rows


def heads_view(values, row_total, seq_count):
    return values.reshape(row_total, seq_count, -1, HEAD)


def contract_rows(left, right):
    return lax.dot_general(
        left, right, (((0,), (0,)), ((), ())), preferred_element_type=jnp.float32
    )


def contract_cols(left, right):
    return lax.dot_general(
        left, right, (((1,), (1,)), ((), ())), preferred_element_type=jnp.float32
    )


def pair_grads(
    query_rows, grad_rows, log_rows, delta_rows, query_pos, key_heads, value_heads, key_pos, scaling
):
    scores = (
        jnp.einsum("qshd,kshd->shqk", query_rows, key_heads, preferred_element_type=jnp.float32)
        * scaling
    )
    allowed = key_pos[None, None, None, :] <= query_pos[None, None, :, None]
    probabilities = jnp.where(allowed, jnp.exp(scores - log_rows[..., None]), 0.0)
    prob_grad = jnp.einsum(
        "qshd,kshd->shqk", grad_rows, value_heads, preferred_element_type=jnp.float32
    )
    score_grad = (probabilities * (prob_grad - delta_rows[..., None])).astype(jnp.bfloat16)
    return (score_grad, probabilities.astype(jnp.bfloat16))


def general_body(
    hidden,
    cotangent,
    pairing,
    ln1_gain,
    ln1_bias,
    qkv_weight,
    qkv_bias,
    out_weight,
    out_bias,
    ln2_gain,
    ln2_bias,
    up_weight,
    up_bias,
    down_weight,
    down_bias,
):
    local_rows, seq_count, model_width = hidden.shape
    block_rows = local_rows // 2
    ctx_count = lax.axis_size("ctx")
    head_count = model_width // HEAD
    scaling = HEAD ** (-0.5)
    tokens = local_rows * seq_count
    total_rows = local_rows * ctx_count
    params = (
        lax.all_gather(ln1_gain, ("ctx", "fsdp"), axis=0, tiled=True),
        lax.all_gather(ln1_bias, ("ctx", "fsdp"), axis=0, tiled=True),
        lax.all_gather(qkv_weight, ("ctx", "fsdp"), axis=0, tiled=True),
        lax.all_gather(qkv_bias, ("ctx", "fsdp"), axis=0, tiled=True),
        lax.all_gather(out_weight, ("ctx", "fsdp"), axis=0, tiled=True),
        lax.all_gather(out_bias, ("ctx", "fsdp"), axis=0, tiled=True),
        lax.all_gather(ln2_gain, ("ctx", "fsdp"), axis=0, tiled=True),
        lax.all_gather(ln2_bias, ("ctx", "fsdp"), axis=0, tiled=True),
        lax.all_gather(up_weight, ("ctx", "fsdp"), axis=0, tiled=True),
        lax.all_gather(up_bias, ("ctx", "fsdp"), axis=0, tiled=True),
        lax.all_gather(down_weight, ("ctx", "fsdp"), axis=0, tiled=True),
        lax.all_gather(down_bias, ("ctx", "fsdp"), axis=0, tiled=True),
    )
    (
        gain_one,
        shift_one,
        w_qkv,
        b_qkv,
        w_out,
        b_out,
        gain_two,
        shift_two,
        w_up,
        b_up,
        w_down,
        b_down,
    ) = params
    ff_width = w_up.shape[1]
    hidden_f = hidden.astype(jnp.float32).reshape(tokens, model_width)
    own_pos = row_positions(
        pairing, lax.axis_index("ctx") * local_rows, local_rows, block_rows, ctx_count
    )
    normed_one, ln_one_pull = jax.vjp(
        layer_norm, hidden_f, gain_one.astype(jnp.float32), shift_one.astype(jnp.float32)
    )
    normed_one_low = normed_one.astype(jnp.bfloat16)
    projected = jnp.dot(normed_one_low, w_qkv, preferred_element_type=jnp.float32) + b_qkv.astype(
        jnp.float32
    )
    query_f, rotation_pull = jax.vjp(
        lambda values: rotate(values, own_pos),
        heads_view(projected[:, :model_width], local_rows, seq_count),
    )
    query_b = query_f.astype(jnp.bfloat16)
    key_b = (
        rotate(
            heads_view(projected[:, model_width : 2 * model_width], local_rows, seq_count), own_pos
        )
        .astype(jnp.bfloat16)
        .reshape(local_rows, seq_count, model_width)
    )
    value_b = (
        projected[:, 2 * model_width :]
        .astype(jnp.bfloat16)
        .reshape(local_rows, seq_count, model_width)
    )
    running_max = jnp.full((seq_count, head_count, local_rows), VERY_LOW, jnp.float32)
    key_piece = lax.all_gather(key_b, "ctx", axis=0, tiled=True)
    value_piece = lax.all_gather(value_b, "ctx", axis=0, tiled=True)
    row_total = key_piece.shape[0]
    key_pos = row_positions(pairing, jnp.int32(0), row_total, block_rows, ctx_count)
    scores = (
        jnp.einsum(
            "qshd,kshd->shqk",
            query_b,
            heads_view(key_piece, row_total, seq_count),
            preferred_element_type=jnp.float32,
        )
        * scaling
    )
    allowed = key_pos[None, None, None, :] <= own_pos[None, None, :, None]
    piece_max = jnp.max(jnp.where(allowed, scores, VERY_LOW), axis=-1)
    new_max = jnp.maximum(running_max, piece_max)
    weights = jnp.where(allowed, jnp.exp(scores - new_max[..., None]), 0.0)
    new_total = jnp.sum(weights, axis=-1)
    mixture = jnp.einsum(
        "shqk,kshd->qshd",
        weights.astype(jnp.bfloat16),
        heads_view(value_piece, row_total, seq_count),
        preferred_element_type=jnp.float32,
    )
    log_total = new_max + jnp.log(new_total)
    attended = mixture / jnp.transpose(new_total, (2, 0, 1))[..., None]
    attended_low = attended.astype(jnp.bfloat16).reshape(tokens, model_width)
    branch_attn = jnp.dot(attended_low, w_out, preferred_element_type=jnp.float32) + b_out.astype(
        jnp.float32
    )
    normed_two, ln_two_pull = jax.vjp(
        layer_norm, hidden_f, gain_two.astype(jnp.float32), shift_two.astype(jnp.float32)
    )
    normed_two_low = normed_two.astype(jnp.bfloat16)
    inner_act = jnp.dot(normed_two_low, w_up, preferred_element_type=jnp.float32) + b_up.astype(
        jnp.float32
    )
    activated_f, gelu_pull = jax.vjp(gelu_exact, inner_act)
    activated = activated_f.astype(jnp.bfloat16)
    branch_mlp = contract_cols(activated, w_down) + b_down.astype(jnp.float32)
    output = (
        (hidden_f + branch_attn + branch_mlp)
        .astype(jnp.bfloat16)
        .reshape(local_rows, seq_count, model_width)
    )
    back_qkv, back_out, back_up, back_down = (
        lax.all_gather(qkv_weight, ("ctx", "fsdp"), axis=0, tiled=True),
        lax.all_gather(out_weight, ("ctx", "fsdp"), axis=0, tiled=True),
        lax.all_gather(up_weight, ("ctx", "fsdp"), axis=0, tiled=True),
        lax.all_gather(down_weight, ("ctx", "fsdp"), axis=0, tiled=True),
    )
    grad_out = cotangent.reshape(tokens, model_width)
    grad_f = grad_out.astype(jnp.float32)
    bias_sum = jnp.sum(grad_f, axis=0)
    up_grad = jnp.dot(grad_out, back_down, preferred_element_type=jnp.float32)
    inner_grad = gelu_pull(up_grad)[0].astype(jnp.bfloat16)
    norm_two_grad = contract_cols(inner_grad, back_up)
    dx_two, dgain_two, dshift_two = ln_two_pull(norm_two_grad)
    up_bias_sum = jnp.sum(inner_grad, axis=0, dtype=jnp.float32)
    mlp_small = jnp.concatenate(
        [
            up_bias_sum.reshape(model_width, -1),
            jnp.stack([bias_sum, dgain_two, dshift_two], axis=1),
        ],
        axis=1,
    )
    up_w_sum, down_w_sum, mlp_small_sum = (
        lax.psum_scatter(
            contract_rows(normed_two_low, inner_grad),
            ("ctx", "fsdp"),
            scatter_dimension=0,
            tiled=True,
        ),
        lax.psum_scatter(
            contract_rows(grad_out, activated), ("ctx", "fsdp"), scatter_dimension=0, tiled=True
        ),
        lax.psum_scatter(mlp_small, ("ctx", "fsdp"), scatter_dimension=0, tiled=True),
    )
    ratio = ff_width // model_width
    attn_grad = contract_cols(grad_out, back_out).astype(jnp.bfloat16)
    out_w_grad = contract_rows(attended_low, grad_out)
    grad_heads = heads_view(attn_grad, local_rows, seq_count)
    row_delta = jnp.einsum("qshd,qshd->shq", grad_heads.astype(jnp.float32), attended)
    keys_all, values_all = (
        lax.all_gather(key_b, "ctx", axis=0, tiled=True),
        lax.all_gather(value_b, "ctx", axis=0, tiled=True),
    )
    key_block = 512
    block_count = total_rows // key_block
    starts = jnp.arange(block_count, dtype=jnp.int32) * key_block

    def query_step(query_grad, inputs):
        key_piece, value_piece, offset = inputs
        key_pos = row_positions(pairing, offset, key_block, block_rows, ctx_count)
        key_heads = heads_view(key_piece, key_block, seq_count)
        value_heads = heads_view(value_piece, key_block, seq_count)
        score_grad, unused = pair_grads(
            query_b,
            grad_heads,
            log_total,
            row_delta,
            own_pos,
            key_heads,
            value_heads,
            key_pos,
            scaling,
        )
        query_grad = (
            query_grad
            + jnp.einsum(
                "shqk,kshd->qshd", score_grad, key_heads, preferred_element_type=jnp.float32
            )
            * scaling
        )
        return (query_grad, None)

    query_grad, unused_out = lax.scan(
        query_step,
        jnp.zeros((local_rows, seq_count, head_count, HEAD), jnp.float32),
        (
            keys_all.reshape(block_count, key_block, seq_count, model_width),
            values_all.reshape(block_count, key_block, seq_count, model_width),
            starts,
        ),
    )
    queries_all, grads_all = (
        lax.all_gather(query_b, "ctx", axis=0, tiled=True),
        lax.all_gather(grad_heads, "ctx", axis=0, tiled=True),
    )
    logs_all, deltas_all = (
        lax.all_gather(log_total, "ctx", axis=2, tiled=True),
        lax.all_gather(row_delta, "ctx", axis=2, tiled=True),
    )
    own_keys = heads_view(key_b, local_rows, seq_count)
    own_values = heads_view(value_b, local_rows, seq_count)

    def key_step(carry, inputs):
        key_acc, value_acc = carry
        query_piece, grad_piece, log_piece, delta_piece, offset = inputs
        query_pos = row_positions(pairing, offset, key_block, block_rows, ctx_count)
        score_grad, probs_low = pair_grads(
            query_piece,
            grad_piece,
            log_piece,
            delta_piece,
            query_pos,
            own_keys,
            own_values,
            own_pos,
            scaling,
        )
        key_acc = (
            key_acc
            + jnp.einsum(
                "shqk,qshd->kshd", score_grad, query_piece, preferred_element_type=jnp.float32
            )
            * scaling
        )
        value_acc = value_acc + jnp.einsum(
            "shqk,qshd->kshd", probs_low, grad_piece, preferred_element_type=jnp.float32
        )
        return ((key_acc, value_acc), None)

    empty_acc = jnp.zeros((local_rows, seq_count, head_count, HEAD), jnp.float32)
    log_blocks = jnp.moveaxis(logs_all.reshape(seq_count, head_count, block_count, key_block), 2, 0)
    delta_blocks = jnp.moveaxis(
        deltas_all.reshape(seq_count, head_count, block_count, key_block), 2, 0
    )
    (key_sum, value_sum), unused_keys = lax.scan(
        key_step,
        (empty_acc, empty_acc),
        (
            queries_all.reshape(block_count, key_block, seq_count, head_count, HEAD),
            grads_all.reshape(block_count, key_block, seq_count, head_count, HEAD),
            log_blocks,
            delta_blocks,
            starts,
        ),
    )
    key_owned = key_sum.reshape(local_rows, seq_count, model_width)
    value_owned = value_sum.reshape(local_rows, seq_count, model_width)
    query_pre = rotation_pull(query_grad)[0].reshape(tokens, model_width)
    key_pre = rotation_pull(heads_view(key_owned, local_rows, seq_count))[0].reshape(
        tokens, model_width
    )
    value_pre = value_owned.reshape(tokens, model_width)
    projected_grad = jnp.concatenate([query_pre, key_pre, value_pre], axis=1).astype(jnp.bfloat16)
    norm_one_grad = contract_cols(projected_grad, back_qkv)
    dx_one, dgain_one, dshift_one = ln_one_pull(norm_one_grad)
    qkv_bias_sum = jnp.sum(projected_grad, axis=0, dtype=jnp.float32)
    attn_small = jnp.concatenate(
        [
            qkv_bias_sum.reshape(model_width, -1),
            jnp.stack([bias_sum, dgain_one, dshift_one], axis=1),
        ],
        axis=1,
    )
    qkv_w_sum, out_w_sum, attn_small_sum = (
        lax.psum_scatter(
            contract_rows(normed_one_low, projected_grad),
            ("ctx", "fsdp"),
            scatter_dimension=0,
            tiled=True,
        ),
        lax.psum_scatter(out_w_grad, ("ctx", "fsdp"), scatter_dimension=0, tiled=True),
        lax.psum_scatter(attn_small, ("ctx", "fsdp"), scatter_dimension=0, tiled=True),
    )
    grad_hidden = (grad_f + dx_one + dx_two).reshape(local_rows, seq_count, model_width)
    return (
        output,
        grad_hidden,
        attn_small_sum[:, 4],
        attn_small_sum[:, 5],
        qkv_w_sum,
        attn_small_sum[:, :3].reshape(-1),
        out_w_sum,
        attn_small_sum[:, 3],
        mlp_small_sum[:, ratio + 1],
        mlp_small_sum[:, ratio + 2],
        up_w_sum,
        mlp_small_sum[:, :ratio].reshape(-1),
        down_w_sum,
        mlp_small_sum[:, ratio],
    )


MESH = pl.DeviceIdType.MESH
CORES = 2
LINE_Y = 2
VMEM_BYTES = 60 * 2**20


def split_fits(mesh):
    return mesh.shape["ctx"] == 16 and mesh.shape["fsdp"] == 2


class Place:
    def __init__(self, ctx_count):
        self.chips = ctx_count // CORES
        self.line = self.chips // LINE_Y
        index = lax.axis_index("ctx")
        self.c = index % CORES
        self.chip = index // CORES
        self.y = self.chip % LINE_Y
        self.z = self.chip // LINE_Y
        self.x = lax.axis_index("fsdp")

    def at(self, z, y, c, x):
        return ((z * LINE_Y + y) * CORES + c, x)

    def other_core(self):
        return self.at(self.z, self.y, 1 - self.c, self.x)

    def other_plane(self):
        return self.at(self.z, self.y, self.c, 1 - self.x)

    def other_y(self):
        return self.at(self.z, 1 - self.y, self.c, self.x)

    def plane_offsets(self):
        return [(dz, dy) for dz in range(self.line) for dy in range(LINE_Y) if dz or dy]

    def shifted(self, dz, dy):
        return (self.z + dz) % self.line, (self.y + dy) % LINE_Y


class Copies:
    def __init__(self, send, recv, local):
        self.send, self.recv, self.local = send, recv, local
        self.remotes, self.locals = 0, 0

    def reserve(self, count):
        self.remotes += count
        return self.remotes - count

    def remote(self, src, dst, device):
        return self.remote_at(self.reserve(1), src, dst, device)

    def remote_at(self, i, src, dst, device):
        return pltpu.make_async_remote_copy(
            src_ref=src,
            dst_ref=dst,
            send_sem=self.send.at[i],
            recv_sem=self.recv.at[i],
            device_id=device,
            device_id_type=MESH,
        )

    def inside(self, src, dst):
        i = self.locals
        self.locals += 1
        return pltpu.make_async_copy(src, dst, self.local.at[i])


def greet(place):
    barrier = pltpu.get_barrier_semaphore()
    partners = [place.other_core(), place.other_plane()]
    for dz, dy in place.plane_offsets():
        z, y = place.shifted(dz, dy)
        partners.append(place.at(z, y, place.c, place.x))
    for partner in partners:
        pl.semaphore_signal(barrier, inc=1, device_id=partner, device_id_type=MESH)
    pl.semaphore_wait(barrier, len(partners))


TOKEN_CHUNKS = 2


class TokenGather:
    def __init__(self, place, copies, own, whole):
        self.place, self.copies, self.whole = place, copies, whole
        c, chip, z, y = place.c, place.chip, place.z, place.y
        rows = own.shape[1]
        block = whole.at[tile(chip * CORES + c, rows)]
        self.first = copies.remote(own.at[1 - c], block, place.other_core())
        self.mine = copies.inside(own.at[c], block)
        self.size = CORES * rows // TOKEN_CHUNKS
        self.last = last = place.line - 1
        up = place.at(jnp.minimum(z + 1, last), y, c, place.x)
        down = place.at(jnp.maximum(z - 1, 0), y, c, place.x)
        over = place.other_y()
        chunks = range(TOKEN_CHUNKS)
        self.ups = [[self.copy(z - j, ch, up) for ch in chunks] for j in range(last)]
        self.downs = [[self.copy(z + j, ch, down) for ch in chunks] for j in range(last)]
        self.over_own = [self.copy(z, ch, over) for ch in chunks]
        self.over_ups = [[self.copy(z - 1 - j, ch, over) for ch in chunks] for j in range(last)]
        self.over_downs = [[self.copy(z + 1 + j, ch, over) for ch in chunks] for j in range(last)]

    def copy(self, z, ch, device):
        chip = jnp.clip(z, 0, self.last) * LINE_Y + self.place.y
        chunk = self.whole.at[tile(chip * TOKEN_CHUNKS + ch, self.size)]
        return self.copies.remote(chunk, chunk, device)

    def start(self):
        self.mine.start()
        self.first.start()

    def spread(self, ch):
        if ch == 0:
            self.mine.wait()
            self.first.wait_recv()
        z = self.place.z
        pl.when(z < self.last)(lambda: self.ups[0][ch].start())
        pl.when(z > 0)(lambda: self.downs[0][ch].start())
        self.over_own[ch].start()

    def step(self, j, ch):
        z, last = self.place.z, self.last

        @pl.when(z - 1 - j >= 0)
        def _():
            self.ups[j][ch].wait_recv()
            if j + 1 < last:
                pl.when(z < last)(lambda: self.ups[j + 1][ch].start())
            self.over_ups[j][ch].start()

        @pl.when(z + 1 + j <= last)
        def _():
            self.downs[j][ch].wait_recv()
            if j + 1 < last:
                pl.when(z > 0)(lambda: self.downs[j + 1][ch].start())
            self.over_downs[j][ch].start()

    def finish(self):
        z, last = self.place.z, self.last
        for ch in range(TOKEN_CHUNKS):
            self.over_own[ch].wait_recv()
            for j in range(last):
                pl.when(z - 1 - j >= 0)(lambda: self.over_ups[j][ch].wait_recv())
                pl.when(z + 1 + j <= last)(lambda: self.over_downs[j][ch].wait_recv())

    def drain(self):
        z, last = self.place.z, self.last
        self.first.wait_send()
        for ch in range(TOKEN_CHUNKS):
            self.over_own[ch].wait_send()
            for j in range(last):
                pl.when((z - j >= 0) & (z < last))(lambda: self.ups[j][ch].wait_send())
                pl.when((z + j <= last) & (z > 0))(lambda: self.downs[j][ch].wait_send())
                pl.when(z - 1 - j >= 0)(lambda: self.over_ups[j][ch].wait_send())
                pl.when(z + 1 + j <= last)(lambda: self.over_downs[j][ch].wait_send())


class WeightGather:
    def __init__(self, place, copies, pieces, whole, columns=slice(None)):
        self.place = place
        group = 2 * place.c + place.x
        self.by_chip = []
        for dz, dy in place.plane_offsets():
            z, y = place.shifted(dz, dy)
            device = place.at(z, y, place.c, place.x)
            self.by_chip.append(
                [copies.remote(src, dst, device) for src, dst in pieces(z * LINE_Y + y, place.chip, group)]
            )
        self.kept = [copies.inside(src, dst) for src, dst in pieces(place.chip, place.chip, group)]
        mine = whole.at[:, group, :, columns]
        self.across = copies.remote(mine, mine, place.other_plane())
        pair = whole.at[:, pl.ds(2 * place.c, 2), :, columns]
        self.swap = copies.remote(pair, pair, place.other_core())

    def send(self, i):
        for copy in self.by_chip[i] + (self.kept if i == 0 else []):
            copy.start()

    def scatter(self):
        for i in range(len(self.by_chip)):
            self.send(i)

    def cross(self):
        for copy in self.kept:
            copy.wait()
        for copies in self.by_chip:
            for copy in copies:
                copy.wait_recv()
        self.across.start()

    def share(self):
        self.across.wait_recv()
        self.swap.start()

    def finish(self):
        self.swap.wait_recv()

    def drain(self):
        for copy in sum(self.by_chip, []) + [self.across, self.swap]:
            copy.wait_send()


NORM_PARTS = 2
DOWN_PARTS = "ab"
GATHER_ORDER = (
    "qkv 6",
    "up a 0",
    "up a 3",
    "qkv 0",
    "up b 2",
    "prepare hid",
    "up b 0",
    "small scatter",
    "hid spread 0",
    "qkv 5",
    "tables",
    "qkv 2",
    "small cross",
    "hid spread 1",
    "prepare cot",
    "hid 0 0",
    "hid 0 1",
    "small share",
    "up a 2",
    "down a 0",
    "out start",
    "hid 1 0",
    "small done",
    "up b 6",
    "down b 5",
    "qkv 1",
    "down a 3",
    "qkv 3",
    "up b 1",
    "hid 1 1",
    "hid 2 0",
    "qkv 4",
    "up a 4",
    "up b 3",
    "cot spread 0",
    "qkv cross",
    "down a 1",
    "hid 2 1",
    "down a 6",
    "up b 4",
    "up b 5",
    "down a 5",
    "down a 4",
    "cot 0 0",
    "up b cross",
    "hid done",
    "up a 5",
    "up a 1",
    "up a 6",
    "norm",
    "qkv share",
    "out share",
    "cot spread 1",
    "cot 1 0",
    "norm",
    "norm done",
    "up a cross",
    "cot 0 1",
    "down a 2",
    "down b 0",
    "project",
    "up a share",
    "up b share",
    "down b 4",
    "down b 6",
    "down b 1",
    "cot 2 0",
    "down a cross",
    "attend",
    "cot 1 1",
    "down b 2",
    "down b 3",
    "inner",
    "down a share",
    "cot 2 1",
    "down b cross",
    "cot done",
    "attended grads",
    "attention back",
    "down b share",
    "down grads",
)


def nn(left, right):
    return lax.dot_general(left, right, (((1,), (0,)), ((), ())), preferred_element_type=jnp.float32)


def tile(i, size):
    return pl.ds(pl.multiple_of(i * size, size), size)


def flat_rows(values):
    return values.reshape(-1, values.shape[-1])


GAIN_ONE, SHIFT_ONE, GAIN_TWO, SHIFT_TWO, OUT_BIAS, DOWN_BIAS, QKV_BIAS, UP_BIAS, SMALL_ROWS = (
    0,
    1,
    2,
    3,
    4,
    5,
    6,
    9,
    16,
)
LANES = 128


def lanes_of(shape):
    return lax.broadcasted_iota(jnp.int32, shape, len(shape) - 1)


def pack_parameters(vectors, tile_ref):
    half = LANES // 2
    ln1_gain, ln1_bias, ln2_gain, ln2_bias, out_bias, down_bias, qkv_bias, up_bias = [
        ref[...].astype(jnp.float32).reshape(1, -1) for ref in vectors
    ]
    tile_ref[...] = jnp.zeros_like(tile_ref)
    for row, values in (
        (GAIN_ONE, ln1_gain),
        (SHIFT_ONE, ln1_bias),
        (GAIN_TWO, ln2_gain),
        (SHIFT_TWO, ln2_bias),
        (OUT_BIAS, out_bias),
        (DOWN_BIAS, down_bias),
    ):
        tile_ref[row : row + 1, :half] = values
        tile_ref[row : row + 1, half:] = values
    tile_ref[QKV_BIAS : QKV_BIAS + 1, :] = qkv_bias[:, :LANES]
    tile_ref[QKV_BIAS + 1 : QKV_BIAS + 2, :half] = qkv_bias[:, LANES:]
    tile_ref[QKV_BIAS + 1 : QKV_BIAS + 2, half:] = qkv_bias[:, :half]
    tile_ref[QKV_BIAS + 2 : QKV_BIAS + 3, :] = qkv_bias[:, half:]
    tile_ref[UP_BIAS : UP_BIAS + 1, :] = up_bias[:, :LANES]
    tile_ref[UP_BIAS + 1 : UP_BIAS + 2, :] = up_bias[:, LANES:]


def position_tables(ctx_count, pairing, cosine, sine, key_pos):
    block_rows = cosine.shape[0] // (2 * ctx_count)
    half_rot = ROT // 2
    lane = lanes_of((block_rows, LANES))
    power = (lane % half_rot).astype(jnp.float32) * (2.0 / ROT)
    frequency = jnp.exp(power * -9.210340371976184)
    row = lax.broadcasted_iota(jnp.int32, (block_rows, LANES), 0)

    @pl.loop(0, ctx_count)
    def _(device):
        owned = pairing[device]
        for late in range(2):
            block = 2 * ctx_count - 1 - owned if late else owned
            where = (block * block_rows + row).astype(jnp.float32)
            angles = where * frequency
            at = tile(2 * device + late, block_rows)
            cosine[at, :] = jnp.where(lane < ROT, jnp.cos(angles), 1.0)
            sin = jnp.sin(angles)
            sine[at, :] = jnp.where(lane < half_rot, -sin, jnp.where(lane < ROT, sin, where))

    lane = lanes_of((8, LANES))
    per = LANES // (2 * block_rows)
    for first in range(0, ctx_count, per):
        block = jnp.zeros((8, LANES), jnp.int32)
        for device in range(per):
            owned = pairing[first + device]
            for late in range(2):
                value = 2 * ctx_count - 1 - owned if late else owned
                block = jnp.where(lane // block_rows == 2 * device + late, value, block)
        at = first * 2 * block_rows
        key_pos[:, at : at + LANES] = (block * block_rows + lane % block_rows).astype(jnp.float32)


def split_sequences(rows, own):
    for i in range(rows.shape[1]):
        own[i] = rows[:, i, :]


def assemble_small(place, small, vec, qkv_rows, qkv_bias, up_bias):
    chips, groups = small.shape[:2]
    low = lanes_of((1, LANES)) < LANES // 2
    for pair in range(chips * groups // 2):
        chip, group = pair // (groups // 2), pair % (groups // 2) * 2
        for row in range(6):
            a = small[chip, group, row : row + 1, :]
            b = small[chip, group + 1, row : row + 1, :]
            vec[row : row + 1, pair * LANES : (pair + 1) * LANES] = jnp.where(low, a, b)
        qkv_rows[3 * pair : 3 * pair + 1, :] = small[chip, group, QKV_BIAS : QKV_BIAS + 1, :]
        a = small[chip, group, QKV_BIAS + 1 : QKV_BIAS + 2, :]
        b = small[chip, group + 1, QKV_BIAS + 1 : QKV_BIAS + 2, :]
        qkv_rows[3 * pair + 1 : 3 * pair + 2, :] = jnp.where(low, a, b)
        qkv_rows[3 * pair + 2 : 3 * pair + 3, :] = small[chip, group + 1, QKV_BIAS + 2 : QKV_BIAS + 3, :]
    third = qkv_rows.shape[0] // 3
    per_head = HEAD // LANES
    for k in range(3):
        for u in range(per_head):
            at = (k * per_head + u) * LANES
            qkv_bias[0:1, at : at + LANES] = qkv_rows[pl.ds(k * third + place.chip * per_head + u, 1), :]
    for group in range(groups):
        for u in range(2):
            at = (group * 2 + u) * LANES
            row = UP_BIAS + u
            up_bias[0:1, at : at + LANES] = small[pl.ds(place.chip, 1), group, row : row + 1, :].reshape(1, LANES)


def norm_rows(start, count, hid, vec, norm_one, norm_two, stats):
    step = 128

    @pl.loop(0, count // step)
    def _(i):
        at = pl.ds(pl.multiple_of(start + i * step, step), step)
        x = hid[at, :].astype(jnp.float32)
        average = jnp.mean(x, axis=1, keepdims=True)
        centered = x - average
        scale = lax.rsqrt(jnp.mean(centered * centered, axis=1, keepdims=True) + LN_EPSILON)
        stats[at, 0:1] = average
        stats[at, 1:2] = scale
        xhat = centered * scale
        norm_one[at, :] = (xhat * vec[0:1, :] + vec[1:2, :]).astype(jnp.bfloat16)
        norm_two[at, :] = (xhat * vec[2:3, :] + vec[3:4, :]).astype(jnp.bfloat16)


def turned_half(values):
    half_rot = ROT // 2
    lane = lanes_of(values.shape)
    width = values.shape[-1]
    return jnp.where(
        lane < half_rot,
        pltpu.roll(values, width - half_rot, 1),
        jnp.where(lane < ROT, pltpu.roll(values, half_rot, 1), 0.0),
    )


def project(norm_one, weight, bias, cosine, sine, query, key, value):
    step = 256

    @pl.loop(0, norm_one.shape[0] // step)
    def _(i):
        at = tile(i, step)
        both = nn(norm_one[at, :], flat_rows(weight[...])) + bias[0:1, :]
        cos, sin = cosine[at, :], sine[at, :]
        for k, target in enumerate((query, key)):
            first = both[:, k * HEAD : k * HEAD + LANES]
            target[at, 0:LANES] = (first * cos + turned_half(first) * sin).astype(jnp.bfloat16)
            target[at, LANES:HEAD] = both[:, k * HEAD + LANES : (k + 1) * HEAD].astype(jnp.bfloat16)
        value[at, :] = both[:, 2 * HEAD :].astype(jnp.bfloat16)


def attend(query, key, value, sine, key_pos, attended, attended_low, probs, probs_low):
    step = 256

    @pl.loop(0, query.shape[0] // step)
    def _(i):
        at = tile(i, step)
        scores = contract_cols(query[at, :], key[...]) * HEAD**-0.5
        allowed = key_pos[0:1, :] <= sine[at, ROT : ROT + 1]
        scores = jnp.where(allowed, scores, VERY_LOW)
        highest = jnp.max(scores, axis=1, keepdims=True)
        weights = jnp.where(allowed, jnp.exp(scores - highest), 0.0)
        weights = weights / jnp.sum(weights, axis=1, keepdims=True)
        low = weights.astype(jnp.bfloat16)
        probs[at, :] = weights
        probs_low[at, :] = low
        total = nn(low, value[...])
        attended[at, :] = total
        attended_low[at, :] = total.astype(jnp.bfloat16)


def feed_inner(norm_two, weight, bias, activated, slope):
    step = 256

    @pl.loop(0, norm_two.shape[0] // step)
    def _(i):
        at = tile(i, step)
        inner = nn(norm_two[at, :], flat_rows(weight[...])) + bias[0:1, :]
        normal = 0.5 + 0.5 * lax.erf(inner * 0.5**0.5)
        activated[at, :] = (inner * normal).astype(jnp.bfloat16)
        density = (2.0 * jnp.pi) ** -0.5 * jnp.exp(-0.5 * inner * inner)
        slope[at, :] = normal + inner * density


def attended_grads(cot, weight, attended_grad):
    step = 256

    @pl.loop(0, cot.shape[0] // step)
    def _(i):
        at = tile(i, step)
        attended_grad[at, :] = contract_cols(cot[at, :], flat_rows(weight[...])).astype(jnp.bfloat16)


def attention_grads(
    query, key, value, cosine, sine, attended, attended_grad, probs, probs_low, score_grad, projected_grad
):
    step = 256
    scaling = HEAD**-0.5

    def put(at, k, grad):
        first = grad[:, 0:LANES]
        back = first * cosine[at, :] - turned_half(first) * sine[at, :]
        projected_grad[at, k * HEAD : k * HEAD + LANES] = back.astype(jnp.bfloat16)
        projected_grad[at, k * HEAD + LANES : (k + 1) * HEAD] = grad[:, LANES:].astype(jnp.bfloat16)

    @pl.loop(0, query.shape[0] // step)
    def _(i):
        at = tile(i, step)
        own = attended_grad[at, :]
        row_delta = jnp.sum(own.astype(jnp.float32) * attended[at, :], axis=1, keepdims=True)
        grad = (probs[at, :] * (contract_cols(own, value[...]) - row_delta)).astype(jnp.bfloat16)
        score_grad[at, :] = grad
        put(at, 0, nn(grad, key[...]) * scaling)

    @pl.loop(0, query.shape[0] // step)
    def _(i):
        at = tile(i, step)
        put(at, 1, contract_rows(score_grad[:, at], query[...]) * scaling)
        projected_grad[at, 2 * HEAD :] = contract_rows(probs_low[:, at], attended_grad[...]).astype(jnp.bfloat16)


def weight_grads(tokens, grads, result, first, count):
    _, groups, rows = result.shape[:3]
    step = groups * rows

    @pl.loop(first, first + count)
    def _(k):
        grad = contract_rows(tokens[:, tile(k, step)], grads[...]).astype(jnp.bfloat16)
        result[k] = grad.reshape(result.shape[1:])


def column_sums(values, result):
    step = 128
    result[...] = jnp.zeros_like(result)

    @pl.loop(0, values.shape[0] // step)
    def _(i):
        part = values[tile(i, step), :].astype(jnp.float32)
        result[...] += jnp.sum(part.reshape(-1, 8, values.shape[1]), axis=0)


def gather_kernel(
    ctx_count,
    hid_in,
    cot_in,
    ln1_gain_in,
    ln1_bias_in,
    ln2_gain_in,
    ln2_bias_in,
    out_bias_in,
    down_bias_in,
    qkv_bias_in,
    up_bias_in,
    qkv,
    up,
    down,
    out,
    pairing,
    hid_all,
    cot_all,
    qkv_all,
    up_all,
    down_all,
    out_all,
    attended_low_out,
    projected_grad_out,
    norm_two_out,
    activated_out,
    slope_out,
    norm_one_out,
    down_grad_out,
    vec_out,
    stats_out,
    hid_rows,
    cot_rows,
    hid,
    cot,
    ln1_gain,
    ln1_bias,
    ln2_gain,
    ln2_bias,
    out_bias,
    down_bias,
    qkv_bias_own,
    up_bias_own,
    small,
    hid_v,
    cot_v,
    qkv_v,
    up_v,
    out_v,
    small_v,
    cosine,
    sine,
    key_pos,
    vec,
    qkv_rows,
    qkv_bias,
    up_bias,
    norm_one,
    norm_two,
    stats,
    query,
    key,
    value,
    attended,
    attended_low,
    probs,
    probs_low,
    activated,
    slope,
    attended_grad,
    score_grad,
    projected_grad,
    send,
    recv,
    local,
):
    place = Place(ctx_count)
    copies = Copies(send, recv, local)
    width = out.shape[1]
    head = qkv_all.shape[3] // 3
    part = up_all.shape[3]

    def qkv_pieces(to, row, group):
        return [
            (
                qkv.at[:, pl.ds(pl.multiple_of(k * width + to * head, head), head)],
                qkv_v.at[row, group, :, pl.ds(k * head, head)],
            )
            for k in range(3)
        ]

    def part_gather(source, whole, first, size):
        columns = pl.ds(first, size)

        def pieces(to, row, group):
            given = pl.ds(pl.multiple_of(to * part + first, size), size)
            return [(source.at[:, given], whole.at[row, group, :, columns])]

        return WeightGather(place, copies, pieces, whole, columns)

    hid_g = TokenGather(place, copies, hid, hid_v)
    cot_g = TokenGather(place, copies, cot, cot_v)
    small_g = WeightGather(place, copies, lambda to, row, group: [(small, small_v.at[row, group])], small_v)
    qkv_g = WeightGather(place, copies, qkv_pieces, qkv_v)
    weights = {"qkv": qkv_g}
    for name, source, whole, letters in (("up", up, up_v, "ab"), ("down", down, down_all, DOWN_PARTS)):
        size = part // len(letters)
        for i, letter in enumerate(letters):
            weights[name + " " + letter] = part_gather(source, whole, i * size, size)
    group = 2 * place.c + place.x
    out_mine = copies.inside(out, out_v.at[group])
    out_across = copies.remote(out, out_v.at[group], place.other_plane())
    out_pair = out_v.at[pl.ds(2 * place.c, 2)]
    out_swap = copies.remote(out_pair, out_pair, place.other_core())
    loads = {
        name: copies.inside(src, dst)
        for name, src, dst in (
            ("hid rows", hid_in, hid_rows),
            ("cot rows", cot_in, cot_rows),
        )
    }
    stores = {
        name: copies.inside(src, dst)
        for name, src, dst in (
            ("hid", hid_v, hid_all),
            ("cot", cot_v, cot_all),
            ("qkv", qkv_v, qkv_all),
            ("up", up_v, up_all),
            ("out", out_v, out_all),
            ("vec", vec, vec_out),
            ("stats", stats, stats_out),
            ("attended_low", attended_low, attended_low_out),
            ("norm_two", norm_two, norm_two_out),
            ("activated", activated, activated_out),
            ("slope", slope, slope_out),
            ("projected_grad", projected_grad, projected_grad_out),
            ("norm_one", norm_one, norm_one_out),
        )
    }

    quarter = place.chips // 4
    down_stores = [
        copies.inside(up_v.at[pl.ds(i * quarter, quarter)], down_grad_out.at[pl.ds(i * quarter, quarter)])
        for i in range(4)
    ]
    rows = hid_v.shape[0]
    normed = iter(range(NORM_PARTS))

    def norm_next():
        part_rows = rows // NORM_PARTS
        norm_rows(next(normed) * part_rows, part_rows, hid_v, vec, norm_one, norm_two, stats)

    def norm_done():
        stores["norm_one"].start()
        stores["norm_two"].start()
        stores["stats"].start()

    def small_done():
        small_g.finish()
        assemble_small(place, small_v, vec, qkv_rows, qkv_bias, up_bias)
        stores["vec"].start()

    def hid_done():
        hid_g.finish()
        stores["hid"].start()

    def project_all():
        qkv_g.finish()
        stores["qkv"].start()
        project(norm_one, qkv_v, qkv_bias, cosine, sine, query, key, value)

    def attend_all():
        attend(query, key, value, sine, key_pos, attended, attended_low, probs, probs_low)
        stores["attended_low"].start()

    def inner_all():
        weights["up a"].finish()
        weights["up b"].finish()
        stores["up"].start()
        feed_inner(norm_two, up_v, up_bias, activated, slope)
        stores["activated"].start()
        stores["slope"].start()

    def out_start():
        out_mine.start()
        out_across.start()

    def out_share():
        out_mine.wait()
        out_across.wait_recv()
        out_swap.start()

    def cot_done():
        cot_g.finish()
        stores["cot"].start()
        out_swap.wait_recv()
        stores["out"].start()

    def out_grads():
        attended_grads(cot_v, out_v, attended_grad)

    def down_grads():
        stores["up"].wait()
        weights["up a"].drain()
        weights["up b"].drain()
        count = place.chips // len(down_stores)
        for i, store in enumerate(down_stores):
            weight_grads(cot_v, activated, up_v, i * count, count)
            store.start()

    def attention_back():
        attention_grads(
            query, key, value, cosine, sine, attended, attended_grad, probs, probs_low, score_grad, projected_grad
        )
        stores["projected_grad"].start()

    steps = {
        "tables": lambda: position_tables(ctx_count, pairing, cosine, sine, key_pos),
        "small cross": small_g.cross,
        "small share": small_g.share,
        "small done": small_done,
        "out start": out_start,
        "out share": out_share,
        "hid done": hid_done,
        "norm": norm_next,
        "norm done": norm_done,
        "project": project_all,
        "attend": attend_all,
        "inner": inner_all,
        "cot done": cot_done,
        "attended grads": out_grads,
        "down grads": down_grads,
        "attention back": attention_back,
    }
    for ch in range(TOKEN_CHUNKS):
        for name, gather in (("hid", hid_g), ("cot", cot_g)):
            steps["%s spread %d" % (name, ch)] = functools.partial(gather.spread, ch)
            for j in range(place.line - 1):
                steps["%s %d %d" % (name, j, ch)] = functools.partial(gather.step, j, ch)
    for name, gather in weights.items():
        for i in range(len(gather.by_chip)):
            steps["%s %d" % (name, i)] = functools.partial(gather.send, i)
        steps[name + " cross"] = gather.cross
        steps[name + " share"] = gather.share

    vectors = (ln1_gain, ln1_bias, ln2_gain, ln2_bias, out_bias, down_bias, qkv_bias_own, up_bias_own)
    vectors_in = (
        ln1_gain_in,
        ln1_bias_in,
        ln2_gain_in,
        ln2_bias_in,
        out_bias_in,
        down_bias_in,
        qkv_bias_in,
        up_bias_in,
    )
    vector_loads = [copies.inside(src, dst) for src, dst in zip(vectors_in, vectors)]
    loads["hid rows"].start()
    for load in vector_loads:
        load.start()
    loads["cot rows"].start()
    greet(place)

    def prepare_hid():
        loads["hid rows"].wait()
        split_sequences(hid_rows, hid)
        hid_g.start()

    def prepare_cot():
        loads["cot rows"].wait()
        split_sequences(cot_rows, cot)
        cot_g.start()

    def prepare_small():
        for load in vector_loads:
            load.wait()
        pack_parameters(vectors, small)
        small_g.scatter()

    steps["prepare hid"] = prepare_hid
    steps["prepare cot"] = prepare_cot
    steps["small scatter"] = prepare_small
    for name in GATHER_ORDER:
        steps[name]()
    for letter in DOWN_PARTS:
        weights["down " + letter].finish()
    for store in down_stores + [stores[name] for name in stores if name != "up"]:
        store.wait()
    for gather in [hid_g, cot_g, small_g] + [weights[name] for name in weights if name[:2] != "up"]:
        gather.drain()
    out_across.wait_send()
    out_swap.wait_send()


def gather_all(ctx_count, hid, cot, vectors, qkv, up, down, out, pairing):
    f32, b16 = jnp.float32, jnp.bfloat16
    chips = ctx_count // CORES
    rows = qkv.shape[0]
    groups = CORES * 2
    tokens = ctx_count * hid.shape[0]
    width = out.shape[1]
    head3, part = qkv.shape[1] // chips, up.shape[1] // chips
    head = head3 // 3
    qkv_s = ((chips, groups, rows, head3), b16)
    part_s = ((chips, groups, rows, part), b16)
    out_s = ((groups, rows, width), b16)
    small = (SMALL_ROWS, LANES)
    small_s = ((chips, groups) + small, f32)
    wide_s, narrow_s = ((tokens, width), b16), ((tokens, head), b16)
    own_s = ((hid.shape[1], hid.shape[0], width), b16)
    results = [
        wide_s,
        wide_s,
        qkv_s,
        part_s,
        part_s,
        out_s,
        narrow_s,
        ((tokens, head3), b16),
        wide_s,
        ((tokens, part), b16),
        ((tokens, part), f32),
        wide_s,
        part_s,
        ((8, width), f32),
        ((tokens, LANES), f32),
    ]
    scratch = [
        (hid.shape, b16),
        (cot.shape, b16),
        own_s,
        own_s,
    ]
    scratch += [(vector.shape, b16) for vector in vectors]
    scratch += [
        (small, f32),
        wide_s,
        wide_s,
        qkv_s,
        part_s,
        out_s,
        small_s,
        ((tokens, LANES), f32),
        ((tokens, LANES), f32),
        ((8, tokens), f32),
        ((8, width), f32),
        ((3 * width // LANES, LANES), f32),
        ((8, head3), f32),
        ((8, part), f32),
        wide_s,
        wide_s,
        ((tokens, LANES), f32),
        narrow_s,
        narrow_s,
        narrow_s,
        ((tokens, head), f32),
        narrow_s,
        ((tokens, tokens), f32),
        ((tokens, tokens), b16),
        ((tokens, part), b16),
        ((tokens, part), f32),
        narrow_s,
        ((tokens, tokens), b16),
        ((tokens, head3), b16),
    ]
    operands = (hid, cot, *vectors, qkv, up, down, out, pairing)
    anywhere = pl.BlockSpec(memory_space=pl.ANY)
    return pl.pallas_call(
        lambda *refs: gather_kernel(ctx_count, *refs),
        out_shape=[jax.ShapeDtypeStruct(*shape) for shape in results],
        in_specs=[anywhere] * (len(operands) - 1) + [pl.BlockSpec(memory_space=pltpu.SMEM)],
        out_specs=[anywhere] * len(results),
        scratch_shapes=[pltpu.VMEM(*shape) for shape in scratch]
        + [
            pltpu.SemaphoreType.DMA((176,)),
            pltpu.SemaphoreType.DMA((176,)),
            pltpu.SemaphoreType.DMA((48,)),
        ],
        compiler_params=pltpu.CompilerParams(
            collective_id=0, has_side_effects=True, vmem_limit_bytes=VMEM_BYTES
        ),
        name="gather_all",
    )(*operands)


def add_rows(total, other):
    step = 64

    @pl.loop(0, total.shape[0] // step)
    def _(i):
        at = tile(i, step)
        both = total[at, :].astype(jnp.float32) + other[at, :].astype(jnp.float32)
        total[at, :] = both.astype(total.dtype)


class GradScatter:
    def __init__(self, place, copies, partial, kept, from_core, from_plane, result, columns=None):
        self.place = place
        c, x, chip = place.c, place.x, place.chip
        self.kept, self.from_core, self.from_plane = kept, from_core, from_plane
        self.columns = cols = slice(0, kept.shape[3]) if columns is None else columns
        self.load = None
        given = partial.at[:, :, :, cols]
        if partial.shape != kept.shape:
            self.load = copies.inside(partial.at[:, pl.ds(2 * c, 2), :, cols], kept.at[:, :, :, cols])
            given = partial.at[:, pl.ds(2 * (1 - c), 2), :, cols]
        self.swap = copies.remote(given, from_core.at[:, :, :, cols], place.other_core())
        self.across = copies.remote(
            kept.at[:, 1 - x, :, cols], from_plane.at[:, :, cols], place.other_plane()
        )
        self.scattered = []
        for dz, dy in place.plane_offsets():
            z, y = place.shifted(dz, dy)
            self.scattered.append(
                copies.remote(
                    kept.at[z * LINE_Y + y, x, :, cols], result.at[chip, :, cols], place.at(z, y, c, x)
                )
            )
        self.own = copies.inside(kept.at[chip, x, :, cols], result.at[chip, :, cols])

    def start(self):
        if self.load is not None:
            self.load.start()
        self.swap.start()

    def cross(self):
        if self.load is not None:
            self.load.wait()
        self.swap.wait_recv()
        x = self.place.x
        self.add(1 - x, self.from_core.at[:, 1 - x])
        self.across.start()
        self.add(x, self.from_core.at[:, x])

    def add(self, x, other):
        cols = self.columns

        @pl.loop(0, self.kept.shape[0])
        def _(k):
            both = self.kept[k, x, :, cols].astype(jnp.float32) + other[k, :, cols].astype(jnp.float32)
            self.kept[k, x, :, cols] = both.astype(self.kept.dtype)

    def scatter(self):
        self.across.wait_recv()
        self.add(self.place.x, self.from_plane)
        for copy in self.scattered + [self.own]:
            copy.start()

    def finish(self):
        self.own.wait()
        for copy in self.scattered:
            copy.wait_recv()

    def drain(self, swapped=False):
        for copy in self.scattered + [self.across] + ([] if swapped else [self.swap]):
            copy.wait_send()


def out_weight_grads(place, attended_low, cot, kept, given):
    step = 512

    @pl.loop(0, cot.shape[1] // step)
    def _(i):
        at = tile(i, step)
        grad = contract_rows(attended_low[...], cot[:, at]).astype(jnp.bfloat16)
        grad = grad.reshape((2,) + kept.shape[:2] + (step,))
        kept[:, :, at] = jnp.where(place.c == 0, grad[0], grad[1])
        given[:, :, at] = jnp.where(place.c == 0, grad[1], grad[0])


def weight_grads_by_core(place, tokens, grads, kept, given, columns):
    chips, half, rows = kept.shape[:3]
    step = 2 * half * rows

    @pl.loop(0, chips)
    def _(k):
        grad = contract_rows(tokens[:, tile(k, step)], grads[:, columns]).astype(jnp.bfloat16)
        grad = grad.reshape(2, half, rows, grad.shape[1])
        kept[k, :, :, columns] = jnp.where(place.c == 0, grad[0], grad[1])
        given[k, :, :, columns] = jnp.where(place.c == 0, grad[1], grad[0])


class TokenScatter:
    def __init__(self, place, copies, part, from_y, slots, total, result):
        self.place, self.copies = place, copies
        z, y, c, x = place.z, place.y, place.c, place.x
        self.part, self.from_y, self.slots, self.total = part, from_y, slots, total
        self.line = place.line
        self.last = last = self.line - 1
        self.rows = total.shape[0]
        self.size = self.rows // TOKEN_CHUNKS
        count = self.line * TOKEN_CHUNKS
        self.over_base = copies.reserve(count)
        self.up_base = copies.reserve(count)
        self.down_base = copies.reserve(count)
        self.above = place.at(jnp.minimum(z + 1, last), y, c, x)
        self.below = place.at(jnp.maximum(z - 1, 0), y, c, x)
        half = self.rows // CORES
        self.swap = copies.remote(total.at[tile(1 - c, half)], result.at[c], place.other_core())
        self.own = copies.inside(total.at[tile(c, half)], result.at[c])

    def order(self, i):
        last = self.last
        chosen = 0
        for z in range(self.line):
            far = sorted(range(self.line), key=lambda k: (-abs(k - z), min(k, last - k)))
            chosen = jnp.where(self.place.z == z, far[i], chosen)
        return chosen

    def chunk(self, ref, k, ch):
        return ref.at[tile(k * TOKEN_CHUNKS + ch, self.size)]

    def held(self, k, ch):
        return self.chunk(self.part, k * LINE_Y + self.place.y, ch)

    def copy(self, base, k, ch, src, dst, device):
        return self.copies.remote_at(base + k * TOKEN_CHUNKS + ch, src, dst, device)

    def over(self, k, ch):
        src = self.chunk(self.part, k * LINE_Y + 1 - self.place.y, ch)
        return self.copy(self.over_base, k, ch, src, self.chunk(self.from_y, k, ch), self.place.other_y())

    def up(self, k, ch):
        return self.copy(self.up_base, k, ch, self.held(k, ch), self.chunk(self.slots, k, ch), self.above)

    def down(self, k, ch):
        slot = jnp.where(self.place.z - 1 == k, self.line, k)
        return self.copy(self.down_base, k, ch, self.held(k, ch), self.chunk(self.slots, slot, ch), self.below)

    def send_over(self, k):
        for ch in range(TOKEN_CHUNKS):
            self.over(k, ch).start()

    def combine(self, k, ch):
        self.over(k, ch).wait_recv()
        add_rows(self.held(k, ch), self.chunk(self.from_y, k, ch))

    def step(self, i, ch):
        z = self.place.z
        k = self.order(i)
        self.combine(k, ch)

        @pl.when(k > z)
        def _():
            @pl.when(z > 0)
            def _():
                self.up(k, ch).wait_recv()
                add_rows(self.held(k, ch), self.chunk(self.slots, k, ch))

            self.up(k, ch).start()

        @pl.when(k < z)
        def _():
            @pl.when(z < self.last)
            def _():
                self.down(k, ch).wait_recv()
                add_rows(self.held(k, ch), self.chunk(self.slots, k, ch))

            self.down(k, ch).start()

    def reduce(self):
        z, y, last = self.place.z, self.place.y, self.last
        step = 64
        for ch in range(TOKEN_CHUNKS):
            self.combine(z, ch)
            pl.when(z > 0)(lambda: self.up(z, ch).wait_recv())
            pl.when(z < last)(lambda: self.down(z, ch).wait_recv())

        @pl.loop(0, self.rows // step)
        def _(i):
            at = tile((z * LINE_Y + y) * (self.rows // step) + i, step)
            self.total[tile(i, step), :] = self.part[at, :].astype(jnp.float32)

        def add(slot):
            @pl.loop(0, self.rows // step)
            def _(i):
                at = tile(slot * (self.rows // step) + i, step)
                self.total[tile(i, step), :] += self.slots[at, :].astype(jnp.float32)

        pl.when(z > 0)(lambda: add(z))
        pl.when(z < last)(lambda: add(last + 1))
        self.swap.start()
        self.own.start()

    def finish(self):
        self.swap.wait_recv()

    def drain(self):
        z = self.place.z
        for k in range(self.line):
            for ch in range(TOKEN_CHUNKS):
                self.over(k, ch).wait_send()
                pl.when(z < k)(lambda: self.up(k, ch).wait_send())
                pl.when(z > k)(lambda: self.down(k, ch).wait_send())


def output_part(scatter, i, attended_low, activated, out_weight, down_weight):
    k = scatter.order(i)
    at = tile(k, LINE_Y * scatter.rows)
    rows = nn(attended_low[at, :], flat_rows(out_weight[...]))
    rows = rows + contract_cols(activated[at, :], flat_rows(down_weight[...]))
    scatter.part[at, :] = rows.astype(scatter.part.dtype)
    scatter.send_over(k)


def inner_grads(cot, down_weight, slope, slope_loads, inner_grad):
    step = slope.shape[1]
    for i, load in enumerate(slope_loads):
        load.wait()
        at = slice(i * step, (i + 1) * step)
        grad = nn(cot[at, :], flat_rows(down_weight[...])) * slope[i % 2]
        inner_grad[at, :] = grad.astype(jnp.bfloat16)
        if i + 2 < len(slope_loads):
            slope_loads[i + 2].start()


def hidden_part(scatter, i, inner_grad, up_weight, projected_grad, qkv_weight, hid, stats, vec, sums):
    def by_eight(values):
        return jnp.sum(values.reshape(-1, 8, values.shape[1]), axis=0)

    k = scatter.order(i)

    @pl.loop(0, LINE_Y)
    def _(y):
        at = tile(k * LINE_Y + y, scatter.rows)
        one = contract_cols(projected_grad[at, :], flat_rows(qkv_weight[...]))
        two = contract_cols(inner_grad[at, :], flat_rows(up_weight[...]))
        xhat = (hid[at, :].astype(jnp.float32) - stats[at, 0:1]) * stats[at, 1:2]
        sums[0] += by_eight(one * xhat)
        sums[1] += by_eight(one)
        sums[2] += by_eight(two * xhat)
        sums[3] += by_eight(two)
        rows = one * vec[0:1, :] + two * vec[2:3, :]
        scatter.part[at, :] = rows.astype(scatter.part.dtype)

    scatter.send_over(k)


COT_SUM, UP_SUM, QKV_SUM = 4, 5, 7


def pack_small(place, sums, cot_sum, up_sum, qkv_sum, qkv_rows, tiles):
    chips, groups = tiles.shape[:2]
    tiles[...] = jnp.zeros_like(tiles)
    qkv_rows[...] = jnp.zeros_like(qkv_rows)
    qkv_total = jnp.sum(qkv_sum[...], axis=0, keepdims=True)
    up_total = jnp.sum(up_sum[...], axis=0, keepdims=True)
    third = qkv_rows.shape[0] // 3
    per_head = HEAD // LANES
    for k in range(3):
        for u in range(per_head):
            at = (k * per_head + u) * LANES
            qkv_rows[pl.ds(k * third + place.chip * per_head + u, 1), :] = qkv_total[:, at : at + LANES]
    first = jnp.where(place.chip == 0, 1.0, 0.0)
    norm_sums = [jnp.sum(sums[row], axis=0, keepdims=True) for row in range(4)]
    norm_sums.append(jnp.sum(cot_sum[...], axis=0, keepdims=True) * first)
    for pair in range(chips * groups // 2):
        chip, group = pair // (groups // 2), pair % (groups // 2) * 2
        at = slice(pair * LANES, (pair + 1) * LANES)
        for g in (group, group + 1):
            for row in range(5):
                tiles[chip, g, row : row + 1, :] = norm_sums[row][:, at]
            tiles[chip, g, QKV_SUM : QKV_SUM + 3, :] = qkv_rows[3 * pair : 3 * pair + 3, :]
    for group in range(groups):
        for u in range(2):
            at = (group * 2 + u) * LANES
            row = UP_SUM + u
            values = up_total[:, at : at + LANES].reshape(1, 1, LANES)
            tiles[pl.ds(place.chip, 1), group, row : row + 1, :] = values


SCATTER_ORDER = (
    "down a swap",
    "outs tile 0",
    "outs tile 1",
    "qkv grads",
    "outs 0 0",
    "down a cross",
    "outs tile 2",
    "down b swap",
    "outs 0 1",
    "out grads",
    "outs 1 0",
    "down b cross",
    "qkv swap",
    "down a scatter",
    "outs tile 3",
    "out swap",
    "inner",
    "outs 1 1",
    "outs 2 0",
    "qkv cross",
    "up a grad",
    "down b scatter",
    "up b grad",
    "hid tile 0",
    "up b swap",
    "outs 2 1",
    "out cross",
    "hid tile 1",
    "hid tile 2",
    "qkv scatter",
    "hid 0 0",
    "up a swap",
    "up b cross",
    "up sum",
    "hid 0 1",
    "hid tile 3",
    "pack",
    "hid 1 0",
    "small swap",
    "out finish",
    "small cross",
    "up b scatter",
    "hid 1 1",
    "hid 2 0",
    "outs reduce",
    "up a cross",
    "hid 2 1",
    "small scatter",
    "up a scatter",
    "hid reduce",
)


def scatter_kernel(
    ctx_count,
    hid_in,
    cot_in,
    qkv_in,
    up_in,
    down_in,
    out_in,
    attended_low_in,
    projected_grad_in,
    norm_two_in,
    activated_in,
    slope_in,
    stats_in,
    vec_in,
    norm_one_in,
    down_grad,
    small_result,
    qkv_result,
    up_result,
    down_result,
    out_grad_result,
    out_result,
    hid_result,
    wide,
    weight,
    slope,
    act,
    attended_low,
    out_weight,
    qkv_weight,
    projected_grad,
    stats,
    vec,
    qkv_sum,
    cot_sum,
    up_sum,
    sums,
    qkv_rows,
    tiles,
    small_kept,
    small_core,
    small_plane,
    qkv_kept,
    qkv_core,
    qkv_plane,
    up_kept,
    up_core,
    up_plane,
    down_kept,
    down_core,
    down_plane,
    out_kept,
    out_core,
    out_plane,
    out_part,
    out_from_y,
    out_slots,
    hid_part,
    hid_from_y,
    hid_slots,
    total,
    out_given,
    send,
    recv,
    local,
):
    place = Place(ctx_count)
    copies = Copies(send, recv, local)
    c, x = place.c, place.x
    qkv_given = up_kept.at[:, :, :, : qkv_kept.shape[3]]
    half = up_kept.shape[3] // 2
    halves = {" a": slice(0, half), " b": slice(half, 2 * half)}
    grads = {
        "qkv": GradScatter(place, copies, qkv_given, qkv_kept, qkv_core, qkv_plane, qkv_result),
        "small": GradScatter(place, copies, tiles, small_kept, small_core, small_plane, small_result),
    }
    for name, cols in halves.items():
        grads["down" + name] = GradScatter(
            place, copies, down_grad, down_kept, down_core, down_plane, down_result, cols
        )
        grads["up" + name] = GradScatter(place, copies, down_core, up_kept, up_core, up_plane, up_result, cols)
    outs_s = TokenScatter(place, copies, out_part, out_from_y, out_slots, total, out_result)
    hid_s = TokenScatter(place, copies, hid_part, hid_from_y, hid_slots, total, hid_result)
    out_swap = copies.remote(out_given, out_core, place.other_core())
    out_across = copies.remote(out_kept.at[1 - x], out_plane, place.other_plane())
    out_own = copies.inside(out_kept.at[x], out_grad_result)
    loads = {
        name: copies.inside(src, dst)
        for name, src, dst in (
            ("activated", activated_in, act),
            ("attended_low", attended_low_in, attended_low),
            ("out", out_in, out_weight),
            ("down", down_in, weight),
            ("cot", cot_in, wide),
            ("norm_two", norm_two_in, wide),
            ("qkv", qkv_in, qkv_weight),
            ("projected_grad", projected_grad_in, projected_grad),
            ("stats", stats_in, stats),
            ("vec", vec_in, vec),
            ("norm_one", norm_one_in, wide),
            ("up", up_in, weight),
            ("hid", hid_in, wide),
        )
    }
    early = ("activated", "attended_low", "out", "down", "projected_grad", "norm_one", "qkv", "stats", "vec")

    def out_cross():
        out_swap.wait_recv()
        for k in range(2):
            add_rows(out_kept.at[k], out_core.at[k])
        out_across.start()

    def out_finish():
        out_across.wait_recv()
        add_rows(out_kept.at[x], out_plane)
        out_own.start()

    step = slope.shape[1]
    slope_loads = [
        copies.inside(slope_in.at[pl.ds(i * step, step)], slope.at[i % 2]) for i in range(slope_in.shape[0] // step)
    ]
    waited = set()

    def need(*names):
        for name in names:
            if name not in waited:
                waited.add(name)
                loads[name].wait()

    def output_tile(i):
        need("activated", "attended_low", "out", "down")
        output_part(outs_s, i, attended_low, act, out_weight, weight)

    def inner_all():
        need("cot")
        inner_grads(wide, weight, slope, slope_loads, act)
        loads["up"].start()
        loads["norm_two"].start()

    def qkv_grads():
        need("projected_grad", "norm_one")
        columns = slice(0, qkv_kept.shape[3])
        weight_grads_by_core(place, wide, projected_grad, qkv_kept, qkv_given, columns)
        loads["cot"].start()
        column_sums(projected_grad, qkv_sum)

    def out_grads():
        need("attended_low", "cot")
        out_weight_grads(place, attended_low, wide, out_kept, out_given)
        column_sums(wide, cot_sum)

    def up_half(name, last):
        if not last:
            grads["qkv"].swap.wait_send()
        need("norm_two")
        weight_grads_by_core(place, wide, act, up_kept, down_core, halves[name])
        if last:
            loads["hid"].start()

    def hidden_tile(i):
        if i == 0:
            need("qkv", "projected_grad", "stats", "vec", "up", "hid")
            sums[...] = jnp.zeros_like(sums)
        hidden_part(hid_s, i, act, weight, projected_grad, qkv_weight, wide, stats, vec, sums)

    def pack():
        pack_small(place, sums, cot_sum, up_sum, qkv_sum, qkv_rows, tiles)

    def hidden_reduce():
        outs_s.own.wait()
        outs_s.swap.wait_send()
        hid_s.reduce()

    steps = {
        "qkv grads": qkv_grads,
        "out grads": out_grads,
        "out swap": out_swap.start,
        "out cross": out_cross,
        "out finish": out_finish,
        "inner": inner_all,
        "up a grad": functools.partial(up_half, " a", False),
        "up b grad": functools.partial(up_half, " b", True),
        "up sum": lambda: column_sums(act, up_sum),
        "pack": pack,
        "outs reduce": outs_s.reduce,
        "hid reduce": hidden_reduce,
    }
    for name, scatter in grads.items():
        steps[name + " swap"] = scatter.start
        steps[name + " cross"] = scatter.cross
        steps[name + " scatter"] = scatter.scatter
    for i in range(outs_s.line):
        steps["outs tile %d" % i] = functools.partial(output_tile, i)
        steps["hid tile %d" % i] = functools.partial(hidden_tile, i)
    for j in range(outs_s.last):
        for ch in range(TOKEN_CHUNKS):
            steps["outs %d %d" % (j, ch)] = functools.partial(outs_s.step, j, ch)
            steps["hid %d %d" % (j, ch)] = functools.partial(hid_s.step, j, ch)

    for name in early:
        loads[name].start()
    slope_loads[0].start()
    slope_loads[1].start()
    greet(place)
    for name in SCATTER_ORDER:
        steps[name]()
    for scatter in list(grads.values()) + [outs_s, hid_s]:
        scatter.finish()
    out_own.wait()
    hid_s.own.wait()
    hid_s.swap.wait_send()
    for name, scatter in grads.items():
        scatter.drain(name == "qkv")
    outs_s.drain()
    hid_s.drain()
    out_swap.wait_send()
    out_across.wait_send()


def scatter_all(ctx_count, local_rows, operands):
    f32, b16 = jnp.float32, jnp.bfloat16
    hid, _, w_qkv, w_up, _, w_out = operands[:6]
    chips, groups, rows, head3 = w_qkv.shape
    part = w_up.shape[3]
    tokens, width = hid.shape
    line = chips // LINE_Y
    small = (SMALL_ROWS, LANES)
    token = (CORES, local_rows, width)
    results = [
        ((chips,) + small, f32),
        ((chips, rows, head3), b16),
        ((chips, rows, part), b16),
        ((chips, rows, part), b16),
        ((rows, width), b16),
        (token, f32),
        (token, f32),
    ]
    scratch = [
        ((tokens, width), b16),
        (w_up.shape, b16),
        ((2, 256, part), f32),
        ((tokens, part), b16),
        ((tokens, head3 // 3), b16),
        (w_out.shape, b16),
        (w_qkv.shape, b16),
        ((tokens, head3), b16),
        ((tokens, LANES), f32),
        ((8, width), f32),
        ((8, head3), f32),
        ((8, width), f32),
        ((8, part), f32),
        ((4, 8, width), f32),
        ((3 * width // LANES, LANES), f32),
        ((chips, groups) + small, f32),
    ]
    for shape, dtype in ((small, f32), ((rows, head3), b16), ((rows, part), b16), ((rows, part), b16)):
        scratch += [((chips, 2) + shape, dtype)] * 2 + [((chips,) + shape, dtype)]
    scratch += [((2, rows, width), b16)] * 2 + [((rows, width), b16)]
    chip_rows = CORES * local_rows
    for _ in range(2):
        scratch += [
            ((tokens, width), b16),
            ((line * chip_rows, width), b16),
            (((line + 1) * chip_rows, width), b16),
        ]
    scratch += [((chip_rows, width), f32), ((2, rows, width), b16)]
    anywhere = pl.BlockSpec(memory_space=pl.ANY)
    return pl.pallas_call(
        lambda *refs: scatter_kernel(ctx_count, *refs),
        out_shape=[jax.ShapeDtypeStruct(*shape) for shape in results],
        in_specs=[anywhere] * len(operands),
        out_specs=[anywhere] * len(results),
        scratch_shapes=[pltpu.VMEM(*shape) for shape in scratch]
        + [
            pltpu.SemaphoreType.DMA((128,)),
            pltpu.SemaphoreType.DMA((128,)),
            pltpu.SemaphoreType.DMA((48,)),
        ],
        compiler_params=pltpu.CompilerParams(
            collective_id=1, has_side_effects=True, vmem_limit_bytes=VMEM_BYTES
        ),
        name="scatter_all",
    )(*operands)


def finish_kernel(
    qkv_in,
    up_in,
    down_in,
    out_in,
    out_rows_in,
    hid_rows_in,
    hidden_in,
    cotangent_in,
    small,
    vec,
    ln1_gain,
    ln1_bias,
    qkv_bias,
    out_bias,
    ln2_gain,
    ln2_bias,
    up_bias,
    down_bias,
    output_out,
    grad_hidden_out,
    qkv_out,
    out_out,
    up_out,
    down_out,
    qkv_rows,
    up_rows,
    down_rows,
    out_piece,
    out_rows,
    hid_rows,
    hidden,
    cotangent,
    output,
    grad_hidden,
    qkv,
    out,
    up,
    down,
    load_sems,
    store_sems,
):
    f32 = jnp.float32
    given = (up_in, down_in, qkv_in, out_in, out_rows_in, hid_rows_in, hidden_in, cotangent_in)
    held = (up_rows, down_rows, qkv_rows, out_piece, out_rows, hid_rows, hidden, cotangent)
    loads = [pltpu.make_async_copy(src, dst, load_sems.at[i]) for i, (src, dst) in enumerate(zip(given, held))]
    made = (up, down, qkv, out, output, grad_hidden)
    asked = (up_out, down_out, qkv_out, out_out, output_out, grad_hidden_out)
    stores = [pltpu.make_async_copy(src, dst, store_sems.at[i]) for i, (src, dst) in enumerate(zip(made, asked))]
    for load in loads:
        load.start()

    total = jnp.sum(small[...], axis=0)
    half = LANES // 2
    odd = lax.axis_index("fsdp") == 1
    halves = jnp.where(odd, total[: COT_SUM + 1, half:], total[: COT_SUM + 1, :half])
    for row, ref in enumerate((ln1_gain, ln1_bias, ln2_gain, ln2_bias, out_bias)):
        ref[...] = halves[row]
    down_bias[...] = halves[COT_SUM]
    for u in range(2):
        up_bias[u * LANES : (u + 1) * LANES] = total[UP_SUM + u]
    first, middle, last = [total[QKV_SUM + u : QKV_SUM + u + 1] for u in range(3)]
    even_row = jnp.concatenate([first, middle[:, :half]], axis=1)
    odd_row = jnp.concatenate([middle[:, half:], last], axis=1)
    qkv_bias[...] = jnp.where(odd, odd_row, even_row)[0]

    chips = up_rows.shape[0]
    for i, rows, made_ref in ((0, up_rows, up), (1, down_rows, down)):
        loads[i].wait()
        size = rows.shape[2]
        for k in range(chips):
            made_ref[:, k * size : (k + 1) * size] = rows[k].astype(f32)
        stores[i].start()
    loads[2].wait()
    third = qkv.shape[1] // 3
    for k in range(chips):
        for t in range(3):
            at = t * third + k * HEAD
            qkv[:, at : at + HEAD] = qkv_rows[k, :, t * HEAD : (t + 1) * HEAD].astype(f32)
    stores[2].start()
    loads[3].wait()
    out[...] = out_piece[...].astype(f32)
    stores[3].start()

    for load in loads[4:]:
        load.wait()
    bias = vec[OUT_BIAS : OUT_BIAS + 1, :] + vec[DOWN_BIAS : DOWN_BIAS + 1, :]
    step = 32

    @pl.loop(0, hidden.shape[0] // step)
    def _(i):
        at = tile(i, step)
        both, grads = [], []
        for s in range(hidden.shape[1]):
            x = hidden[at, s, :].astype(f32)
            both.append(x + out_rows[s, at, :] + bias)
            average = jnp.mean(x, axis=1, keepdims=True)
            centered = x - average
            scale = lax.rsqrt(jnp.mean(centered * centered, axis=1, keepdims=True) + LN_EPSILON)
            xhat = centered * scale
            e = hid_rows[s, at, :]
            slope = jnp.mean(e * xhat, axis=1, keepdims=True)
            back = scale * (e - jnp.mean(e, axis=1, keepdims=True) - xhat * slope)
            grads.append(cotangent[at, s, :].astype(f32) + back)
        output[at] = jnp.stack(both, axis=1).astype(output.dtype)
        for s in range(hidden.shape[1]):
            grad_hidden[at, s, :] = grads[s]

    stores[4].start()
    stores[5].start()
    for store in stores:
        store.wait()


def finish_all(qkv_rows, up_rows, down_rows, out_sum, out_rows, hid_rows, hidden, cotangent, small, vec):
    f32 = jnp.float32
    rows, width = out_sum.shape
    part, head3 = up_rows.shape[0] * up_rows.shape[2], qkv_rows.shape[0] * qkv_rows.shape[2]
    vectors = [rows, rows, 3 * rows, rows, rows, rows, part // width * rows, rows]
    big = [
        (hidden.shape, hidden.dtype),
        (hidden.shape, f32),
        ((rows, head3), f32),
        ((rows, width), f32),
        ((rows, part), f32),
        ((rows, part), f32),
    ]
    operands = (qkv_rows, up_rows, down_rows, out_sum, out_rows, hid_rows, hidden, cotangent)
    anywhere, held = pl.BlockSpec(memory_space=pl.ANY), pl.BlockSpec(memory_space=pltpu.VMEM)
    return pl.pallas_call(
        finish_kernel,
        out_shape=[jax.ShapeDtypeStruct((n,), f32) for n in vectors]
        + [jax.ShapeDtypeStruct(*shape) for shape in big],
        in_specs=[anywhere] * len(operands) + [held, held],
        out_specs=[held] * len(vectors) + [anywhere] * len(big),
        scratch_shapes=[pltpu.VMEM(o.shape, o.dtype) for o in operands]
        + [pltpu.VMEM(*shape) for shape in big]
        + [pltpu.SemaphoreType.DMA((8,)), pltpu.SemaphoreType.DMA((8,))],
        compiler_params=pltpu.CompilerParams(vmem_limit_bytes=VMEM_BYTES),
        name="finish_all",
    )(*operands, small, vec)


def split_body(
    hidden,
    cotangent,
    pairing,
    ln1_gain,
    ln1_bias,
    qkv_weight,
    qkv_bias,
    out_weight,
    out_bias,
    ln2_gain,
    ln2_bias,
    up_weight,
    up_bias,
    down_weight,
    down_bias,
):
    ctx_count = lax.axis_size("ctx")
    (
        hid_all,
        cot_all,
        w_qkv,
        w_up,
        w_down,
        w_out,
        attended_low,
        projected_grad,
        norm_two,
        activated,
        slope,
        norm_one,
        grad_down,
        vec,
        stats,
    ) = gather_all(
        ctx_count,
        hidden,
        cotangent,
        (ln1_gain, ln1_bias, ln2_gain, ln2_bias, out_bias, down_bias, qkv_bias, up_bias),
        qkv_weight,
        up_weight,
        down_weight,
        out_weight,
        pairing,
    )
    small_sum, qkv_rows, up_rows, down_rows, out_sum, out_rows, hid_rows = scatter_all(
        ctx_count,
        hidden.shape[0],
        (
            hid_all,
            cot_all,
            w_qkv,
            w_up,
            w_down,
            w_out,
            attended_low,
            projected_grad,
            norm_two,
            activated,
            slope,
            stats,
            vec,
            norm_one,
            grad_down,
        ),
    )
    (
        grad_ln1_gain,
        grad_ln1_bias,
        grad_qkv_bias,
        grad_out_bias,
        grad_ln2_gain,
        grad_ln2_bias,
        grad_up_bias,
        grad_down_bias,
        output,
        grad_hidden,
        grad_qkv_weight,
        grad_out_weight,
        grad_up_weight,
        grad_down_weight,
    ) = finish_all(
        qkv_rows, up_rows, down_rows, out_sum, out_rows, hid_rows, hidden, cotangent, small_sum, vec
    )
    return (
        output,
        grad_hidden,
        grad_ln1_gain,
        grad_ln1_bias,
        grad_qkv_weight,
        grad_qkv_bias,
        grad_out_weight,
        grad_out_bias,
        grad_ln2_gain,
        grad_ln2_bias,
        grad_up_weight,
        grad_up_bias,
        grad_down_weight,
        grad_down_bias,
    )


def solution(mesh):
    body = split_body if split_fits(mesh) else general_body
    return jax.shard_map(
        body,
        mesh=mesh,
        in_specs=(
            P("ctx", "fsdp", None),
            P("ctx", "fsdp", None),
            P(),
            P(("ctx", "fsdp")),
            P(("ctx", "fsdp")),
            P(("ctx", "fsdp"), None),
            P(("ctx", "fsdp")),
            P(("ctx", "fsdp"), None),
            P(("ctx", "fsdp")),
            P(("ctx", "fsdp")),
            P(("ctx", "fsdp")),
            P(("ctx", "fsdp"), None),
            P(("ctx", "fsdp")),
            P(("ctx", "fsdp"), None),
            P(("ctx", "fsdp")),
        ),
        out_specs=(
            P("ctx", "fsdp", None),
            P("ctx", "fsdp", None),
            P(("ctx", "fsdp")),
            P(("ctx", "fsdp")),
            P(("ctx", "fsdp"), None),
            P(("ctx", "fsdp")),
            P(("ctx", "fsdp"), None),
            P(("ctx", "fsdp")),
            P(("ctx", "fsdp")),
            P(("ctx", "fsdp")),
            P(("ctx", "fsdp"), None),
            P(("ctx", "fsdp")),
            P(("ctx", "fsdp"), None),
            P(("ctx", "fsdp")),
        ),
        check_vma=False,
    )
```
